32 devices in a mesh: fsdp: 4 (over z), proto: 4 (over y, core), dp: 2 (over x).
Axes of the slice: x: 2, y: 2, z: 4, core: 2. Of those that a mesh axis runs over, the one named last changes fastest.
Arguments:
- teacher_weight: float32 [192, 65536], P(None, ('proto', 'fsdp')), may hold values from -0.4375 to 0.4375
- student_weight: float32 [192, 65536], P(None, ('proto', 'fsdp')), may hold values from -0.4375 to 0.4375
- teacher_feats: bfloat16 [2, 1024, 192], P('dp', 'fsdp'), may hold values from -6 to 6
- student_feats: bfloat16 [2, 1024, 192], P('dp', 'fsdp'), may hold values from -6 to 6
- pairing: int32 [2, 1024], P('dp', 'fsdp'), may hold values from 0 to 255
- center: float32 [65536], P('proto'), may hold values from -10.3 to -3.7
Outputs:
- teacher_new: float32 [192, 65536], P(None, ('proto', 'fsdp'))
- student_grad: float32 [192, 65536], P(None, ('proto', 'fsdp', 'dp'))
The draws below stay inside these ranges and needn't reach their ends.
Inputs may be any that keep to these rules, and one draw needn't show every extreme that they name: pairing[v, r] indexes a crop of the other view in the same block of 256 crops.
All inputs are finite; a program needn't handle non-finite values.
Results may differ from the reference program's by a relative error of at most 0.012.
Values may be sent and summed in bfloat16 or wider, within the bound.
No kernel may reach another device: no remote copies, remote signals or barrier semaphores. Data moves between devices by JAX's collectives and lax.ppermute only.
A program may use at most 128 MiB of HBM per device.

```python
import jax
import jax.numpy as jnp
from jax import lax

BOT = 192
PROTO = 65536
CROP_DEV = 256
CROPS = 1024


def draw_center(key, part):
    key_shift = jax.random.fold_in(key, 11)
    key_rough = jax.random.fold_in(key, 12)
    shift = jax.random.uniform(key_shift, (), jnp.float32, 4.0, 6.0)
    rough = jnp.clip(0.05 * jax.random.normal(key_rough, (PROTO,), jnp.float32), -0.3, 0.3)
    return (rough - shift).astype(jnp.float32)


def with_ends(entries, stream_key, low, top_value):
    spot = [jax.random.randint(jax.random.fold_in(stream_key, axis), (), 0, length) for axis, length in enumerate(entries.shape)]
    longest = entries.shape.index(max(entries.shape))
    next_to = spot[:longest] + [(spot[longest] + 1) % entries.shape[longest]] + spot[longest + 1:]
    return entries.at[tuple(spot)].set(low).at[tuple(next_to)].set(top_value)


def block_levels(own_key, extent, cuts, low, high):
    factor_of, own = 1.0, jax.random.fold_in(own_key, 6)
    for axis_at, parts in cuts:
        steps = jnp.exp(jax.random.uniform(jax.random.fold_in(own, axis_at), (parts,), jnp.float32, low / len(cuts), high / len(cuts)))
        factor_of = factor_of * jnp.repeat(steps, extent[axis_at] // parts).reshape([-1 if axis == axis_at else 1 for axis in range(len(extent))])
    return factor_of


def scatter_about(rng, extent, spread, reach, cuts=(), kind=jnp.bfloat16):
    loudness = block_levels(rng, extent, cuts, -0.22, 0.18) if cuts else 1.0
    values = jax.random.normal(rng, extent, jnp.float32) * spread * loudness
    return jnp.minimum(jnp.maximum(values, -reach), reach).astype(kind)


def setup_inputs(seed: int = 0) -> dict:
    streams_of = jax.random.split(jax.random.key(seed), 7)
    teacher_weight = scatter_about(streams_of[0], (BOT, PROTO), BOT ** -0.5, 0.4375, ((1, 16),), jnp.float32)
    student_weight = scatter_about(streams_of[1], (BOT, PROTO), BOT ** -0.5, 0.4375, ((1, 16),), jnp.float32)
    teacher_feats = scatter_about(streams_of[2], (2, CROPS, BOT), 1.0, 6.0, ((0, 2), (1, 4)))
    student_feats = scatter_about(streams_of[3], (2, CROPS, BOT), 1.0, 6.0, ((0, 2), (1, 4)))
    pairing = with_ends(jax.random.randint(streams_of[4], (2, CROPS), 0, CROP_DEV), jax.random.fold_in(streams_of[4], 1), 0, CROP_DEV - 1).astype(jnp.int32)
    center = draw_center(jax.random.fold_in(streams_of[6], 71), 0)
    return {"teacher_weight": teacher_weight, "student_weight": student_weight, "teacher_feats": teacher_feats, "student_feats": student_feats, "pairing": pairing, "center": center}


def normalize_cols(weights):
    return weights * lax.rsqrt(lax.optimization_barrier(jnp.sum(weights * weights, axis=0, keepdims=True)) + 1e-06)

def normalize_rows(feats):
    values = feats.astype(jnp.float32)
    return values * lax.rsqrt(lax.optimization_barrier(jnp.sum(values * values, axis=-1, keepdims=True)) + 1e-06)

def reference(teacher_weight, student_weight, teacher_feats, student_feats, pairing, center):
    teacher_new = 0.994 * teacher_weight + 0.006 * student_weight
    w_teacher = normalize_cols(teacher_new).astype(jnp.bfloat16)
    w_student = normalize_cols(student_weight).astype(jnp.bfloat16)
    z_teacher = normalize_rows(teacher_feats).astype(jnp.bfloat16)
    z_student = normalize_rows(student_feats).astype(jnp.bfloat16)
    base = jnp.arange(CROPS, dtype=jnp.int32) // CROP_DEV * CROP_DEV
    index = (base[None, :] + pairing).astype(jnp.int32)
    other = z_teacher[::-1]
    paired = jax.vmap(lambda table, rows: jnp.take(table, rows, axis=0))(other, index)
    total_rows = 2 * CROPS
    block = 2 * CROP_DEV
    paired_blocks = paired.reshape(total_rows // block, block, BOT)
    student_blocks = z_student.reshape(total_rows // block, block, BOT)

    def step(grad_sum, pieces):
        zp, zs = pieces
        scores_t = (jnp.dot(zp, w_teacher, preferred_element_type=jnp.float32) - center[None, :]) / 0.04
        probs_t = jax.nn.softmax(scores_t, axis=-1)
        scores_s = jnp.dot(zs, w_student, preferred_element_type=jnp.float32) / 0.1
        probs_s = jax.nn.softmax(scores_s, axis=-1)
        derivs = ((probs_s - probs_t) / 0.1).astype(jnp.bfloat16)
        grad_sum = grad_sum + jnp.dot(zs.T, derivs, preferred_element_type=jnp.float32)
        return (grad_sum, None)
    start = jnp.zeros((BOT, PROTO), jnp.float32)
    grad_sum, _ = lax.scan(step, start, (paired_blocks, student_blocks))
    norms = jnp.sqrt(lax.optimization_barrier(jnp.sum(student_weight * student_weight, axis=0, keepdims=True)) + 1e-06)
    unit = student_weight / norms
    student_grad = (grad_sum - unit * lax.optimization_barrier(jnp.sum(unit * grad_sum, axis=0, keepdims=True))) / norms
    return (teacher_new, student_grad)
```

```python
import functools
import math

import jax
import jax.numpy as jnp
from jax import lax
from jax.experimental import pallas as pl
from jax.experimental.pallas import tpu as pltpu
from jax.sharding import PartitionSpec as P

EPS = 1e-06
DEPTH = 256
ROWS = 256
LOG2E = math.log2(math.e)
GAIN_T = LOG2E / 0.04
GAIN_S = LOG2E / 0.1
LEVELS = (5.35, 8.65)
SPLIT = 7.0
VMEM = 56 * 1024 * 1024


def cast_split(row):
    high = row.astype(jnp.bfloat16).astype(jnp.float32)
    mid = (row - high).astype(jnp.bfloat16).astype(jnp.float32)
    return high, mid, row - high - mid


def prep_kernel(n_own, which, teacher_ref, student_ref, center_ref, all_center_ref, new_ref, wt_ref, ws_ref):
    student = student_ref[...]
    new = 0.994 * teacher_ref[...] + 0.006 * student
    new_ref[...] = new

    @pl.when(pl.program_id(0) < n_own)
    def _():
        bot, width = new.shape
        peak = jnp.max(-all_center_ref[...], axis=1, keepdims=True)
        high, mid, low = cast_split(-center_ref[...] - peak)
        row = lax.broadcasted_iota(jnp.int32, (DEPTH - bot, width), 0)
        zero = jnp.zeros((DEPTH - bot, width), jnp.float32)
        extra = jnp.where(row == 0, high, jnp.where(row == 1, mid, jnp.where(row == 2, low, zero)))
        unit_t = new * lax.rsqrt(jnp.sum(new * new, axis=0, keepdims=True) + EPS)
        unit_s = student * lax.rsqrt(jnp.sum(student * student, axis=0, keepdims=True) + EPS)
        wt_ref[...] = jnp.concatenate([unit_t, extra], axis=0).astype(jnp.bfloat16).T
        ws_ref[...] = jnp.concatenate([unit_s, zero], axis=0).astype(jnp.bfloat16).T


def prepare(teacher_weight, student_weight, center_own, dp, n_dp):
    bot, cols = teacher_weight.shape
    own = cols // n_dp
    width = min(512, own)
    n_own, n_all = own // width, cols // width
    which = jnp.reshape(dp, (1,)).astype(jnp.int32)

    def place(i, which):
        return (0, lax.rem(i + which[0] * n_own, n_all))

    def held(i, which):
        return (lax.min(i, n_own - 1), 0)

    return pl.pallas_call(
        functools.partial(prep_kernel, n_own),
        grid_spec=pltpu.PrefetchScalarGridSpec(
            num_scalar_prefetch=1,
            grid=(n_all,),
            in_specs=[
                pl.BlockSpec((bot, width), place),
                pl.BlockSpec((bot, width), place),
                pl.BlockSpec((1, width), lambda i, which: (0, lax.min(i, n_own - 1))),
                pl.BlockSpec((1, own), lambda i, which: (0, 0)),
            ],
            out_specs=[
                pl.BlockSpec((bot, width), place),
                pl.BlockSpec((width, DEPTH), held),
                pl.BlockSpec((width, DEPTH), held),
            ],
        ),
        out_shape=[
            jax.ShapeDtypeStruct((bot, cols), jnp.float32),
            jax.ShapeDtypeStruct((own, DEPTH), jnp.bfloat16),
            jax.ShapeDtypeStruct((own, DEPTH), jnp.bfloat16),
        ],
        compiler_params=pltpu.CompilerParams(vmem_limit_bytes=VMEM),
        cost_estimate=pl.CostEstimate(flops=20 * bot * cols, bytes_accessed=12 * bot * cols, transcendentals=0),
        name="prep",
    )(which, teacher_weight, student_weight, center_own, center_own)


def score_kernel(teacher, gain, feats_ref, w_ref, *rest):
    if teacher:
        center_ref, exp_ref, total_ref, lhs = rest
    else:
        exp_ref, total_ref, trans_ref, lhs = rest
    bot = feats_ref.shape[1]

    @pl.when(pl.program_id(0) == 0)
    def _():
        half = DEPTH // 2
        lane = lax.broadcasted_iota(jnp.int32, (ROWS, half), 1) + half
        ones = jnp.where((lane >= bot) & (lane < bot + 3), 1.0, 0.0)
        lhs[:, half:] = ones.astype(jnp.bfloat16)

    values = feats_ref[...].astype(jnp.float32)
    unit = (values * lax.rsqrt(jnp.sum(values * values, axis=1, keepdims=True) + EPS)).astype(jnp.bfloat16)
    lhs[:, :bot] = unit
    if not teacher:
        trans_ref[...] = unit.T
    stationary = lhs[...]
    cols = w_ref.shape[0]
    step = min(256, cols)
    total = jnp.zeros((8, ROWS), jnp.float32)
    for at in range(0, cols, step):
        score = lax.dot_general(
            w_ref[at:at + step, :], stationary, (((1,), (1,)), ((), ())), preferred_element_type=jnp.float32
        )
        exps = jnp.exp2(score * gain)
        total = total + jnp.sum(exps.reshape(step // 8, 8, ROWS), axis=0)
        exp_ref[at:at + step, :] = exps.astype(jnp.bfloat16)
    total = jnp.sum(total, axis=0, keepdims=True)
    if teacher:
        peak = jnp.max(-center_ref[...], axis=1, keepdims=True)
        upper = peak >= SPLIT
        scaled = total * jnp.exp2((peak - jnp.where(upper, LEVELS[1], LEVELS[0])) * GAIN_T)
        total_ref[0:1, :] = jnp.where(upper, 0.0, scaled)
        total_ref[1:2, :] = jnp.where(upper, scaled, 0.0)
    else:
        total_ref[...] = total


def scores(teacher, feats, weights, center_own=None):
    rows, bot = feats.shape
    cols = weights.shape[0]
    steps = rows // ROWS
    half = steps // 2 if teacher else 0

    def source(i):
        return (lax.rem(i + half, steps), 0)

    in_specs = [pl.BlockSpec((ROWS, bot), source), pl.BlockSpec((cols, DEPTH), lambda i: (0, 0))]
    args = [feats, weights]
    exp_spec = pl.BlockSpec((cols, ROWS), lambda i: (0, i))
    exp_shape = jax.ShapeDtypeStruct((cols, rows), jnp.bfloat16)
    if teacher:
        in_specs.append(pl.BlockSpec((1, cols), lambda i: (0, 0)))
        args.append(center_own)
        out_specs = [exp_spec, pl.BlockSpec((2, ROWS), lambda i: (0, i))]
        out_shape = [exp_shape, jax.ShapeDtypeStruct((2, rows), jnp.float32)]
    else:
        out_specs = [exp_spec, pl.BlockSpec((1, ROWS), lambda i: (0, i)), pl.BlockSpec((bot, ROWS), lambda i: (0, i))]
        out_shape = [
            exp_shape,
            jax.ShapeDtypeStruct((1, rows), jnp.float32),
            jax.ShapeDtypeStruct((bot, rows), jnp.bfloat16),
        ]
    return pl.pallas_call(
        functools.partial(score_kernel, teacher, GAIN_T if teacher else GAIN_S),
        grid=(steps,),
        in_specs=in_specs,
        out_specs=out_specs,
        out_shape=out_shape,
        scratch_shapes=[pltpu.VMEM((ROWS, DEPTH), jnp.bfloat16)],
        compiler_params=pltpu.CompilerParams(vmem_limit_bytes=VMEM),
        cost_estimate=pl.CostEstimate(
            flops=2 * rows * cols * DEPTH, bytes_accessed=2 * rows * cols, transcendentals=rows * cols
        ),
        name="scores_t" if teacher else "scores_s",
    )(*args)


def grad_kernel(which, exp_s_ref, exp_t_ref, trans_ref, total_s_ref, total_t_ref, center_ref, weight_ref, out_ref, feats_s, feats_t):
    @pl.when(pl.program_id(0) == 0)
    def _():
        feats = trans_ref[...].astype(jnp.float32)
        feats_s[...] = (feats * (10.0 / total_s_ref[...])).astype(jnp.bfloat16)
        peak = jnp.max(-center_ref[...], axis=1, keepdims=True)
        low = jnp.log2(total_t_ref[0:1, :]) + GAIN_T * LEVELS[0]
        high = jnp.log2(total_t_ref[1:2, :]) + GAIN_T * LEVELS[1]
        top = jnp.maximum(low, high)
        log_total = top + jnp.log2(jnp.exp2(low - top) + jnp.exp2(high - top))
        feats_t[...] = (feats * (-10.0 * jnp.exp2(GAIN_T * peak - log_total))).astype(jnp.bfloat16)

    contract = (((1,), (1,)), ((), ()))
    grad = lax.dot_general(exp_s_ref[...], feats_s[...], contract, preferred_element_type=jnp.float32)
    grad = grad + lax.dot_general(exp_t_ref[...], feats_t[...], contract, preferred_element_type=jnp.float32)
    grad = grad.T
    weight = weight_ref[...]
    scale = lax.rsqrt(jnp.sum(weight * weight, axis=0, keepdims=True) + EPS)
    unit = weight * scale
    out_ref[...] = (grad - unit * jnp.sum(unit * grad, axis=0, keepdims=True)) * scale


def gradient(exp_s, exp_t, trans, total_s, total_t, center_own, student_weight, dp):
    cols, rows = exp_s.shape
    bot = trans.shape[0]
    width = min(cols, max(128, (1 << 19) // rows))
    steps = cols // width
    which = jnp.reshape(dp, (1,)).astype(jnp.int32)
    whole = lambda i, which: (0, 0)
    return pl.pallas_call(
        grad_kernel,
        grid_spec=pltpu.PrefetchScalarGridSpec(
            num_scalar_prefetch=1,
            grid=(steps,),
            in_specs=[
                pl.BlockSpec((width, rows), lambda i, which: (i, 0)),
                pl.BlockSpec((width, rows), lambda i, which: (i, 0)),
                pl.BlockSpec((bot, rows), whole),
                pl.BlockSpec((1, rows), whole),
                pl.BlockSpec((2, rows), whole),
                pl.BlockSpec((1, cols), whole),
                pl.BlockSpec((bot, width), lambda i, which: (0, which[0] * steps + i)),
            ],
            out_specs=pl.BlockSpec((bot, width), lambda i, which: (0, i)),
            scratch_shapes=[pltpu.VMEM((bot, rows), jnp.bfloat16), pltpu.VMEM((bot, rows), jnp.bfloat16)],
        ),
        out_shape=jax.ShapeDtypeStruct((bot, cols), jnp.float32),
        compiler_params=pltpu.CompilerParams(vmem_limit_bytes=VMEM),
        cost_estimate=pl.CostEstimate(
            flops=4 * rows * cols * DEPTH, bytes_accessed=4 * rows * cols, transcendentals=0
        ),
        name="gradient",
    )(which, exp_s, exp_t, trans, total_s, total_t, center_own, student_weight)


def shards(teacher_weight, student_weight, teacher_feats, student_feats, pairing, center):
    n_dp = lax.axis_size("dp")
    n_proto = lax.axis_size("proto")
    dp = lax.axis_index("dp")
    everyone = ("dp", "fsdp", "proto")
    crops = student_feats.shape[1]
    share = crops // n_proto
    mine = lax.axis_index("proto") * share

    partner = [(i, i ^ 1) for i in range(n_dp)]
    index = lax.ppermute(lax.dynamic_slice_in_dim(pairing[0], mine, share, 0), "dp", partner)
    feats_s = lax.all_gather(lax.dynamic_slice_in_dim(student_feats[0], mine, share, 0), everyone, axis=0, tiled=True)
    feats_t = lax.all_gather(jnp.take(teacher_feats[0], index, axis=0), everyone, axis=0, tiled=True)

    own = teacher_weight.shape[1] // n_dp
    first = (lax.axis_index("fsdp") * n_dp + dp) * own
    center_own = lax.dynamic_slice_in_dim(center, first, own, 0)[None, :]
    teacher_new, w_t, w_s = prepare(teacher_weight, student_weight, center_own, dp, n_dp)
    exp_s, total_s, trans = scores(False, feats_s, w_s)
    exp_t, total_t = scores(True, feats_t, w_t, center_own)
    total_s, total_t = lax.psum((total_s, total_t), everyone)
    student_grad = gradient(exp_s, exp_t, trans, total_s, total_t, center_own, student_weight, dp)
    return (teacher_new, student_grad)


def solution(mesh):
    placed = (
        P(None, ("proto", "fsdp")),
        P(None, ("proto", "fsdp")),
        P("dp", "fsdp", None),
        P("dp", "fsdp", None),
        P("dp", "fsdp"),
        P("proto"),
    )
    return jax.shard_map(
        shards,
        mesh=mesh,
        in_specs=placed,
        out_specs=(P(None, ("proto", "fsdp")), P(None, ("proto", "fsdp", "dp"))),
        check_vma=False,
    )
```

```python
import functools
import math

import jax
import jax.numpy as jnp
from jax import lax
from jax.experimental import pallas as pl
from jax.experimental.pallas import tpu as pltpu
from jax.sharding import PartitionSpec as P

EPS = 1e-06
DEPTH = 256
ROWS = 512
LOG2E = math.log2(math.e)
GAIN_T = LOG2E / 0.04
GAIN_S = LOG2E / 0.1
LEVELS = (5.35, 8.65)
SPLIT = 7.0
VMEM = 56 * 1024 * 1024


def cast_split(row):
    high = row.astype(jnp.bfloat16).astype(jnp.float32)
    mid = (row - high).astype(jnp.bfloat16).astype(jnp.float32)
    return high, mid, row - high - mid


def prep_kernel(n_own, which, teacher_ref, student_ref, center_ref, all_center_ref, new_ref, wt_ref, ws_ref):
    student = student_ref[...]
    new = 0.994 * teacher_ref[...] + 0.006 * student
    new_ref[...] = new

    @pl.when(pl.program_id(0) < n_own)
    def _():
        bot, width = new.shape
        peak = jnp.max(-all_center_ref[...], axis=1, keepdims=True)
        high, mid, low = cast_split(-center_ref[...] - peak)
        row = lax.broadcasted_iota(jnp.int32, (DEPTH - bot, width), 0)
        zero = jnp.zeros((DEPTH - bot, width), jnp.float32)
        extra = jnp.where(row == 0, high, jnp.where(row == 1, mid, jnp.where(row == 2, low, zero)))
        unit_t = new * lax.rsqrt(jnp.sum(new * new, axis=0, keepdims=True) + EPS)
        unit_s = student * lax.rsqrt(jnp.sum(student * student, axis=0, keepdims=True) + EPS)
        wt_ref[...] = jnp.concatenate([unit_t, extra], axis=0).astype(jnp.bfloat16).T
        ws_ref[...] = jnp.concatenate([unit_s, zero], axis=0).astype(jnp.bfloat16).T


def prepare(teacher_weight, student_weight, center_own, dp, n_dp):
    bot, cols = teacher_weight.shape
    own = cols // n_dp
    width = min(1024, own)
    n_own, n_all = own // width, cols // width
    which = jnp.reshape(dp, (1,)).astype(jnp.int32)

    def place(i, which):
        return (0, lax.rem(i + which[0] * n_own, n_all))

    def held(i, which):
        return (lax.min(i, n_own - 1), 0)

    return pl.pallas_call(
        functools.partial(prep_kernel, n_own),
        grid_spec=pltpu.PrefetchScalarGridSpec(
            num_scalar_prefetch=1,
            grid=(n_all,),
            in_specs=[
                pl.BlockSpec((bot, width), place),
                pl.BlockSpec((bot, width), place),
                pl.BlockSpec((1, width), lambda i, which: (0, lax.min(i, n_own - 1))),
                pl.BlockSpec((1, own), lambda i, which: (0, 0)),
            ],
            out_specs=[
                pl.BlockSpec((bot, width), place),
                pl.BlockSpec((width, DEPTH), held),
                pl.BlockSpec((width, DEPTH), held),
            ],
        ),
        out_shape=[
            jax.ShapeDtypeStruct((bot, cols), jnp.float32),
            jax.ShapeDtypeStruct((own, DEPTH), jnp.bfloat16),
            jax.ShapeDtypeStruct((own, DEPTH), jnp.bfloat16),
        ],
        compiler_params=pltpu.CompilerParams(vmem_limit_bytes=VMEM),
        cost_estimate=pl.CostEstimate(flops=20 * bot * cols, bytes_accessed=12 * bot * cols, transcendentals=0),
        name="prep",
    )(which, teacher_weight, student_weight, center_own, center_own)


def score_kernel(teacher, gain, core, mine_ref, pair_ref, w_ref, *rest):
    if teacher:
        center_ref, exp_ref, total_ref, lhs = rest
    else:
        exp_ref, total_ref, trans_ref, lhs = rest
    bot = mine_ref.shape[1]
    own_half = (pl.program_id(0) * 2 >= pl.num_programs(0)) == (core[0] == 1)

    @pl.when(pl.program_id(0) == 0)
    def _():
        half = DEPTH // 2
        lane = lax.broadcasted_iota(jnp.int32, (ROWS, half), 1) + half
        ones = jnp.where((lane >= bot) & (lane < bot + 3), 1.0, 0.0)
        lhs[:, half:] = ones.astype(jnp.bfloat16)

    values = jnp.where(own_half, mine_ref[...], pair_ref[...]).astype(jnp.float32)
    unit = (values * lax.rsqrt(jnp.sum(values * values, axis=1, keepdims=True) + EPS)).astype(jnp.bfloat16)
    lhs[:, :bot] = unit
    if not teacher:
        trans_ref[...] = unit.T
    stationary = lhs[...]
    cols = w_ref.shape[0]
    step = min(256, cols)
    total = jnp.zeros((8, ROWS), jnp.float32)
    for at in range(0, cols, step):
        score = lax.dot_general(
            w_ref[at:at + step, :], stationary, (((1,), (1,)), ((), ())), preferred_element_type=jnp.float32
        )
        exps = jnp.exp2(score * gain)
        total = total + jnp.sum(exps.reshape(step // 8, 8, ROWS), axis=0)
        exp_ref[0, at:at + step, :] = exps.astype(jnp.bfloat16)
    total = jnp.sum(total, axis=0, keepdims=True)
    if teacher:
        peak = jnp.max(-center_ref[...], axis=1, keepdims=True)
        upper = peak >= SPLIT
        scaled = total * jnp.exp2((peak - jnp.where(upper, LEVELS[1], LEVELS[0])) * GAIN_T)
        total_ref[0:1, :] = jnp.where(upper, 0.0, scaled)
        total_ref[1:2, :] = jnp.where(upper, scaled, 0.0)
    else:
        total_ref[...] = total


def scores(teacher, core, feats, weights, center_own=None):
    held, bot = feats[0].shape
    cols = weights.shape[0]
    rows = 2 * held
    steps = rows // ROWS
    halves = steps // 2
    turn = halves // 2 if teacher else 0

    def source(i, core):
        return (lax.rem(lax.rem(i, halves) + turn, halves), 0)

    def whole(i, core):
        return (0, 0)

    def along(i, core):
        return (0, i)

    in_specs = [pl.BlockSpec((ROWS, bot), source), pl.BlockSpec((ROWS, bot), source), pl.BlockSpec((cols, DEPTH), whole)]
    args = [*feats, weights]
    exp_spec = pl.BlockSpec((1, cols, ROWS), lambda i, core: (i, 0, 0))
    exp_shape = jax.ShapeDtypeStruct((steps, cols, ROWS), jnp.bfloat16)
    if teacher:
        in_specs.append(pl.BlockSpec((1, cols), whole))
        args.append(center_own)
        out_specs = [exp_spec, pl.BlockSpec((2, ROWS), along)]
        out_shape = [exp_shape, jax.ShapeDtypeStruct((2, rows), jnp.float32)]
    else:
        out_specs = [exp_spec, pl.BlockSpec((1, ROWS), along), pl.BlockSpec((bot, ROWS), along)]
        out_shape = [
            exp_shape,
            jax.ShapeDtypeStruct((1, rows), jnp.float32),
            jax.ShapeDtypeStruct((bot, rows), jnp.bfloat16),
        ]
    return pl.pallas_call(
        functools.partial(score_kernel, teacher, GAIN_T if teacher else GAIN_S),
        grid_spec=pltpu.PrefetchScalarGridSpec(
            num_scalar_prefetch=1,
            grid=(steps,),
            in_specs=in_specs,
            out_specs=out_specs,
            scratch_shapes=[pltpu.VMEM((ROWS, DEPTH), jnp.bfloat16)],
        ),
        out_shape=out_shape,
        compiler_params=pltpu.CompilerParams(vmem_limit_bytes=VMEM),
        cost_estimate=pl.CostEstimate(
            flops=2 * rows * cols * DEPTH, bytes_accessed=2 * rows * cols, transcendentals=rows * cols
        ),
        name="scores_t" if teacher else "scores_s",
    )(jnp.reshape(core, (1,)).astype(jnp.int32), *args)


def grad_kernel(which, exp_s_ref, exp_t_ref, trans_ref, total_s_ref, total_t_ref, center_ref, weight_ref, out_ref, acc):
    feats = trans_ref[...].astype(jnp.float32)
    feats_s = (feats * (10.0 / total_s_ref[...])).astype(jnp.bfloat16)
    peak = jnp.max(-center_ref[...], axis=1, keepdims=True)
    low = jnp.log2(total_t_ref[0:1, :]) + GAIN_T * LEVELS[0]
    high = jnp.log2(total_t_ref[1:2, :]) + GAIN_T * LEVELS[1]
    top = jnp.maximum(low, high)
    log_total = top + jnp.log2(jnp.exp2(low - top) + jnp.exp2(high - top))
    feats_t = (feats * (-10.0 * jnp.exp2(GAIN_T * peak - log_total))).astype(jnp.bfloat16)
    cols = acc.shape[0]
    step = min(256, cols)
    first, last = pl.program_id(0) == 0, pl.program_id(0) == pl.num_programs(0) - 1

    @pl.when(first)
    def _():
        acc[...] = jnp.zeros_like(acc)

    contract = (((1,), (1,)), ((), ()))
    for at in range(0, cols, step):
        part = lax.dot_general(exp_s_ref[0, at:at + step, :], feats_s, contract, preferred_element_type=jnp.float32)
        part = part + lax.dot_general(exp_t_ref[0, at:at + step, :], feats_t, contract, preferred_element_type=jnp.float32)
        acc[at:at + step, :] += part

    @pl.when(last)
    def _():
        for at in range(0, cols, step):
            grad = acc[at:at + step, :].T
            weight = weight_ref[:, at:at + step]
            scale = lax.rsqrt(jnp.sum(weight * weight, axis=0, keepdims=True) + EPS)
            unit = weight * scale
            out_ref[:, at:at + step] = (grad - unit * jnp.sum(unit * grad, axis=0, keepdims=True)) * scale


def gradient(exp_s, exp_t, trans, total_s, total_t, center_own, student_weight, dp):
    steps, cols, _ = exp_s.shape
    bot, rows = trans.shape
    which = jnp.reshape(dp, (1,)).astype(jnp.int32)
    block = lambda i, which: (i, 0, 0)
    along = lambda i, which: (0, i)
    return pl.pallas_call(
        grad_kernel,
        grid_spec=pltpu.PrefetchScalarGridSpec(
            num_scalar_prefetch=1,
            grid=(steps,),
            in_specs=[
                pl.BlockSpec((1, cols, ROWS), block),
                pl.BlockSpec((1, cols, ROWS), block),
                pl.BlockSpec((bot, ROWS), along),
                pl.BlockSpec((1, ROWS), along),
                pl.BlockSpec((2, ROWS), along),
                pl.BlockSpec((1, cols), lambda i, which: (0, 0)),
                pl.BlockSpec((bot, cols), lambda i, which: (0, which[0])),
            ],
            out_specs=pl.BlockSpec((bot, cols), lambda i, which: (0, 0)),
            scratch_shapes=[pltpu.VMEM((cols, bot), jnp.float32)],
        ),
        out_shape=jax.ShapeDtypeStruct((bot, cols), jnp.float32),
        compiler_params=pltpu.CompilerParams(vmem_limit_bytes=VMEM),
        cost_estimate=pl.CostEstimate(
            flops=4 * rows * cols * DEPTH, bytes_accessed=4 * rows * cols, transcendentals=0
        ),
        name="gradient",
    )(which, exp_s, exp_t, trans, total_s, total_t, center_own, student_weight)


def spread(shard, axes, n):
    return lax.all_to_all(jnp.broadcast_to(shard[None], (n, *shard.shape)), axes, 0, 0, tiled=True)


def shards(teacher_weight, student_weight, teacher_feats, student_feats, pairing, center):
    n_dp = lax.axis_size("dp")
    n_proto = lax.axis_size("proto")
    dp = lax.axis_index("dp")
    others = ("dp", "fsdp")
    n_others = n_dp * lax.axis_size("fsdp")
    crops, bot = student_feats.shape[1:]
    share = crops // 2
    core = lax.rem(lax.axis_index("proto"), 2)
    mine = core * share

    partner = [(i, i ^ 1) for i in range(n_dp)]
    pair = [(i, i ^ 1) for i in range(n_proto)]
    index = lax.ppermute(lax.dynamic_slice_in_dim(pairing[0], mine, share, 0), "dp", partner)

    def collect(shard):
        held = spread(shard, others, n_others).reshape(n_others * share, bot)
        return held, lax.ppermute(held, "proto", pair)

    feats_s = collect(lax.dynamic_slice_in_dim(student_feats[0], mine, share, 0))
    feats_t = collect(jnp.take(teacher_feats[0], index, axis=0))

    own = teacher_weight.shape[1] // n_dp
    first = (lax.axis_index("fsdp") * n_dp + dp) * own
    center_own = lax.dynamic_slice_in_dim(center, first, own, 0)[None, :]
    teacher_new, w_t, w_s = prepare(teacher_weight, student_weight, center_own, dp, n_dp)
    exp_s, total_s, trans = scores(False, core, feats_s, w_s)
    exp_t, total_t = scores(True, core, feats_t, w_t, center_own)
    totals = jnp.concatenate([total_s, total_t], axis=0)
    totals = jnp.sum(spread(totals, "proto", n_proto), axis=0)
    totals = jnp.sum(spread(totals, others, n_others), axis=0)
    total_s, total_t = totals[:1], totals[1:]
    student_grad = gradient(exp_s, exp_t, trans, total_s, total_t, center_own, student_weight, dp)
    return (teacher_new, student_grad)


def solution(mesh):
    placed = (
        P(None, ("proto", "fsdp")),
        P(None, ("proto", "fsdp")),
        P("dp", "fsdp", None),
        P("dp", "fsdp", None),
        P("dp", "fsdp"),
        P("proto"),
    )
    return jax.shard_map(
        shards,
        mesh=mesh,
        in_specs=placed,
        out_specs=(P(None, ("proto", "fsdp")), P(None, ("proto", "fsdp", "dp"))),
        check_vma=False,
    )
```

```python
import functools
import math

import jax
import jax.numpy as jnp
from jax import lax
from jax.experimental import pallas as pl
from jax.experimental.pallas import tpu as pltpu
from jax.sharding import PartitionSpec as P

EPS = 1e-06
DEPTH = 256
GROUP = 512
STEP = 256
LOG2E = math.log2(math.e)
GAIN_T = LOG2E / 0.04
GAIN_S = LOG2E / 0.1
LIMIT = 24 * 1024 * 1024
ON_CHIP = pl.BlockSpec(memory_space=pltpu.VMEM)
SCALARS = pl.BlockSpec(memory_space=pltpu.SMEM)


def shape(*dims, dtype=jnp.float32):
    return jax.ShapeDtypeStruct(dims, dtype)


def params():
    return pltpu.CompilerParams(vmem_limit_bytes=LIMIT)


def cost(flops=0, moved=0, exps=0):
    return pl.CostEstimate(flops=int(flops), bytes_accessed=int(moved), transcendentals=int(exps))


def cast_split(row):
    high = row.astype(jnp.bfloat16).astype(jnp.float32)
    mid = (row - high).astype(jnp.bfloat16).astype(jnp.float32)
    return high, mid, row - high - mid


def prep_kernel(n_own, which, teacher_ref, student_ref, center_ref, new_ref, wt_ref, ws_ref, peak_ref):
    student = student_ref[...]
    new = 0.994 * teacher_ref[...] + 0.006 * student
    new_ref[...] = new
    i = pl.program_id(0)

    @pl.when(i < n_own)
    def _():
        bot, width = new.shape
        peak = jnp.max(-center_ref[...], axis=1, keepdims=True)
        peak_ref[...] = jnp.broadcast_to(peak, peak_ref.shape)
        high, mid, low = cast_split(-center_ref[:, pl.ds(pl.multiple_of(i * width, width), width)] - peak)
        row = lax.broadcasted_iota(jnp.int32, (DEPTH - bot, width), 0)
        zero = jnp.zeros((DEPTH - bot, width), jnp.float32)
        extra = jnp.where(row == 0, high, jnp.where(row == 1, mid, jnp.where(row == 2, low, zero)))
        unit_t = new * lax.rsqrt(jnp.sum(new * new, axis=0, keepdims=True) + EPS)
        unit_s = student * lax.rsqrt(jnp.sum(student * student, axis=0, keepdims=True) + EPS)
        wt_ref[...] = jnp.concatenate([unit_t, extra], axis=0).astype(jnp.bfloat16).T
        ws_ref[...] = jnp.concatenate([unit_s, zero], axis=0).astype(jnp.bfloat16).T


def prepare(which, teacher_weight, student_weight, center, n_dp):
    bot, cols = teacher_weight.shape
    own = cols // n_dp
    width = min(1024, own)
    n_own, n_all = own // width, cols // width

    def place(i, which):
        return (0, lax.rem(i + which[0] * n_own, n_all))

    def held(i, which):
        return (lax.min(i, n_own - 1), 0)

    return pl.pallas_call(
        functools.partial(prep_kernel, n_own),
        grid_spec=pltpu.PrefetchScalarGridSpec(
            num_scalar_prefetch=1,
            grid=(n_all,),
            in_specs=[
                pl.BlockSpec((bot, width), place),
                pl.BlockSpec((bot, width), place),
                pl.BlockSpec((1, own), lambda i, which: (0, which[1])),
            ],
            out_specs=[
                pl.BlockSpec((bot, width), place),
                pl.BlockSpec((width, DEPTH), held),
                pl.BlockSpec((width, DEPTH), held),
                pl.BlockSpec((1, 128), lambda i, which: (0, 0)),
            ],
        ),
        out_shape=[
            shape(bot, cols),
            pltpu.VMEM((own, DEPTH), jnp.bfloat16),
            pltpu.VMEM((own, DEPTH), jnp.bfloat16),
            shape(1, 128),
        ],
        compiler_params=params(),
        cost_estimate=cost(20 * bot * cols, 12 * bot * cols),
        name="prep",
    )(which, teacher_weight, student_weight, center)


def pack_kernel(which, feats_ref, *rest):
    out_ref = rest[-1]
    half = out_ref.shape[2]
    lower = which[2] == 0
    if len(rest) == 2:
        index = rest[0][...]
        index = jnp.where(lower, index[:, :half], index[:, half:])
        row = lax.broadcasted_iota(jnp.int32, (feats_ref.shape[1], half), 0)
        pick = jnp.where(row == index, 1.0, 0.0).astype(jnp.bfloat16)
        mine = jnp.dot(feats_ref[...], pick, preferred_element_type=jnp.float32).astype(jnp.bfloat16)
    else:
        mine = jnp.where(lower, feats_ref[:, :half], feats_ref[:, half:])
    for i in range(out_ref.shape[0]):
        out_ref[i] = mine


def pack(which, n, feats, index=None):
    bot, crops = feats.shape
    args = [feats] if index is None else [feats, index]
    return pl.pallas_call(
        pack_kernel,
        in_specs=[SCALARS] + [ON_CHIP] * len(args),
        out_specs=ON_CHIP,
        out_shape=shape(n, bot, crops // 2, dtype=jnp.bfloat16),
        compiler_params=params(),
        cost_estimate=cost(2 * bot * crops * crops, n * bot * crops),
        name="pack_s" if index is None else "pack_t",
    )(which, *args)


def log_sum(parts):
    top = functools.reduce(jnp.maximum, parts)
    return top + jnp.log2(sum(jnp.exp2(part - top) for part in parts))


def score_kernel(teacher, last, *refs):
    if last:
        which, refs = refs[0], refs[1:]
        before, refs = refs[:3], refs[3:]
    feats_ref, w_ref, refs = refs[0], refs[1], refs[2:]
    if teacher:
        peak_ref, exp_ref, total_ref = refs
    else:
        exp_ref, total_ref, unit_ref = refs
    n, bot, width = feats_ref.shape
    cols = w_ref.shape[0]
    step = min(STEP, cols)
    per = max(1, min(n, GROUP // width))
    row = lax.broadcasted_iota(jnp.int32, (DEPTH - bot, per * width), 0)
    extra = jnp.where(row < (3 if teacher else 0), 1.0, 0.0).astype(jnp.bfloat16)
    turn = n // 2 if teacher else 0
    totals = []
    for group in range(n // per):
        values = [feats_ref[(group * per + k + turn) % n].astype(jnp.float32) for k in range(per)]
        values = jnp.concatenate(values, axis=1)
        unit = (values * lax.rsqrt(jnp.sum(values * values, axis=0, keepdims=True) + EPS)).astype(jnp.bfloat16)
        lanes = slice(group * per * width, (group + 1) * per * width)
        if not teacher:
            unit_ref[:, lanes] = unit
        held = jnp.concatenate([unit, extra], axis=0)
        total = jnp.zeros((8, per * width), jnp.float32)
        for at in range(0, cols, step):
            score = jnp.dot(w_ref[at:at + step, :], held, preferred_element_type=jnp.float32)
            exps = jnp.exp2(score * (GAIN_T if teacher else GAIN_S))
            total = total + jnp.sum(exps.reshape(step // 8, 8, per * width), axis=0)
            exp_ref[at:at + step, lanes] = exps.astype(jnp.bfloat16)
        totals.append(jnp.sum(total, axis=0, keepdims=True))
    total = jnp.concatenate(totals, axis=1)
    if teacher:
        total = jnp.log2(total) + GAIN_T * peak_ref[:, :1]
    if not last:
        total_ref[...] = total
        return
    lower = which[2] == 0
    s_mine, s_pair, t_mine = [ref[...] for ref in before]
    rows = [
        jnp.where(lower, s_mine, s_pair),
        jnp.where(lower, s_pair, s_mine),
        jnp.where(lower, t_mine, total),
        jnp.where(lower, total, t_mine),
    ]
    rows = jnp.concatenate(rows, axis=0)
    for i in range(total_ref.shape[0]):
        total_ref[i] = rows


def scores(teacher, feats, weights, peak=None, last=None):
    n, bot, width = feats.shape
    cols = weights.shape[0]
    rows = n * width
    args, in_specs = [feats, weights], [ON_CHIP] * 2
    if teacher:
        args, in_specs = args + [peak], in_specs + [ON_CHIP]
    if last is not None:
        which, copies, before = last
        args, in_specs = [which, *before, *args], [SCALARS] + [ON_CHIP] * 3 + in_specs
    out_shape = [
        pltpu.VMEM((cols, rows), jnp.bfloat16),
        shape(1, rows) if last is None else shape(copies, 4, rows),
    ]
    if not teacher:
        out_shape.append(pltpu.VMEM((bot, rows), jnp.bfloat16))
    return pl.pallas_call(
        functools.partial(score_kernel, teacher, last is not None),
        in_specs=in_specs,
        out_specs=[ON_CHIP] * len(out_shape),
        out_shape=out_shape,
        compiler_params=params(),
        cost_estimate=cost(2 * rows * cols * DEPTH, 2 * rows * cols, rows * cols),
        name="scores_t" if teacher else "scores_s",
    )(*args)


def combine(parts):
    total_s = sum(part[:2] for part in parts)
    return total_s, log_sum([part[2:] for part in parts])


def relay_kernel(in_ref, out_ref):
    rows = jnp.concatenate(combine([in_ref[i] for i in range(in_ref.shape[0])]), axis=0)
    for i in range(out_ref.shape[0]):
        out_ref[i] = rows


def relay(parts, copies):
    return pl.pallas_call(
        relay_kernel,
        in_specs=[ON_CHIP],
        out_specs=ON_CHIP,
        out_shape=shape(copies, *parts.shape[1:]),
        compiler_params=params(),
        cost_estimate=cost(0, copies * parts[0].size * 4),
        name="relay",
    )(parts)


def grad_kernel(which, totals_ref, peak_ref, unit_a, unit_b, exps_a, exps_b, expt_a, expt_b, weight_ref, out_ref):
    total_s, log_t = combine([totals_ref[i] for i in range(totals_ref.shape[0])])
    scale_s = 10.0 / total_s
    scale_t = -10.0 * jnp.exp2(GAIN_T * peak_ref[:, :1] - log_t)
    lower = which[2] == 0
    sides = []
    for at, unit_ref, exp_s, exp_t in ((0, unit_a, exps_a, expt_a), (1, unit_b, exps_b, expt_b)):
        unit = unit_ref[...].astype(jnp.float32)
        for scale, exp_ref in ((scale_s, exp_s), (scale_t, exp_t)):
            mine = jnp.where(lower, scale[at:at + 1], scale[1 - at:2 - at])
            sides.append(((unit * mine).astype(jnp.bfloat16), exp_ref))
    cols = weight_ref.shape[1]
    step = min(512, cols)
    for at in range(0, cols, step):
        grad = sum(
            lax.dot_general(
                exp_ref[at:at + step, :], feats, (((1,), (1,)), ((), ())), preferred_element_type=jnp.float32
            )
            for feats, exp_ref in sides
        )
        grad = grad.T
        weight = weight_ref[:, at:at + step]
        scale = lax.rsqrt(jnp.sum(weight * weight, axis=0, keepdims=True) + EPS)
        unit = weight * scale
        out_ref[:, at:at + step] = (grad - unit * jnp.sum(unit * grad, axis=0, keepdims=True)) * scale


def gradient(which, totals, peak, units, exps_s, exps_t, student_weight):
    cols, rows = exps_s[0].shape
    bot = units[0].shape[0]
    own = lambda i, which: (0, which[0])
    whole = ON_CHIP
    return pl.pallas_call(
        grad_kernel,
        grid_spec=pltpu.PrefetchScalarGridSpec(
            num_scalar_prefetch=1,
            grid=(1,),
            in_specs=[whole] * 8 + [pl.BlockSpec((bot, cols), own)],
            out_specs=pl.BlockSpec((bot, cols), lambda i, which: (0, 0)),
        ),
        out_shape=shape(bot, cols),
        compiler_params=params(),
        cost_estimate=cost(8 * rows * cols * DEPTH, 8 * bot * cols),
        name="gradient",
    )(which, totals, peak, *units, *exps_s, *exps_t, student_weight)


def shards(teacher_weight, student_weight, teacher_feats, student_feats, pairing, center):
    n_dp, n_fsdp, n_proto = [lax.axis_size(axis) for axis in ("dp", "fsdp", "proto")]
    dp = lax.axis_index("dp")
    others = ("dp", "fsdp")
    n_others = n_dp * n_fsdp
    core = lax.rem(lax.axis_index("proto"), 2)
    which = jnp.stack([dp, lax.axis_index("fsdp") * n_dp + dp, core]).astype(jnp.int32)

    def spread(copies, axes):
        return lax.all_to_all(copies, axes, 0, 0, tiled=True)

    def from_pair(mine):
        return lax.ppermute(mine, "proto", [(i, i ^ 1) for i in range(n_proto)])

    index = lax.ppermute(pairing, "dp", [(i, i ^ 1) for i in range(n_dp)])
    mine_s = spread(pack(which, n_others, student_feats[0].T), others)
    mine_t = spread(pack(which, n_others, teacher_feats[0].T, index), others)
    teacher_new, w_t, w_s, peak = prepare(which, teacher_weight, student_weight, center[None, :], n_dp)
    pair_s = from_pair(mine_s)
    exps_a, total_a, unit_a = scores(False, mine_s, w_s)
    exps_b, total_b, unit_b = scores(False, pair_s, w_s)
    pair_t = from_pair(mine_t)
    expt_a, total_c = scores(True, mine_t, w_t, peak)
    expt_b, totals = scores(True, pair_t, w_t, peak, (which, n_proto, (total_a, total_b, total_c)))
    totals = spread(relay(spread(totals, "proto"), n_others), others)
    student_grad = gradient(which, totals, peak, (unit_a, unit_b), (exps_a, exps_b), (expt_a, expt_b), student_weight)
    return (teacher_new, student_grad)


def solution(mesh):
    placed = (
        P(None, ("proto", "fsdp")),
        P(None, ("proto", "fsdp")),
        P("dp", "fsdp", None),
        P("dp", "fsdp", None),
        P("dp", "fsdp"),
        P("proto"),
    )
    return jax.shard_map(
        shards,
        mesh=mesh,
        in_specs=placed,
        out_specs=(P(None, ("proto", "fsdp")), P(None, ("proto", "fsdp", "dp"))),
        check_vma=False,
    )
```

```python
import functools
import math

import jax
import jax.numpy as jnp
from jax import lax
from jax.experimental import pallas as pl
from jax.experimental.pallas import tpu as pltpu
from jax.sharding import PartitionSpec as P

EPS = 1e-06
DEPTH = 256
GROUP = 512
STEP = 256
LOG2E = math.log2(math.e)
GAIN_T = LOG2E / 0.04
GAIN_S = LOG2E / 0.1
LIMIT = 24 * 1024 * 1024
ON_CHIP = pl.BlockSpec(memory_space=pltpu.VMEM)
SCALARS = pl.BlockSpec(memory_space=pltpu.SMEM)


def shape(*dims, dtype=jnp.float32):
    return jax.ShapeDtypeStruct(dims, dtype)


def params():
    return pltpu.CompilerParams(vmem_limit_bytes=LIMIT)


def cost(flops=0, moved=0, exps=0):
    return pl.CostEstimate(flops=int(flops), bytes_accessed=int(moved), transcendentals=int(exps))


def cast_split(row):
    high = row.astype(jnp.bfloat16).astype(jnp.float32)
    mid = (row - high).astype(jnp.bfloat16).astype(jnp.float32)
    return high, mid, row - high - mid


def prep_kernel(n_own, which, teacher_ref, student_ref, center_ref, new_ref, wt_ref, ws_ref, peak_ref):
    student = student_ref[...]
    new = 0.994 * teacher_ref[...] + 0.006 * student
    new_ref[...] = new
    i = pl.program_id(0)

    @pl.when(i < n_own)
    def _():
        bot, width = new.shape
        peak = jnp.max(-center_ref[...], axis=1, keepdims=True)
        peak_ref[...] = jnp.broadcast_to(peak, peak_ref.shape)
        high, mid, low = cast_split(-center_ref[:, pl.ds(pl.multiple_of(i * width, width), width)] - peak)
        row = lax.broadcasted_iota(jnp.int32, (DEPTH - bot, width), 0)
        zero = jnp.zeros((DEPTH - bot, width), jnp.float32)
        extra = jnp.where(row == 0, high, jnp.where(row == 1, mid, jnp.where(row == 2, low, zero)))
        unit_t = new * lax.rsqrt(jnp.sum(new * new, axis=0, keepdims=True) + EPS)
        unit_s = student * lax.rsqrt(jnp.sum(student * student, axis=0, keepdims=True) + EPS)
        wt_ref[...] = jnp.concatenate([unit_t, extra], axis=0).astype(jnp.bfloat16).T
        ws_ref[...] = jnp.concatenate([unit_s, zero], axis=0).astype(jnp.bfloat16).T


def prepare(which, teacher_weight, student_weight, center, n_dp):
    bot, cols = teacher_weight.shape
    teacher_weight = pltpu.with_memory_space_constraint(teacher_weight, pltpu.HBM)
    student_weight = pltpu.with_memory_space_constraint(student_weight, pltpu.HBM)
    own = cols // n_dp
    width = min(1024, own)
    n_own, n_all = own // width, cols // width

    def place(i, which):
        return (0, lax.rem(i + which[0] * n_own, n_all))

    def held(i, which):
        return (lax.min(i, n_own - 1), 0)

    return pl.pallas_call(
        functools.partial(prep_kernel, n_own),
        grid_spec=pltpu.PrefetchScalarGridSpec(
            num_scalar_prefetch=1,
            grid=(n_all,),
            in_specs=[
                pl.BlockSpec((bot, width), place),
                pl.BlockSpec((bot, width), place),
                pl.BlockSpec((1, own), lambda i, which: (0, which[1])),
            ],
            out_specs=[
                pl.BlockSpec((bot, width), place),
                pl.BlockSpec((width, DEPTH), held),
                pl.BlockSpec((width, DEPTH), held),
                pl.BlockSpec((1, 128), lambda i, which: (0, 0)),
            ],
        ),
        out_shape=[
            shape(bot, cols),
            pltpu.VMEM((own, DEPTH), jnp.bfloat16),
            pltpu.VMEM((own, DEPTH), jnp.bfloat16),
            shape(1, 128),
        ],
        compiler_params=params(),
        cost_estimate=cost(20 * bot * cols, 12 * bot * cols),
        name="prep",
    )(which, teacher_weight, student_weight, center)


def pack_kernel(which, feats_ref, *rest):
    out_ref = rest[-1]
    half = out_ref.shape[2]
    lower = which[2] == 0
    if len(rest) > 1:
        index = rest[0][...]
        index = jnp.where(lower, index[:, :half], index[:, half:])
        row = lax.broadcasted_iota(jnp.int32, (feats_ref.shape[1], half), 0)
        pick = jnp.where(row == index, 1.0, 0.0).astype(jnp.bfloat16)
        mine = jnp.dot(feats_ref[...], pick, preferred_element_type=jnp.float32).astype(jnp.bfloat16)
    else:
        mine = jnp.where(lower, feats_ref[:, :half], feats_ref[:, half:])
    for i in range(out_ref.shape[0]):
        out_ref[i] = mine


def pack(which, n, feats, index=None, after=None):
    bot, crops = feats.shape
    args = [feats] if index is None else [feats, index, after]
    return pl.pallas_call(
        pack_kernel,
        in_specs=[SCALARS] + [ON_CHIP] * len(args),
        out_specs=ON_CHIP,
        out_shape=shape(n, bot, crops // 2, dtype=jnp.bfloat16),
        compiler_params=params(),
        cost_estimate=cost(2 * bot * crops * crops, n * bot * crops),
        name="pack_s" if index is None else "pack_t",
    )(which, *args)


def gate_kernel(feats_ref, after_ref, out_ref):
    pass


def gate(feats, after):
    return pl.pallas_call(
        gate_kernel,
        in_specs=[pl.BlockSpec(memory_space=pl.ANY)] * 2,
        out_specs=pl.BlockSpec(memory_space=pl.ANY),
        out_shape=pltpu.VMEM(feats.shape, feats.dtype),
        input_output_aliases={0: 0},
        compiler_params=params(),
        cost_estimate=cost(),
        name="gate",
    )(feats, after)


def log_sum(parts):
    top = functools.reduce(jnp.maximum, parts)
    return top + jnp.log2(sum(jnp.exp2(part - top) for part in parts))


def by_view(which, rows):
    half = rows.shape[1] // 2
    return jnp.where(which[0] == 0, rows, jnp.concatenate([rows[:, half:], rows[:, :half]], axis=1))


def score_kernel(teacher, last, *refs):
    if last:
        which, refs = refs[0], refs[1:]
        before, refs = refs[:3], refs[3:]
    feats_refs, w_ref, refs = refs[:2], refs[2], refs[3:]
    if teacher:
        peak_ref, exp_ref, total_ref = refs
    else:
        exp_ref, total_ref, unit_ref = refs
    n, bot, width = feats_refs[0].shape
    cols = w_ref.shape[0]
    step = min(STEP, cols)
    per = max(1, min(n, GROUP // width))
    row = lax.broadcasted_iota(jnp.int32, (DEPTH - bot, per * width), 0)
    extra = jnp.where(row < (3 if teacher else 0), 1.0, 0.0).astype(jnp.bfloat16)
    totals = []
    for group in range(2 * n // per):
        at = [divmod(group * per + k, n) for k in range(per)]
        values = [feats_refs[view][block].astype(jnp.float32) for view, block in at]
        values = jnp.concatenate(values, axis=1)
        unit = (values * lax.rsqrt(jnp.sum(values * values, axis=0, keepdims=True) + EPS)).astype(jnp.bfloat16)
        lanes = slice(group * per * width, (group + 1) * per * width)
        if not teacher:
            unit_ref[:, lanes] = unit
        held = jnp.concatenate([unit, extra], axis=0)
        total = jnp.zeros((8, per * width), jnp.float32)
        for at in range(0, cols, step):
            score = jnp.dot(w_ref[at:at + step, :], held, preferred_element_type=jnp.float32)
            exps = jnp.exp2(score * (GAIN_T if teacher else GAIN_S))
            total = total + jnp.sum(exps.reshape(step // 8, 8, per * width), axis=0)
            exp_ref[at:at + step, lanes] = exps.astype(jnp.bfloat16)
        totals.append(jnp.sum(total, axis=0, keepdims=True))
    total = jnp.concatenate(totals, axis=1)
    if teacher:
        total = jnp.log2(total) + GAIN_T * peak_ref[:, :1]
    if not last:
        total_ref[...] = total
        return
    lower = which[2] == 0
    s_mine, s_pair, t_mine = [ref[...] for ref in before]
    rows = [
        jnp.where(lower, s_mine, s_pair),
        jnp.where(lower, s_pair, s_mine),
        jnp.where(lower, t_mine, total),
        jnp.where(lower, total, t_mine),
    ]
    rows = by_view(which, jnp.concatenate(rows, axis=0))
    for i in range(total_ref.shape[0]):
        total_ref[i] = rows


def scores(teacher, feats, weights, peak=None, last=None):
    n, bot, width = feats[0].shape
    cols = weights.shape[0]
    rows = 2 * n * width
    args, in_specs = [*feats, weights], [ON_CHIP] * 3
    if teacher:
        args, in_specs = args + [peak], in_specs + [ON_CHIP]
    if last is not None:
        which, copies, before = last
        args, in_specs = [which, *before, *args], [SCALARS] + [ON_CHIP] * 3 + in_specs
    out_shape = [
        pltpu.VMEM((cols, rows), jnp.bfloat16),
        shape(1, rows) if last is None else shape(copies, 4, rows),
    ]
    if not teacher:
        out_shape.append(pltpu.VMEM((bot, rows), jnp.bfloat16))
    return pl.pallas_call(
        functools.partial(score_kernel, teacher, last is not None),
        in_specs=in_specs,
        out_specs=[ON_CHIP] * len(out_shape),
        out_shape=out_shape,
        compiler_params=params(),
        cost_estimate=cost(2 * rows * cols * DEPTH, 2 * rows * cols, rows * cols),
        name="scores_t" if teacher else "scores_s",
    )(*args)


def combine(parts):
    total_s = sum(part[:2] for part in parts)
    return total_s, log_sum([part[2:] for part in parts])


def relay_kernel(in_ref, out_ref):
    rows = jnp.concatenate(combine([in_ref[i] for i in range(in_ref.shape[0])]), axis=0)
    for i in range(out_ref.shape[0]):
        out_ref[i] = rows


def relay(parts, copies):
    return pl.pallas_call(
        relay_kernel,
        in_specs=[ON_CHIP],
        out_specs=ON_CHIP,
        out_shape=shape(copies, *parts.shape[1:]),
        compiler_params=params(),
        cost_estimate=cost(0, copies * parts[0].size * 4),
        name="relay",
    )(parts)


def grad_kernel(which, totals_ref, peak_ref, unit_a, unit_b, exps_a, exps_b, expt_a, expt_b, weight_ref, out_ref):
    total_s, log_t = combine([totals_ref[i] for i in range(totals_ref.shape[0])])
    scale_s = by_view(which, 10.0 / total_s)
    scale_t = by_view(which, -10.0 * jnp.exp2(GAIN_T * peak_ref[:, :1] - log_t))
    lower = which[2] == 0
    sides = []
    for at, unit_ref, exp_s, exp_t in ((0, unit_a, exps_a, expt_a), (1, unit_b, exps_b, expt_b)):
        unit = unit_ref[...].astype(jnp.float32)
        for scale, exp_ref in ((scale_s, exp_s), (scale_t, exp_t)):
            mine = jnp.where(lower, scale[at:at + 1], scale[1 - at:2 - at])
            sides.append(((unit * mine).astype(jnp.bfloat16), exp_ref))
    cols = weight_ref.shape[1]
    step = min(512, cols)
    for at in range(0, cols, step):
        grad = sum(
            lax.dot_general(
                exp_ref[at:at + step, :], feats, (((1,), (1,)), ((), ())), preferred_element_type=jnp.float32
            )
            for feats, exp_ref in sides
        )
        grad = grad.T
        weight = weight_ref[:, at:at + step]
        scale = lax.rsqrt(jnp.sum(weight * weight, axis=0, keepdims=True) + EPS)
        unit = weight * scale
        out_ref[:, at:at + step] = (grad - unit * jnp.sum(unit * grad, axis=0, keepdims=True)) * scale


def gradient(which, totals, peak, units, exps_s, exps_t, student_weight):
    cols, rows = exps_s[0].shape
    bot = units[0].shape[0]
    own = lambda i, which: (0, which[0])
    whole = ON_CHIP
    return pl.pallas_call(
        grad_kernel,
        grid_spec=pltpu.PrefetchScalarGridSpec(
            num_scalar_prefetch=1,
            grid=(1,),
            in_specs=[whole] * 8 + [pl.BlockSpec((bot, cols), own)],
            out_specs=pl.BlockSpec((bot, cols), lambda i, which: (0, 0)),
        ),
        out_shape=shape(bot, cols),
        compiler_params=params(),
        cost_estimate=cost(8 * rows * cols * DEPTH, 8 * bot * cols),
        name="gradient",
    )(which, totals, peak, *units, *exps_s, *exps_t, student_weight)


def shards(teacher_weight, student_weight, teacher_feats, student_feats, pairing, center):
    n_dp, n_fsdp, n_proto = [lax.axis_size(axis) for axis in ("dp", "fsdp", "proto")]
    dp = lax.axis_index("dp")
    others = ("dp", "fsdp")
    n_others = n_dp * n_fsdp
    core = lax.rem(lax.axis_index("proto"), 2)
    which = jnp.stack([dp, lax.axis_index("fsdp") * n_dp + dp, core]).astype(jnp.int32)

    def spread(copies, axes):
        return lax.all_to_all(copies, axes, 0, 0, tiled=True)

    def from_pair(mine):
        return lax.ppermute(mine, "proto", [(i, i ^ 1) for i in range(n_proto)])

    def from_view(mine):
        return lax.ppermute(mine, "dp", [(i, i ^ 1) for i in range(n_dp)])

    index = from_view(pairing)
    own_s = spread(pack(which, n_fsdp, student_feats[0].T), "fsdp")
    teacher_new, w_t, w_s, peak = prepare(which, teacher_weight, student_weight, center[None, :], n_dp)
    own_t = spread(pack(which, n_fsdp, teacher_feats[0].T, index, peak), "fsdp")
    other_s = from_view(own_s)
    exps_a, total_a, unit_a = scores(False, (own_s, other_s), w_s)
    exps_b, total_b, unit_b = scores(False, (from_pair(own_s), from_pair(other_s)), w_s)
    other_t = gate(from_view(own_t), total_b)
    expt_a, total_c = scores(True, (other_t, own_t), w_t, peak)
    last = (which, n_proto, (total_a, total_b, total_c))
    expt_b, totals = scores(True, (from_pair(other_t), from_pair(own_t)), w_t, peak, last)
    totals = spread(relay(spread(totals, "proto"), n_others), others)
    student_grad = gradient(which, totals, peak, (unit_a, unit_b), (exps_a, exps_b), (expt_a, expt_b), student_weight)
    return (teacher_new, student_grad)


def solution(mesh):
    placed = (
        P(None, ("proto", "fsdp")),
        P(None, ("proto", "fsdp")),
        P("dp", "fsdp", None),
        P("dp", "fsdp", None),
        P("dp", "fsdp"),
        P("proto"),
    )
    return jax.shard_map(
        shards,
        mesh=mesh,
        in_specs=placed,
        out_specs=(P(None, ("proto", "fsdp")), P(None, ("proto", "fsdp", "dp"))),
        check_vma=False,
    )
```

```python
import functools
import math

import jax
import jax.numpy as jnp
from jax import lax
from jax.experimental import pallas as pl
from jax.experimental.pallas import tpu as pltpu
from jax.sharding import PartitionSpec as P

EPS = 1e-06
DEPTH = 256
GROUP = 512
STEP = 256
DIRECT = 8
LOG2E = math.log2(math.e)
GAIN_T = LOG2E / 0.04
GAIN_S = LOG2E / 0.1
LIMIT = 24 * 1024 * 1024
ON_CHIP = pl.BlockSpec(memory_space=pltpu.VMEM)
IN_HBM = pl.BlockSpec(memory_space=pl.ANY)


def shape(*dims, dtype=jnp.float32):
    return jax.ShapeDtypeStruct(dims, dtype)


def held(*dims, dtype=jnp.float32):
    return pltpu.VMEM(dims, dtype)


def call(kernel, name, out_shape, args, cost=(0, 0, 0), **more):
    many = isinstance(out_shape, (list, tuple))
    specs = dict(in_specs=[ON_CHIP] * len(args), out_specs=[ON_CHIP] * len(out_shape) if many else ON_CHIP)
    flops, moved, exps = map(int, cost)
    return pl.pallas_call(
        kernel,
        out_shape=out_shape,
        compiler_params=pltpu.CompilerParams(vmem_limit_bytes=LIMIT),
        cost_estimate=pl.CostEstimate(flops=flops, bytes_accessed=moved, transcendentals=exps),
        name=name,
        **{**specs, **more},
    )(*args)


def here():
    return lax.axis_index("dp"), lax.axis_index("fsdp"), lax.rem(lax.axis_index("proto"), 2)


def cast_split(row):
    high = row.astype(jnp.bfloat16).astype(jnp.float32)
    mid = (row - high).astype(jnp.bfloat16).astype(jnp.float32)
    return high, mid, row - high - mid


def prep_kernel(n_dp, teacher_hbm, student_hbm, center_ref, new_hbm, wt_ref, ws_ref, unit_ref, scale_ref, peak_ref, *scratch):
    teacher_buf, student_buf, new_buf, in_t, in_s, out = scratch
    chunks, bot, width = new_buf.shape
    own = chunks // n_dp
    dp, fsdp, _ = here()
    at = [slice(i * width, (i + 1) * width) for i in range(chunks)]
    loads = [
        (
            pltpu.make_async_copy(teacher_hbm.at[:, at[i]], teacher_buf.at[i], in_t.at[i]),
            pltpu.make_async_copy(student_hbm.at[:, at[i]], student_buf.at[i], in_s.at[i]),
        )
        for i in range(chunks)
    ]
    stores = [pltpu.make_async_copy(new_buf.at[i], new_hbm.at[:, at[i]], out.at[i]) for i in range(chunks)]
    for pair in loads:
        for load in pair:
            load.start()
    start = pl.multiple_of((fsdp * n_dp + dp) * (own * width), 128)
    center = center_ref[:, pl.ds(start, own * width)]
    peak = jnp.max(-center, axis=1, keepdims=True)
    peak_ref[...] = jnp.broadcast_to(peak, peak_ref.shape)
    splits = cast_split(-center - peak)
    for i in range(chunks):
        for load in loads[i]:
            load.wait()
        student = student_buf[i]
        new = 0.994 * teacher_buf[i] + 0.006 * student
        new_buf[i] = new
        stores[i].start()

        @pl.when(dp == i // own)
        def _():
            to = at[i % own]
            high, mid, low = [part[:, to] for part in splits]
            row = lax.broadcasted_iota(jnp.int32, (DEPTH - bot, width), 0)
            zero = jnp.zeros((DEPTH - bot, width), jnp.float32)
            extra = jnp.where(row == 0, high, jnp.where(row == 1, mid, jnp.where(row == 2, low, zero)))
            scale = lax.rsqrt(jnp.sum(student * student, axis=0, keepdims=True) + EPS)
            unit_s = student * scale
            unit_t = new * lax.rsqrt(jnp.sum(new * new, axis=0, keepdims=True) + EPS)
            wt_ref[to, :] = jnp.concatenate([unit_t, extra], axis=0).astype(jnp.bfloat16).T
            ws_ref[to, :] = jnp.concatenate([unit_s, zero], axis=0).astype(jnp.bfloat16).T
            unit_ref[:, to] = unit_s
            scale_ref[:, to] = scale

    for store in stores:
        store.wait()


def prepare(teacher_weight, student_weight, center, n_dp):
    bot, cols = teacher_weight.shape
    own = cols // n_dp
    width = min(512, own)
    chunks = cols // width
    teacher_weight = pltpu.with_memory_space_constraint(teacher_weight, pltpu.HBM)
    student_weight = pltpu.with_memory_space_constraint(student_weight, pltpu.HBM)
    return call(
        functools.partial(prep_kernel, n_dp),
        "prep",
        [
            pltpu.HBM((bot, cols), jnp.float32),
            held(own, DEPTH, dtype=jnp.bfloat16),
            held(own, DEPTH, dtype=jnp.bfloat16),
            held(bot, own),
            held(1, own),
            held(1, 128),
        ],
        (teacher_weight, student_weight, center),
        (20 * bot * cols, 12 * bot * cols, 0),
        in_specs=[IN_HBM, IN_HBM, ON_CHIP],
        out_specs=[IN_HBM] + [ON_CHIP] * 5,
        scratch_shapes=[held(chunks, bot, width)] * 3 + [pltpu.SemaphoreType.DMA((chunks,))] * 3,
    )


def pack_kernel(student_ref, teacher_ref, index_ref, out_ref):
    half = out_ref.shape[2]
    lower = here()[2] == 0
    out_ref[0] = jnp.where(lower, student_ref[:, :half], student_ref[:, half:])
    index = jnp.where(lower, index_ref[:, :half], index_ref[:, half:])
    row = lax.broadcasted_iota(jnp.int32, (teacher_ref.shape[1], half), 0)
    pick = jnp.where(row == index, 1.0, 0.0).astype(jnp.bfloat16)
    out_ref[1] = jnp.dot(teacher_ref[...], pick, preferred_element_type=jnp.float32).astype(jnp.bfloat16)


def pack(student, teacher, index):
    bot, crops = student.shape
    return call(pack_kernel, "pack", held(2, bot, crops // 2, dtype=jnp.bfloat16), (student, teacher, index))


def join_kernel(n_in, n_after, *refs):
    blocks = []
    for ref in refs[:n_in]:
        blocks += [ref] if len(ref.shape) == 3 else [ref.at[i] for i in range(ref.shape[0])]
    for ref in refs[n_in + n_after:]:
        skip = len(blocks) - ref.shape[0]
        for i in range(ref.shape[0]):
            ref[i] = blocks[skip + i][...]


def join(parts, counts, after):
    block = parts[0].shape[-3:]
    outs = [held(count, *block, dtype=jnp.bfloat16) for count in counts]
    kernel = functools.partial(join_kernel, len(parts), len(after))
    return call(kernel, "join", outs, (*parts, *after), in_specs=[ON_CHIP] * len(parts) + [IN_HBM] * len(after))


def log_sum(parts):
    top = functools.reduce(jnp.maximum, parts)
    return top + jnp.log2(sum(jnp.exp2(part - top) for part in parts))


def combine(parts):
    half = parts[0].shape[0] // 2
    return sum(part[:half] for part in parts), log_sum([part[half:] for part in parts])


def slot(k, n):
    return lax.axis_index("fsdp") ^ k if n <= DIRECT else k


def score_kernel(last, *refs):
    before, refs = (refs[:3], refs[3:]) if last else ((), refs)
    feats_ref, ws_ref, wt_ref, peak_ref, exps_ref, expt_ref, unit_ref, total_ref, *mine = refs
    own_ref = mine[0] if last else total_ref
    n, _, bot, width = feats_ref.shape
    cols = ws_ref.shape[0]
    step = min(STEP, cols)
    per = max(1, min(n, GROUP // width))
    row = lax.broadcasted_iota(jnp.int32, (DEPTH - bot, per * width), 0)
    for which, w_ref, exp_ref, gain in ((0, ws_ref, exps_ref, GAIN_S), (1, wt_ref, expt_ref, GAIN_T)):
        extra = jnp.where(row < 3 * which, 1.0, 0.0).astype(jnp.bfloat16)
        for group in range(n // per):
            values = [feats_ref[group * per + k, which].astype(jnp.float32) for k in range(per)]
            values = jnp.concatenate(values, axis=1)
            unit = (values * lax.rsqrt(jnp.sum(values * values, axis=0, keepdims=True) + EPS)).astype(jnp.bfloat16)
            lanes = slice(group * per * width, (group + 1) * per * width)
            if which == 0:
                unit_ref[:, lanes] = unit
            stationary = jnp.concatenate([unit, extra], axis=0)
            total = jnp.zeros((8, per * width), jnp.float32)
            for at in range(0, cols, step):
                score = jnp.dot(w_ref[at:at + step, :], stationary, preferred_element_type=jnp.float32)
                exps = jnp.exp2(score * gain)
                total = total + jnp.sum(exps.reshape(step // 8, 8, per * width), axis=0)
                exp_ref[at:at + step, lanes] = exps.astype(jnp.bfloat16)
            total = jnp.sum(total, axis=0, keepdims=True)
            if which == 1:
                total = jnp.log2(total) + GAIN_T * peak_ref[:, :1]
            own_ref[which:which + 1, lanes] = total
    if not last:
        return
    dp, _, core = here()
    own, pair, other = before
    parts = ((own, other), (pair, own_ref))
    rows = []
    for which in (0, 1):
        for half in (0, 1):
            pieces = []
            for view in (0, 1):
                first = (dp == view) if which == 0 else (dp != view)
                for place in range(n):
                    at = pl.ds(pl.multiple_of(slot(place, n) * width, width), width)
                    read = [[part[which:which + 1, at] for part in side] for side in parts]
                    mine, theirs = [jnp.where(first, *side) for side in read]
                    pieces.append(jnp.where(core == half, mine, theirs))
            rows.append(jnp.concatenate(pieces, axis=1))
    rows = jnp.concatenate(rows, axis=0)
    for i in range(total_ref.shape[0]):
        total_ref[i] = rows


def scores(feats, ws, wt, peak, last=None):
    n, _, bot, width = feats.shape
    cols, rows = ws.shape[0], n * width
    copies, before = last or (0, ())
    return call(
        functools.partial(score_kernel, last is not None),
        "scores",
        [
            held(cols, rows, dtype=jnp.bfloat16),
            held(cols, rows, dtype=jnp.bfloat16),
            held(bot, rows, dtype=jnp.bfloat16),
            held(copies, 4, 2 * rows) if last else held(2, rows),
        ],
        (*before, feats, ws, wt, peak),
        (4 * rows * cols * DEPTH, 4 * rows * cols, 2 * rows * cols),
        scratch_shapes=[held(2, rows)] if last else [],
    )


def relay_kernel(in_ref, out_ref):
    rows = jnp.concatenate(combine([in_ref[i] for i in range(in_ref.shape[0])]), axis=0)
    for i in range(out_ref.shape[0]):
        out_ref[i] = rows


def relay(parts, copies):
    return call(relay_kernel, "relay", held(copies, *parts.shape[1:]), (parts,))


def grad_kernel(here_ref, there_ref, peak_ref, weight_unit, weight_scale, *refs):
    units, exps, expt, out_ref, scales = refs[:4], refs[4:8], refs[8:12], refs[12], refs[13]
    dp, _, core = here()
    total_s, log_t = combine([here_ref[0], there_ref[0]])
    scales[0:2, :] = 10.0 / total_s
    scales[2:4, :] = -10.0 * jnp.exp2(GAIN_T * peak_ref[:, :1] - log_t)
    bot, rows = units[0].shape
    width = 128
    n = rows // width
    sides = []
    for part in range(4):
        view, half = divmod(part, 2)
        base = (dp ^ view) * rows
        at = [pl.ds(pl.multiple_of(base + slot(k, n) * width, width), width) for k in range(n)]
        unit = units[part][...].astype(jnp.float32)
        for which, exp_ref in ((0, exps[part]), (1, expt[part ^ 2])):
            picked = [
                jnp.where(core == half, scales[2 * which:2 * which + 1, where], scales[2 * which + 1:2 * which + 2, where])
                for where in at
            ]
            sides.append(((unit * jnp.concatenate(picked, axis=1)).astype(jnp.bfloat16), exp_ref))
    cols = out_ref.shape[1]
    step = min(512, cols)
    for at in range(0, cols, step):
        grad = sum(
            lax.dot_general(
                exp_ref[at:at + step, :], feats, (((1,), (1,)), ((), ())), preferred_element_type=jnp.float32
            )
            for feats, exp_ref in sides
        )
        grad = grad.T
        unit = weight_unit[:, at:at + step]
        proj = unit * jnp.sum(unit * grad, axis=0, keepdims=True)
        out_ref[:, at:at + step] = (grad - proj) * weight_scale[:, at:at + step]


def gradient(here_total, there_total, peak, weight_unit, weight_scale, units, exps, expt):
    cols, rows = exps[0].shape
    bot = units[0].shape[0]
    return call(
        grad_kernel,
        "gradient",
        shape(bot, cols),
        (here_total, there_total, peak, weight_unit, weight_scale, *units, *exps, *expt),
        (16 * rows * cols * DEPTH, 8 * bot * cols, 0),
        scratch_shapes=[held(4, 2 * rows)],
    )


def shards(teacher_weight, student_weight, teacher_feats, student_feats, pairing, center):
    n_dp, n_fsdp, n_proto = [lax.axis_size(axis) for axis in ("dp", "fsdp", "proto")]

    def spread(copies, axis):
        return lax.all_to_all(copies, axis, 0, 0, tiled=True)

    def swap(block, axis, apart=1):
        return lax.ppermute(block, axis, [(i, i ^ apart) for i in range(lax.axis_size(axis))])

    teacher_new, wt, ws, unit, scale, peak = prepare(teacher_weight, student_weight, center[None, :], n_dp)
    weights = (ws, wt, peak)
    mine = pack(student_feats[0].T, teacher_feats[0].T, swap(pairing, "dp"))
    if n_fsdp <= DIRECT:
        along = [swap(mine, "fsdp", k) for k in range(1, n_fsdp)]
        other = swap(mine, "dp")
        own, rest = join([mine, *along], [n_fsdp, n_fsdp - 1], (other, peak))
        parts = [scores(own, *weights), scores(swap(own, "proto"), *weights)]
        (other,) = join([other, swap(rest, "dp")], [n_fsdp], [part[3] for part in parts])
    else:
        own = spread(jnp.broadcast_to(mine[None], (n_fsdp, *mine.shape)), "fsdp")
        other = swap(own, "dp")
        parts = [scores(own, *weights), scores(swap(own, "proto"), *weights)]
    parts.append(scores(other, *weights))
    before = [part[3] for part in parts]
    parts.append(scores(swap(other, "proto"), *weights, last=(n_proto, before)))
    exps, expt, units, totals = zip(*parts)
    total = relay(spread(relay(spread(totals[3], "proto"), n_fsdp), "fsdp"), 1)
    student_grad = gradient(total, swap(total, "dp"), peak, unit, scale, units, exps, expt)
    return (teacher_new, student_grad)


def solution(mesh):
    placed = (
        P(None, ("proto", "fsdp")),
        P(None, ("proto", "fsdp")),
        P("dp", "fsdp", None),
        P("dp", "fsdp", None),
        P("dp", "fsdp"),
        P("proto"),
    )
    return jax.shard_map(
        shards,
        mesh=mesh,
        in_specs=placed,
        out_specs=(P(None, ("proto", "fsdp")), P(None, ("proto", "fsdp", "dp"))),
        check_vma=False,
    )
```

```python
import functools
import math

import jax
import jax.numpy as jnp
from jax import lax
from jax.experimental import pallas as pl
from jax.experimental.pallas import tpu as pltpu
from jax.sharding import PartitionSpec as P

EPS = 1e-06
DEPTH = 256
GROUP = 512
STEP = 256
DIRECT = 8
LOG2E = math.log2(math.e)
GAIN_T = LOG2E / 0.04
GAIN_S = LOG2E / 0.1
LIMIT = 24 * 1024 * 1024
ON_CHIP = pl.BlockSpec(memory_space=pltpu.VMEM)
IN_HBM = pl.BlockSpec(memory_space=pl.ANY)


def shape(*dims, dtype=jnp.float32):
    return jax.ShapeDtypeStruct(dims, dtype)


def held(*dims, dtype=jnp.float32):
    return pltpu.VMEM(dims, dtype)


def call(kernel, name, out_shape, args, **more):
    many = isinstance(out_shape, (list, tuple))
    specs = dict(in_specs=[ON_CHIP] * len(args), out_specs=[ON_CHIP] * len(out_shape) if many else ON_CHIP)
    return pl.pallas_call(
        kernel,
        out_shape=out_shape,
        compiler_params=pltpu.CompilerParams(vmem_limit_bytes=LIMIT),
        cost_estimate=pl.CostEstimate(flops=1, bytes_accessed=1, transcendentals=0),
        name=name,
        **{**specs, **more},
    )(*args)


def swap(block, axis, apart=1):
    return lax.ppermute(block, axis, [(i, i ^ apart) for i in range(lax.axis_size(axis))])


def here():
    return lax.axis_index("dp"), lax.axis_index("fsdp"), lax.rem(lax.axis_index("proto"), 2)


def cast_split(row):
    high = row.astype(jnp.bfloat16).astype(jnp.float32)
    mid = (row - high).astype(jnp.bfloat16).astype(jnp.float32)
    return high, mid, row - high - mid


def prep_kernel(n_dp, teacher_hbm, student_hbm, center_hbm, new_hbm, wt_ref, ws_ref, unit_ref, scale_ref, peak_ref, *scratch):
    teacher_buf, student_buf, new_buf, center_buf, in_t, in_s, out, in_c = scratch
    chunks, bot, width = new_buf.shape
    dp, fsdp, _ = here()
    first = dp * (chunks * width)
    at = [slice(i * width, (i + 1) * width) for i in range(chunks)]
    far = [pl.ds(pl.multiple_of(first + i * width, width), width) for i in range(chunks)]
    start = pl.multiple_of((fsdp * n_dp + dp) * (chunks * width), 128)
    center_load = pltpu.make_async_copy(center_hbm.at[:, pl.ds(start, chunks * width)], center_buf, in_c)
    loads = [
        (
            pltpu.make_async_copy(teacher_hbm.at[:, far[i]], teacher_buf.at[i], in_t.at[i]),
            pltpu.make_async_copy(student_hbm.at[:, far[i]], student_buf.at[i], in_s.at[i]),
        )
        for i in range(chunks)
    ]
    stores = [pltpu.make_async_copy(new_buf.at[i], new_hbm.at[:, far[i]], out.at[i]) for i in range(chunks)]
    center_load.start()
    for pair in loads:
        for load in pair:
            load.start()
    center_load.wait()
    center = center_buf[...]
    peak = jnp.max(-center, axis=1, keepdims=True)
    peak_ref[...] = jnp.broadcast_to(peak, peak_ref.shape)
    splits = cast_split(-center - peak)
    row = lax.broadcasted_iota(jnp.int32, (DEPTH - bot, width), 0)
    zero = jnp.zeros((DEPTH - bot, width), jnp.float32)
    for i in range(chunks):
        for load in loads[i]:
            load.wait()
        student = student_buf[i]
        new = 0.994 * teacher_buf[i] + 0.006 * student
        new_buf[i] = new
        stores[i].start()
        high, mid, low = [part[:, at[i]] for part in splits]
        extra = jnp.where(row == 0, high, jnp.where(row == 1, mid, jnp.where(row == 2, low, zero)))
        scale = lax.rsqrt(jnp.sum(student * student, axis=0, keepdims=True) + EPS)
        unit_s = student * scale
        unit_t = new * lax.rsqrt(jnp.sum(new * new, axis=0, keepdims=True) + EPS)
        wt_ref[at[i], :] = jnp.concatenate([unit_t, extra], axis=0).astype(jnp.bfloat16).T
        ws_ref[at[i], :] = jnp.concatenate([unit_s, zero], axis=0).astype(jnp.bfloat16).T
        unit_ref[:, at[i]] = unit_s
        scale_ref[:, at[i]] = scale
    for store in stores:
        store.wait()


def prepare(teacher_weight, student_weight, center, n_dp):
    bot, cols = teacher_weight.shape
    own = cols // n_dp
    width = min(512, own)
    chunks = own // width
    return call(
        functools.partial(prep_kernel, n_dp),
        "prep",
        [
            pltpu.HBM((bot, cols), jnp.float32),
            held(own, DEPTH, dtype=jnp.bfloat16),
            held(own, DEPTH, dtype=jnp.bfloat16),
            held(bot, own),
            held(1, own),
            held(1, 128),
        ],
        (teacher_weight, student_weight, center),
        in_specs=[IN_HBM] * 3,
        out_specs=[IN_HBM] + [ON_CHIP] * 5,
        scratch_shapes=[held(chunks, bot, width)] * 3
        + [held(1, own)]
        + [pltpu.SemaphoreType.DMA((chunks,))] * 3
        + [pltpu.SemaphoreType.DMA],
    )


def rest_kernel(teacher_hbm, student_hbm, after, before_hbm, new_hbm, done_ref, *scratch):
    teacher_buf, student_buf, new_buf, in_t, in_s, out = scratch
    chunks, bot, width = new_buf.shape
    own = chunks * width
    parts = teacher_hbm.shape[1] // own - 1
    dp = here()[0]
    done_ref[...] = jnp.zeros_like(done_ref)
    for part in range(parts):
        first = lax.rem(dp + 1 + part, parts + 1) * own
        far = [pl.ds(pl.multiple_of(first + i * width, width), width) for i in range(chunks)]
        loads = [
            (
                pltpu.make_async_copy(teacher_hbm.at[:, far[i]], teacher_buf.at[i], in_t.at[i]),
                pltpu.make_async_copy(student_hbm.at[:, far[i]], student_buf.at[i], in_s.at[i]),
            )
            for i in range(chunks)
        ]
        stores = [pltpu.make_async_copy(new_buf.at[i], new_hbm.at[:, far[i]], out.at[i]) for i in range(chunks)]
        for pair in loads:
            for load in pair:
                load.start()
        for i in range(chunks):
            for load in loads[i]:
                load.wait()
            new_buf[i] = 0.994 * teacher_buf[i] + 0.006 * student_buf[i]
            stores[i].start()
        for store in stores:
            store.wait()


def update_rest(teacher_weight, student_weight, after, new, own):
    bot, cols = teacher_weight.shape
    width = min(512, own)
    chunks = own // width
    return call(
        rest_kernel,
        "rest",
        [pltpu.HBM((bot, cols), jnp.float32), held(8, 128)],
        (teacher_weight, student_weight, after, new),
        in_specs=[IN_HBM] * 4,
        out_specs=[IN_HBM, ON_CHIP],
        input_output_aliases={3: 0},
        scratch_shapes=[held(chunks, bot, width)] * 3 + [pltpu.SemaphoreType.DMA((chunks,))] * 3,
    )


def fetch_kernel(student_hbm, teacher_hbm, student_ref, teacher_ref, sems):
    half = student_ref.shape[1]
    side = pl.ds(pl.multiple_of(here()[2] * half, half), half)
    loads = [
        pltpu.make_async_copy(student_hbm.at[:, side], student_ref, sems.at[0]),
        pltpu.make_async_copy(teacher_hbm, teacher_ref, sems.at[1]),
    ]
    for load in loads:
        load.start()
    for load in loads:
        load.wait()


def fetch(student, teacher):
    bot, crops = student.shape
    return call(
        fetch_kernel,
        "fetch",
        [held(bot, crops // 2, dtype=jnp.bfloat16), held(bot, crops, dtype=jnp.bfloat16)],
        (student, teacher),
        in_specs=[IN_HBM] * 2,
        scratch_shapes=[pltpu.SemaphoreType.DMA((2,))],
    )


def pack_kernel(student_ref, teacher_ref, index_ref, out_ref):
    half = out_ref.shape[2]
    lower = here()[2] == 0
    out_ref[0] = student_ref[...]
    index = jnp.where(lower, index_ref[:, :half], index_ref[:, half:])
    row = lax.broadcasted_iota(jnp.int32, (teacher_ref.shape[1], half), 0)
    pick = jnp.where(row == index, 1.0, 0.0).astype(jnp.bfloat16)
    out_ref[1] = jnp.dot(teacher_ref[...], pick, preferred_element_type=jnp.float32).astype(jnp.bfloat16)


def pack(student, teacher, index):
    bot, half = student.shape
    return call(pack_kernel, "pack", held(2, bot, half, dtype=jnp.bfloat16), (student, teacher, index))


def join_kernel(n_in, n_after, *refs):
    blocks = []
    for ref in refs[:n_in]:
        blocks += [ref] if len(ref.shape) == 3 else [ref.at[i] for i in range(ref.shape[0])]
    for ref in refs[n_in + n_after:]:
        skip = len(blocks) - ref.shape[0]
        for i in range(ref.shape[0]):
            ref[i] = blocks[skip + i][...]


def join(parts, counts, after):
    block = parts[0].shape[-3:]
    outs = [held(count, *block, dtype=jnp.bfloat16) for count in counts]
    kernel = functools.partial(join_kernel, len(parts), len(after))
    return call(kernel, "join", outs, (*parts, *after), in_specs=[ON_CHIP] * len(parts) + [IN_HBM] * len(after))


def log_sum(parts):
    top = functools.reduce(jnp.maximum, parts)
    return top + jnp.log2(sum(jnp.exp2(part - top) for part in parts))


def combine(parts):
    half = parts[0].shape[0] // 2
    return sum(part[:half] for part in parts), log_sum([part[half:] for part in parts])


def slot(k, n):
    return lax.axis_index("fsdp") ^ k if n <= DIRECT else k


def score_kernel(last, *refs):
    before, refs = (refs[:3], refs[3:]) if last else ((), refs)
    feats_ref, ws_ref, wt_ref, peak_ref, exps_ref, expt_ref, unit_ref, total_ref, *mine = refs
    own_ref = mine[0] if last else total_ref
    n, _, bot, width = feats_ref.shape
    cols = ws_ref.shape[0]
    step = min(STEP, cols)
    per = max(1, min(n, GROUP // width))
    row = lax.broadcasted_iota(jnp.int32, (DEPTH - bot, per * width), 0)
    for which, w_ref, exp_ref, gain in ((0, ws_ref, exps_ref, GAIN_S), (1, wt_ref, expt_ref, GAIN_T)):
        extra = jnp.where(row < 3 * which, 1.0, 0.0).astype(jnp.bfloat16)
        for group in range(n // per):
            values = [feats_ref[group * per + k, which].astype(jnp.float32) for k in range(per)]
            values = jnp.concatenate(values, axis=1)
            unit = (values * lax.rsqrt(jnp.sum(values * values, axis=0, keepdims=True) + EPS)).astype(jnp.bfloat16)
            lanes = slice(group * per * width, (group + 1) * per * width)
            if which == 0:
                unit_ref[:, lanes] = unit
            stationary = jnp.concatenate([unit, extra], axis=0)
            total = jnp.zeros((8, per * width), jnp.float32)
            for at in range(0, cols, step):
                score = jnp.dot(w_ref[at:at + step, :], stationary, preferred_element_type=jnp.float32)
                exps = jnp.exp2(score * gain)
                total = total + jnp.sum(exps.reshape(step // 8, 8, per * width), axis=0)
                exp_ref[at:at + step, lanes] = exps.astype(jnp.bfloat16)
            total = jnp.sum(total, axis=0, keepdims=True)
            if which == 1:
                total = jnp.log2(total) + GAIN_T * peak_ref[:, :1]
            own_ref[which:which + 1, lanes] = total
    if not last:
        return
    dp, _, core = here()
    own, pair, other = before
    parts = ((own, other), (pair, own_ref))
    rows = []
    for which in (0, 1):
        for half in (0, 1):
            pieces = []
            for view in (0, 1):
                first = (dp == view) if which == 0 else (dp != view)
                for place in range(n):
                    at = pl.ds(pl.multiple_of(slot(place, n) * width, width), width)
                    read = [[part[which:which + 1, at] for part in side] for side in parts]
                    mine, theirs = [jnp.where(first, *side) for side in read]
                    pieces.append(jnp.where(core == half, mine, theirs))
            rows.append(jnp.concatenate(pieces, axis=1))
    total_ref[...] = jnp.concatenate(rows, axis=0)


def scores(feats, ws, wt, peak, last=()):
    n, _, bot, width = feats.shape
    cols, rows = ws.shape[0], n * width
    return call(
        functools.partial(score_kernel, bool(last)),
        "scores",
        [
            held(cols, rows, dtype=jnp.bfloat16),
            held(cols, rows, dtype=jnp.bfloat16),
            held(bot, rows, dtype=jnp.bfloat16),
            held(4, 2 * rows) if last else held(2, rows),
        ],
        (*last, feats, ws, wt, peak),
        scratch_shapes=[held(2, rows)] if last else [],
    )


def relay_kernel(*refs):
    parts = [ref[...] for ref in refs[:-1]]
    if len(parts[0].shape) == 3:
        parts = [parts[0][i] for i in range(parts[0].shape[0])]
    refs[-1][...] = jnp.concatenate(combine(parts), axis=0)


def add_up(total, axis):
    n = lax.axis_size(axis)
    if n <= DIRECT:
        parts = [total, *[swap(total, axis, k) for k in range(1, n)]]
    else:
        parts = [lax.all_to_all(jnp.broadcast_to(total[None], (n, *total.shape)), axis, 0, 0, tiled=True)]
    return call(relay_kernel, "relay", held(*total.shape), parts)


def grad_kernel(here_ref, there_ref, peak_ref, weight_unit, weight_scale, *refs):
    units, exps, expt, out_ref, scales = refs[:4], refs[4:8], refs[8:12], refs[12], refs[13]
    dp, _, core = here()
    total_s, log_t = combine([here_ref[...], there_ref[...]])
    scales[0:2, :] = 10.0 / total_s
    scales[2:4, :] = -10.0 * jnp.exp2(GAIN_T * peak_ref[:, :1] - log_t)
    bot, rows = units[0].shape
    width = 128
    n = rows // width
    sides = []
    for part in range(4):
        view, half = divmod(part, 2)
        base = (dp ^ view) * rows
        at = [pl.ds(pl.multiple_of(base + slot(k, n) * width, width), width) for k in range(n)]
        unit = units[part][...].astype(jnp.float32)
        for which, exp_ref in ((0, exps[part]), (1, expt[part ^ 2])):
            picked = [
                jnp.where(core == half, scales[2 * which:2 * which + 1, where], scales[2 * which + 1:2 * which + 2, where])
                for where in at
            ]
            sides.append(((unit * jnp.concatenate(picked, axis=1)).astype(jnp.bfloat16), exp_ref))
    cols = out_ref.shape[1]
    step = min(512, cols)
    for at in range(0, cols, step):
        grad = sum(
            lax.dot_general(
                exp_ref[at:at + step, :], feats, (((1,), (1,)), ((), ())), preferred_element_type=jnp.float32
            )
            for feats, exp_ref in sides
        )
        grad = grad.T
        unit = weight_unit[:, at:at + step]
        proj = unit * jnp.sum(unit * grad, axis=0, keepdims=True)
        out_ref[:, at:at + step] = (grad - proj) * weight_scale[:, at:at + step]


def gradient(here_total, there_total, peak, weight_unit, weight_scale, units, exps, expt):
    cols, rows = exps[0].shape
    bot = units[0].shape[0]
    return call(
        grad_kernel,
        "gradient",
        shape(bot, cols),
        (here_total, there_total, peak, weight_unit, weight_scale, *units, *exps, *expt),
        scratch_shapes=[held(4, 2 * rows)],
    )


def shards(teacher_weight, student_weight, teacher_feats, student_feats, pairing, center):
    n_dp, n_fsdp = lax.axis_size("dp"), lax.axis_size("fsdp")
    in_hbm = lambda array: pltpu.with_memory_space_constraint(array, pltpu.HBM)
    teacher_weight, student_weight, center = in_hbm(teacher_weight), in_hbm(student_weight), in_hbm(center[None, :])

    index = swap(pairing, "dp")
    mine = pack(*fetch(in_hbm(student_feats[0].T), in_hbm(teacher_feats[0].T)), index)
    new, wt, ws, unit, scale, peak = prepare(teacher_weight, student_weight, center, n_dp)
    weights = (ws, wt, peak)
    own_cols = ws.shape[0]
    if n_fsdp <= DIRECT:
        along = [swap(mine, "fsdp", k) for k in range(1, n_fsdp)]
        other = swap(mine, "dp")
        (rest,) = join(along, [n_fsdp - 1], (other, peak))
        teacher_new, done = update_rest(teacher_weight, student_weight, rest, new, own_cols)
        (own,) = join([mine, *along], [n_fsdp], (done,))
        parts = [scores(own, *weights), scores(swap(own, "proto"), *weights)]
        (other,) = join([other, swap(rest, "dp")], [n_fsdp], [part[3] for part in parts])
    else:
        own = lax.all_to_all(jnp.broadcast_to(mine[None], (n_fsdp, *mine.shape)), "fsdp", 0, 0, tiled=True)
        other = swap(own, "dp")
        teacher_new, _ = update_rest(teacher_weight, student_weight, own, new, own_cols)
        parts = [scores(own, *weights), scores(swap(own, "proto"), *weights)]
    parts.append(scores(other, *weights))
    parts.append(scores(swap(other, "proto"), *weights, last=[part[3] for part in parts]))
    exps, expt, units, totals = zip(*parts)
    total = add_up(add_up(totals[3], "proto"), "fsdp")
    student_grad = gradient(total, swap(total, "dp"), peak, unit, scale, units, exps, expt)
    return (teacher_new, student_grad)


def solution(mesh):
    placed = (
        P(None, ("proto", "fsdp")),
        P(None, ("proto", "fsdp")),
        P("dp", "fsdp", None),
        P("dp", "fsdp", None),
        P("dp", "fsdp"),
        P("proto"),
    )
    return jax.shard_map(
        shards,
        mesh=mesh,
        in_specs=placed,
        out_specs=(P(None, ("proto", "fsdp")), P(None, ("proto", "fsdp", "dp"))),
        check_vma=False,
    )
```

```python
import functools
import math

import jax
import jax.numpy as jnp
from jax import lax
from jax.experimental import pallas as pl
from jax.experimental.pallas import tpu as pltpu
from jax.sharding import PartitionSpec as P

EPS = 1e-06
DEPTH = 256
GROUP = 512
STEP = 256
DIRECT = 8
LOG2E = math.log2(math.e)
GAIN_T = LOG2E / 0.04
GAIN_S = LOG2E / 0.1
LIMIT = 24 * 1024 * 1024
ON_CHIP = pl.BlockSpec(memory_space=pltpu.VMEM)
IN_HBM = pl.BlockSpec(memory_space=pl.ANY)


def shape(*dims, dtype=jnp.float32):
    return jax.ShapeDtypeStruct(dims, dtype)


def held(*dims, dtype=jnp.float32):
    return pltpu.VMEM(dims, dtype)


def call(kernel, name, out_shape, args, **more):
    many = isinstance(out_shape, (list, tuple))
    specs = dict(in_specs=[ON_CHIP] * len(args), out_specs=[ON_CHIP] * len(out_shape) if many else ON_CHIP)
    return pl.pallas_call(
        kernel,
        out_shape=out_shape,
        compiler_params=pltpu.CompilerParams(vmem_limit_bytes=LIMIT),
        cost_estimate=pl.CostEstimate(flops=1, bytes_accessed=1, transcendentals=0),
        name=name,
        **{**specs, **more},
    )(*args)


def swap(block, axis, apart=1):
    return lax.ppermute(block, axis, [(i, i ^ apart) for i in range(lax.axis_size(axis))])


def here():
    return lax.axis_index("dp"), lax.axis_index("fsdp"), lax.rem(lax.axis_index("proto"), 2)


def cast_split(row):
    high = row.astype(jnp.bfloat16).astype(jnp.float32)
    mid = (row - high).astype(jnp.bfloat16).astype(jnp.float32)
    return high, mid, row - high - mid


def prep_kernel(n_dp, teacher_hbm, student_hbm, center_hbm, new_hbm, wt_ref, ws_ref, unit_ref, scale_ref, peak_ref, *scratch):
    teacher_buf, student_buf, new_buf, center_buf, in_t, in_s, out, in_c = scratch
    chunks, bot, width = new_buf.shape
    dp, fsdp, _ = here()
    first = dp * (chunks * width)
    at = [slice(i * width, (i + 1) * width) for i in range(chunks)]
    far = [pl.ds(pl.multiple_of(first + i * width, width), width) for i in range(chunks)]
    start = pl.multiple_of((fsdp * n_dp + dp) * (chunks * width), 128)
    center_load = pltpu.make_async_copy(center_hbm.at[:, pl.ds(start, chunks * width)], center_buf, in_c)
    loads = [
        (
            pltpu.make_async_copy(teacher_hbm.at[:, far[i]], teacher_buf.at[i], in_t.at[i]),
            pltpu.make_async_copy(student_hbm.at[:, far[i]], student_buf.at[i], in_s.at[i]),
        )
        for i in range(chunks)
    ]
    stores = [pltpu.make_async_copy(new_buf.at[i], new_hbm.at[:, far[i]], out.at[i]) for i in range(chunks)]
    center_load.start()
    for pair in loads:
        for load in pair:
            load.start()
    center_load.wait()
    center = center_buf[...]
    peak = jnp.max(-center, axis=1, keepdims=True)
    peak_ref[...] = jnp.broadcast_to(peak, peak_ref.shape)
    splits = cast_split(-center - peak)
    row = lax.broadcasted_iota(jnp.int32, (DEPTH - bot, width), 0)
    zero = jnp.zeros((DEPTH - bot, width), jnp.float32)
    for i in range(chunks):
        for load in loads[i]:
            load.wait()
        student = student_buf[i]
        new = 0.994 * teacher_buf[i] + 0.006 * student
        new_buf[i] = new
        stores[i].start()
        high, mid, low = [part[:, at[i]] for part in splits]
        extra = jnp.where(row == 0, high, jnp.where(row == 1, mid, jnp.where(row == 2, low, zero)))
        scale = lax.rsqrt(jnp.sum(student * student, axis=0, keepdims=True) + EPS)
        unit_s = student * scale
        unit_t = new * lax.rsqrt(jnp.sum(new * new, axis=0, keepdims=True) + EPS)
        wt_ref[at[i], :] = jnp.concatenate([unit_t, extra], axis=0).astype(jnp.bfloat16).T
        ws_ref[at[i], :] = jnp.concatenate([unit_s, zero], axis=0).astype(jnp.bfloat16).T
        unit_ref[:, at[i]] = unit_s
        scale_ref[:, at[i]] = scale
    for store in stores:
        store.wait()


def prepare(teacher_weight, student_weight, center, n_dp):
    bot, cols = teacher_weight.shape
    own = cols // n_dp
    width = min(512, own)
    chunks = own // width
    return call(
        functools.partial(prep_kernel, n_dp),
        "prep",
        [
            pltpu.HBM((bot, cols), jnp.float32),
            held(own, DEPTH, dtype=jnp.bfloat16),
            held(own, DEPTH, dtype=jnp.bfloat16),
            held(bot, own),
            held(1, own),
            held(1, 128),
        ],
        (teacher_weight, student_weight, center),
        in_specs=[IN_HBM] * 3,
        out_specs=[IN_HBM] + [ON_CHIP] * 5,
        scratch_shapes=[held(chunks, bot, width)] * 3
        + [held(1, own)]
        + [pltpu.SemaphoreType.DMA((chunks,))] * 3
        + [pltpu.SemaphoreType.DMA],
    )


def rest_kernel(teacher_hbm, student_hbm, after, before_hbm, new_hbm, done_ref, *scratch):
    teacher_buf, student_buf, new_buf, in_t, in_s, out = scratch
    chunks, bot, width = new_buf.shape
    own = chunks * width
    parts = teacher_hbm.shape[1] // own - 1
    dp = here()[0]
    done_ref[...] = jnp.zeros_like(done_ref)
    for part in range(parts):
        first = lax.rem(dp + 1 + part, parts + 1) * own
        far = [pl.ds(pl.multiple_of(first + i * width, width), width) for i in range(chunks)]
        loads = [
            (
                pltpu.make_async_copy(teacher_hbm.at[:, far[i]], teacher_buf.at[i], in_t.at[i]),
                pltpu.make_async_copy(student_hbm.at[:, far[i]], student_buf.at[i], in_s.at[i]),
            )
            for i in range(chunks)
        ]
        stores = [pltpu.make_async_copy(new_buf.at[i], new_hbm.at[:, far[i]], out.at[i]) for i in range(chunks)]
        for pair in loads:
            for load in pair:
                load.start()
        for i in range(chunks):
            for load in loads[i]:
                load.wait()
            new_buf[i] = 0.994 * teacher_buf[i] + 0.006 * student_buf[i]
            stores[i].start()
        for store in stores:
            store.wait()


def update_rest(teacher_weight, student_weight, after, new, own):
    bot, cols = teacher_weight.shape
    width = min(512, own)
    chunks = own // width
    return call(
        rest_kernel,
        "rest",
        [pltpu.HBM((bot, cols), jnp.float32), held(8, 128)],
        (teacher_weight, student_weight, after, new),
        in_specs=[IN_HBM] * 4,
        out_specs=[IN_HBM, ON_CHIP],
        input_output_aliases={3: 0},
        scratch_shapes=[held(chunks, bot, width)] * 3 + [pltpu.SemaphoreType.DMA((chunks,))] * 3,
    )


def fetch_kernel(student_hbm, teacher_hbm, student_ref, teacher_ref, sems):
    half = student_ref.shape[1]
    side = pl.ds(pl.multiple_of(here()[2] * half, half), half)
    loads = [
        pltpu.make_async_copy(student_hbm.at[:, side], student_ref, sems.at[0]),
        pltpu.make_async_copy(teacher_hbm, teacher_ref, sems.at[1]),
    ]
    for load in loads:
        load.start()
    for load in loads:
        load.wait()


def fetch(student, teacher):
    bot, crops = student.shape
    return call(
        fetch_kernel,
        "fetch",
        [held(bot, crops // 2, dtype=jnp.bfloat16), held(bot, crops, dtype=jnp.bfloat16)],
        (student, teacher),
        in_specs=[IN_HBM] * 2,
        scratch_shapes=[pltpu.SemaphoreType.DMA((2,))],
    )


def pack_kernel(student_ref, teacher_ref, index_ref, out_ref):
    half = out_ref.shape[2]
    lower = here()[2] == 0
    out_ref[0] = student_ref[...]
    index = jnp.where(lower, index_ref[:, :half], index_ref[:, half:])
    row = lax.broadcasted_iota(jnp.int32, (teacher_ref.shape[1], half), 0)
    pick = jnp.where(row == index, 1.0, 0.0).astype(jnp.bfloat16)
    out_ref[1] = jnp.dot(teacher_ref[...], pick, preferred_element_type=jnp.float32).astype(jnp.bfloat16)


def pack(student, teacher, index):
    bot, half = student.shape
    return call(pack_kernel, "pack", held(2, bot, half, dtype=jnp.bfloat16), (student, teacher, index))


def join_kernel(n_in, n_after, *refs):
    blocks = []
    for ref in refs[:n_in]:
        blocks += [ref] if len(ref.shape) == 3 else [ref.at[i] for i in range(ref.shape[0])]
    for ref in refs[n_in + n_after:]:
        skip = len(blocks) - ref.shape[0]
        for i in range(ref.shape[0]):
            ref[i] = blocks[skip + i][...]


def join(parts, counts, after):
    block = parts[0].shape[-3:]
    outs = [held(count, *block, dtype=jnp.bfloat16) for count in counts]
    kernel = functools.partial(join_kernel, len(parts), len(after))
    return call(kernel, "join", outs, (*parts, *after), in_specs=[ON_CHIP] * len(parts) + [IN_HBM] * len(after))


def log_sum(parts):
    top = functools.reduce(jnp.maximum, parts)
    return top + jnp.log2(sum(jnp.exp2(part - top) for part in parts))


def combine(parts):
    half = parts[0].shape[0] // 2
    return sum(part[:half] for part in parts), log_sum([part[half:] for part in parts])


def slot(k, n):
    return lax.axis_index("fsdp") ^ k if n <= DIRECT else k


def score_kernel(part, *refs):
    last = part == 3
    before, refs = (refs[:3], refs[3:]) if last else ((), refs)
    feats_ref, ws_ref, wt_ref, peak_ref, *refs = refs
    exp_ref, unit_ref, total_ref, *mine = refs[1:] if part else refs
    own_ref = mine[0] if last else total_ref
    n, _, bot, width = feats_ref.shape
    cols = ws_ref.shape[0]
    step = min(STEP, cols)
    per = max(1, min(n, GROUP // width))
    row = lax.broadcasted_iota(jnp.int32, (DEPTH - bot, per * width), 0)
    for which, w_ref, gain in ((0, ws_ref, GAIN_S), (1, wt_ref, GAIN_T)):
        base = (2 * part + which) * n * width
        extra = jnp.where(row < 3 * which, 1.0, 0.0).astype(jnp.bfloat16)
        for group in range(n // per):
            values = [feats_ref[group * per + k, which].astype(jnp.float32) for k in range(per)]
            values = jnp.concatenate(values, axis=1)
            unit = (values * lax.rsqrt(jnp.sum(values * values, axis=0, keepdims=True) + EPS)).astype(jnp.bfloat16)
            lanes = slice(group * per * width, (group + 1) * per * width)
            if which == 0:
                unit_ref[:, lanes] = unit
            stationary = jnp.concatenate([unit, extra], axis=0)
            total = jnp.zeros((8, per * width), jnp.float32)
            for at in range(0, cols, step):
                score = jnp.dot(w_ref[at:at + step, :], stationary, preferred_element_type=jnp.float32)
                exps = jnp.exp2(score * gain)
                total = total + jnp.sum(exps.reshape(step // 8, 8, per * width), axis=0)
                exp_ref[at:at + step, base + lanes.start:base + lanes.stop] = exps.astype(jnp.bfloat16)
            total = jnp.sum(total, axis=0, keepdims=True)
            if which == 1:
                total = jnp.log2(total) + GAIN_T * peak_ref[:, :1]
            own_ref[which:which + 1, lanes] = total
    if not last:
        return
    dp, _, core = here()
    own, pair, other = before
    parts = ((own, other), (pair, own_ref))
    rows = []
    for which in (0, 1):
        for half in (0, 1):
            pieces = []
            for view in (0, 1):
                first = (dp == view) if which == 0 else (dp != view)
                for place in range(n):
                    at = pl.ds(pl.multiple_of(slot(place, n) * width, width), width)
                    read = [[part[which:which + 1, at] for part in side] for side in parts]
                    mine, theirs = [jnp.where(first, *side) for side in read]
                    pieces.append(jnp.where(core == half, mine, theirs))
            rows.append(jnp.concatenate(pieces, axis=1))
    total_ref[...] = jnp.concatenate(rows, axis=0)


def scores(part, feats, weights, before=(), exps=None):
    n, _, bot, width = feats.shape
    cols, rows = weights[0].shape[0], n * width
    args = (*before, feats, *weights, *([exps] if part else []))
    return call(
        functools.partial(score_kernel, part),
        "scores",
        [
            held(cols, 8 * rows, dtype=jnp.bfloat16),
            held(bot, rows, dtype=jnp.bfloat16),
            held(4, 2 * rows) if part == 3 else held(2, rows),
        ],
        args,
        in_specs=[ON_CHIP] * (len(args) - bool(part)) + [IN_HBM] * bool(part),
        input_output_aliases={len(args) - 1: 0} if part else {},
        scratch_shapes=[held(2, rows)] if part == 3 else [],
    )


def relay_kernel(*refs):
    parts = [ref[...] for ref in refs[:-1]]
    if len(parts[0].shape) == 3:
        parts = [parts[0][i] for i in range(parts[0].shape[0])]
    refs[-1][...] = jnp.concatenate(combine(parts), axis=0)


def add_up(total, axis):
    n = lax.axis_size(axis)
    if n <= DIRECT:
        parts = [total, *[swap(total, axis, k) for k in range(1, n)]]
    else:
        parts = [lax.all_to_all(jnp.broadcast_to(total[None], (n, *total.shape)), axis, 0, 0, tiled=True)]
    return call(relay_kernel, "relay", held(*total.shape), parts)


def grad_kernel(here_ref, there_ref, peak_ref, weight_unit, weight_scale, *refs):
    units, exp_ref, out_hbm, scales, feats, buf, sems = refs[:4], *refs[4:]
    dp, _, core = here()
    total_s, log_t = combine([here_ref[...], there_ref[...]])
    scales[0:2, :] = 10.0 / total_s
    scales[2:4, :] = -10.0 * jnp.exp2(GAIN_T * peak_ref[:, :1] - log_t)
    bot, rows = units[0].shape
    width = 128
    n = rows // width
    for part in range(4):
        view, half = divmod(part, 2)
        base = (dp ^ view) * rows
        at = [pl.ds(pl.multiple_of(base + slot(k, n) * width, width), width) for k in range(n)]
        unit = units[part][...].astype(jnp.float32)
        for which, lies in ((0, part), (1, part ^ 2)):
            picked = [
                jnp.where(core == half, scales[2 * which:2 * which + 1, where], scales[2 * which + 1:2 * which + 2, where])
                for where in at
            ]
            scaled = (unit * jnp.concatenate(picked, axis=1)).astype(jnp.bfloat16)
            feats[(2 * lies + which) * rows:(2 * lies + which + 1) * rows, :] = scaled.T
    chunks, _, step = buf.shape
    stores = []
    for i in range(chunks):
        at = slice(i * step, (i + 1) * step)
        grad = jnp.dot(exp_ref[at, :], feats[...], preferred_element_type=jnp.float32).T
        unit = weight_unit[:, at]
        proj = unit * jnp.sum(unit * grad, axis=0, keepdims=True)
        buf[i] = (grad - proj) * weight_scale[:, at]
        stores.append(pltpu.make_async_copy(buf.at[i], out_hbm.at[:, at], sems.at[i]))
        stores[i].start()
    for store in stores:
        store.wait()


def gradient(here_total, there_total, peak, weight_unit, weight_scale, units, exps):
    cols, all_rows = exps.shape
    bot, rows = units[0].shape
    step = min(512, cols)
    args = (here_total, there_total, peak, weight_unit, weight_scale, *units, exps)
    return call(
        grad_kernel,
        "gradient",
        pltpu.HBM((bot, cols), jnp.float32),
        args,
        out_specs=IN_HBM,
        scratch_shapes=[
            held(4, 2 * rows),
            held(all_rows, bot, dtype=jnp.bfloat16),
            held(cols // step, bot, step),
            pltpu.SemaphoreType.DMA((cols // step,)),
        ],
    )


def shards(teacher_weight, student_weight, teacher_feats, student_feats, pairing, center):
    n_dp, n_fsdp = lax.axis_size("dp"), lax.axis_size("fsdp")
    in_hbm = lambda array: pltpu.with_memory_space_constraint(array, pltpu.HBM)
    teacher_weight, student_weight, center = in_hbm(teacher_weight), in_hbm(student_weight), in_hbm(center[None, :])

    index = swap(pairing, "dp")
    mine = pack(*fetch(in_hbm(student_feats[0].T), in_hbm(teacher_feats[0].T)), index)
    new, wt, ws, unit, scale, peak = prepare(teacher_weight, student_weight, center, n_dp)
    weights = (ws, wt, peak)
    own_cols = ws.shape[0]
    if n_fsdp <= DIRECT:
        other = [swap(mine, "dp")]
        along = [swap(mine, "fsdp", k) for k in range(1, n_fsdp)]
        other.append(swap(other[0], "fsdp"))
        own, far = join([mine, *along], [n_fsdp, n_fsdp - 2], (other[1], peak))
        exps, unit_a, total_a = scores(0, own, weights)
        teacher_new, done = update_rest(teacher_weight, student_weight, total_a, new, own_cols)
        (other,) = join([*other, swap(far, "dp")], [n_fsdp], (done,))
    else:
        own = lax.all_to_all(jnp.broadcast_to(mine[None], (n_fsdp, *mine.shape)), "fsdp", 0, 0, tiled=True)
        other = swap(own, "dp")
        teacher_new, _ = update_rest(teacher_weight, student_weight, own, new, own_cols)
        exps, unit_a, total_a = scores(0, own, weights)
    exps, unit_c, total_c = scores(2, other, weights, exps=exps)
    exps, unit_b, total_b = scores(1, swap(own, "proto"), weights, exps=exps)
    exps, unit_d, totals = scores(3, swap(other, "proto"), weights, (total_a, total_b, total_c), exps)
    total = add_up(add_up(totals, "proto"), "fsdp")
    units = (unit_a, unit_b, unit_c, unit_d)
    student_grad = gradient(total, swap(total, "dp"), peak, unit, scale, units, exps)
    return (teacher_new, student_grad)


def solution(mesh):
    placed = (
        P(None, ("proto", "fsdp")),
        P(None, ("proto", "fsdp")),
        P("dp", "fsdp", None),
        P("dp", "fsdp", None),
        P("dp", "fsdp"),
        P("proto"),
    )
    return jax.shard_map(
        shards,
        mesh=mesh,
        in_specs=placed,
        out_specs=(P(None, ("proto", "fsdp")), P(None, ("proto", "fsdp", "dp"))),
        check_vma=False,
    )
```

```python
import functools
import math

import jax
import jax.numpy as jnp
from jax import lax
from jax.experimental import pallas as pl
from jax.experimental.pallas import tpu as pltpu
from jax.sharding import PartitionSpec as P

EPS = 1e-06
DEPTH = 256
GROUP = 512
STEP = 256
DIRECT = 8
LOG2E = math.log2(math.e)
GAIN_T = LOG2E / 0.04
GAIN_S = LOG2E / 0.1
LIMIT = 24 * 1024 * 1024
ON_CHIP = pl.BlockSpec(memory_space=pltpu.VMEM)
IN_HBM = pl.BlockSpec(memory_space=pl.ANY)


def shape(*dims, dtype=jnp.float32):
    return jax.ShapeDtypeStruct(dims, dtype)


def held(*dims, dtype=jnp.float32):
    return pltpu.VMEM(dims, dtype)


def call(kernel, name, out_shape, args, **more):
    many = isinstance(out_shape, (list, tuple))
    specs = dict(in_specs=[ON_CHIP] * len(args), out_specs=[ON_CHIP] * len(out_shape) if many else ON_CHIP)
    return pl.pallas_call(
        kernel,
        out_shape=out_shape,
        compiler_params=pltpu.CompilerParams(vmem_limit_bytes=LIMIT),
        cost_estimate=pl.CostEstimate(flops=1, bytes_accessed=1, transcendentals=0),
        name=name,
        **{**specs, **more},
    )(*args)


def swap(block, axis, apart=1):
    return lax.ppermute(block, axis, [(i, i ^ apart) for i in range(lax.axis_size(axis))])


def here():
    return lax.axis_index("dp"), lax.axis_index("fsdp"), lax.rem(lax.axis_index("proto"), 2)


def cast_split(row):
    high = row.astype(jnp.bfloat16).astype(jnp.float32)
    mid = (row - high).astype(jnp.bfloat16).astype(jnp.float32)
    return high, mid, row - high - mid


def prep_kernel(n_dp, teacher_hbm, student_hbm, center_hbm, new_hbm, wt_ref, ws_ref, unit_ref, scale_ref, peak_ref, *scratch):
    teacher_buf, student_buf, new_buf, center_buf, in_t, in_s, out, in_c = scratch
    chunks, bot, width = new_buf.shape
    own = chunks // n_dp
    dp, fsdp, _ = here()
    at = [slice(i * width, (i + 1) * width) for i in range(own)]
    far = [
        pl.ds(pl.multiple_of((lax.rem(dp + i // own, n_dp) * own + i % own) * width, width), width) for i in range(chunks)
    ]
    start = pl.multiple_of((fsdp * n_dp + dp) * (own * width), 128)
    center_load = pltpu.make_async_copy(center_hbm.at[:, pl.ds(start, own * width)], center_buf, in_c)
    loads = [
        (
            pltpu.make_async_copy(teacher_hbm.at[:, far[i]], teacher_buf.at[i], in_t.at[i]),
            pltpu.make_async_copy(student_hbm.at[:, far[i]], student_buf.at[i], in_s.at[i]),
        )
        for i in range(chunks)
    ]
    stores = [pltpu.make_async_copy(new_buf.at[i], new_hbm.at[:, far[i]], out.at[i]) for i in range(chunks)]
    center_load.start()
    for pair in loads:
        for load in pair:
            load.start()
    center_load.wait()
    center = center_buf[...]
    peak = jnp.max(-center, axis=1, keepdims=True)
    peak_ref[...] = jnp.broadcast_to(peak, peak_ref.shape)
    splits = cast_split(-center - peak)
    row = lax.broadcasted_iota(jnp.int32, (DEPTH - bot, width), 0)
    zero = jnp.zeros((DEPTH - bot, width), jnp.float32)
    for i in range(chunks):
        for load in loads[i]:
            load.wait()
        student = student_buf[i]
        new = 0.994 * teacher_buf[i] + 0.006 * student
        new_buf[i] = new
        stores[i].start()
        if i >= own:
            continue
        high, mid, low = [part[:, at[i]] for part in splits]
        extra = jnp.where(row == 0, high, jnp.where(row == 1, mid, jnp.where(row == 2, low, zero)))
        scale = lax.rsqrt(jnp.sum(student * student, axis=0, keepdims=True) + EPS)
        unit_s = student * scale
        unit_t = new * lax.rsqrt(jnp.sum(new * new, axis=0, keepdims=True) + EPS)
        wt_ref[at[i], :] = jnp.concatenate([unit_t, extra], axis=0).astype(jnp.bfloat16).T
        ws_ref[at[i], :] = jnp.concatenate([unit_s, zero], axis=0).astype(jnp.bfloat16).T
        unit_ref[:, at[i]] = unit_s
        scale_ref[:, at[i]] = scale
    for store in stores:
        store.wait()


def prepare(teacher_weight, student_weight, center, n_dp):
    bot, cols = teacher_weight.shape
    own = cols // n_dp
    width = min(512, own)
    chunks = cols // width
    return call(
        functools.partial(prep_kernel, n_dp),
        "prep",
        [
            pltpu.HBM((bot, cols), jnp.float32),
            held(own, DEPTH, dtype=jnp.bfloat16),
            held(own, DEPTH, dtype=jnp.bfloat16),
            held(bot, own),
            held(1, own),
            held(1, 128),
        ],
        (teacher_weight, student_weight, center),
        in_specs=[IN_HBM] * 3,
        out_specs=[IN_HBM] + [ON_CHIP] * 5,
        scratch_shapes=[held(chunks, bot, width)] * 3
        + [held(1, own)]
        + [pltpu.SemaphoreType.DMA((chunks,))] * 3
        + [pltpu.SemaphoreType.DMA],
    )


def fetch_kernel(student_hbm, teacher_hbm, student_ref, teacher_ref, sems):
    half = student_ref.shape[1]
    side = pl.ds(pl.multiple_of(here()[2] * half, half), half)
    loads = [
        pltpu.make_async_copy(student_hbm.at[:, side], student_ref, sems.at[0]),
        pltpu.make_async_copy(teacher_hbm, teacher_ref, sems.at[1]),
    ]
    for load in loads:
        load.start()
    for load in loads:
        load.wait()


def fetch(student, teacher):
    bot, crops = student.shape
    return call(
        fetch_kernel,
        "fetch",
        [held(bot, crops // 2, dtype=jnp.bfloat16), held(bot, crops, dtype=jnp.bfloat16)],
        (student, teacher),
        in_specs=[IN_HBM] * 2,
        scratch_shapes=[pltpu.SemaphoreType.DMA((2,))],
    )


def pack_kernel(student_ref, teacher_ref, index_ref, out_ref):
    half = out_ref.shape[2]
    lower = here()[2] == 0
    out_ref[0] = student_ref[...]
    index = jnp.where(lower, index_ref[:, :half], index_ref[:, half:])
    row = lax.broadcasted_iota(jnp.int32, (teacher_ref.shape[1], half), 0)
    pick = jnp.where(row == index, 1.0, 0.0).astype(jnp.bfloat16)
    out_ref[1] = jnp.dot(teacher_ref[...], pick, preferred_element_type=jnp.float32).astype(jnp.bfloat16)


def pack(student, teacher, index):
    bot, half = student.shape
    return call(pack_kernel, "pack", held(2, bot, half, dtype=jnp.bfloat16), (student, teacher, index))


def join_kernel(n_in, n_after, *refs):
    blocks = []
    for ref in refs[:n_in]:
        blocks += [ref] if len(ref.shape) == 3 else [ref.at[i] for i in range(ref.shape[0])]
    for ref in refs[n_in + n_after:]:
        skip = len(blocks) - ref.shape[0]
        for i in range(ref.shape[0]):
            ref[i] = blocks[skip + i][...]


def join(parts, counts, after):
    block = parts[0].shape[-3:]
    outs = [held(count, *block, dtype=jnp.bfloat16) for count in counts]
    kernel = functools.partial(join_kernel, len(parts), len(after))
    return call(kernel, "join", outs, (*parts, *after), in_specs=[ON_CHIP] * len(parts) + [IN_HBM] * len(after))


def log_sum(parts):
    top = functools.reduce(jnp.maximum, parts)
    return top + jnp.log2(sum(jnp.exp2(part - top) for part in parts))


def combine(parts):
    half = parts[0].shape[0] // 2
    return sum(part[:half] for part in parts), log_sum([part[half:] for part in parts])


def slot(k, n):
    return lax.axis_index("fsdp") ^ k if n <= DIRECT else k


def score_kernel(part, *refs):
    last = part == 3
    before, refs = (refs[:3], refs[3:]) if last else ((), refs)
    feats_ref, ws_ref, wt_ref, peak_ref, *refs = refs
    exp_ref, unit_ref, total_ref, *mine = refs[1:] if part else refs
    own_ref = mine[0] if last else total_ref
    n, _, bot, width = feats_ref.shape
    cols = ws_ref.shape[0]
    step = min(STEP, cols)
    per = max(1, min(n, GROUP // width))
    row = lax.broadcasted_iota(jnp.int32, (DEPTH - bot, per * width), 0)
    for which, w_ref, gain in ((0, ws_ref, GAIN_S), (1, wt_ref, GAIN_T)):
        base = (2 * part + which) * n * width
        extra = jnp.where(row < 3 * which, 1.0, 0.0).astype(jnp.bfloat16)
        for group in range(n // per):
            values = [feats_ref[group * per + k, which].astype(jnp.float32) for k in range(per)]
            values = jnp.concatenate(values, axis=1)
            unit = (values * lax.rsqrt(jnp.sum(values * values, axis=0, keepdims=True) + EPS)).astype(jnp.bfloat16)
            lanes = slice(group * per * width, (group + 1) * per * width)
            if which == 0:
                unit_ref[lanes, :] = unit.T
            stationary = jnp.concatenate([unit, extra], axis=0)
            total = jnp.zeros((8, per * width), jnp.float32)
            for at in range(0, cols, step):
                score = jnp.dot(w_ref[at:at + step, :], stationary, preferred_element_type=jnp.float32)
                exps = jnp.exp2(score * gain)
                total = total + jnp.sum(exps.reshape(step // 8, 8, per * width), axis=0)
                exp_ref[at:at + step, base + lanes.start:base + lanes.stop] = exps.astype(jnp.bfloat16)
            total = jnp.sum(total, axis=0, keepdims=True)
            if which == 1:
                total = jnp.log2(total) + GAIN_T * peak_ref[:, :1]
            own_ref[which:which + 1, lanes] = total
    if not last:
        return
    dp, _, core = here()
    own, pair, other = before
    parts = ((own, other), (pair, own_ref))
    rows = []
    for which in (0, 1):
        for half in (0, 1):
            pieces = []
            for view in (0, 1):
                first = (dp == view) if which == 0 else (dp != view)
                for place in range(n):
                    at = pl.ds(pl.multiple_of(slot(place, n) * width, width), width)
                    read = [[part[which:which + 1, at] for part in side] for side in parts]
                    mine, theirs = [jnp.where(first, *side) for side in read]
                    pieces.append(jnp.where(core == half, mine, theirs))
            rows.append(jnp.concatenate(pieces, axis=1))
    total_ref[...] = jnp.concatenate(rows, axis=0)


def scores(part, feats, weights, before=(), exps=None):
    n, _, bot, width = feats.shape
    cols, rows = weights[0].shape[0], n * width
    args = (*before, feats, *weights, *([exps] if part else []))
    return call(
        functools.partial(score_kernel, part),
        "scores",
        [
            held(cols, 8 * rows, dtype=jnp.bfloat16),
            held(rows, bot, dtype=jnp.bfloat16),
            held(4, 2 * rows) if part == 3 else held(2, rows),
        ],
        args,
        in_specs=[ON_CHIP] * (len(args) - bool(part)) + [IN_HBM] * bool(part),
        input_output_aliases={len(args) - 1: 0} if part else {},
        scratch_shapes=[held(2, rows)] if part == 3 else [],
    )


def relay_kernel(*refs):
    parts = [ref[...] for ref in refs[:-1]]
    if len(parts[0].shape) == 3:
        parts = [parts[0][i] for i in range(parts[0].shape[0])]
    refs[-1][...] = jnp.concatenate(combine(parts), axis=0)


def add_up(total, axis):
    n = lax.axis_size(axis)
    if n <= DIRECT:
        parts = [total, *[swap(total, axis, k) for k in range(1, n)]]
    else:
        parts = [lax.all_to_all(jnp.broadcast_to(total[None], (n, *total.shape)), axis, 0, 0, tiled=True)]
    return call(relay_kernel, "relay", held(*total.shape), parts)


def grad_kernel(here_ref, there_ref, peak_ref, weight_unit, weight_scale, *refs):
    units, exp_ref, out_hbm, scales, buf, sems = refs[:4], *refs[4:]
    dp, _, core = here()
    total_s, log_t = combine([here_ref[...], there_ref[...]])
    scales[0:2, :] = 10.0 / total_s
    scales[2:4, :] = 10.0 * jnp.exp2(GAIN_T * peak_ref[:, :1] - log_t)
    rows = units[0].shape[0]
    width = 128
    n = rows // width
    factors = []
    for part in range(4):
        view, half = divmod(part, 2)
        base = (dp ^ view) * rows
        at = [pl.ds(pl.multiple_of(base + slot(k, n) * width, width), width) for k in range(n)]
        for which in (0, 1):
            picked = [
                jnp.where(core == half, scales[2 * which:2 * which + 1, where], scales[2 * which + 1:2 * which + 2, where])
                for where in at
            ]
            factors.append(jnp.concatenate(picked, axis=1).astype(jnp.bfloat16))
    feats = jnp.concatenate([unit[...] for unit in units], axis=0)
    chunks, _, step = buf.shape
    stores = []
    for i in range(chunks):
        at = slice(i * step, (i + 1) * step)
        derivs = []
        for part in range(4):
            lies_s, lies_t = 2 * part * rows, (2 * (part ^ 2) + 1) * rows
            probs_s = exp_ref[at, lies_s:lies_s + rows] * factors[2 * part]
            probs_t = exp_ref[at, lies_t:lies_t + rows] * factors[2 * part + 1]
            derivs.append(probs_s - probs_t)
        derivs = jnp.concatenate(derivs, axis=1)
        grad = jnp.dot(derivs, feats, preferred_element_type=jnp.float32).T
        unit = weight_unit[:, at]
        proj = unit * jnp.sum(unit * grad, axis=0, keepdims=True)
        buf[i] = (grad - proj) * weight_scale[:, at]
        stores.append(pltpu.make_async_copy(buf.at[i], out_hbm.at[:, at], sems.at[i]))
        stores[i].start()
    for store in stores:
        store.wait()


def gradient(here_total, there_total, peak, weight_unit, weight_scale, units, exps):
    cols = exps.shape[0]
    rows, bot = units[0].shape
    step = min(512, cols)
    args = (here_total, there_total, peak, weight_unit, weight_scale, *units, exps)
    return call(
        grad_kernel,
        "gradient",
        pltpu.HBM((bot, cols), jnp.float32),
        args,
        out_specs=IN_HBM,
        scratch_shapes=[held(4, 2 * rows), held(cols // step, bot, step), pltpu.SemaphoreType.DMA((cols // step,))],
    )


def shards(teacher_weight, student_weight, teacher_feats, student_feats, pairing, center):
    n_dp, n_fsdp = lax.axis_size("dp"), lax.axis_size("fsdp")
    in_hbm = lambda array: pltpu.with_memory_space_constraint(array, pltpu.HBM)
    teacher_weight, student_weight, center = in_hbm(teacher_weight), in_hbm(student_weight), in_hbm(center[None, :])

    index = swap(pairing, "dp")
    mine = pack(*fetch(in_hbm(student_feats[0].T), in_hbm(teacher_feats[0].T)), index)
    teacher_new, wt, ws, unit, scale, peak = prepare(teacher_weight, student_weight, center, n_dp)
    weights = (ws, wt, peak)
    if n_fsdp <= DIRECT:
        other = [swap(mine, "dp")]
        along = [swap(mine, "fsdp", k) for k in range(1, n_fsdp)]
        other.append(swap(other[0], "fsdp"))
        own, far = join([mine, *along], [n_fsdp, n_fsdp - 2], (other[1], peak))
        exps, unit_a, total_a = scores(0, own, weights)
        (other,) = join([*other, swap(far, "dp")], [n_fsdp], (total_a,))
    else:
        own = lax.all_to_all(jnp.broadcast_to(mine[None], (n_fsdp, *mine.shape)), "fsdp", 0, 0, tiled=True)
        other = swap(own, "dp")
        exps, unit_a, total_a = scores(0, own, weights)
    exps, unit_c, total_c = scores(2, other, weights, exps=exps)
    exps, unit_b, total_b = scores(1, swap(own, "proto"), weights, exps=exps)
    exps, unit_d, totals = scores(3, swap(other, "proto"), weights, (total_a, total_b, total_c), exps)
    total = add_up(add_up(totals, "proto"), "fsdp")
    units = (unit_a, unit_b, unit_c, unit_d)
    student_grad = gradient(total, swap(total, "dp"), peak, unit, scale, units, exps)
    return (teacher_new, student_grad)


def solution(mesh):
    placed = (
        P(None, ("proto", "fsdp")),
        P(None, ("proto", "fsdp")),
        P("dp", "fsdp", None),
        P("dp", "fsdp", None),
        P("dp", "fsdp"),
        P("proto"),
    )
    return jax.shard_map(
        shards,
        mesh=mesh,
        in_specs=placed,
        out_specs=(P(None, ("proto", "fsdp")), P(None, ("proto", "fsdp", "dp"))),
        check_vma=False,
    )
```

```python
import functools
import math

import jax
import jax.numpy as jnp
from jax import lax
from jax.experimental import pallas as pl
from jax.experimental.pallas import tpu as pltpu
from jax.sharding import PartitionSpec as P

EPS = 1e-06
DEPTH = 256
GROUP = 512
STEP = 256
DIRECT = 8
LOG2E = math.log2(math.e)
GAIN_T = LOG2E / 0.04
GAIN_S = LOG2E / 0.1
LIMIT = 24 * 1024 * 1024
ON_CHIP = pl.BlockSpec(memory_space=pltpu.VMEM)
IN_HBM = pl.BlockSpec(memory_space=pl.ANY)


def shape(*dims, dtype=jnp.float32):
    return jax.ShapeDtypeStruct(dims, dtype)


def held(*dims, dtype=jnp.float32):
    return pltpu.VMEM(dims, dtype)


def call(kernel, name, out_shape, args, **more):
    many = isinstance(out_shape, (list, tuple))
    specs = dict(in_specs=[ON_CHIP] * len(args), out_specs=[ON_CHIP] * len(out_shape) if many else ON_CHIP)
    return pl.pallas_call(
        kernel,
        out_shape=out_shape,
        compiler_params=pltpu.CompilerParams(vmem_limit_bytes=LIMIT),
        cost_estimate=pl.CostEstimate(flops=1, bytes_accessed=1, transcendentals=0),
        name=name,
        **{**specs, **more},
    )(*args)


def swap(block, axis, apart=1):
    return lax.ppermute(block, axis, [(i, i ^ apart) for i in range(lax.axis_size(axis))])


def here():
    return lax.axis_index("dp"), lax.axis_index("fsdp"), lax.rem(lax.axis_index("proto"), 2)


def cast_split(row):
    high = row.astype(jnp.bfloat16).astype(jnp.float32)
    mid = (row - high).astype(jnp.bfloat16).astype(jnp.float32)
    return high, mid, row - high - mid


def prep_kernel(n_dp, teacher_hbm, student_hbm, center_hbm, new_hbm, wt_ref, ws_ref, unit_ref, scale_ref, peak_ref, *scratch):
    teacher_buf, student_buf, new_buf, center_buf, in_t, in_s, out, in_c = scratch
    chunks, bot, width = new_buf.shape
    own = chunks // n_dp
    dp, fsdp, _ = here()
    at = [slice(i * width, (i + 1) * width) for i in range(own)]
    far = [
        pl.ds(pl.multiple_of((lax.rem(dp + i // own, n_dp) * own + i % own) * width, width), width) for i in range(chunks)
    ]
    start = pl.multiple_of((fsdp * n_dp + dp) * (own * width), 128)
    center_load = pltpu.make_async_copy(center_hbm.at[:, pl.ds(start, own * width)], center_buf, in_c)
    loads = [
        (
            pltpu.make_async_copy(teacher_hbm.at[:, far[i]], teacher_buf.at[i], in_t.at[i]),
            pltpu.make_async_copy(student_hbm.at[:, far[i]], student_buf.at[i], in_s.at[i]),
        )
        for i in range(chunks)
    ]
    stores = [pltpu.make_async_copy(new_buf.at[i], new_hbm.at[:, far[i]], out.at[i]) for i in range(chunks)]
    center_load.start()
    for pair in loads:
        for load in pair:
            load.start()
    center_load.wait()
    center = center_buf[...]
    peak = jnp.max(-center, axis=1, keepdims=True)
    peak_ref[...] = jnp.broadcast_to(peak, peak_ref.shape)
    splits = cast_split(-center - peak)
    row = lax.broadcasted_iota(jnp.int32, (DEPTH - bot, width), 0)
    zero = jnp.zeros((DEPTH - bot, width), jnp.float32)
    for i in range(chunks):
        for load in loads[i]:
            load.wait()
        student = student_buf[i]
        new = 0.994 * teacher_buf[i] + 0.006 * student
        new_buf[i] = new
        stores[i].start()
        if i >= own:
            continue
        high, mid, low = [part[:, at[i]] for part in splits]
        extra = jnp.where(row == 0, high, jnp.where(row == 1, mid, jnp.where(row == 2, low, zero)))
        scale = lax.rsqrt(jnp.sum(student * student, axis=0, keepdims=True) + EPS)
        unit_s = student * scale
        unit_t = new * lax.rsqrt(jnp.sum(new * new, axis=0, keepdims=True) + EPS)
        wt_ref[at[i], :] = jnp.concatenate([unit_t, extra], axis=0).astype(jnp.bfloat16).T
        ws_ref[at[i], :] = jnp.concatenate([unit_s, zero], axis=0).astype(jnp.bfloat16).T
        unit_ref[:, at[i]] = unit_s
        scale_ref[:, at[i]] = scale
    for store in stores:
        store.wait()


def prepare(teacher_weight, student_weight, center, n_dp):
    bot, cols = teacher_weight.shape
    own = cols // n_dp
    width = min(512, own)
    chunks = cols // width
    return call(
        functools.partial(prep_kernel, n_dp),
        "prep",
        [
            pltpu.HBM((bot, cols), jnp.float32),
            held(own, DEPTH, dtype=jnp.bfloat16),
            held(own, DEPTH, dtype=jnp.bfloat16),
            held(bot, own),
            held(1, own),
            held(1, 128),
        ],
        (teacher_weight, student_weight, center),
        in_specs=[IN_HBM] * 3,
        out_specs=[IN_HBM] + [ON_CHIP] * 5,
        scratch_shapes=[held(chunks, bot, width)] * 3
        + [held(1, own)]
        + [pltpu.SemaphoreType.DMA((chunks,))] * 3
        + [pltpu.SemaphoreType.DMA],
    )


def fetch_kernel(student_hbm, teacher_hbm, student_ref, teacher_ref, sems):
    half = student_ref.shape[1]
    side = pl.ds(pl.multiple_of(here()[2] * half, half), half)
    loads = [
        pltpu.make_async_copy(student_hbm.at[:, side], student_ref, sems.at[0]),
        pltpu.make_async_copy(teacher_hbm, teacher_ref, sems.at[1]),
    ]
    for load in loads:
        load.start()
    for load in loads:
        load.wait()


def fetch(student, teacher):
    bot, crops = student.shape
    return call(
        fetch_kernel,
        "fetch",
        [held(bot, crops // 2, dtype=jnp.bfloat16), held(bot, crops, dtype=jnp.bfloat16)],
        (student, teacher),
        in_specs=[IN_HBM] * 2,
        scratch_shapes=[pltpu.SemaphoreType.DMA((2,))],
    )


def pack_kernel(student_ref, teacher_ref, index_ref, out_ref):
    half = out_ref.shape[2]
    lower = here()[2] == 0
    out_ref[0] = student_ref[...]
    index = jnp.where(lower, index_ref[:, :half], index_ref[:, half:])
    row = lax.broadcasted_iota(jnp.int32, (teacher_ref.shape[1], half), 0)
    pick = jnp.where(row == index, 1.0, 0.0).astype(jnp.bfloat16)
    out_ref[1] = jnp.dot(teacher_ref[...], pick, preferred_element_type=jnp.float32).astype(jnp.bfloat16)


def pack(student, teacher, index):
    bot, half = student.shape
    return call(pack_kernel, "pack", held(2, bot, half, dtype=jnp.bfloat16), (student, teacher, index))


def join_kernel(n_in, n_after, *refs):
    blocks = []
    for ref in refs[:n_in]:
        blocks += [ref] if len(ref.shape) == 3 else [ref.at[i] for i in range(ref.shape[0])]
    for ref in refs[n_in + n_after:]:
        skip = len(blocks) - ref.shape[0]
        for i in range(ref.shape[0]):
            ref[i] = blocks[skip + i][...]


def join(parts, counts, after):
    block = parts[0].shape[-3:]
    outs = [held(count, *block, dtype=jnp.bfloat16) for count in counts]
    kernel = functools.partial(join_kernel, len(parts), len(after))
    return call(kernel, "join", outs, (*parts, *after), in_specs=[ON_CHIP] * len(parts) + [IN_HBM] * len(after))


def log_sum(parts):
    top = functools.reduce(jnp.maximum, parts)
    return top + jnp.log2(sum(jnp.exp2(part - top) for part in parts))


def combine(parts):
    half = parts[0].shape[0] // 2
    return sum(part[:half] for part in parts), log_sum([part[half:] for part in parts])


def slot(k, n):
    return lax.axis_index("fsdp") ^ k if n <= DIRECT else k


def score_kernel(part, *refs):
    last = part == 3
    before, refs = (refs[:3], refs[3:]) if last else ((), refs)
    feats_ref, ws_ref, wt_ref, peak_ref, *refs = refs
    exp_ref, unit_ref, total_ref, *mine = refs[1:] if part else refs
    own_ref = mine[0] if last else total_ref
    n, _, bot, width = feats_ref.shape
    cols = ws_ref.shape[0]
    step = min(STEP, cols)
    per = max(1, min(n, GROUP // width))
    row = lax.broadcasted_iota(jnp.int32, (DEPTH - bot, per * width), 0)
    for which, w_ref, gain in ((0, ws_ref, GAIN_S), (1, wt_ref, GAIN_T)):
        base = (2 * part + which) * n * width
        extra = jnp.where(row < 3 * which, 1.0, 0.0).astype(jnp.bfloat16)
        for group in range(n // per):
            values = [feats_ref[group * per + k, which].astype(jnp.float32) for k in range(per)]
            values = jnp.concatenate(values, axis=1)
            unit = (values * lax.rsqrt(jnp.sum(values * values, axis=0, keepdims=True) + EPS)).astype(jnp.bfloat16)
            lanes = slice(group * per * width, (group + 1) * per * width)
            if which == 0:
                unit_ref[lanes, :] = unit.T
            stationary = jnp.concatenate([unit, extra], axis=0)
            total = jnp.zeros((8, per * width), jnp.float32)
            for at in range(0, cols, step):
                score = jnp.dot(w_ref[at:at + step, :], stationary, preferred_element_type=jnp.float32)
                exps = jnp.exp2(score * gain)
                total = total + jnp.sum(exps.reshape(step // 8, 8, per * width), axis=0)
                exp_ref[at:at + step, base + lanes.start:base + lanes.stop] = exps.astype(jnp.bfloat16)
            total = jnp.sum(total, axis=0, keepdims=True)
            if which == 1:
                total = jnp.log2(total) + GAIN_T * peak_ref[:, :1]
            own_ref[which:which + 1, lanes] = total
    if not last:
        return
    dp, _, core = here()
    own, pair, other = before
    parts = ((own, other), (pair, own_ref))
    rows = []
    for which in (0, 1):
        for half in (0, 1):
            pieces = []
            for view in (0, 1):
                first = (dp == view) if which == 0 else (dp != view)
                for place in range(n):
                    at = pl.ds(pl.multiple_of(slot(place, n) * width, width), width)
                    read = [[part[which:which + 1, at] for part in side] for side in parts]
                    mine, theirs = [jnp.where(first, *side) for side in read]
                    pieces.append(jnp.where(core == half, mine, theirs))
            rows.append(jnp.concatenate(pieces, axis=1))
    total_ref[...] = jnp.concatenate(rows, axis=0)


def scores(part, feats, weights, before=(), exps=None):
    n, _, bot, width = feats.shape
    cols, rows = weights[0].shape[0], n * width
    args = (*before, feats, *weights, *([exps] if part else []))
    return call(
        functools.partial(score_kernel, part),
        "scores",
        [
            held(cols, 8 * rows, dtype=jnp.bfloat16),
            held(rows, bot, dtype=jnp.bfloat16),
            held(4, 2 * rows) if part == 3 else held(2, rows),
        ],
        args,
        in_specs=[ON_CHIP] * (len(args) - bool(part)) + [IN_HBM] * bool(part),
        input_output_aliases={len(args) - 1: 0} if part else {},
        scratch_shapes=[held(2, rows)] if part == 3 else [],
    )


def relay_kernel(*refs):
    parts = [ref[...] for ref in refs[:-1]]
    if len(parts[0].shape) == 3:
        parts = [parts[0][i] for i in range(parts[0].shape[0])]
    refs[-1][...] = jnp.concatenate(combine(parts), axis=0)


def add_up(total, axis):
    n = lax.axis_size(axis)
    if axis == "proto":
        pairs = lambda k: [(i, i ^ k) for i in range(n) if (i ^ k) % 2]
        parts = [total, *[lax.ppermute(total, axis, pairs(k)) for k in range(1, n)]]
    elif n <= DIRECT:
        n_proto = lax.axis_size("proto")
        axes = ("fsdp", "proto") if axis == "fsdp" else ("proto", "dp")
        place = (lambda i, p: i * n_proto + p) if axis == "fsdp" else (lambda i, p: p * n + i)
        pairs = lambda k: [(place(i, p), place(i ^ k, p)) for p in range(1, n_proto, 2) for i in range(n)]
        parts = [total, *[lax.ppermute(total, axes, pairs(k)) for k in range(1, n)]]
    else:
        parts = [lax.all_to_all(jnp.broadcast_to(total[None], (n, *total.shape)), axis, 0, 0, tiled=True)]
    return call(relay_kernel, "relay", held(*total.shape), parts)


def grad_kernel(led_ref, given_ref, peak_ref, weight_unit, weight_scale, *refs):
    units, exp_ref, out_hbm, scales, buf, sems = refs[:4], *refs[4:]
    dp, _, core = here()
    total = jnp.where(core == 1, led_ref[...], given_ref[...])
    scales[0:2, :] = 10.0 / total[:2]
    log_t = total[2:]
    scales[2:4, :] = 10.0 * jnp.exp2(GAIN_T * peak_ref[:, :1] - log_t)
    rows = units[0].shape[0]
    width = 128
    n = rows // width
    factors = []
    for part in range(4):
        view, half = divmod(part, 2)
        base = (dp ^ view) * rows
        at = [pl.ds(pl.multiple_of(base + slot(k, n) * width, width), width) for k in range(n)]
        for which in (0, 1):
            picked = [
                jnp.where(core == half, scales[2 * which:2 * which + 1, where], scales[2 * which + 1:2 * which + 2, where])
                for where in at
            ]
            factors.append(jnp.concatenate(picked, axis=1).astype(jnp.bfloat16))
    feats = jnp.concatenate([unit[...] for unit in units], axis=0)
    chunks, _, step = buf.shape
    stores = []
    for i in range(chunks):
        at = slice(i * step, (i + 1) * step)
        derivs = []
        for part in range(4):
            lies_s, lies_t = 2 * part * rows, (2 * (part ^ 2) + 1) * rows
            probs_s = exp_ref[at, lies_s:lies_s + rows] * factors[2 * part]
            probs_t = exp_ref[at, lies_t:lies_t + rows] * factors[2 * part + 1]
            derivs.append(probs_s - probs_t)
        derivs = jnp.concatenate(derivs, axis=1)
        grad = jnp.dot(derivs, feats, preferred_element_type=jnp.float32).T
        unit = weight_unit[:, at]
        proj = unit * jnp.sum(unit * grad, axis=0, keepdims=True)
        buf[i] = (grad - proj) * weight_scale[:, at]
        stores.append(pltpu.make_async_copy(buf.at[i], out_hbm.at[:, at], sems.at[i]))
        stores[i].start()
    for store in stores:
        store.wait()


def gradient(led, given, peak, weight_unit, weight_scale, units, exps):
    cols = exps.shape[0]
    rows, bot = units[0].shape
    step = min(512, cols)
    args = (led, given, peak, weight_unit, weight_scale, *units, exps)
    return call(
        grad_kernel,
        "gradient",
        pltpu.HBM((bot, cols), jnp.float32),
        args,
        out_specs=IN_HBM,
        scratch_shapes=[held(4, 2 * rows), held(cols // step, bot, step), pltpu.SemaphoreType.DMA((cols // step,))],
    )


def shards(teacher_weight, student_weight, teacher_feats, student_feats, pairing, center):
    n_dp, n_fsdp = lax.axis_size("dp"), lax.axis_size("fsdp")
    in_hbm = lambda array: pltpu.with_memory_space_constraint(array, pltpu.HBM)
    teacher_weight, student_weight, center = in_hbm(teacher_weight), in_hbm(student_weight), in_hbm(center[None, :])

    index = swap(pairing, "dp")
    mine = pack(*fetch(in_hbm(student_feats[0].T), in_hbm(teacher_feats[0].T)), index)
    teacher_new, wt, ws, unit, scale, peak = prepare(teacher_weight, student_weight, center, n_dp)
    weights = (ws, wt, peak)
    if n_fsdp <= DIRECT:
        other = [swap(mine, "dp")]
        along = [swap(mine, "fsdp", k) for k in range(1, n_fsdp)]
        other.append(swap(other[0], "fsdp"))
        own, far = join([mine, *along], [n_fsdp, n_fsdp - 2], (other[1], peak))
    else:
        own = lax.all_to_all(jnp.broadcast_to(mine[None], (n_fsdp, *mine.shape)), "fsdp", 0, 0, tiled=True)
        other = swap(own, "dp")
    exps, unit_a, total_a = scores(0, own, weights)
    exps, unit_b, total_b = scores(1, swap(own, "proto"), weights, exps=exps)
    if n_fsdp <= DIRECT:
        (other,) = join([*other, swap(far, "dp")], [n_fsdp], (total_b,))
    exps, unit_c, total_c = scores(2, other, weights, exps=exps)
    exps, unit_d, total = scores(3, swap(other, "proto"), weights, (total_a, total_b, total_c), exps)
    for axis in ("proto", "fsdp", "dp"):
        total = add_up(total, axis)
    given = lax.ppermute(total, "proto", [(i, i ^ 1) for i in range(1, lax.axis_size("proto"), 2)])
    student_grad = gradient(total, given, peak, unit, scale, (unit_a, unit_b, unit_c, unit_d), exps)
    return (teacher_new, student_grad)


def solution(mesh):
    placed = (
        P(None, ("proto", "fsdp")),
        P(None, ("proto", "fsdp")),
        P("dp", "fsdp", None),
        P("dp", "fsdp", None),
        P("dp", "fsdp"),
        P("proto"),
    )
    return jax.shard_map(
        shards,
        mesh=mesh,
        in_specs=placed,
        out_specs=(P(None, ("proto", "fsdp")), P(None, ("proto", "fsdp", "dp"))),
        check_vma=False,
    )
```

```python
import functools
import math

import jax
import jax.numpy as jnp
from jax import lax
from jax.experimental import pallas as pl
from jax.experimental.pallas import tpu as pltpu
from jax.sharding import PartitionSpec as P

EPS = 1e-06
DEPTH = 256
GROUP = 512
STEP = 256
DIRECT = 8
LOG2E = math.log2(math.e)
GAIN_T = LOG2E / 0.04
GAIN_S = LOG2E / 0.1
LIMIT = 24 * 1024 * 1024
ON_CHIP = pl.BlockSpec(memory_space=pltpu.VMEM)
IN_HBM = pl.BlockSpec(memory_space=pl.ANY)


def shape(*dims, dtype=jnp.float32):
    return jax.ShapeDtypeStruct(dims, dtype)


def held(*dims, dtype=jnp.float32):
    return pltpu.VMEM(dims, dtype)


def call(kernel, name, out_shape, args, **more):
    many = isinstance(out_shape, (list, tuple))
    specs = dict(in_specs=[ON_CHIP] * len(args), out_specs=[ON_CHIP] * len(out_shape) if many else ON_CHIP)
    return pl.pallas_call(
        kernel,
        out_shape=out_shape,
        compiler_params=pltpu.CompilerParams(vmem_limit_bytes=LIMIT),
        cost_estimate=pl.CostEstimate(flops=1, bytes_accessed=1, transcendentals=0),
        name=name,
        **{**specs, **more},
    )(*args)


def swap(block, axis, apart=1):
    return lax.ppermute(block, axis, [(i, i ^ apart) for i in range(lax.axis_size(axis))])


def here():
    return lax.axis_index("dp"), lax.axis_index("fsdp"), lax.rem(lax.axis_index("proto"), 2)


def cast_split(row):
    high = row.astype(jnp.bfloat16).astype(jnp.float32)
    mid = (row - high).astype(jnp.bfloat16).astype(jnp.float32)
    return high, mid, row - high - mid


def prep_kernel(n_dp, teacher_hbm, student_hbm, center_hbm, new_hbm, wt_ref, ws_ref, unit_ref, scale_ref, peak_ref, *scratch):
    teacher_buf, student_buf, new_buf, center_buf, in_t, in_s, out, in_c = scratch
    chunks, bot, width = new_buf.shape
    dp, fsdp, _ = here()
    first = dp * (chunks * width)
    at = [slice(i * width, (i + 1) * width) for i in range(chunks)]
    far = [pl.ds(pl.multiple_of(first + i * width, width), width) for i in range(chunks)]
    start = pl.multiple_of((fsdp * n_dp + dp) * (chunks * width), 128)
    center_load = pltpu.make_async_copy(center_hbm.at[:, pl.ds(start, chunks * width)], center_buf, in_c)
    loads = [
        (
            pltpu.make_async_copy(teacher_hbm.at[:, far[i]], teacher_buf.at[i], in_t.at[i]),
            pltpu.make_async_copy(student_hbm.at[:, far[i]], student_buf.at[i], in_s.at[i]),
        )
        for i in range(chunks)
    ]
    stores = [pltpu.make_async_copy(new_buf.at[i], new_hbm.at[:, far[i]], out.at[i]) for i in range(chunks)]
    center_load.start()
    for pair in loads:
        for load in pair:
            load.start()
    center_load.wait()
    center = center_buf[...]
    peak = jnp.max(-center, axis=1, keepdims=True)
    peak_ref[...] = jnp.broadcast_to(peak, peak_ref.shape)
    splits = cast_split(-center - peak)
    row = lax.broadcasted_iota(jnp.int32, (DEPTH - bot, width), 0)
    zero = jnp.zeros((DEPTH - bot, width), jnp.float32)
    for i in range(chunks):
        for load in loads[i]:
            load.wait()
        student = student_buf[i]
        new = 0.994 * teacher_buf[i] + 0.006 * student
        new_buf[i] = new
        stores[i].start()
        high, mid, low = [part[:, at[i]] for part in splits]
        extra = jnp.where(row == 0, high, jnp.where(row == 1, mid, jnp.where(row == 2, low, zero)))
        scale = lax.rsqrt(jnp.sum(student * student, axis=0, keepdims=True) + EPS)
        unit_s = student * scale
        unit_t = new * lax.rsqrt(jnp.sum(new * new, axis=0, keepdims=True) + EPS)
        wt_ref[at[i], :] = jnp.concatenate([unit_t, extra], axis=0).astype(jnp.bfloat16).T
        ws_ref[at[i], :] = jnp.concatenate([unit_s, zero], axis=0).astype(jnp.bfloat16).T
        unit_ref[:, at[i]] = unit_s
        scale_ref[:, at[i]] = scale
    for store in stores:
        store.wait()


def prepare(teacher_weight, student_weight, center, n_dp):
    bot, cols = teacher_weight.shape
    own = cols // n_dp
    width = min(512, own)
    chunks = own // width
    return call(
        functools.partial(prep_kernel, n_dp),
        "prep",
        [
            pltpu.HBM((bot, cols), jnp.float32),
            held(own, DEPTH, dtype=jnp.bfloat16),
            held(own, DEPTH, dtype=jnp.bfloat16),
            held(bot, own),
            held(1, own),
            held(1, 128),
        ],
        (teacher_weight, student_weight, center),
        in_specs=[IN_HBM] * 3,
        out_specs=[IN_HBM] + [ON_CHIP] * 5,
        scratch_shapes=[held(chunks, bot, width)] * 3
        + [held(1, own)]
        + [pltpu.SemaphoreType.DMA((chunks,))] * 3
        + [pltpu.SemaphoreType.DMA],
    )


def rest_kernel(teacher_hbm, student_hbm, after, before_hbm, new_hbm, done_ref, *scratch):
    teacher_buf, student_buf, new_buf, in_t, in_s, out = scratch
    chunks, bot, width = new_buf.shape
    own = chunks * width
    parts = teacher_hbm.shape[1] // own - 1
    dp = here()[0]
    done_ref[...] = jnp.zeros_like(done_ref)
    for part in range(parts):
        first = lax.rem(dp + 1 + part, parts + 1) * own
        far = [pl.ds(pl.multiple_of(first + i * width, width), width) for i in range(chunks)]
        loads = [
            (
                pltpu.make_async_copy(teacher_hbm.at[:, far[i]], teacher_buf.at[i], in_t.at[i]),
                pltpu.make_async_copy(student_hbm.at[:, far[i]], student_buf.at[i], in_s.at[i]),
            )
            for i in range(chunks)
        ]
        stores = [pltpu.make_async_copy(new_buf.at[i], new_hbm.at[:, far[i]], out.at[i]) for i in range(chunks)]
        for pair in loads:
            for load in pair:
                load.start()
        for i in range(chunks):
            for load in loads[i]:
                load.wait()
            new_buf[i] = 0.994 * teacher_buf[i] + 0.006 * student_buf[i]
            stores[i].start()
        for store in stores:
            store.wait()


def update_rest(teacher_weight, student_weight, after, new, own):
    bot, cols = teacher_weight.shape
    width = min(512, own)
    chunks = own // width
    return call(
        rest_kernel,
        "rest",
        [pltpu.HBM((bot, cols), jnp.float32), held(8, 128)],
        (teacher_weight, student_weight, after, new),
        in_specs=[IN_HBM] * 4,
        out_specs=[IN_HBM, ON_CHIP],
        input_output_aliases={3: 0},
        scratch_shapes=[held(chunks, bot, width)] * 3 + [pltpu.SemaphoreType.DMA((chunks,))] * 3,
    )


def fetch_kernel(student_hbm, teacher_hbm, student_ref, teacher_ref, sems):
    half = student_ref.shape[1]
    side = pl.ds(pl.multiple_of(here()[2] * half, half), half)
    loads = [
        pltpu.make_async_copy(student_hbm.at[:, side], student_ref, sems.at[0]),
        pltpu.make_async_copy(teacher_hbm, teacher_ref, sems.at[1]),
    ]
    for load in loads:
        load.start()
    for load in loads:
        load.wait()


def fetch(student, teacher):
    bot, crops = student.shape
    return call(
        fetch_kernel,
        "fetch",
        [held(bot, crops // 2, dtype=jnp.bfloat16), held(bot, crops, dtype=jnp.bfloat16)],
        (student, teacher),
        in_specs=[IN_HBM] * 2,
        scratch_shapes=[pltpu.SemaphoreType.DMA((2,))],
    )


def pack_kernel(student_ref, teacher_ref, index_ref, out_ref):
    half = out_ref.shape[2]
    lower = here()[2] == 0
    out_ref[0] = student_ref[...]
    index = jnp.where(lower, index_ref[:, :half], index_ref[:, half:])
    row = lax.broadcasted_iota(jnp.int32, (teacher_ref.shape[1], half), 0)
    pick = jnp.where(row == index, 1.0, 0.0).astype(jnp.bfloat16)
    out_ref[1] = jnp.dot(teacher_ref[...], pick, preferred_element_type=jnp.float32).astype(jnp.bfloat16)


def pack(student, teacher, index):
    bot, half = student.shape
    return call(pack_kernel, "pack", held(2, bot, half, dtype=jnp.bfloat16), (student, teacher, index))


def join_kernel(n_in, n_after, *refs):
    blocks = []
    for ref in refs[:n_in]:
        blocks += [ref] if len(ref.shape) == 3 else [ref.at[i] for i in range(ref.shape[0])]
    for ref in refs[n_in + n_after:]:
        skip = len(blocks) - ref.shape[0]
        for i in range(ref.shape[0]):
            ref[i] = blocks[skip + i][...]


def join(parts, counts, after):
    block = parts[0].shape[-3:]
    outs = [held(count, *block, dtype=jnp.bfloat16) for count in counts]
    kernel = functools.partial(join_kernel, len(parts), len(after))
    return call(kernel, "join", outs, (*parts, *after), in_specs=[ON_CHIP] * len(parts) + [IN_HBM] * len(after))


def log_sum(parts):
    top = functools.reduce(jnp.maximum, parts)
    return top + jnp.log2(sum(jnp.exp2(part - top) for part in parts))


def combine(parts):
    half = parts[0].shape[0] // 2
    return sum(part[:half] for part in parts), log_sum([part[half:] for part in parts])


def slot(k, n):
    return lax.axis_index("fsdp") ^ k if n <= DIRECT else k


def score_kernel(part, *refs):
    last = part == 3
    before, refs = (refs[:3], refs[3:]) if last else ((), refs)
    feats_ref, ws_ref, wt_ref, peak_ref, *refs = refs
    exp_ref, unit_ref, total_ref, *mine = refs[1:] if part else refs
    own_ref = mine[0] if last else total_ref
    n, _, bot, width = feats_ref.shape
    cols = ws_ref.shape[0]
    step = min(STEP, cols)
    per = max(1, min(n, GROUP // width))
    row = lax.broadcasted_iota(jnp.int32, (DEPTH - bot, per * width), 0)
    for which, w_ref, gain in ((0, ws_ref, GAIN_S), (1, wt_ref, GAIN_T)):
        base = (2 * part + which) * n * width
        extra = jnp.where(row < 3 * which, 1.0, 0.0).astype(jnp.bfloat16)
        for group in range(n // per):
            values = [feats_ref[group * per + k, which].astype(jnp.float32) for k in range(per)]
            values = jnp.concatenate(values, axis=1)
            unit = (values * lax.rsqrt(jnp.sum(values * values, axis=0, keepdims=True) + EPS)).astype(jnp.bfloat16)
            lanes = slice(group * per * width, (group + 1) * per * width)
            if which == 0:
                unit_ref[lanes, :] = unit.T
            stationary = jnp.concatenate([unit, extra], axis=0)
            total = jnp.zeros((8, per * width), jnp.float32)
            for at in range(0, cols, step):
                score = jnp.dot(w_ref[at:at + step, :], stationary, preferred_element_type=jnp.float32)
                exps = jnp.exp2(score * gain)
                total = total + jnp.sum(exps.reshape(step // 8, 8, per * width), axis=0)
                exp_ref[at:at + step, base + lanes.start:base + lanes.stop] = exps.astype(jnp.bfloat16)
            total = jnp.sum(total, axis=0, keepdims=True)
            if which == 1:
                total = jnp.log2(total) + GAIN_T * peak_ref[:, :1]
            own_ref[which:which + 1, lanes] = total
    if not last:
        return
    dp, _, core = here()
    own, pair, other = before
    parts = ((own, other), (pair, own_ref))
    rows = []
    for which in (0, 1):
        for half in (0, 1):
            pieces = []
            for view in (0, 1):
                first = (dp == view) if which == 0 else (dp != view)
                for place in range(n):
                    at = pl.ds(pl.multiple_of(slot(place, n) * width, width), width)
                    read = [[part[which:which + 1, at] for part in side] for side in parts]
                    mine, theirs = [jnp.where(first, *side) for side in read]
                    pieces.append(jnp.where(core == half, mine, theirs))
            rows.append(jnp.concatenate(pieces, axis=1))
    total_ref[...] = jnp.concatenate(rows, axis=0)


def scores(part, feats, weights, before=(), exps=None):
    n, _, bot, width = feats.shape
    cols, rows = weights[0].shape[0], n * width
    args = (*before, feats, *weights, *([exps] if part else []))
    return call(
        functools.partial(score_kernel, part),
        "scores",
        [
            held(cols, 8 * rows, dtype=jnp.bfloat16),
            held(rows, bot, dtype=jnp.bfloat16),
            held(4, 2 * rows) if part == 3 else held(2, rows),
        ],
        args,
        in_specs=[ON_CHIP] * (len(args) - bool(part)) + [IN_HBM] * bool(part),
        input_output_aliases={len(args) - 1: 0} if part else {},
        scratch_shapes=[held(2, rows)] if part == 3 else [],
    )


def relay_kernel(*refs):
    parts = [ref[...] for ref in refs[:-1]]
    if len(parts[0].shape) == 3:
        parts = [parts[0][i] for i in range(parts[0].shape[0])]
    refs[-1][...] = jnp.concatenate(combine(parts), axis=0)


def add_up(total, *others):
    return call(relay_kernel, "relay", held(*total.shape), [total, *others])


def add_up_all(total):
    n_proto, n_dp, n_fsdp = [lax.axis_size(axis) for axis in ("proto", "dp", "fsdp")]
    total = add_up(total, swap(total, "proto"))

    def across(up, over):
        places = [(p, d) for p in range(n_proto) for d in range(n_dp)]
        pairs = [(p * n_dp + d, (p ^ up) * n_dp + (d ^ over)) for p, d in places]
        return lax.ppermute(total, ("proto", "dp"), pairs)

    steps = [(up, over) for up in range(0, n_proto, 2) for over in range(n_dp)][1:]
    total = add_up(total, *[across(*step) for step in steps])
    if n_fsdp <= DIRECT:
        return add_up(total, *[swap(total, "fsdp", k) for k in range(1, n_fsdp)])
    copies = jnp.broadcast_to(total[None], (n_fsdp, *total.shape))
    parts = lax.all_to_all(copies, "fsdp", 0, 0, tiled=True)
    return call(relay_kernel, "relay", held(*total.shape), [parts])


def grad_kernel(total_ref, peak_ref, weight_unit, weight_scale, *refs):
    units, exp_ref, out_hbm, scales, buf, sems = refs[:4], *refs[4:]
    dp, _, core = here()
    scales[0:2, :] = 10.0 / total_ref[0:2, :]
    scales[2:4, :] = 10.0 * jnp.exp2(GAIN_T * peak_ref[:, :1] - total_ref[2:4, :])
    rows = units[0].shape[0]
    width = 128
    n = rows // width
    factors = []
    for part in range(4):
        view, half = divmod(part, 2)
        base = (dp ^ view) * rows
        at = [pl.ds(pl.multiple_of(base + slot(k, n) * width, width), width) for k in range(n)]
        for which in (0, 1):
            picked = [
                jnp.where(core == half, scales[2 * which:2 * which + 1, where], scales[2 * which + 1:2 * which + 2, where])
                for where in at
            ]
            factors.append(jnp.concatenate(picked, axis=1).astype(jnp.bfloat16))
    feats = jnp.concatenate([unit[...] for unit in units], axis=0)
    chunks, _, step = buf.shape
    stores = []
    for i in range(chunks):
        at = slice(i * step, (i + 1) * step)
        derivs = []
        for part in range(4):
            lies_s, lies_t = 2 * part * rows, (2 * (part ^ 2) + 1) * rows
            probs_s = exp_ref[at, lies_s:lies_s + rows] * factors[2 * part]
            probs_t = exp_ref[at, lies_t:lies_t + rows] * factors[2 * part + 1]
            derivs.append(probs_s - probs_t)
        derivs = jnp.concatenate(derivs, axis=1)
        grad = jnp.dot(derivs, feats, preferred_element_type=jnp.float32).T
        unit = weight_unit[:, at]
        proj = unit * jnp.sum(unit * grad, axis=0, keepdims=True)
        buf[i] = (grad - proj) * weight_scale[:, at]
        stores.append(pltpu.make_async_copy(buf.at[i], out_hbm.at[:, at], sems.at[i]))
        stores[i].start()
    for store in stores:
        store.wait()


def gradient(total, peak, weight_unit, weight_scale, units, exps):
    cols = exps.shape[0]
    rows, bot = units[0].shape
    step = min(512, cols)
    args = (total, peak, weight_unit, weight_scale, *units, exps)
    return call(
        grad_kernel,
        "gradient",
        pltpu.HBM((bot, cols), jnp.float32),
        args,
        out_specs=IN_HBM,
        scratch_shapes=[held(4, 2 * rows), held(cols // step, bot, step), pltpu.SemaphoreType.DMA((cols // step,))],
    )


def shards(teacher_weight, student_weight, teacher_feats, student_feats, pairing, center):
    n_dp, n_fsdp = lax.axis_size("dp"), lax.axis_size("fsdp")
    in_hbm = lambda array: pltpu.with_memory_space_constraint(array, pltpu.HBM)
    teacher_weight, student_weight, center = in_hbm(teacher_weight), in_hbm(student_weight), in_hbm(center[None, :])

    index = swap(pairing, "dp")
    mine = pack(*fetch(in_hbm(student_feats[0].T), in_hbm(teacher_feats[0].T)), index)
    new, wt, ws, unit, scale, peak = prepare(teacher_weight, student_weight, center, n_dp)
    weights = (ws, wt, peak)
    if n_fsdp <= DIRECT:
        other = [swap(mine, "dp")]
        along = [swap(mine, "fsdp", k) for k in range(1, n_fsdp)]
        own, far = join([mine, *along], [n_fsdp, n_fsdp - 2], (other[0], peak))
        other += [swap(other[0], "fsdp"), swap(far, "dp")]
    else:
        own = lax.all_to_all(jnp.broadcast_to(mine[None], (n_fsdp, *mine.shape)), "fsdp", 0, 0, tiled=True)
        other = [swap(own, "dp")]
    exps, unit_a, total_a = scores(0, own, weights)
    teacher_new, done = update_rest(teacher_weight, student_weight, total_a, new, ws.shape[0])
    (other,) = join(other, [n_fsdp], (done,))
    exps, unit_c, total_c = scores(2, other, weights, exps=exps)
    exps, unit_b, total_b = scores(1, swap(own, "proto"), weights, exps=exps)
    exps, unit_d, total = scores(3, swap(other, "proto"), weights, (total_a, total_b, total_c), exps)
    total = add_up_all(total)
    student_grad = gradient(total, peak, unit, scale, (unit_a, unit_b, unit_c, unit_d), exps)
    return (teacher_new, student_grad)


def solution(mesh):
    placed = (
        P(None, ("proto", "fsdp")),
        P(None, ("proto", "fsdp")),
        P("dp", "fsdp", None),
        P("dp", "fsdp", None),
        P("dp", "fsdp"),
        P("proto"),
    )
    return jax.shard_map(
        shards,
        mesh=mesh,
        in_specs=placed,
        out_specs=(P(None, ("proto", "fsdp")), P(None, ("proto", "fsdp", "dp"))),
        check_vma=False,
    )
```

```python
import functools
import math

import jax
import jax.numpy as jnp
from jax import lax
from jax.experimental import pallas as pl
from jax.experimental.pallas import tpu as pltpu
from jax.sharding import PartitionSpec as P

EPS = 1e-06
DEPTH = 256
GROUP = 512
STEP = 256
DIRECT = 8
LOG2E = math.log2(math.e)
GAIN_T = LOG2E / 0.04
GAIN_S = LOG2E / 0.1
LIMIT = 24 * 1024 * 1024
ON_CHIP = pl.BlockSpec(memory_space=pltpu.VMEM)
IN_HBM = pl.BlockSpec(memory_space=pl.ANY)


def shape(*dims, dtype=jnp.float32):
    return jax.ShapeDtypeStruct(dims, dtype)


def held(*dims, dtype=jnp.float32):
    return pltpu.VMEM(dims, dtype)


def call(kernel, name, out_shape, args, **more):
    many = isinstance(out_shape, (list, tuple))
    specs = dict(in_specs=[ON_CHIP] * len(args), out_specs=[ON_CHIP] * len(out_shape) if many else ON_CHIP)
    return pl.pallas_call(
        kernel,
        out_shape=out_shape,
        compiler_params=pltpu.CompilerParams(vmem_limit_bytes=LIMIT),
        cost_estimate=pl.CostEstimate(flops=1, bytes_accessed=1, transcendentals=0),
        name=name,
        **{**specs, **more},
    )(*args)


def swap(block, axis, apart=1):
    return lax.ppermute(block, axis, [(i, i ^ apart) for i in range(lax.axis_size(axis))])


def here():
    return lax.axis_index("dp"), lax.axis_index("fsdp"), lax.rem(lax.axis_index("proto"), 2)


def cast_split(row):
    high = row.astype(jnp.bfloat16).astype(jnp.float32)
    mid = (row - high).astype(jnp.bfloat16).astype(jnp.float32)
    return high, mid, row - high - mid


def prep_kernel(n_dp, teacher_hbm, student_hbm, center_hbm, new_hbm, wt_ref, ws_ref, unit_ref, scale_ref, peak_ref, *scratch):
    teacher_buf, student_buf, new_buf, center_buf, in_t, in_s, out, in_c = scratch
    chunks, bot, width = new_buf.shape
    dp, fsdp, _ = here()
    first = dp * (chunks * width)
    at = [slice(i * width, (i + 1) * width) for i in range(chunks)]
    far = [pl.ds(pl.multiple_of(first + i * width, width), width) for i in range(chunks)]
    start = pl.multiple_of((fsdp * n_dp + dp) * (chunks * width), 128)
    center_load = pltpu.make_async_copy(center_hbm.at[:, pl.ds(start, chunks * width)], center_buf, in_c)
    loads = [
        (
            pltpu.make_async_copy(teacher_hbm.at[:, far[i]], teacher_buf.at[i], in_t.at[i]),
            pltpu.make_async_copy(student_hbm.at[:, far[i]], student_buf.at[i], in_s.at[i]),
        )
        for i in range(chunks)
    ]
    stores = [pltpu.make_async_copy(new_buf.at[i], new_hbm.at[:, far[i]], out.at[i]) for i in range(chunks)]
    center_load.start()
    for pair in loads:
        for load in pair:
            load.start()
    center_load.wait()
    center = center_buf[...]
    peak = jnp.max(-center, axis=1, keepdims=True)
    peak_ref[...] = jnp.broadcast_to(peak, peak_ref.shape)
    splits = cast_split(-center - peak)
    row = lax.broadcasted_iota(jnp.int32, (DEPTH - bot, width), 0)
    zero = jnp.zeros((DEPTH - bot, width), jnp.float32)
    for i in range(chunks):
        for load in loads[i]:
            load.wait()
        student = student_buf[i]
        new = 0.994 * teacher_buf[i] + 0.006 * student
        new_buf[i] = new
        stores[i].start()
        high, mid, low = [part[:, at[i]] for part in splits]
        extra = jnp.where(row == 0, high, jnp.where(row == 1, mid, jnp.where(row == 2, low, zero)))
        scale = lax.rsqrt(jnp.sum(student * student, axis=0, keepdims=True) + EPS)
        unit_s = student * scale
        unit_t = new * lax.rsqrt(jnp.sum(new * new, axis=0, keepdims=True) + EPS)
        wt_ref[at[i], :] = jnp.concatenate([unit_t, extra], axis=0).astype(jnp.bfloat16).T
        ws_ref[at[i], :] = jnp.concatenate([unit_s, zero], axis=0).astype(jnp.bfloat16).T
        unit_ref[:, at[i]] = unit_s
        scale_ref[:, at[i]] = scale
    for store in stores:
        store.wait()


def prepare(teacher_weight, student_weight, center, n_dp):
    bot, cols = teacher_weight.shape
    own = cols // n_dp
    width = min(512, own)
    chunks = own // width
    return call(
        functools.partial(prep_kernel, n_dp),
        "prep",
        [
            pltpu.HBM((bot, cols), jnp.float32),
            held(own, DEPTH, dtype=jnp.bfloat16),
            held(own, DEPTH, dtype=jnp.bfloat16),
            held(bot, own),
            held(1, own),
            held(1, 128),
        ],
        (teacher_weight, student_weight, center),
        in_specs=[IN_HBM] * 3,
        out_specs=[IN_HBM] + [ON_CHIP] * 5,
        scratch_shapes=[held(chunks, bot, width)] * 3
        + [held(1, own)]
        + [pltpu.SemaphoreType.DMA((chunks,))] * 3
        + [pltpu.SemaphoreType.DMA],
    )


def rest_kernel(teacher_hbm, student_hbm, after, before_hbm, new_hbm, done_ref, *scratch):
    teacher_buf, student_buf, new_buf, in_t, in_s, out = scratch
    chunks, bot, width = new_buf.shape
    own = chunks * width
    parts = teacher_hbm.shape[1] // own - 1
    dp = here()[0]
    done_ref[...] = jnp.zeros_like(done_ref)
    for part in range(parts):
        first = lax.rem(dp + 1 + part, parts + 1) * own
        far = [pl.ds(pl.multiple_of(first + i * width, width), width) for i in range(chunks)]
        loads = [
            (
                pltpu.make_async_copy(teacher_hbm.at[:, far[i]], teacher_buf.at[i], in_t.at[i]),
                pltpu.make_async_copy(student_hbm.at[:, far[i]], student_buf.at[i], in_s.at[i]),
            )
            for i in range(chunks)
        ]
        stores = [pltpu.make_async_copy(new_buf.at[i], new_hbm.at[:, far[i]], out.at[i]) for i in range(chunks)]
        for pair in loads:
            for load in pair:
                load.start()
        for i in range(chunks):
            for load in loads[i]:
                load.wait()
            new_buf[i] = 0.994 * teacher_buf[i] + 0.006 * student_buf[i]
            stores[i].start()
        for store in stores:
            store.wait()


def update_rest(teacher_weight, student_weight, after, new, own):
    bot, cols = teacher_weight.shape
    width = min(512, own)
    chunks = own // width
    return call(
        rest_kernel,
        "rest",
        [pltpu.HBM((bot, cols), jnp.float32), held(8, 128)],
        (teacher_weight, student_weight, after, new),
        in_specs=[IN_HBM] * 4,
        out_specs=[IN_HBM, ON_CHIP],
        input_output_aliases={3: 0},
        scratch_shapes=[held(chunks, bot, width)] * 3 + [pltpu.SemaphoreType.DMA((chunks,))] * 3,
    )


def fetch_kernel(student_hbm, teacher_hbm, student_ref, teacher_ref, sems):
    half = student_ref.shape[1]
    side = pl.ds(pl.multiple_of(here()[2] * half, half), half)
    loads = [
        pltpu.make_async_copy(student_hbm.at[:, side], student_ref, sems.at[0]),
        pltpu.make_async_copy(teacher_hbm, teacher_ref, sems.at[1]),
    ]
    for load in loads:
        load.start()
    for load in loads:
        load.wait()


def fetch(student, teacher):
    bot, crops = student.shape
    return call(
        fetch_kernel,
        "fetch",
        [held(bot, crops // 2, dtype=jnp.bfloat16), held(bot, crops, dtype=jnp.bfloat16)],
        (student, teacher),
        in_specs=[IN_HBM] * 2,
        scratch_shapes=[pltpu.SemaphoreType.DMA((2,))],
    )


def pack_kernel(student_ref, teacher_ref, index_ref, out_ref):
    half = out_ref.shape[2]
    lower = here()[2] == 0
    out_ref[0] = student_ref[...]
    index = jnp.where(lower, index_ref[:, :half], index_ref[:, half:])
    row = lax.broadcasted_iota(jnp.int32, (teacher_ref.shape[1], half), 0)
    pick = jnp.where(row == index, 1.0, 0.0).astype(jnp.bfloat16)
    out_ref[1] = jnp.dot(teacher_ref[...], pick, preferred_element_type=jnp.float32).astype(jnp.bfloat16)


def pack(student, teacher, index):
    bot, half = student.shape
    return call(pack_kernel, "pack", held(2, bot, half, dtype=jnp.bfloat16), (student, teacher, index))


def join_kernel(n_in, n_after, *refs):
    blocks = []
    for ref in refs[:n_in]:
        blocks += [ref] if len(ref.shape) == 3 else [ref.at[i] for i in range(ref.shape[0])]
    for ref in refs[n_in + n_after:]:
        skip = len(blocks) - ref.shape[0]
        for i in range(ref.shape[0]):
            ref[i] = blocks[skip + i][...]


def join(parts, counts, after):
    block = parts[0].shape[-3:]
    outs = [held(count, *block, dtype=jnp.bfloat16) for count in counts]
    kernel = functools.partial(join_kernel, len(parts), len(after))
    return call(kernel, "join", outs, (*parts, *after), in_specs=[ON_CHIP] * len(parts) + [IN_HBM] * len(after))


def log_sum(parts):
    top = functools.reduce(jnp.maximum, parts)
    return top + jnp.log2(sum(jnp.exp2(part - top) for part in parts))


def combine(parts):
    half = parts[0].shape[0] // 2
    return sum(part[:half] for part in parts), log_sum([part[half:] for part in parts])


def slot(k, n):
    return lax.axis_index("fsdp") ^ k if n <= DIRECT else k


def score_kernel(part, *refs):
    last = part == 3
    before, refs = (refs[:3], refs[3:]) if last else ((), refs)
    feats_ref, ws_ref, wt_ref, peak_ref, *refs = refs
    exp_ref, unit_ref, total_ref, *mine = refs[1:] if part else refs
    own_ref = mine[0] if last else total_ref
    n, _, bot, width = feats_ref.shape
    cols = ws_ref.shape[0]
    step = min(STEP, cols)
    per = max(1, min(n, GROUP // width))
    row = lax.broadcasted_iota(jnp.int32, (DEPTH - bot, per * width), 0)
    for which, w_ref, gain in ((0, ws_ref, GAIN_S), (1, wt_ref, GAIN_T)):
        base = (2 * part + which) * n * width
        extra = jnp.where(row < 3 * which, 1.0, 0.0).astype(jnp.bfloat16)
        for group in range(n // per):
            values = [feats_ref[group * per + k, which].astype(jnp.float32) for k in range(per)]
            values = jnp.concatenate(values, axis=1)
            unit = (values * lax.rsqrt(jnp.sum(values * values, axis=0, keepdims=True) + EPS)).astype(jnp.bfloat16)
            lanes = slice(group * per * width, (group + 1) * per * width)
            if which == 0:
                unit_ref[lanes, :] = unit.T
            stationary = jnp.concatenate([unit, extra], axis=0)
            total = jnp.zeros((8, per * width), jnp.float32)
            for at in range(0, cols, step):
                score = jnp.dot(w_ref[at:at + step, :], stationary, preferred_element_type=jnp.float32)
                exps = jnp.exp2(score * gain)
                total = total + jnp.sum(exps.reshape(step // 8, 8, per * width), axis=0)
                exp_ref[at:at + step, base + lanes.start:base + lanes.stop] = exps.astype(jnp.bfloat16)
            total = jnp.sum(total, axis=0, keepdims=True)
            if which == 1:
                total = jnp.log2(total) + GAIN_T * peak_ref[:, :1]
            own_ref[which:which + 1, lanes] = total
    if not last:
        return
    dp, _, core = here()
    own, pair, other = before
    parts = ((own, other), (pair, own_ref))
    rows = []
    for which in (0, 1):
        for half in (0, 1):
            pieces = []
            for view in (0, 1):
                first = (dp == view) if which == 0 else (dp != view)
                for place in range(n):
                    at = pl.ds(pl.multiple_of(slot(place, n) * width, width), width)
                    read = [[part[which:which + 1, at] for part in side] for side in parts]
                    mine, theirs = [jnp.where(first, *side) for side in read]
                    pieces.append(jnp.where(core == half, mine, theirs))
            rows.append(jnp.concatenate(pieces, axis=1))
    total_ref[...] = jnp.concatenate(rows, axis=0)


def scores(part, feats, weights, before=(), exps=None):
    n, _, bot, width = feats.shape
    cols, rows = weights[0].shape[0], n * width
    args = (*before, feats, *weights, *([exps] if part else []))
    return call(
        functools.partial(score_kernel, part),
        "scores",
        [
            held(cols, 8 * rows, dtype=jnp.bfloat16),
            held(rows, bot, dtype=jnp.bfloat16),
            held(4, 2 * rows) if part == 3 else held(2, rows),
        ],
        args,
        in_specs=[ON_CHIP] * (len(args) - bool(part)) + [IN_HBM] * bool(part),
        input_output_aliases={len(args) - 1: 0} if part else {},
        scratch_shapes=[held(2, rows)] if part == 3 else [],
    )


def relay_kernel(*refs):
    parts = [ref[...] for ref in refs[:-1]]
    if len(parts[0].shape) == 3:
        parts = [parts[0][i] for i in range(parts[0].shape[0])]
    refs[-1][...] = jnp.concatenate(combine(parts), axis=0)


def add_up(total, *others):
    return call(relay_kernel, "relay", held(*total.shape), [total, *others])


def add_up_all(total):
    n_proto, n_dp, n_fsdp = [lax.axis_size(axis) for axis in ("proto", "dp", "fsdp")]
    total = add_up(total, swap(total, "proto"))

    def across(up, over):
        places = [(p, d) for p in range(n_proto) for d in range(n_dp)]
        pairs = [(p * n_dp + d, (p ^ up) * n_dp + (d ^ over)) for p, d in places]
        return lax.ppermute(total, ("proto", "dp"), pairs)

    steps = [(up, 0) for up in range(2, n_proto, 2)]
    steps += [(up, over) for over in range(1, n_dp) for up in range(n_proto - 2, -1, -2)]
    total = add_up(total, *[across(*step) for step in steps])
    if n_fsdp <= DIRECT:
        return add_up(total, *[swap(total, "fsdp", k) for k in range(1, n_fsdp)])
    copies = jnp.broadcast_to(total[None], (n_fsdp, *total.shape))
    parts = lax.all_to_all(copies, "fsdp", 0, 0, tiled=True)
    return call(relay_kernel, "relay", held(*total.shape), [parts])


def grad_kernel(total_ref, peak_ref, weight_unit, weight_scale, *refs):
    units, exp_ref, out_hbm, scales, buf, sems = refs[:4], *refs[4:]
    dp, _, core = here()
    scales[0:2, :] = 10.0 / total_ref[0:2, :]
    scales[2:4, :] = 10.0 * jnp.exp2(GAIN_T * peak_ref[:, :1] - total_ref[2:4, :])
    rows = units[0].shape[0]
    width = 128
    n = rows // width
    factors = []
    for part in range(4):
        view, half = divmod(part, 2)
        base = (dp ^ view) * rows
        at = [pl.ds(pl.multiple_of(base + slot(k, n) * width, width), width) for k in range(n)]
        for which in (0, 1):
            picked = [
                jnp.where(core == half, scales[2 * which:2 * which + 1, where], scales[2 * which + 1:2 * which + 2, where])
                for where in at
            ]
            factors.append(jnp.concatenate(picked, axis=1).astype(jnp.bfloat16))
    feats = jnp.concatenate([unit[...] for unit in units], axis=0)
    chunks, _, step = buf.shape
    stores = []
    for i in range(chunks):
        at = slice(i * step, (i + 1) * step)
        derivs = []
        for part in range(4):
            lies_s, lies_t = 2 * part * rows, (2 * (part ^ 2) + 1) * rows
            probs_s = exp_ref[at, lies_s:lies_s + rows] * factors[2 * part]
            probs_t = exp_ref[at, lies_t:lies_t + rows] * factors[2 * part + 1]
            derivs.append(probs_s - probs_t)
        derivs = jnp.concatenate(derivs, axis=1)
        grad = jnp.dot(derivs, feats, preferred_element_type=jnp.float32).T
        unit = weight_unit[:, at]
        proj = unit * jnp.sum(unit * grad, axis=0, keepdims=True)
        buf[i] = (grad - proj) * weight_scale[:, at]
        stores.append(pltpu.make_async_copy(buf.at[i], out_hbm.at[:, at], sems.at[i]))
        stores[i].start()
    for store in stores:
        store.wait()


def gradient(total, peak, weight_unit, weight_scale, units, exps):
    cols = exps.shape[0]
    rows, bot = units[0].shape
    step = min(256, cols)
    args = (total, peak, weight_unit, weight_scale, *units, exps)
    return call(
        grad_kernel,
        "gradient",
        pltpu.HBM((bot, cols), jnp.float32),
        args,
        out_specs=IN_HBM,
        scratch_shapes=[held(4, 2 * rows), held(cols // step, bot, step), pltpu.SemaphoreType.DMA((cols // step,))],
    )


def shards(teacher_weight, student_weight, teacher_feats, student_feats, pairing, center):
    n_dp, n_fsdp = lax.axis_size("dp"), lax.axis_size("fsdp")
    in_hbm = lambda array: pltpu.with_memory_space_constraint(array, pltpu.HBM)
    teacher_weight, student_weight, center = in_hbm(teacher_weight), in_hbm(student_weight), in_hbm(center[None, :])

    index = swap(pairing, "dp")
    mine = pack(*fetch(in_hbm(student_feats[0].T), in_hbm(teacher_feats[0].T)), index)
    new, wt, ws, unit, scale, peak = prepare(teacher_weight, student_weight, center, n_dp)
    weights = (ws, wt, peak)
    if n_fsdp <= DIRECT:
        other = [swap(mine, "dp")]
        along = [swap(mine, "fsdp", k) for k in range(1, n_fsdp)]
        own, far = join([mine, *along], [n_fsdp, n_fsdp - 2], (other[0], peak))
        other += [swap(other[0], "fsdp"), swap(far, "dp")]
    else:
        own = lax.all_to_all(jnp.broadcast_to(mine[None], (n_fsdp, *mine.shape)), "fsdp", 0, 0, tiled=True)
        other = [swap(own, "dp")]
    exps, unit_a, total_a = scores(0, own, weights)
    teacher_new, done = update_rest(teacher_weight, student_weight, total_a, new, ws.shape[0])
    (other,) = join(other, [n_fsdp], (done,))
    exps, unit_c, total_c = scores(2, other, weights, exps=exps)
    exps, unit_b, total_b = scores(1, swap(own, "proto"), weights, exps=exps)
    exps, unit_d, total = scores(3, swap(other, "proto"), weights, (total_a, total_b, total_c), exps)
    total = add_up_all(total)
    student_grad = gradient(total, peak, unit, scale, (unit_a, unit_b, unit_c, unit_d), exps)
    return (teacher_new, student_grad)


def solution(mesh):
    placed = (
        P(None, ("proto", "fsdp")),
        P(None, ("proto", "fsdp")),
        P("dp", "fsdp", None),
        P("dp", "fsdp", None),
        P("dp", "fsdp"),
        P("proto"),
    )
    return jax.shard_map(
        shards,
        mesh=mesh,
        in_specs=placed,
        out_specs=(P(None, ("proto", "fsdp")), P(None, ("proto", "fsdp", "dp"))),
        check_vma=False,
    )
```

```python
import functools
import math

import jax
import jax.numpy as jnp
from jax import lax
from jax.experimental import pallas as pl
from jax.experimental.pallas import tpu as pltpu
from jax.sharding import PartitionSpec as P

EPS = 1e-06
DEPTH = 256
GROUP = 512
STEP = 256
DIRECT = 8
LOG2E = math.log2(math.e)
GAIN_T = LOG2E / 0.04
GAIN_S = LOG2E / 0.1
LIMIT = 24 * 1024 * 1024
ON_CHIP = pl.BlockSpec(memory_space=pltpu.VMEM)
IN_HBM = pl.BlockSpec(memory_space=pl.ANY)


def shape(*dims, dtype=jnp.float32):
    return jax.ShapeDtypeStruct(dims, dtype)


def held(*dims, dtype=jnp.float32):
    return pltpu.VMEM(dims, dtype)


def call(kernel, name, out_shape, args, **more):
    many = isinstance(out_shape, (list, tuple))
    specs = dict(in_specs=[ON_CHIP] * len(args), out_specs=[ON_CHIP] * len(out_shape) if many else ON_CHIP)
    return pl.pallas_call(
        kernel,
        out_shape=out_shape,
        compiler_params=pltpu.CompilerParams(vmem_limit_bytes=LIMIT),
        cost_estimate=pl.CostEstimate(flops=1, bytes_accessed=1, transcendentals=0),
        name=name,
        **{**specs, **more},
    )(*args)


def swap(block, axis, apart=1):
    return lax.ppermute(block, axis, [(i, i ^ apart) for i in range(lax.axis_size(axis))])


def here():
    return lax.axis_index("dp"), lax.axis_index("fsdp"), lax.rem(lax.axis_index("proto"), 2)


def cast_split(row):
    high = row.astype(jnp.bfloat16).astype(jnp.float32)
    mid = (row - high).astype(jnp.bfloat16).astype(jnp.float32)
    return high, mid, row - high - mid


def prep_kernel(n_dp, teacher_hbm, student_hbm, center_hbm, new_hbm, wt_ref, ws_ref, unit_ref, scale_ref, peak_ref, *scratch):
    teacher_buf, student_buf, new_buf, center_buf, in_t, in_s, out, in_c = scratch
    chunks, bot, width = new_buf.shape
    dp, fsdp, _ = here()
    first = dp * (chunks * width)
    at = [slice(i * width, (i + 1) * width) for i in range(chunks)]
    far = [pl.ds(pl.multiple_of(first + i * width, width), width) for i in range(chunks)]
    start = pl.multiple_of((fsdp * n_dp + dp) * (chunks * width), 128)
    center_load = pltpu.make_async_copy(center_hbm.at[:, pl.ds(start, chunks * width)], center_buf, in_c)
    loads = [
        (
            pltpu.make_async_copy(teacher_hbm.at[:, far[i]], teacher_buf.at[i], in_t.at[i]),
            pltpu.make_async_copy(student_hbm.at[:, far[i]], student_buf.at[i], in_s.at[i]),
        )
        for i in range(chunks)
    ]
    stores = [pltpu.make_async_copy(new_buf.at[i], new_hbm.at[:, far[i]], out.at[i]) for i in range(chunks)]
    center_load.start()
    for pair in loads:
        for load in pair:
            load.start()
    center_load.wait()
    center = center_buf[...]
    peak = jnp.max(-center, axis=1, keepdims=True)
    peak_ref[...] = jnp.broadcast_to(peak, peak_ref.shape)
    splits = cast_split(-center - peak)
    row = lax.broadcasted_iota(jnp.int32, (DEPTH - bot, width), 0)
    zero = jnp.zeros((DEPTH - bot, width), jnp.float32)
    for i in range(chunks):
        for load in loads[i]:
            load.wait()
        student = student_buf[i]
        new = 0.994 * teacher_buf[i] + 0.006 * student
        new_buf[i] = new
        stores[i].start()
        high, mid, low = [part[:, at[i]] for part in splits]
        extra = jnp.where(row == 0, high, jnp.where(row == 1, mid, jnp.where(row == 2, low, zero)))
        scale = lax.rsqrt(jnp.sum(student * student, axis=0, keepdims=True) + EPS)
        unit_s = student * scale
        unit_t = new * lax.rsqrt(jnp.sum(new * new, axis=0, keepdims=True) + EPS)
        wt_ref[at[i], :] = jnp.concatenate([unit_t, extra], axis=0).astype(jnp.bfloat16).T
        ws_ref[at[i], :] = jnp.concatenate([unit_s, zero], axis=0).astype(jnp.bfloat16).T
        unit_ref[:, at[i]] = unit_s
        scale_ref[:, at[i]] = scale
    for store in stores:
        store.wait()


def prepare(teacher_weight, student_weight, center, n_dp):
    bot, cols = teacher_weight.shape
    own = cols // n_dp
    width = min(512, own)
    chunks = own // width
    return call(
        functools.partial(prep_kernel, n_dp),
        "prep",
        [
            pltpu.HBM((bot, cols), jnp.float32),
            held(own, DEPTH, dtype=jnp.bfloat16),
            held(own, DEPTH, dtype=jnp.bfloat16),
            held(bot, own),
            held(1, own),
            held(1, 128),
        ],
        (teacher_weight, student_weight, center),
        in_specs=[IN_HBM] * 3,
        out_specs=[IN_HBM] + [ON_CHIP] * 5,
        scratch_shapes=[held(chunks, bot, width)] * 3
        + [held(1, own)]
        + [pltpu.SemaphoreType.DMA((chunks,))] * 3
        + [pltpu.SemaphoreType.DMA],
    )


def rest_kernel(lo, hi, own, teacher_hbm, student_hbm, after, before_hbm, new_hbm, done_ref, *scratch):
    teacher_buf, student_buf, new_buf, in_t, in_s, out = scratch
    width = hi - lo
    parts = teacher_hbm.shape[1] // own - 1
    dp = here()[0]
    done_ref[...] = jnp.zeros_like(done_ref)
    far = [pl.ds(pl.multiple_of(lax.rem(dp + 1 + i, parts + 1) * own + lo, 128), width) for i in range(parts)]
    loads = [
        (
            pltpu.make_async_copy(teacher_hbm.at[:, far[i]], teacher_buf.at[i], in_t.at[i]),
            pltpu.make_async_copy(student_hbm.at[:, far[i]], student_buf.at[i], in_s.at[i]),
        )
        for i in range(parts)
    ]
    stores = [pltpu.make_async_copy(new_buf.at[i], new_hbm.at[:, far[i]], out.at[i]) for i in range(parts)]
    for pair in loads:
        for load in pair:
            load.start()
    for i in range(parts):
        for load in loads[i]:
            load.wait()
        new_buf[i] = 0.994 * teacher_buf[i] + 0.006 * student_buf[i]
        stores[i].start()
    for store in stores:
        store.wait()


def update_rest(teacher_weight, student_weight, after, new, own, lo, hi):
    bot, cols = teacher_weight.shape
    parts = cols // own - 1
    return call(
        functools.partial(rest_kernel, lo, hi, own),
        "rest",
        [pltpu.HBM((bot, cols), jnp.float32), held(8, 128)],
        (teacher_weight, student_weight, after, new),
        in_specs=[IN_HBM] * 4,
        out_specs=[IN_HBM, ON_CHIP],
        input_output_aliases={3: 0},
        scratch_shapes=[held(parts, bot, hi - lo)] * 3 + [pltpu.SemaphoreType.DMA((parts,))] * 3,
    )


def fetch_kernel(student_hbm, teacher_hbm, student_ref, teacher_ref, sems):
    half = student_ref.shape[1]
    side = pl.ds(pl.multiple_of(here()[2] * half, half), half)
    loads = [
        pltpu.make_async_copy(student_hbm.at[:, side], student_ref, sems.at[0]),
        pltpu.make_async_copy(teacher_hbm, teacher_ref, sems.at[1]),
    ]
    for load in loads:
        load.start()
    for load in loads:
        load.wait()


def fetch(student, teacher):
    bot, crops = student.shape
    return call(
        fetch_kernel,
        "fetch",
        [held(bot, crops // 2, dtype=jnp.bfloat16), held(bot, crops, dtype=jnp.bfloat16)],
        (student, teacher),
        in_specs=[IN_HBM] * 2,
        scratch_shapes=[pltpu.SemaphoreType.DMA((2,))],
    )


def pack_kernel(student_ref, teacher_ref, index_ref, out_ref):
    half = out_ref.shape[2]
    lower = here()[2] == 0
    out_ref[0] = student_ref[...]
    index = jnp.where(lower, index_ref[:, :half], index_ref[:, half:])
    row = lax.broadcasted_iota(jnp.int32, (teacher_ref.shape[1], half), 0)
    pick = jnp.where(row == index, 1.0, 0.0).astype(jnp.bfloat16)
    out_ref[1] = jnp.dot(teacher_ref[...], pick, preferred_element_type=jnp.float32).astype(jnp.bfloat16)


def pack(student, teacher, index):
    bot, half = student.shape
    return call(pack_kernel, "pack", held(2, bot, half, dtype=jnp.bfloat16), (student, teacher, index))


def join_kernel(n_in, n_after, firsts, bot, *refs):
    blocks = []
    for ref in refs[:n_in]:
        blocks += [ref] if len(ref.shape) == 3 else [ref.at[i] for i in range(ref.shape[0])]
    for first, ref in zip(firsts, refs[n_in + n_after:]):
        for i in range(ref.shape[0]):
            block = blocks[first + i][:, :bot, :]
            ref[i, :, :bot, :] = block
            if ref.shape[2] > bot:
                ref[i, :, bot:, :] = block[:, :ref.shape[2] - bot]


def join(parts, outs, after, bot):
    width = parts[0].shape[-1]
    shapes = [held(count, 2, rows, width, dtype=jnp.bfloat16) for _, count, rows in outs]
    kernel = functools.partial(join_kernel, len(parts), len(after), [first for first, _, _ in outs], bot)
    return call(kernel, "join", shapes, (*parts, *after), in_specs=[ON_CHIP] * len(parts) + [IN_HBM] * len(after))


def log_sum(parts):
    top = functools.reduce(jnp.maximum, parts)
    return top + jnp.log2(sum(jnp.exp2(part - top) for part in parts))


def combine(parts):
    half = parts[0].shape[0] // 2
    return sum(part[:half] for part in parts), log_sum([part[half:] for part in parts])


def slot(k, n):
    return lax.axis_index("fsdp") ^ k if n <= DIRECT else k


def score_kernel(part, n_feats, *refs):
    last = part == 3
    before, refs = (refs[:3], refs[3:]) if last else ((), refs)
    feats_refs, (ws_ref, wt_ref, peak_ref, *refs) = refs[:n_feats], refs[n_feats:]
    blocks = [ref.at[i] for ref in feats_refs for i in range(ref.shape[0])]
    exp_ref, unit_ref, total_ref, *mine = refs[1:] if part else refs
    own_ref = mine[0] if last else total_ref
    n, (_, bot, width) = len(blocks), blocks[0].shape
    cols = ws_ref.shape[0]
    step = min(STEP, cols)
    per = max(1, min(n, GROUP // width))
    row = lax.broadcasted_iota(jnp.int32, (DEPTH - bot, per * width), 0)
    for which, w_ref, gain in ((0, ws_ref, GAIN_S), (1, wt_ref, GAIN_T)):
        base = (2 * part + which) * n * width
        extra = jnp.where(row < 3 * which, 1.0, 0.0).astype(jnp.bfloat16)
        for group in range(n // per):
            values = [blocks[group * per + k][which].astype(jnp.float32) for k in range(per)]
            values = jnp.concatenate(values, axis=1)
            unit = (values * lax.rsqrt(jnp.sum(values * values, axis=0, keepdims=True) + EPS)).astype(jnp.bfloat16)
            lanes = slice(group * per * width, (group + 1) * per * width)
            if which == 0:
                unit_ref[lanes, :] = unit.T
            stationary = jnp.concatenate([unit, extra], axis=0)
            total = jnp.zeros((8, per * width), jnp.float32)
            for at in range(0, cols, step):
                score = jnp.dot(w_ref[at:at + step, :], stationary, preferred_element_type=jnp.float32)
                exps = jnp.exp2(score * gain)
                total = total + jnp.sum(exps.reshape(step // 8, 8, per * width), axis=0)
                exp_ref[at:at + step, base + lanes.start:base + lanes.stop] = exps.astype(jnp.bfloat16)
            total = jnp.sum(total, axis=0, keepdims=True)
            if which == 1:
                total = jnp.log2(total) + GAIN_T * peak_ref[:, :1]
            own_ref[which:which + 1, lanes] = total
    if not last:
        return
    dp, _, core = here()
    own, pair, other = before
    parts = ((own, other), (pair, own_ref))
    rows = []
    for which in (0, 1):
        for half in (0, 1):
            pieces = []
            for view in (0, 1):
                first = (dp == view) if which == 0 else (dp != view)
                for place in range(n):
                    at = pl.ds(pl.multiple_of(slot(place, n) * width, width), width)
                    read = [[part[which:which + 1, at] for part in side] for side in parts]
                    mine, theirs = [jnp.where(first, *side) for side in read]
                    pieces.append(jnp.where(core == half, mine, theirs))
            rows.append(jnp.concatenate(pieces, axis=1))
    total_ref[...] = jnp.concatenate(rows, axis=0)


def scores(part, feats, weights, before=(), exps=None):
    _, _, bot, width = feats[0].shape
    cols, rows = weights[0].shape[0], sum(part.shape[0] for part in feats) * width
    args = (*before, *feats, *weights, *([exps] if part else []))
    return call(
        functools.partial(score_kernel, part, len(feats)),
        "scores",
        [
            held(cols, 8 * rows, dtype=jnp.bfloat16),
            held(rows, bot, dtype=jnp.bfloat16),
            held(4, 2 * rows) if part == 3 else held(2, rows),
        ],
        args,
        in_specs=[ON_CHIP] * (len(args) - bool(part)) + [IN_HBM] * bool(part),
        input_output_aliases={len(args) - 1: 0} if part else {},
        scratch_shapes=[held(2, rows)] if part == 3 else [],
    )


def relay_kernel(n_in, *refs):
    parts = [ref[...] for ref in refs[:n_in]]
    if len(parts[0].shape) == 3:
        parts = [parts[0][i] for i in range(parts[0].shape[0])]
    refs[-1][...] = jnp.concatenate(combine(parts), axis=0)


def add_up(parts, *after):
    specs = [ON_CHIP] * len(parts) + [IN_HBM] * len(after)
    out = held(*parts[0].shape[-2:])
    return call(functools.partial(relay_kernel, len(parts)), "relay", out, (*parts, *after), in_specs=specs)


def across(total, up, over):
    n_proto, n_dp = lax.axis_size("proto"), lax.axis_size("dp")
    places = [(p, d) for p in range(n_proto) for d in range(n_dp)]
    pairs = [(p * n_dp + d, (p ^ up) * n_dp + (d ^ over)) for p, d in places]
    return lax.ppermute(total, ("proto", "dp"), pairs)


def along_fsdp(total):
    n = lax.axis_size("fsdp")
    if n <= DIRECT:
        return [total, *[swap(total, "fsdp", k) for k in range(1, n)]]
    return [lax.all_to_all(jnp.broadcast_to(total[None], (n, *total.shape)), "fsdp", 0, 0, tiled=True)]


def grad_kernel(total_ref, peak_ref, weight_unit, weight_scale, *refs):
    units, exp_ref, out_hbm, scales, buf, sems = refs[:4], *refs[4:]
    dp, _, core = here()
    scales[0:2, :] = 10.0 / total_ref[0:2, :]
    scales[2:4, :] = 10.0 * jnp.exp2(GAIN_T * peak_ref[:, :1] - total_ref[2:4, :])
    rows = units[0].shape[0]
    width = 128
    n = rows // width
    factors = []
    for part in range(4):
        view, half = divmod(part, 2)
        base = (dp ^ view) * rows
        at = [pl.ds(pl.multiple_of(base + slot(k, n) * width, width), width) for k in range(n)]
        for which in (0, 1):
            picked = [
                jnp.where(core == half, scales[2 * which:2 * which + 1, where], scales[2 * which + 1:2 * which + 2, where])
                for where in at
            ]
            factors.append(jnp.concatenate(picked, axis=1).astype(jnp.bfloat16))
    feats = jnp.concatenate([unit[...] for unit in units], axis=0)
    chunks, _, step = buf.shape
    stores = []
    for i in range(chunks):
        at = slice(i * step, (i + 1) * step)
        derivs = []
        for part in range(4):
            lies_s, lies_t = 2 * part * rows, (2 * (part ^ 2) + 1) * rows
            probs_s = exp_ref[at, lies_s:lies_s + rows] * factors[2 * part]
            probs_t = exp_ref[at, lies_t:lies_t + rows] * factors[2 * part + 1]
            derivs.append(probs_s - probs_t)
        derivs = jnp.concatenate(derivs, axis=1)
        grad = jnp.dot(derivs, feats, preferred_element_type=jnp.float32).T
        unit = weight_unit[:, at]
        proj = unit * jnp.sum(unit * grad, axis=0, keepdims=True)
        buf[i] = (grad - proj) * weight_scale[:, at]
        stores.append(pltpu.make_async_copy(buf.at[i], out_hbm.at[:, at], sems.at[i]))
        stores[i].start()
    for store in stores:
        store.wait()


def gradient(total, peak, weight_unit, weight_scale, units, exps):
    cols = exps.shape[0]
    rows, bot = units[0].shape
    step = min(512, cols)
    args = (total, peak, weight_unit, weight_scale, *units, exps)
    return call(
        grad_kernel,
        "gradient",
        pltpu.HBM((bot, cols), jnp.float32),
        args,
        out_specs=IN_HBM,
        scratch_shapes=[held(4, 2 * rows), held(cols // step, bot, step), pltpu.SemaphoreType.DMA((cols // step,))],
    )


def shards(teacher_weight, student_weight, teacher_feats, student_feats, pairing, center):
    n_dp, n_fsdp = lax.axis_size("dp"), lax.axis_size("fsdp")
    in_hbm = lambda array: pltpu.with_memory_space_constraint(array, pltpu.HBM)
    teacher_weight, student_weight, center = in_hbm(teacher_weight), in_hbm(student_weight), in_hbm(center[None, :])

    index = swap(pairing, "dp")
    mine = pack(*fetch(in_hbm(student_feats[0].T), in_hbm(teacher_feats[0].T)), index)
    new, wt, ws, unit, scale, peak = prepare(teacher_weight, student_weight, center, n_dp)
    weights = (ws, wt, peak)
    bot = mine.shape[1]
    if n_fsdp <= DIRECT:
        other = [swap(mine, "dp")]
        along = [swap(mine, "fsdp", k) for k in range(1, n_fsdp)]
        half = n_fsdp // 2
        outs = [(0, n_fsdp, bot), (2, n_fsdp - 2, bot + 16), (0, half, bot), (half, half, bot)]
        own, far, *halves = join([mine, *along], outs, (other[0], peak), bot)
        other += [swap(other[0], "fsdp"), swap(far, "dp")]
    else:
        own = lax.all_to_all(jnp.broadcast_to(mine[None], (n_fsdp, *mine.shape)), "fsdp", 0, 0, tiled=True)
        other, halves = [swap(own, "dp")], [own]
    exps, unit_a, total_a = scores(0, [own], weights)
    exps, unit_b, total_b = scores(1, [swap(half, "proto") for half in halves], weights, exps=exps)
    (other,) = join(other, [(0, n_fsdp, bot)], (total_b,), bot)
    exps, unit_c, total_c = scores(2, [other], weights, exps=exps)
    exps, unit_d, total = scores(3, [swap(other, "proto")], weights, (total_a, total_b, total_c), exps)
    n_proto, own_cols = lax.axis_size("proto"), ws.shape[0]
    middle = own_cols // 2
    total = add_up([total, swap(total, "proto")])
    new, done = update_rest(teacher_weight, student_weight, total, new, own_cols, 0, middle)
    steps = [(up, over) for up in range(0, n_proto, 2) for over in range(n_dp)][1:]
    total = add_up([total, *[across(total, *step) for step in steps]], done)
    teacher_new, done = update_rest(teacher_weight, student_weight, total, new, own_cols, middle, own_cols)
    total = add_up(along_fsdp(total), done)
    student_grad = gradient(total, peak, unit, scale, (unit_a, unit_b, unit_c, unit_d), exps)
    return (teacher_new, student_grad)


def solution(mesh):
    placed = (
        P(None, ("proto", "fsdp")),
        P(None, ("proto", "fsdp")),
        P("dp", "fsdp", None),
        P("dp", "fsdp", None),
        P("dp", "fsdp"),
        P("proto"),
    )
    return jax.shard_map(
        shards,
        mesh=mesh,
        in_specs=placed,
        out_specs=(P(None, ("proto", "fsdp")), P(None, ("proto", "fsdp", "dp"))),
        check_vma=False,
    )
```

```python
import functools
import math

import jax
import jax.numpy as jnp
from jax import lax
from jax.experimental import pallas as pl
from jax.experimental.pallas import tpu as pltpu
from jax.sharding import PartitionSpec as P

EPS = 1e-06
DEPTH = 256
GROUP = 512
STEP = 256
DIRECT = 8
LOG2E = math.log2(math.e)
GAIN_T = LOG2E / 0.04
GAIN_S = LOG2E / 0.1
LIMIT = 24 * 1024 * 1024
ON_CHIP = pl.BlockSpec(memory_space=pltpu.VMEM)
IN_HBM = pl.BlockSpec(memory_space=pl.ANY)


def shape(*dims, dtype=jnp.float32):
    return jax.ShapeDtypeStruct(dims, dtype)


def held(*dims, dtype=jnp.float32):
    return pltpu.VMEM(dims, dtype)


def call(kernel, name, out_shape, args, **more):
    many = isinstance(out_shape, (list, tuple))
    specs = dict(in_specs=[ON_CHIP] * len(args), out_specs=[ON_CHIP] * len(out_shape) if many else ON_CHIP)
    return pl.pallas_call(
        kernel,
        out_shape=out_shape,
        compiler_params=pltpu.CompilerParams(vmem_limit_bytes=LIMIT),
        cost_estimate=pl.CostEstimate(flops=1, bytes_accessed=1, transcendentals=0),
        name=name,
        **{**specs, **more},
    )(*args)


def swap(block, axis, apart=1):
    return lax.ppermute(block, axis, [(i, i ^ apart) for i in range(lax.axis_size(axis))])


def here():
    return lax.axis_index("dp"), lax.axis_index("fsdp"), lax.rem(lax.axis_index("proto"), 2)


def cast_split(row):
    high = row.astype(jnp.bfloat16).astype(jnp.float32)
    mid = (row - high).astype(jnp.bfloat16).astype(jnp.float32)
    return high, mid, row - high - mid


def prep_kernel(n_dp, teacher_hbm, student_hbm, center_hbm, new_hbm, wt_ref, ws_ref, unit_ref, scale_ref, peak_ref, *scratch):
    teacher_buf, student_buf, new_buf, center_buf, in_t, in_s, out, in_c = scratch
    chunks, bot, width = new_buf.shape
    dp, fsdp, _ = here()
    first = dp * (chunks * width)
    at = [slice(i * width, (i + 1) * width) for i in range(chunks)]
    far = [pl.ds(pl.multiple_of(first + i * width, width), width) for i in range(chunks)]
    start = pl.multiple_of((fsdp * n_dp + dp) * (chunks * width), 128)
    center_load = pltpu.make_async_copy(center_hbm.at[:, pl.ds(start, chunks * width)], center_buf, in_c)
    loads = [
        (
            pltpu.make_async_copy(teacher_hbm.at[:, far[i]], teacher_buf.at[i], in_t.at[i]),
            pltpu.make_async_copy(student_hbm.at[:, far[i]], student_buf.at[i], in_s.at[i]),
        )
        for i in range(chunks)
    ]
    stores = [pltpu.make_async_copy(new_buf.at[i], new_hbm.at[:, far[i]], out.at[i]) for i in range(chunks)]
    center_load.start()
    for pair in loads:
        for load in pair:
            load.start()
    center_load.wait()
    center = center_buf[...]
    peak = jnp.max(-center, axis=1, keepdims=True)
    peak_ref[...] = jnp.broadcast_to(peak, peak_ref.shape)
    splits = cast_split(-center - peak)
    row = lax.broadcasted_iota(jnp.int32, (DEPTH - bot, width), 0)
    zero = jnp.zeros((DEPTH - bot, width), jnp.float32)
    for i in range(chunks):
        for load in loads[i]:
            load.wait()
        student = student_buf[i]
        new = 0.994 * teacher_buf[i] + 0.006 * student
        new_buf[i] = new
        stores[i].start()
        high, mid, low = [part[:, at[i]] for part in splits]
        extra = jnp.where(row == 0, high, jnp.where(row == 1, mid, jnp.where(row == 2, low, zero)))
        scale = lax.rsqrt(jnp.sum(student * student, axis=0, keepdims=True) + EPS)
        unit_s = student * scale
        unit_t = new * lax.rsqrt(jnp.sum(new * new, axis=0, keepdims=True) + EPS)
        wt_ref[at[i], :] = jnp.concatenate([unit_t, extra], axis=0).astype(jnp.bfloat16).T
        ws_ref[at[i], :] = jnp.concatenate([unit_s, zero], axis=0).astype(jnp.bfloat16).T
        unit_ref[:, at[i]] = unit_s
        scale_ref[:, at[i]] = scale
    for store in stores:
        store.wait()


def prepare(teacher_weight, student_weight, center, n_dp):
    bot, cols = teacher_weight.shape
    own = cols // n_dp
    width = min(512, own)
    chunks = own // width
    return call(
        functools.partial(prep_kernel, n_dp),
        "prep",
        [
            pltpu.HBM((bot, cols), jnp.float32),
            held(own, DEPTH, dtype=jnp.bfloat16),
            held(own, DEPTH, dtype=jnp.bfloat16),
            held(bot, own),
            held(1, own),
            held(1, 128),
        ],
        (teacher_weight, student_weight, center),
        in_specs=[IN_HBM] * 3,
        out_specs=[IN_HBM] + [ON_CHIP] * 5,
        scratch_shapes=[held(chunks, bot, width)] * 3
        + [held(1, own)]
        + [pltpu.SemaphoreType.DMA((chunks,))] * 3
        + [pltpu.SemaphoreType.DMA],
    )


def rest_kernel(lo, hi, own, teacher_hbm, student_hbm, after, before_hbm, new_hbm, done_ref, *scratch):
    teacher_buf, student_buf, new_buf, in_t, in_s, out = scratch
    width = hi - lo
    parts = teacher_hbm.shape[1] // own - 1
    dp = here()[0]
    done_ref[...] = jnp.zeros_like(done_ref)
    far = [pl.ds(pl.multiple_of(lax.rem(dp + 1 + i, parts + 1) * own + lo, 128), width) for i in range(parts)]
    loads = [
        (
            pltpu.make_async_copy(teacher_hbm.at[:, far[i]], teacher_buf.at[i], in_t.at[i]),
            pltpu.make_async_copy(student_hbm.at[:, far[i]], student_buf.at[i], in_s.at[i]),
        )
        for i in range(parts)
    ]
    stores = [pltpu.make_async_copy(new_buf.at[i], new_hbm.at[:, far[i]], out.at[i]) for i in range(parts)]
    for pair in loads:
        for load in pair:
            load.start()
    for i in range(parts):
        for load in loads[i]:
            load.wait()
        new_buf[i] = 0.994 * teacher_buf[i] + 0.006 * student_buf[i]
        stores[i].start()
    for store in stores:
        store.wait()


def update_rest(teacher_weight, student_weight, after, new, own, lo, hi):
    bot, cols = teacher_weight.shape
    parts = cols // own - 1
    return call(
        functools.partial(rest_kernel, lo, hi, own),
        "rest",
        [pltpu.HBM((bot, cols), jnp.float32), held(8, 128)],
        (teacher_weight, student_weight, after, new),
        in_specs=[IN_HBM] * 4,
        out_specs=[IN_HBM, ON_CHIP],
        input_output_aliases={3: 0},
        scratch_shapes=[held(parts, bot, hi - lo)] * 3 + [pltpu.SemaphoreType.DMA((parts,))] * 3,
    )


def fetch_kernel(student_hbm, teacher_hbm, student_ref, teacher_ref, sems):
    half = student_ref.shape[1]
    side = pl.ds(pl.multiple_of(here()[2] * half, half), half)
    loads = [
        pltpu.make_async_copy(student_hbm.at[:, side], student_ref, sems.at[0]),
        pltpu.make_async_copy(teacher_hbm, teacher_ref, sems.at[1]),
    ]
    for load in loads:
        load.start()
    for load in loads:
        load.wait()


def fetch(student, teacher):
    bot, crops = student.shape
    return call(
        fetch_kernel,
        "fetch",
        [held(bot, crops // 2, dtype=jnp.bfloat16), held(bot, crops, dtype=jnp.bfloat16)],
        (student, teacher),
        in_specs=[IN_HBM] * 2,
        scratch_shapes=[pltpu.SemaphoreType.DMA((2,))],
    )


def normalize(values):
    return (values * lax.rsqrt(jnp.sum(values * values, axis=0, keepdims=True) + EPS)).astype(jnp.bfloat16)


def pack_kernel(student_ref, teacher_ref, index_ref, out_ref):
    half = out_ref.shape[2]
    lower = here()[2] == 0
    out_ref[0] = normalize(student_ref[...].astype(jnp.float32))
    index = jnp.where(lower, index_ref[:, :half], index_ref[:, half:])
    row = lax.broadcasted_iota(jnp.int32, (teacher_ref.shape[1], half), 0)
    pick = jnp.where(row == index, 1.0, 0.0).astype(jnp.bfloat16)
    out_ref[1] = normalize(jnp.dot(teacher_ref[...], pick, preferred_element_type=jnp.float32))


def pack(student, teacher, index):
    bot, half = student.shape
    return call(pack_kernel, "pack", held(2, bot, half, dtype=jnp.bfloat16), (student, teacher, index))


def join_kernel(n_in, n_after, picks, bot, *refs):
    refs = refs[n_after:]
    blocks = []
    for ref in refs[:n_in]:
        blocks += [ref] if len(ref.shape) == 3 else [ref.at[i] for i in range(ref.shape[0])]
    for pick, ref in zip(picks, refs[n_in:]):
        for i, at in enumerate(pick):
            block = blocks[at][:, :bot, :]
            ref[i, :, :bot, :] = block
            if ref.shape[2] > bot:
                ref[i, :, bot:, :] = block[:, :ref.shape[2] - bot]


def join(parts, outs, after, bot):
    width = parts[0].shape[-1]
    shapes = [held(len(pick), 2, rows, width, dtype=jnp.bfloat16) for pick, rows in outs]
    kernel = functools.partial(join_kernel, len(parts), len(after), [pick for pick, _ in outs], bot)
    return call(kernel, "join", shapes, (*after, *parts), in_specs=[IN_HBM] * len(after) + [ON_CHIP] * len(parts))


def log_sum(parts):
    top = functools.reduce(jnp.maximum, parts)
    return top + jnp.log2(sum(jnp.exp2(part - top) for part in parts))


def combine(parts):
    half = parts[0].shape[0] // 2
    return sum(part[:half] for part in parts), log_sum([part[half:] for part in parts])


def slot(k, n):
    return lax.axis_index("fsdp") ^ k if n <= DIRECT else k


def place(half, j, n):
    return half * 2 * n + j


def score_kernel(n, plan, earlier, *refs):
    before, refs = refs[:len(earlier)], refs[len(earlier):]
    blocks, at = [], 0
    while len(blocks) < len(plan):
        blocks += [refs[at].at[i] for i in range(refs[at].shape[0])]
        at += 1
    ws_ref, wt_ref, peak_ref, *refs = refs[at:]
    exp_ref, unit_ref, total_ref, *scratch = refs[2:] if refs[0].shape == refs[2].shape else refs
    _, bot, width = blocks[0].shape
    cols = ws_ref.shape[0]
    teacher_side = 4 * n * width
    step = min(STEP, cols)
    per = max(1, min(len(plan), GROUP // width))
    own = {}
    for first in range(0, len(plan), per):
        group = range(first, min(first + per, len(plan)))
        size = len(group) * width
        row = lax.broadcasted_iota(jnp.int32, (DEPTH - bot, size), 0)
        for which, w_ref, gain in ((0, ws_ref, GAIN_S), (1, wt_ref, GAIN_T)):
            extra = jnp.where(row < 3 * which, 1.0, 0.0).astype(jnp.bfloat16)
            unit = jnp.concatenate([blocks[k][which] for k in group], axis=1)
            stationary = jnp.concatenate([unit, extra], axis=0)
            total = jnp.zeros((8, size), jnp.float32)
            for at in range(0, cols, step):
                score = jnp.dot(w_ref[at:at + step, :], stationary, preferred_element_type=jnp.float32)
                exps = jnp.exp2(score * gain)
                total = total + jnp.sum(exps.reshape(step // 8, 8, size), axis=0)
                exps = exps.astype(jnp.bfloat16)
                for k in group:
                    half, j = plan[k]
                    lies = place(half, (j + which * n) % (2 * n), n) * width + which * teacher_side
                    exp_ref[at:at + step, lies:lies + width] = exps[:, (k - first) * width:(k - first + 1) * width]
            total = jnp.sum(total, axis=0, keepdims=True)
            if which == 1:
                total = jnp.log2(total) + GAIN_T * peak_ref[:, :1]
            for k in group:
                own[which, k] = total[:, (k - first) * width:(k - first + 1) * width]
    for k, (half, j) in enumerate(plan):
        lies = place(half, j, n) * width
        unit_ref[lies:lies + width, :] = blocks[k][0].T
    if not earlier:
        for which, k in own:
            total_ref[which:which + 1, k * width:(k + 1) * width] = own[which, k]
        return
    (gathered,) = scratch
    for known, ref in [*zip(earlier, before), (plan, None)]:
        for k, (half, j) in enumerate(known):
            for which in (0, 1):
                lies = place(half, (j + which * n) % (2 * n), n) * width
                part = own[which, k] if ref is None else ref[which:which + 1, k * width:(k + 1) * width]
                gathered[which:which + 1, lies:lies + width] = part
    dp, _, core = here()
    rows = []
    for which in (0, 1):
        for half in (0, 1):
            pieces = []
            for view in (0, 1):
                for k in range(n):
                    lies = ((dp ^ view) * n + slot(k, n)) * width
                    mine, theirs = [
                        gathered[which:which + 1, pl.ds(pl.multiple_of(side * 2 * n * width + lies, width), width)]
                        for side in (0, 1)
                    ]
                    pieces.append(jnp.where(core == half, mine, theirs))
            rows.append(jnp.concatenate(pieces, axis=1))
    total_ref[...] = jnp.concatenate(rows, axis=0)


def scores(n, plan, feats, weights, buffers=(), earlier=(), before=()):
    _, _, bot, width = feats[0].shape
    cols, rows = weights[0].shape[0], 4 * n * width
    args = (*before, *feats, *weights, *buffers)
    plain = len(args) - len(buffers)
    exps, units, total = call(
        functools.partial(score_kernel, n, plan, earlier),
        "scores",
        [
            held(cols, 2 * rows, dtype=jnp.bfloat16),
            held(rows, bot, dtype=jnp.bfloat16),
            held(4, rows // 2) if earlier else held(2, len(plan) * width),
        ],
        args,
        in_specs=[ON_CHIP] * plain + [IN_HBM] * len(buffers),
        input_output_aliases={plain + i: i for i in range(len(buffers))},
        scratch_shapes=[held(2, rows)] if earlier else [],
    )
    return (exps, units), total


def relay_kernel(n_in, *refs):
    parts = [ref[...] for ref in refs[:n_in]]
    if len(parts[0].shape) == 3:
        parts = [parts[0][i] for i in range(parts[0].shape[0])]
    refs[-1][...] = jnp.concatenate(combine(parts), axis=0)


def add_up(parts, *after):
    specs = [ON_CHIP] * len(parts) + [IN_HBM] * len(after)
    out = held(*parts[0].shape[-2:])
    return call(functools.partial(relay_kernel, len(parts)), "relay", out, (*parts, *after), in_specs=specs)


def across(total, up, over):
    n_proto, n_dp = lax.axis_size("proto"), lax.axis_size("dp")
    places = [(p, d) for p in range(n_proto) for d in range(n_dp)]
    pairs = [(p * n_dp + d, (p ^ up) * n_dp + (d ^ over)) for p, d in places]
    return lax.ppermute(total, ("proto", "dp"), pairs)


def along_fsdp(total):
    n = lax.axis_size("fsdp")
    if n <= DIRECT:
        return [total, *[swap(total, "fsdp", k) for k in range(1, n)]]
    return [lax.all_to_all(jnp.broadcast_to(total[None], (n, *total.shape)), "fsdp", 0, 0, tiled=True)]


def grad_kernel(total_ref, peak_ref, weight_unit, weight_scale, unit_ref, exp_ref, out_hbm, scales, buf, sems):
    dp, _, core = here()
    scales[0:2, :] = 10.0 / total_ref[0:2, :]
    scales[2:4, :] = 10.0 * jnp.exp2(GAIN_T * peak_ref[:, :1] - total_ref[2:4, :])
    rows = unit_ref.shape[0]
    width = 128
    n = rows // width // 4
    factors = []
    for which in (0, 1):
        picked = []
        for half in (0, 1):
            for j in range(2 * n):
                lies = ((dp ^ (j // n)) * n + slot(j % n, n)) * width
                upper, lower = [
                    scales[2 * which + i:2 * which + i + 1, pl.ds(pl.multiple_of(lies, width), width)] for i in (0, 1)
                ]
                picked.append(jnp.where(core == half, upper, lower))
        factors.append(jnp.concatenate(picked, axis=1).astype(jnp.bfloat16))
    chunks, _, step = buf.shape
    stores = []
    for i in range(chunks):
        at = slice(i * step, (i + 1) * step)
        derivs = exp_ref[at, :rows] * factors[0] - exp_ref[at, rows:] * factors[1]
        grad = jnp.dot(derivs, unit_ref[...], preferred_element_type=jnp.float32).T
        unit = weight_unit[:, at]
        proj = unit * jnp.sum(unit * grad, axis=0, keepdims=True)
        buf[i] = (grad - proj) * weight_scale[:, at]
        stores.append(pltpu.make_async_copy(buf.at[i], out_hbm.at[:, at], sems.at[i]))
        stores[i].start()
    for store in stores:
        store.wait()


def gradient(total, peak, weight_unit, weight_scale, units, exps):
    cols = exps.shape[0]
    rows, bot = units.shape
    step = min(512, cols)
    return call(
        grad_kernel,
        "gradient",
        pltpu.HBM((bot, cols), jnp.float32),
        (total, peak, weight_unit, weight_scale, units, exps),
        out_specs=IN_HBM,
        scratch_shapes=[held(4, rows // 2), held(cols // step, bot, step), pltpu.SemaphoreType.DMA((cols // step,))],
    )


def shards(teacher_weight, student_weight, teacher_feats, student_feats, pairing, center):
    n_dp, n_fsdp = lax.axis_size("dp"), lax.axis_size("fsdp")
    in_hbm = lambda array: pltpu.with_memory_space_constraint(array, pltpu.HBM)
    teacher_weight, student_weight, center = in_hbm(teacher_weight), in_hbm(student_weight), in_hbm(center[None, :])

    index = swap(pairing, "dp")
    mine = pack(*fetch(in_hbm(student_feats[0].T), in_hbm(teacher_feats[0].T)), index)
    new, wt, ws, unit, scale, peak = prepare(teacher_weight, student_weight, center, n_dp)
    weights = (ws, wt, peak)
    bot = mine.shape[1]
    bot, n = mine.shape[1], n_fsdp
    named = lambda half, js: [(half, j) for j in js]
    if n <= DIRECT:
        other = swap(mine, "dp")
        along = [swap(mine, "fsdp", k) for k in range(1, n)]
        order = range(n - 1, -1, -1)
        outs = [(order, bot), (order[2:], bot + 16), (order[:n // 2], bot), (order[n // 2:], bot)]
        own, far, *halves = join([*along[::-1], mine], outs, (other, peak), bot)
        rest = [swap(other, "fsdp"), swap(far, "dp")]
        early, late = [other[None], swap(other, "proto")[None]], range(n + 1, 2 * n)
        first, second, third = named(0, range(n)), named(1, range(n)), [(0, n), (1, n)]
        buffers, total_a = scores(n, first, [own], weights)
        buffers, total_b = scores(n, second, [swap(half, "proto") for half in halves], weights, buffers)
        buffers, total_c = scores(n, third, early, weights, buffers)
        (rest,) = join(rest, [(range(n - 1), bot)], (total_c,), bot)
        buffers, total_d = scores(n, named(0, late), [rest], weights, buffers)
        earlier, before = [first, second, third, named(0, late)], [total_a, total_b, total_c, total_d]
    else:
        own = lax.all_to_all(jnp.broadcast_to(mine[None], (n, *mine.shape)), "fsdp", 0, 0, tiled=True)
        rest, late = swap(own, "dp"), range(n, 2 * n)
        first, second = named(0, range(n)), named(1, range(n))
        buffers, total_a = scores(n, first, [own], weights)
        buffers, total_b = scores(n, second, [swap(own, "proto")], weights, buffers)
        buffers, total_c = scores(n, named(0, late), [rest], weights, buffers)
        earlier, before = [first, second, named(0, late)], [total_a, total_b, total_c]
    (exps, units), total = scores(n, named(1, late), [swap(rest, "proto")], weights, buffers, earlier, before)
    n_proto, own_cols = lax.axis_size("proto"), ws.shape[0]
    middle = own_cols // 2
    total = add_up([total, swap(total, "proto")])
    new, done = update_rest(teacher_weight, student_weight, total, new, own_cols, 0, middle)
    steps = [(up, over) for up in range(0, n_proto, 2) for over in range(n_dp)][1:]
    total = add_up([total, *[across(total, *step) for step in steps]], done)
    teacher_new, done = update_rest(teacher_weight, student_weight, total, new, own_cols, middle, own_cols)
    total = add_up(along_fsdp(total), done)
    student_grad = gradient(total, peak, unit, scale, units, exps)
    return (teacher_new, student_grad)


def solution(mesh):
    placed = (
        P(None, ("proto", "fsdp")),
        P(None, ("proto", "fsdp")),
        P("dp", "fsdp", None),
        P("dp", "fsdp", None),
        P("dp", "fsdp"),
        P("proto"),
    )
    return jax.shard_map(
        shards,
        mesh=mesh,
        in_specs=placed,
        out_specs=(P(None, ("proto", "fsdp")), P(None, ("proto", "fsdp", "dp"))),
        check_vma=False,
    )
```

```python
import functools
import math

import jax
import jax.numpy as jnp
from jax import lax
from jax.experimental import pallas as pl
from jax.experimental.pallas import tpu as pltpu
from jax.sharding import PartitionSpec as P

EPS = 1e-06
DEPTH = 256
GROUP = 512
STEP = 256
DIRECT = 8
LOG2E = math.log2(math.e)
GAIN_T = LOG2E / 0.04
GAIN_S = LOG2E / 0.1
LIMIT = 24 * 1024 * 1024
ON_CHIP = pl.BlockSpec(memory_space=pltpu.VMEM)
IN_HBM = pl.BlockSpec(memory_space=pl.ANY)


def shape(*dims, dtype=jnp.float32):
    return jax.ShapeDtypeStruct(dims, dtype)


def held(*dims, dtype=jnp.float32):
    return pltpu.VMEM(dims, dtype)


def call(kernel, name, out_shape, args, **more):
    many = isinstance(out_shape, (list, tuple))
    specs = dict(in_specs=[ON_CHIP] * len(args), out_specs=[ON_CHIP] * len(out_shape) if many else ON_CHIP)
    return pl.pallas_call(
        kernel,
        out_shape=out_shape,
        compiler_params=pltpu.CompilerParams(vmem_limit_bytes=LIMIT),
        cost_estimate=pl.CostEstimate(flops=1, bytes_accessed=1, transcendentals=0),
        name=name,
        **{**specs, **more},
    )(*args)


def swap(block, axis, apart=1):
    return lax.ppermute(block, axis, [(i, i ^ apart) for i in range(lax.axis_size(axis))])


def here():
    return lax.axis_index("dp"), lax.axis_index("fsdp"), lax.rem(lax.axis_index("proto"), 2)


def cast_split(row):
    high = row.astype(jnp.bfloat16).astype(jnp.float32)
    mid = (row - high).astype(jnp.bfloat16).astype(jnp.float32)
    return high, mid, row - high - mid


def prep_kernel(n_dp, teacher_hbm, student_hbm, center_hbm, new_hbm, wt_ref, ws_ref, unit_ref, scale_ref, peak_ref, *scratch):
    teacher_buf, student_buf, new_buf, center_buf, in_t, in_s, out, in_c = scratch
    chunks, bot, width = new_buf.shape
    dp, fsdp, _ = here()
    first = dp * (chunks * width)
    at = [slice(i * width, (i + 1) * width) for i in range(chunks)]
    far = [pl.ds(pl.multiple_of(first + i * width, width), width) for i in range(chunks)]
    start = pl.multiple_of((fsdp * n_dp + dp) * (chunks * width), 128)
    center_load = pltpu.make_async_copy(center_hbm.at[:, pl.ds(start, chunks * width)], center_buf, in_c)
    loads = [
        (
            pltpu.make_async_copy(teacher_hbm.at[:, far[i]], teacher_buf.at[i], in_t.at[i]),
            pltpu.make_async_copy(student_hbm.at[:, far[i]], student_buf.at[i], in_s.at[i]),
        )
        for i in range(chunks)
    ]
    stores = [pltpu.make_async_copy(new_buf.at[i], new_hbm.at[:, far[i]], out.at[i]) for i in range(chunks)]
    center_load.start()
    for pair in loads:
        for load in pair:
            load.start()
    center_load.wait()
    center = center_buf[...]
    peak = jnp.max(-center, axis=1, keepdims=True)
    peak_ref[...] = jnp.broadcast_to(peak, peak_ref.shape)
    splits = cast_split(-center - peak)
    row = lax.broadcasted_iota(jnp.int32, (DEPTH - bot, width), 0)
    zero = jnp.zeros((DEPTH - bot, width), jnp.float32)
    for i in range(chunks):
        for load in loads[i]:
            load.wait()
        student = student_buf[i]
        new = 0.994 * teacher_buf[i] + 0.006 * student
        new_buf[i] = new
        stores[i].start()
        high, mid, low = [part[:, at[i]] for part in splits]
        extra = jnp.where(row == 0, high, jnp.where(row == 1, mid, jnp.where(row == 2, low, zero)))
        scale = lax.rsqrt(jnp.sum(student * student, axis=0, keepdims=True) + EPS)
        unit_s = student * scale
        unit_t = new * lax.rsqrt(jnp.sum(new * new, axis=0, keepdims=True) + EPS)
        wt_ref[at[i], :] = jnp.concatenate([unit_t, extra], axis=0).astype(jnp.bfloat16).T
        ws_ref[at[i], :] = jnp.concatenate([unit_s, zero], axis=0).astype(jnp.bfloat16).T
        unit_ref[:, at[i]] = unit_s
        scale_ref[:, at[i]] = scale
    for store in stores:
        store.wait()


def prepare(teacher_weight, student_weight, center, n_dp):
    bot, cols = teacher_weight.shape
    own = cols // n_dp
    width = min(512, own)
    chunks = own // width
    return call(
        functools.partial(prep_kernel, n_dp),
        "prep",
        [
            pltpu.HBM((bot, cols), jnp.float32),
            held(own, DEPTH, dtype=jnp.bfloat16),
            held(own, DEPTH, dtype=jnp.bfloat16),
            held(bot, own),
            held(1, own),
            held(1, 128),
        ],
        (teacher_weight, student_weight, center),
        in_specs=[IN_HBM] * 3,
        out_specs=[IN_HBM] + [ON_CHIP] * 5,
        scratch_shapes=[held(chunks, bot, width)] * 3
        + [held(1, own)]
        + [pltpu.SemaphoreType.DMA((chunks,))] * 3
        + [pltpu.SemaphoreType.DMA],
    )


def rest_kernel(lo, hi, own, teacher_hbm, student_hbm, after, before_hbm, new_hbm, done_ref, *scratch):
    teacher_buf, student_buf, new_buf, in_t, in_s, out = scratch
    width = hi - lo
    parts = teacher_hbm.shape[1] // own - 1
    dp = here()[0]
    done_ref[...] = jnp.zeros_like(done_ref)
    far = [pl.ds(pl.multiple_of(lax.rem(dp + 1 + i, parts + 1) * own + lo, 128), width) for i in range(parts)]
    loads = [
        (
            pltpu.make_async_copy(teacher_hbm.at[:, far[i]], teacher_buf.at[i], in_t.at[i]),
            pltpu.make_async_copy(student_hbm.at[:, far[i]], student_buf.at[i], in_s.at[i]),
        )
        for i in range(parts)
    ]
    stores = [pltpu.make_async_copy(new_buf.at[i], new_hbm.at[:, far[i]], out.at[i]) for i in range(parts)]
    for pair in loads:
        for load in pair:
            load.start()
    for i in range(parts):
        for load in loads[i]:
            load.wait()
        new_buf[i] = 0.994 * teacher_buf[i] + 0.006 * student_buf[i]
        stores[i].start()
    for store in stores:
        store.wait()


def update_rest(teacher_weight, student_weight, after, new, own, lo, hi):
    bot, cols = teacher_weight.shape
    parts = cols // own - 1
    return call(
        functools.partial(rest_kernel, lo, hi, own),
        "rest",
        [pltpu.HBM((bot, cols), jnp.float32), held(8, 128)],
        (teacher_weight, student_weight, after, new),
        in_specs=[IN_HBM] * 4,
        out_specs=[IN_HBM, ON_CHIP],
        input_output_aliases={3: 0},
        scratch_shapes=[held(parts, bot, hi - lo)] * 3 + [pltpu.SemaphoreType.DMA((parts,))] * 3,
    )


def fetch_kernel(student_hbm, teacher_hbm, student_ref, teacher_ref, sems):
    half = student_ref.shape[1]
    side = pl.ds(pl.multiple_of(here()[2] * half, half), half)
    loads = [
        pltpu.make_async_copy(student_hbm.at[:, side], student_ref, sems.at[0]),
        pltpu.make_async_copy(teacher_hbm, teacher_ref, sems.at[1]),
    ]
    for load in loads:
        load.start()
    for load in loads:
        load.wait()


def fetch(student, teacher):
    bot, crops = student.shape
    return call(
        fetch_kernel,
        "fetch",
        [held(bot, crops // 2, dtype=jnp.bfloat16), held(bot, crops, dtype=jnp.bfloat16)],
        (student, teacher),
        in_specs=[IN_HBM] * 2,
        scratch_shapes=[pltpu.SemaphoreType.DMA((2,))],
    )


def normalize(values):
    return (values * lax.rsqrt(jnp.sum(values * values, axis=0, keepdims=True) + EPS)).astype(jnp.bfloat16)


def pack_kernel(student_ref, teacher_ref, index_ref, out_ref):
    half = out_ref.shape[2]
    lower = here()[2] == 0
    out_ref[0] = normalize(student_ref[...].astype(jnp.float32))
    index = jnp.where(lower, index_ref[:, :half], index_ref[:, half:])
    row = lax.broadcasted_iota(jnp.int32, (teacher_ref.shape[1], half), 0)
    pick = jnp.where(row == index, 1.0, 0.0).astype(jnp.bfloat16)
    out_ref[1] = normalize(jnp.dot(teacher_ref[...], pick, preferred_element_type=jnp.float32))


def pack(student, teacher, index):
    bot, half = student.shape
    return call(pack_kernel, "pack", held(2, bot, half, dtype=jnp.bfloat16), (student, teacher, index))


def join_kernel(n_in, n_after, firsts, bot, *refs):
    blocks = []
    for ref in refs[:n_in]:
        blocks += [ref] if len(ref.shape) == 3 else [ref.at[i] for i in range(ref.shape[0])]
    for first, ref in zip(firsts, refs[n_in + n_after:]):
        for i in range(ref.shape[0]):
            block = blocks[first + i][:, :bot, :]
            ref[i, :, :bot, :] = block
            if ref.shape[2] > bot:
                ref[i, :, bot:, :] = block[:, :ref.shape[2] - bot]


def join(parts, outs, after, bot):
    width = parts[0].shape[-1]
    shapes = [held(count, 2, rows, width, dtype=jnp.bfloat16) for _, count, rows in outs]
    kernel = functools.partial(join_kernel, len(parts), len(after), [first for first, _, _ in outs], bot)
    return call(kernel, "join", shapes, (*parts, *after), in_specs=[ON_CHIP] * len(parts) + [IN_HBM] * len(after))


def log_sum(parts):
    top = functools.reduce(jnp.maximum, parts)
    return top + jnp.log2(sum(jnp.exp2(part - top) for part in parts))


def combine(parts):
    half = parts[0].shape[0] // 2
    return sum(part[:half] for part in parts), log_sum([part[half:] for part in parts])


def slot(k, n):
    return lax.axis_index("fsdp") ^ k if n <= DIRECT else k


def score_kernel(part, n_feats, *refs):
    last = part == 3
    before, refs = (refs[:3], refs[3:]) if last else ((), refs)
    feats_refs, (ws_ref, wt_ref, peak_ref, *refs) = refs[:n_feats], refs[n_feats:]
    blocks = [ref.at[i] for ref in feats_refs for i in range(ref.shape[0])]
    exp_ref, unit_ref, total_ref, *mine = refs[1:] if part else refs
    own_ref = mine[0] if last else total_ref
    n, (_, bot, width) = len(blocks), blocks[0].shape
    cols = ws_ref.shape[0]
    step = min(STEP, cols)
    per = max(1, min(n, GROUP // width))
    row = lax.broadcasted_iota(jnp.int32, (DEPTH - bot, per * width), 0)
    for which, w_ref, gain in ((0, ws_ref, GAIN_S), (1, wt_ref, GAIN_T)):
        base = (2 * part + which) * n * width
        extra = jnp.where(row < 3 * which, 1.0, 0.0).astype(jnp.bfloat16)
        for group in range(n // per):
            unit = jnp.concatenate([blocks[group * per + k][which] for k in range(per)], axis=1)
            lanes = slice(group * per * width, (group + 1) * per * width)
            if which == 0:
                unit_ref[lanes, :] = unit.T
            stationary = jnp.concatenate([unit, extra], axis=0)
            total = jnp.zeros((8, per * width), jnp.float32)
            for at in range(0, cols, step):
                score = jnp.dot(w_ref[at:at + step, :], stationary, preferred_element_type=jnp.float32)
                exps = jnp.exp2(score * gain)
                total = total + jnp.sum(exps.reshape(step // 8, 8, per * width), axis=0)
                exp_ref[at:at + step, base + lanes.start:base + lanes.stop] = exps.astype(jnp.bfloat16)
            total = jnp.sum(total, axis=0, keepdims=True)
            if which == 1:
                total = jnp.log2(total) + GAIN_T * peak_ref[:, :1]
            own_ref[which:which + 1, lanes] = total
    if not last:
        return
    dp, _, core = here()
    own, pair, other = before
    parts = ((own, other), (pair, own_ref))
    rows = []
    for which in (0, 1):
        for half in (0, 1):
            pieces = []
            for view in (0, 1):
                first = (dp == view) if which == 0 else (dp != view)
                for place in range(n):
                    at = pl.ds(pl.multiple_of(slot(place, n) * width, width), width)
                    read = [[part[which:which + 1, at] for part in side] for side in parts]
                    mine, theirs = [jnp.where(first, *side) for side in read]
                    pieces.append(jnp.where(core == half, mine, theirs))
            rows.append(jnp.concatenate(pieces, axis=1))
    total_ref[...] = jnp.concatenate(rows, axis=0)


def scores(part, feats, weights, before=(), exps=None):
    _, _, bot, width = feats[0].shape
    cols, rows = weights[0].shape[0], sum(part.shape[0] for part in feats) * width
    args = (*before, *feats, *weights, *([exps] if part else []))
    return call(
        functools.partial(score_kernel, part, len(feats)),
        "scores",
        [
            held(cols, 8 * rows, dtype=jnp.bfloat16),
            held(rows, bot, dtype=jnp.bfloat16),
            held(4, 2 * rows) if part == 3 else held(2, rows),
        ],
        args,
        in_specs=[ON_CHIP] * (len(args) - bool(part)) + [IN_HBM] * bool(part),
        input_output_aliases={len(args) - 1: 0} if part else {},
        scratch_shapes=[held(2, rows)] if part == 3 else [],
    )


def relay_kernel(n_in, *refs):
    parts = [ref[...] for ref in refs[:n_in]]
    if len(parts[0].shape) == 3:
        parts = [parts[0][i] for i in range(parts[0].shape[0])]
    refs[-1][...] = jnp.concatenate(combine(parts), axis=0)


def add_up(parts, *after):
    specs = [ON_CHIP] * len(parts) + [IN_HBM] * len(after)
    out = held(*parts[0].shape[-2:])
    return call(functools.partial(relay_kernel, len(parts)), "relay", out, (*parts, *after), in_specs=specs)


def across(total, up, over):
    n_proto, n_dp = lax.axis_size("proto"), lax.axis_size("dp")
    places = [(p, d) for p in range(n_proto) for d in range(n_dp)]
    pairs = [(p * n_dp + d, (p ^ up) * n_dp + (d ^ over)) for p, d in places]
    return lax.ppermute(total, ("proto", "dp"), pairs)


def along_fsdp(total):
    n = lax.axis_size("fsdp")
    if n <= DIRECT:
        return [total, *[swap(total, "fsdp", k) for k in range(1, n)]]
    return [lax.all_to_all(jnp.broadcast_to(total[None], (n, *total.shape)), "fsdp", 0, 0, tiled=True)]


def grad_kernel(total_ref, peak_ref, weight_unit, weight_scale, *refs):
    units, exp_ref, out_hbm, scales, feats, *derivs, buf, sems = refs[:4], *refs[4:]
    dp, _, core = here()
    scales[0:2, :] = 10.0 / total_ref[0:2, :]
    scales[2:4, :] = 10.0 * jnp.exp2(GAIN_T * peak_ref[:, :1] - total_ref[2:4, :])
    rows = units[0].shape[0]
    width = 128
    n = rows // width
    factors = []
    for part in range(4):
        view, half = divmod(part, 2)
        base = (dp ^ view) * rows
        at = [pl.ds(pl.multiple_of(base + slot(k, n) * width, width), width) for k in range(n)]
        for which in (0, 1):
            picked = [
                jnp.where(core == half, scales[2 * which:2 * which + 1, where], scales[2 * which + 1:2 * which + 2, where])
                for where in at
            ]
            factors.append(jnp.concatenate(picked, axis=1).astype(jnp.bfloat16))
    for part, unit in enumerate(units):
        feats[part * rows:(part + 1) * rows, :] = unit[...]
    chunks, _, step = buf.shape
    stores = []

    def derive(i):
        at = slice(i * step, (i + 1) * step)
        for part in range(4):
            lies_s, lies_t = 2 * part * rows, (2 * (part ^ 2) + 1) * rows
            probs_s = exp_ref[at, lies_s:lies_s + rows] * factors[2 * part]
            probs_t = exp_ref[at, lies_t:lies_t + rows] * factors[2 * part + 1]
            derivs[i % 2][:, part * rows:(part + 1) * rows] = probs_s - probs_t

    derive(0)
    for i in range(chunks):
        if i + 1 < chunks:
            derive(i + 1)
        at = slice(i * step, (i + 1) * step)
        grad = jnp.dot(derivs[i % 2][...], feats[...], preferred_element_type=jnp.float32).T
        unit = weight_unit[:, at]
        proj = unit * jnp.sum(unit * grad, axis=0, keepdims=True)
        buf[i] = (grad - proj) * weight_scale[:, at]
        stores.append(pltpu.make_async_copy(buf.at[i], out_hbm.at[:, at], sems.at[i]))
        stores[i].start()
    for store in stores:
        store.wait()


def gradient(total, peak, weight_unit, weight_scale, units, exps):
    cols = exps.shape[0]
    rows, bot = units[0].shape
    step = min(256, cols)
    args = (total, peak, weight_unit, weight_scale, *units, exps)
    return call(
        grad_kernel,
        "gradient",
        pltpu.HBM((bot, cols), jnp.float32),
        args,
        out_specs=IN_HBM,
        scratch_shapes=[
            held(4, 2 * rows),
            held(4 * rows, bot, dtype=jnp.bfloat16),
            *[held(step, 4 * rows, dtype=jnp.bfloat16)] * 2,
            held(cols // step, bot, step),
            pltpu.SemaphoreType.DMA((cols // step,)),
        ],
    )


def shards(teacher_weight, student_weight, teacher_feats, student_feats, pairing, center):
    n_dp, n_fsdp = lax.axis_size("dp"), lax.axis_size("fsdp")
    in_hbm = lambda array: pltpu.with_memory_space_constraint(array, pltpu.HBM)
    teacher_weight, student_weight, center = in_hbm(teacher_weight), in_hbm(student_weight), in_hbm(center[None, :])

    index = swap(pairing, "dp")
    mine = pack(*fetch(in_hbm(student_feats[0].T), in_hbm(teacher_feats[0].T)), index)
    new, wt, ws, unit, scale, peak = prepare(teacher_weight, student_weight, center, n_dp)
    weights = (ws, wt, peak)
    bot = mine.shape[1]
    if n_fsdp <= DIRECT:
        along = [swap(mine, "fsdp", k) for k in range(1, n_fsdp)]
        other = [swap(mine, "dp")]
        other.append(swap(other[0], "fsdp"))
        half = n_fsdp // 2
        outs = [(0, n_fsdp, bot), (2, n_fsdp - 2, bot + 16), (0, half, bot), (half, half, bot)]
        own, far, *halves = join([mine, *along], outs, (other[1], peak), bot)
        other.append(swap(far, "dp"))
    else:
        own = lax.all_to_all(jnp.broadcast_to(mine[None], (n_fsdp, *mine.shape)), "fsdp", 0, 0, tiled=True)
        other, halves = [swap(own, "dp")], [own]
    exps, unit_a, total_a = scores(0, [own], weights)
    exps, unit_b, total_b = scores(1, [swap(half, "proto") for half in halves], weights, exps=exps)
    (other,) = join(other, [(0, n_fsdp, bot)], (total_b,), bot)
    exps, unit_c, total_c = scores(2, [other], weights, exps=exps)
    exps, unit_d, total = scores(3, [swap(other, "proto")], weights, (total_a, total_b, total_c), exps)
    n_proto, own_cols = lax.axis_size("proto"), ws.shape[0]
    middle = own_cols // 2
    total = add_up([total, swap(total, "proto")])
    new, done = update_rest(teacher_weight, student_weight, total, new, own_cols, 0, middle)
    steps = [(up, over) for up in range(0, n_proto, 2) for over in range(n_dp)][1:]
    total = add_up([total, *[across(total, *step) for step in steps]], done)
    teacher_new, done = update_rest(teacher_weight, student_weight, total, new, own_cols, middle, own_cols)
    total = add_up(along_fsdp(total), done)
    student_grad = gradient(total, peak, unit, scale, (unit_a, unit_b, unit_c, unit_d), exps)
    return (teacher_new, student_grad)


def solution(mesh):
    placed = (
        P(None, ("proto", "fsdp")),
        P(None, ("proto", "fsdp")),
        P("dp", "fsdp", None),
        P("dp", "fsdp", None),
        P("dp", "fsdp"),
        P("proto"),
    )
    return jax.shard_map(
        shards,
        mesh=mesh,
        in_specs=placed,
        out_specs=(P(None, ("proto", "fsdp")), P(None, ("proto", "fsdp", "dp"))),
        check_vma=False,
    )
```

```python
import functools
import math

import jax
import jax.numpy as jnp
from jax import lax
from jax.experimental import pallas as pl
from jax.experimental.pallas import tpu as pltpu
from jax.sharding import PartitionSpec as P

EPS = 1e-06
DEPTH = 256
GROUP = 512
STEP = 256
DIRECT = 8
LOG2E = math.log2(math.e)
GAIN_T = LOG2E / 0.04
GAIN_S = LOG2E / 0.1
LIMIT = 24 * 1024 * 1024
ON_CHIP = pl.BlockSpec(memory_space=pltpu.VMEM)
IN_HBM = pl.BlockSpec(memory_space=pl.ANY)


def shape(*dims, dtype=jnp.float32):
    return jax.ShapeDtypeStruct(dims, dtype)


def held(*dims, dtype=jnp.float32):
    return pltpu.VMEM(dims, dtype)


def call(kernel, name, out_shape, args, **more):
    many = isinstance(out_shape, (list, tuple))
    specs = dict(in_specs=[ON_CHIP] * len(args), out_specs=[ON_CHIP] * len(out_shape) if many else ON_CHIP)
    return pl.pallas_call(
        kernel,
        out_shape=out_shape,
        compiler_params=pltpu.CompilerParams(vmem_limit_bytes=LIMIT),
        cost_estimate=pl.CostEstimate(flops=1, bytes_accessed=1, transcendentals=0),
        name=name,
        **{**specs, **more},
    )(*args)


def swap(block, axis, apart=1):
    return lax.ppermute(block, axis, [(i, i ^ apart) for i in range(lax.axis_size(axis))])


def here():
    return lax.axis_index("dp"), lax.axis_index("fsdp"), lax.rem(lax.axis_index("proto"), 2)


def cast_split(row):
    high = row.astype(jnp.bfloat16).astype(jnp.float32)
    mid = (row - high).astype(jnp.bfloat16).astype(jnp.float32)
    return high, mid, row - high - mid


def prep_kernel(n_dp, teacher_hbm, student_hbm, center_hbm, new_hbm, wt_ref, ws_ref, unit_ref, scale_ref, peak_ref, *scratch):
    teacher_buf, student_buf, new_buf, center_buf, in_t, in_s, out, in_c = scratch
    chunks, bot, width = new_buf.shape
    dp, fsdp, _ = here()
    first = dp * (chunks * width)
    at = [slice(i * width, (i + 1) * width) for i in range(chunks)]
    far = [pl.ds(pl.multiple_of(first + i * width, width), width) for i in range(chunks)]
    start = pl.multiple_of((fsdp * n_dp + dp) * (chunks * width), 128)
    center_load = pltpu.make_async_copy(center_hbm.at[:, pl.ds(start, chunks * width)], center_buf, in_c)
    loads = [
        (
            pltpu.make_async_copy(teacher_hbm.at[:, far[i]], teacher_buf.at[i], in_t.at[i]),
            pltpu.make_async_copy(student_hbm.at[:, far[i]], student_buf.at[i], in_s.at[i]),
        )
        for i in range(chunks)
    ]
    stores = [pltpu.make_async_copy(new_buf.at[i], new_hbm.at[:, far[i]], out.at[i]) for i in range(chunks)]
    center_load.start()
    for pair in loads:
        for load in pair:
            load.start()
    center_load.wait()
    center = center_buf[...]
    peak = jnp.max(-center, axis=1, keepdims=True)
    peak_ref[...] = jnp.broadcast_to(peak, peak_ref.shape)
    splits = cast_split(-center - peak)
    row = lax.broadcasted_iota(jnp.int32, (DEPTH - bot, width), 0)
    zero = jnp.zeros((DEPTH - bot, width), jnp.float32)
    for i in range(chunks):
        for load in loads[i]:
            load.wait()
        student = student_buf[i]
        new = 0.994 * teacher_buf[i] + 0.006 * student
        new_buf[i] = new
        stores[i].start()
        high, mid, low = [part[:, at[i]] for part in splits]
        extra = jnp.where(row == 0, high, jnp.where(row == 1, mid, jnp.where(row == 2, low, zero)))
        scale = lax.rsqrt(jnp.sum(student * student, axis=0, keepdims=True) + EPS)
        unit_s = student * scale
        unit_t = new * lax.rsqrt(jnp.sum(new * new, axis=0, keepdims=True) + EPS)
        wt_ref[at[i], :] = jnp.concatenate([unit_t, extra], axis=0).astype(jnp.bfloat16).T
        ws_ref[at[i], :] = jnp.concatenate([unit_s, zero], axis=0).astype(jnp.bfloat16).T
        unit_ref[:, at[i]] = unit_s
        scale_ref[:, at[i]] = scale
    for store in stores:
        store.wait()


def prepare(teacher_weight, student_weight, center, n_dp):
    bot, cols = teacher_weight.shape
    own = cols // n_dp
    width = min(512, own)
    chunks = own // width
    return call(
        functools.partial(prep_kernel, n_dp),
        "prep",
        [
            pltpu.HBM((bot, cols), jnp.float32),
            held(own, DEPTH, dtype=jnp.bfloat16),
            held(own, DEPTH, dtype=jnp.bfloat16),
            held(bot, own),
            held(1, own),
            held(1, 128),
        ],
        (teacher_weight, student_weight, center),
        in_specs=[IN_HBM] * 3,
        out_specs=[IN_HBM] + [ON_CHIP] * 5,
        scratch_shapes=[held(chunks, bot, width)] * 3
        + [held(1, own)]
        + [pltpu.SemaphoreType.DMA((chunks,))] * 3
        + [pltpu.SemaphoreType.DMA],
    )


def rest_kernel(lo, hi, own, teacher_hbm, student_hbm, after, before_hbm, new_hbm, done_ref, *scratch):
    teacher_buf, student_buf, new_buf, in_t, in_s, out = scratch
    width = hi - lo
    parts = teacher_hbm.shape[1] // own - 1
    dp = here()[0]
    done_ref[...] = jnp.zeros_like(done_ref)
    far = [pl.ds(pl.multiple_of(lax.rem(dp + 1 + i, parts + 1) * own + lo, 128), width) for i in range(parts)]
    loads = [
        (
            pltpu.make_async_copy(teacher_hbm.at[:, far[i]], teacher_buf.at[i], in_t.at[i]),
            pltpu.make_async_copy(student_hbm.at[:, far[i]], student_buf.at[i], in_s.at[i]),
        )
        for i in range(parts)
    ]
    stores = [pltpu.make_async_copy(new_buf.at[i], new_hbm.at[:, far[i]], out.at[i]) for i in range(parts)]
    for pair in loads:
        for load in pair:
            load.start()
    for i in range(parts):
        for load in loads[i]:
            load.wait()
        new_buf[i] = 0.994 * teacher_buf[i] + 0.006 * student_buf[i]
        stores[i].start()
    for store in stores:
        store.wait()


def update_rest(teacher_weight, student_weight, after, new, own, lo, hi):
    bot, cols = teacher_weight.shape
    parts = cols // own - 1
    return call(
        functools.partial(rest_kernel, lo, hi, own),
        "rest",
        [pltpu.HBM((bot, cols), jnp.float32), held(8, 128)],
        (teacher_weight, student_weight, after, new),
        in_specs=[IN_HBM] * 4,
        out_specs=[IN_HBM, ON_CHIP],
        input_output_aliases={3: 0},
        scratch_shapes=[held(parts, bot, hi - lo)] * 3 + [pltpu.SemaphoreType.DMA((parts,))] * 3,
    )


def fetch_kernel(student_hbm, teacher_hbm, student_ref, teacher_ref, sems):
    half = student_ref.shape[1]
    side = pl.ds(pl.multiple_of(here()[2] * half, half), half)
    loads = [
        pltpu.make_async_copy(student_hbm.at[:, side], student_ref, sems.at[0]),
        pltpu.make_async_copy(teacher_hbm, teacher_ref, sems.at[1]),
    ]
    for load in loads:
        load.start()
    for load in loads:
        load.wait()


def fetch(student, teacher):
    bot, crops = student.shape
    return call(
        fetch_kernel,
        "fetch",
        [held(bot, crops // 2, dtype=jnp.bfloat16), held(bot, crops, dtype=jnp.bfloat16)],
        (student, teacher),
        in_specs=[IN_HBM] * 2,
        scratch_shapes=[pltpu.SemaphoreType.DMA((2,))],
    )


def normalize(values):
    return (values * lax.rsqrt(jnp.sum(values * values, axis=0, keepdims=True) + EPS)).astype(jnp.bfloat16)


def pack_kernel(student_ref, teacher_ref, index_ref, out_ref):
    half = out_ref.shape[2]
    lower = here()[2] == 0
    out_ref[0] = normalize(student_ref[...].astype(jnp.float32))
    index = jnp.where(lower, index_ref[:, :half], index_ref[:, half:])
    row = lax.broadcasted_iota(jnp.int32, (teacher_ref.shape[1], half), 0)
    pick = jnp.where(row == index, 1.0, 0.0).astype(jnp.bfloat16)
    out_ref[1] = normalize(jnp.dot(teacher_ref[...], pick, preferred_element_type=jnp.float32))


def pack(student, teacher, index):
    bot, half = student.shape
    return call(pack_kernel, "pack", held(2, bot, half, dtype=jnp.bfloat16), (student, teacher, index))


def join_kernel(n_in, n_after, firsts, bot, *refs):
    blocks = []
    for ref in refs[:n_in]:
        blocks += [ref] if len(ref.shape) == 3 else [ref.at[i] for i in range(ref.shape[0])]
    for first, ref in zip(firsts, refs[n_in + n_after:]):
        for i in range(ref.shape[0]):
            block = blocks[first + i][:, :bot, :]
            ref[i, :, :bot, :] = block
            if ref.shape[2] > bot:
                ref[i, :, bot:, :] = block[:, :ref.shape[2] - bot]


def join(parts, outs, after, bot):
    width = parts[0].shape[-1]
    shapes = [held(count, 2, rows, width, dtype=jnp.bfloat16) for _, count, rows in outs]
    kernel = functools.partial(join_kernel, len(parts), len(after), [first for first, _, _ in outs], bot)
    return call(kernel, "join", shapes, (*parts, *after), in_specs=[ON_CHIP] * len(parts) + [IN_HBM] * len(after))


def log_sum(parts):
    top = functools.reduce(jnp.maximum, parts)
    return top + jnp.log2(sum(jnp.exp2(part - top) for part in parts))


def combine(parts):
    half = parts[0].shape[0] // 2
    return sum(part[:half] for part in parts), log_sum([part[half:] for part in parts])


def slot(k, n):
    return lax.axis_index("fsdp") ^ k if n <= DIRECT else k


def score_kernel(part, n_feats, *refs):
    last = part == 3
    before, refs = (refs[:3], refs[3:]) if last else ((), refs)
    feats_refs, (ws_ref, wt_ref, peak_ref, *refs) = refs[:n_feats], refs[n_feats:]
    blocks = [ref.at[i] for ref in feats_refs for i in range(ref.shape[0])]
    exp_ref, unit_ref, total_ref, *mine = refs[1:] if part else refs
    own_ref = mine[0] if last else total_ref
    n, (_, bot, width) = len(blocks), blocks[0].shape
    cols = ws_ref.shape[0]
    step = min(STEP, cols)
    per = max(1, min(n, GROUP // width))
    row = lax.broadcasted_iota(jnp.int32, (DEPTH - bot, per * width), 0)
    for which, w_ref, gain in ((0, ws_ref, GAIN_S), (1, wt_ref, GAIN_T)):
        base = (2 * part + which) * n * width
        extra = jnp.where(row < 3 * which, 1.0, 0.0).astype(jnp.bfloat16)
        for group in range(n // per):
            unit = jnp.concatenate([blocks[group * per + k][which] for k in range(per)], axis=1)
            lanes = slice(group * per * width, (group + 1) * per * width)
            if which == 0:
                unit_ref[lanes, :] = unit.T
            stationary = jnp.concatenate([unit, extra], axis=0)
            total = jnp.zeros((8, per * width), jnp.float32)
            for at in range(0, cols, step):
                score = jnp.dot(w_ref[at:at + step, :], stationary, preferred_element_type=jnp.float32)
                exps = jnp.exp2(score * gain)
                total = total + jnp.sum(exps.reshape(step // 8, 8, per * width), axis=0)
                exp_ref[at:at + step, base + lanes.start:base + lanes.stop] = exps.astype(jnp.bfloat16)
            total = jnp.sum(total, axis=0, keepdims=True)
            if which == 1:
                total = jnp.log2(total) + GAIN_T * peak_ref[:, :1]
            own_ref[which:which + 1, lanes] = total
    if not last:
        return
    dp, _, core = here()
    own, pair, other = before
    parts = ((own, other), (pair, own_ref))
    rows = []
    for which in (0, 1):
        for half in (0, 1):
            pieces = []
            for view in (0, 1):
                first = (dp == view) if which == 0 else (dp != view)
                for place in range(n):
                    at = pl.ds(pl.multiple_of(slot(place, n) * width, width), width)
                    read = [[part[which:which + 1, at] for part in side] for side in parts]
                    mine, theirs = [jnp.where(first, *side) for side in read]
                    pieces.append(jnp.where(core == half, mine, theirs))
            rows.append(jnp.concatenate(pieces, axis=1))
    total_ref[...] = jnp.concatenate(rows, axis=0)


def scores(part, feats, weights, before=(), exps=None):
    _, _, bot, width = feats[0].shape
    cols, rows = weights[0].shape[0], sum(part.shape[0] for part in feats) * width
    args = (*before, *feats, *weights, *([exps] if part else []))
    return call(
        functools.partial(score_kernel, part, len(feats)),
        "scores",
        [
            held(cols, 8 * rows, dtype=jnp.bfloat16),
            held(rows, bot, dtype=jnp.bfloat16),
            held(4, 2 * rows) if part == 3 else held(2, rows),
        ],
        args,
        in_specs=[ON_CHIP] * (len(args) - bool(part)) + [IN_HBM] * bool(part),
        input_output_aliases={len(args) - 1: 0} if part else {},
        scratch_shapes=[held(2, rows)] if part == 3 else [],
    )


def relay_kernel(n_in, *refs):
    parts = [ref[...] for ref in refs[:n_in]]
    if len(parts[0].shape) == 3:
        parts = [parts[0][i] for i in range(parts[0].shape[0])]
    refs[-1][...] = jnp.concatenate(combine(parts), axis=0)


def add_up(parts, *after):
    specs = [ON_CHIP] * len(parts) + [IN_HBM] * len(after)
    out = held(*parts[0].shape[-2:])
    return call(functools.partial(relay_kernel, len(parts)), "relay", out, (*parts, *after), in_specs=specs)


def across(total, up, over):
    n_proto, n_dp = lax.axis_size("proto"), lax.axis_size("dp")
    places = [(p, d) for p in range(n_proto) for d in range(n_dp)]
    pairs = [(p * n_dp + d, (p ^ up) * n_dp + (d ^ over)) for p, d in places]
    return lax.ppermute(total, ("proto", "dp"), pairs)


def along_fsdp(total):
    n = lax.axis_size("fsdp")
    if n <= DIRECT:
        return [total, *[swap(total, "fsdp", k) for k in range(1, n)]]
    return [lax.all_to_all(jnp.broadcast_to(total[None], (n, *total.shape)), "fsdp", 0, 0, tiled=True)]


def grad_kernel(total_ref, peak_ref, weight_unit, weight_scale, *refs):
    units, exp_ref, out_hbm, scales, feats, *derivs, buf, sems = refs[:4], *refs[4:]
    dp, _, core = here()
    scales[0:2, :] = 10.0 / total_ref[0:2, :]
    scales[2:4, :] = 10.0 * jnp.exp2(GAIN_T * peak_ref[:, :1] - total_ref[2:4, :])
    rows = units[0].shape[0]
    width = 128
    n = rows // width
    factors = []
    for part in range(4):
        view, half = divmod(part, 2)
        base = (dp ^ view) * rows
        at = [pl.ds(pl.multiple_of(base + slot(k, n) * width, width), width) for k in range(n)]
        for which in (0, 1):
            picked = [
                jnp.where(core == half, scales[2 * which:2 * which + 1, where], scales[2 * which + 1:2 * which + 2, where])
                for where in at
            ]
            factors.append(jnp.concatenate(picked, axis=1).astype(jnp.bfloat16))
    for part, unit in enumerate(units):
        feats[part * rows:(part + 1) * rows, :] = unit[...]
    chunks, _, step = buf.shape
    stores = []

    def derive(i):
        at = slice(i * step, (i + 1) * step)
        for part in range(4):
            lies_s, lies_t = 2 * part * rows, (2 * (part ^ 2) + 1) * rows
            probs_s = exp_ref[at, lies_s:lies_s + rows] * factors[2 * part]
            probs_t = exp_ref[at, lies_t:lies_t + rows] * factors[2 * part + 1]
            derivs[i % 2][:, part * rows:(part + 1) * rows] = probs_s - probs_t

    derive(0)
    for i in range(chunks):
        if i + 1 < chunks:
            derive(i + 1)
        at = slice(i * step, (i + 1) * step)
        grad = jnp.dot(derivs[i % 2][...], feats[...], preferred_element_type=jnp.float32).T
        unit = weight_unit[:, at]
        proj = unit * jnp.sum(unit * grad, axis=0, keepdims=True)
        buf[i] = (grad - proj) * weight_scale[:, at]
        stores.append(pltpu.make_async_copy(buf.at[i], out_hbm.at[:, at], sems.at[i]))
        stores[i].start()
    for store in stores:
        store.wait()


def gradient(total, peak, weight_unit, weight_scale, units, exps):
    cols = exps.shape[0]
    rows, bot = units[0].shape
    step = min(256, cols)
    args = (total, peak, weight_unit, weight_scale, *units, exps)
    return call(
        grad_kernel,
        "gradient",
        pltpu.HBM((bot, cols), jnp.float32),
        args,
        out_specs=IN_HBM,
        scratch_shapes=[
            held(4, 2 * rows),
            held(4 * rows, bot, dtype=jnp.bfloat16),
            *[held(step, 4 * rows, dtype=jnp.bfloat16)] * 2,
            held(cols // step, bot, step),
            pltpu.SemaphoreType.DMA((cols // step,)),
        ],
    )


def shards(teacher_weight, student_weight, teacher_feats, student_feats, pairing, center):
    n_dp, n_fsdp = lax.axis_size("dp"), lax.axis_size("fsdp")
    in_hbm = lambda array: pltpu.with_memory_space_constraint(array, pltpu.HBM)
    teacher_weight, student_weight, center = in_hbm(teacher_weight), in_hbm(student_weight), in_hbm(center[None, :])

    index = swap(pairing, "dp")
    mine = pack(*fetch(in_hbm(student_feats[0].T), in_hbm(teacher_feats[0].T)), index)
    new, wt, ws, unit, scale, peak = prepare(teacher_weight, student_weight, center, n_dp)
    weights = (ws, wt, peak)
    bot = mine.shape[1]
    if n_fsdp <= DIRECT:
        other = [swap(mine, "dp")]
        along = [swap(mine, "fsdp", k) for k in range(1, n_fsdp)]
        half = n_fsdp // 2
        outs = [(0, n_fsdp, bot), (2, n_fsdp - 2, bot + 16), (0, half, bot), (half, half, bot)]
        own, far, *halves = join([mine, *along], outs, (other[0], peak), bot)
        other += [swap(other[0], "fsdp"), swap(far, "dp")]
    else:
        own = lax.all_to_all(jnp.broadcast_to(mine[None], (n_fsdp, *mine.shape)), "fsdp", 0, 0, tiled=True)
        other, halves = [swap(own, "dp")], [own]
    exps, unit_a, total_a = scores(0, [own], weights)
    exps, unit_b, total_b = scores(1, [swap(half, "proto") for half in halves], weights, exps=exps)
    (other,) = join(other, [(0, n_fsdp, bot)], (total_b,), bot)
    exps, unit_c, total_c = scores(2, [other], weights, exps=exps)
    exps, unit_d, total = scores(3, [swap(other, "proto")], weights, (total_a, total_b, total_c), exps)
    n_proto, own_cols = lax.axis_size("proto"), ws.shape[0]
    middle = own_cols // 2
    total = add_up([total, swap(total, "proto")])
    new, done = update_rest(teacher_weight, student_weight, total, new, own_cols, 0, middle)
    steps = [(up, over) for up in range(0, n_proto, 2) for over in range(n_dp)][1:]
    total = add_up([total, *[across(total, *step) for step in steps]], done)
    teacher_new, done = update_rest(teacher_weight, student_weight, total, new, own_cols, middle, own_cols)
    total = add_up(along_fsdp(total), done)
    student_grad = gradient(total, peak, unit, scale, (unit_a, unit_b, unit_c, unit_d), exps)
    return (teacher_new, student_grad)


def solution(mesh):
    placed = (
        P(None, ("proto", "fsdp")),
        P(None, ("proto", "fsdp")),
        P("dp", "fsdp", None),
        P("dp", "fsdp", None),
        P("dp", "fsdp"),
        P("proto"),
    )
    return jax.shard_map(
        shards,
        mesh=mesh,
        in_specs=placed,
        out_specs=(P(None, ("proto", "fsdp")), P(None, ("proto", "fsdp", "dp"))),
        check_vma=False,
    )
```

```python
import functools
import math

import jax
import jax.numpy as jnp
from jax import lax
from jax.experimental import pallas as pl
from jax.experimental.pallas import tpu as pltpu
from jax.sharding import PartitionSpec as P

EPS = 1e-06
DEPTH = 256
GROUP = 512
STEP = 256
DIRECT = 8
LOG2E = math.log2(math.e)
GAIN_T = LOG2E / 0.04
GAIN_S = LOG2E / 0.1
LIMIT = 24 * 1024 * 1024
ON_CHIP = pl.BlockSpec(memory_space=pltpu.VMEM)
IN_HBM = pl.BlockSpec(memory_space=pl.ANY)


def shape(*dims, dtype=jnp.float32):
    return jax.ShapeDtypeStruct(dims, dtype)


def held(*dims, dtype=jnp.float32):
    return pltpu.VMEM(dims, dtype)


def call(kernel, name, out_shape, args, **more):
    many = isinstance(out_shape, (list, tuple))
    specs = dict(in_specs=[ON_CHIP] * len(args), out_specs=[ON_CHIP] * len(out_shape) if many else ON_CHIP)
    return pl.pallas_call(
        kernel,
        out_shape=out_shape,
        compiler_params=pltpu.CompilerParams(vmem_limit_bytes=LIMIT),
        cost_estimate=pl.CostEstimate(flops=1, bytes_accessed=1, transcendentals=0),
        name=name,
        **{**specs, **more},
    )(*args)


def swap(block, axis, apart=1):
    return lax.ppermute(block, axis, [(i, i ^ apart) for i in range(lax.axis_size(axis))])


def here():
    return lax.axis_index("dp"), lax.axis_index("fsdp"), lax.rem(lax.axis_index("proto"), 2)


def cast_split(row):
    high = row.astype(jnp.bfloat16).astype(jnp.float32)
    mid = (row - high).astype(jnp.bfloat16).astype(jnp.float32)
    return high, mid, row - high - mid


def prep_kernel(n_dp, n_own, teacher_hbm, student_hbm, center_hbm, before_hbm, new_hbm, wt_ref, ws_ref, unit_ref, scale_ref, peak_ref, *scratch):
    teacher_buf, student_buf, new_buf, center_buf, in_t, in_s, out, in_c = scratch
    chunks, bot, width = new_buf.shape
    dp, fsdp, _ = here()
    own = n_own * width
    at = [slice(i * width, (i + 1) * width) for i in range(n_own)]
    firsts = [dp * own + i * width for i in range(n_own)]
    more = (chunks - n_own) // (n_dp - 1) if n_dp > 1 else 0
    firsts += [lax.rem(dp + 1 + i // more, n_dp) * own + (n_own - more + i % more) * width for i in range(chunks - n_own)]
    far = [pl.ds(pl.multiple_of(first, width), width) for first in firsts]
    start = pl.multiple_of((fsdp * n_dp + dp) * own, 128)
    center_load = pltpu.make_async_copy(center_hbm.at[:, pl.ds(start, own)], center_buf, in_c)
    loads = [
        (
            pltpu.make_async_copy(teacher_hbm.at[:, far[i]], teacher_buf.at[i], in_t.at[i]),
            pltpu.make_async_copy(student_hbm.at[:, far[i]], student_buf.at[i], in_s.at[i]),
        )
        for i in range(chunks)
    ]
    stores = [pltpu.make_async_copy(new_buf.at[i], new_hbm.at[:, far[i]], out.at[i]) for i in range(chunks)]
    center_load.start()
    for pair in loads:
        for load in pair:
            load.start()
    center_load.wait()
    center = center_buf[...]
    peak = jnp.max(-center, axis=1, keepdims=True)
    peak_ref[...] = jnp.broadcast_to(peak, peak_ref.shape)
    splits = cast_split(-center - peak)
    row = lax.broadcasted_iota(jnp.int32, (DEPTH - bot, width), 0)
    zero = jnp.zeros((DEPTH - bot, width), jnp.float32)
    for i in range(chunks):
        for load in loads[i]:
            load.wait()
        student = student_buf[i]
        new = 0.994 * teacher_buf[i] + 0.006 * student
        new_buf[i] = new
        stores[i].start()
        if i >= n_own:
            continue
        high, mid, low = [part[:, at[i]] for part in splits]
        extra = jnp.where(row == 0, high, jnp.where(row == 1, mid, jnp.where(row == 2, low, zero)))
        scale = lax.rsqrt(jnp.sum(student * student, axis=0, keepdims=True) + EPS)
        unit_s = student * scale
        unit_t = new * lax.rsqrt(jnp.sum(new * new, axis=0, keepdims=True) + EPS)
        wt_ref[at[i], :] = jnp.concatenate([unit_t, extra], axis=0).astype(jnp.bfloat16).T
        ws_ref[at[i], :] = jnp.concatenate([unit_s, zero], axis=0).astype(jnp.bfloat16).T
        unit_ref[:, at[i]] = unit_s
        scale_ref[:, at[i]] = scale
    for store in stores:
        store.wait()


def prepare(teacher_weight, student_weight, center, new, n_dp, more):
    bot, cols = teacher_weight.shape
    own = cols // n_dp
    width = math.gcd(min(512, own), more)
    n_own = own // width
    chunks = n_own + (n_dp - 1) * (more // width)
    return call(
        functools.partial(prep_kernel, n_dp, n_own),
        "prep",
        [
            pltpu.HBM((bot, cols), jnp.float32),
            held(own, DEPTH, dtype=jnp.bfloat16),
            held(own, DEPTH, dtype=jnp.bfloat16),
            held(bot, own),
            held(1, own),
            held(1, 128),
        ],
        (teacher_weight, student_weight, center, new),
        in_specs=[IN_HBM] * 4,
        out_specs=[IN_HBM] + [ON_CHIP] * 5,
        input_output_aliases={3: 0},
        scratch_shapes=[held(chunks, bot, width)] * 3
        + [held(1, own)]
        + [pltpu.SemaphoreType.DMA((chunks,))] * 3
        + [pltpu.SemaphoreType.DMA],
    )


def rest_kernel(lo, hi, own, teacher_hbm, student_hbm, new_hbm, done_ref, *scratch):
    teacher_buf, student_buf, new_buf, in_t, in_s, out = scratch
    width = hi - lo
    parts = teacher_hbm.shape[1] // own - 1
    dp = here()[0]
    done_ref[...] = jnp.zeros_like(done_ref)
    far = [pl.ds(pl.multiple_of(lax.rem(dp + 1 + i, parts + 1) * own + lo, 128), width) for i in range(parts)]
    loads = [
        (
            pltpu.make_async_copy(teacher_hbm.at[:, far[i]], teacher_buf.at[i], in_t.at[i]),
            pltpu.make_async_copy(student_hbm.at[:, far[i]], student_buf.at[i], in_s.at[i]),
        )
        for i in range(parts)
    ]
    stores = [pltpu.make_async_copy(new_buf.at[i], new_hbm.at[:, far[i]], out.at[i]) for i in range(parts)]
    for pair in loads:
        for load in pair:
            load.start()
    for i in range(parts):
        for load in loads[i]:
            load.wait()
        new_buf[i] = 0.994 * teacher_buf[i] + 0.006 * student_buf[i]
        stores[i].start()
    for store in stores:
        store.wait()


def update_rest(teacher_weight, student_weight, own, lo, hi):
    bot, cols = teacher_weight.shape
    parts = cols // own - 1
    return call(
        functools.partial(rest_kernel, lo, hi, own),
        "rest",
        [pltpu.HBM((bot, cols), jnp.float32), held(8, 128)],
        (teacher_weight, student_weight),
        in_specs=[IN_HBM] * 2,
        out_specs=[IN_HBM, ON_CHIP],
        scratch_shapes=[held(parts, bot, hi - lo)] * 3 + [pltpu.SemaphoreType.DMA((parts,))] * 3,
    )


def fetch_kernel(student_hbm, teacher_hbm, student_ref, teacher_ref, sems):
    half = student_ref.shape[1]
    side = pl.ds(pl.multiple_of(here()[2] * half, half), half)
    loads = [
        pltpu.make_async_copy(student_hbm.at[:, side], student_ref, sems.at[0]),
        pltpu.make_async_copy(teacher_hbm, teacher_ref, sems.at[1]),
    ]
    for load in loads:
        load.start()
    for load in loads:
        load.wait()


def fetch(student, teacher):
    bot, crops = student.shape
    return call(
        fetch_kernel,
        "fetch",
        [held(bot, crops // 2, dtype=jnp.bfloat16), held(bot, crops, dtype=jnp.bfloat16)],
        (student, teacher),
        in_specs=[IN_HBM] * 2,
        scratch_shapes=[pltpu.SemaphoreType.DMA((2,))],
    )


def normalize(values):
    return (values * lax.rsqrt(jnp.sum(values * values, axis=0, keepdims=True) + EPS)).astype(jnp.bfloat16)


def pack_kernel(student_ref, teacher_ref, index_ref, after, out_ref):
    half = out_ref.shape[2]
    lower = here()[2] == 0
    out_ref[0] = normalize(student_ref[...].astype(jnp.float32))
    index = jnp.where(lower, index_ref[:, :half], index_ref[:, half:])
    row = lax.broadcasted_iota(jnp.int32, (teacher_ref.shape[1], half), 0)
    pick = jnp.where(row == index, 1.0, 0.0).astype(jnp.bfloat16)
    out_ref[1] = normalize(jnp.dot(teacher_ref[...], pick, preferred_element_type=jnp.float32))


def pack(student, teacher, index, after):
    bot, half = student.shape
    out = held(2, bot, half, dtype=jnp.bfloat16)
    return call(pack_kernel, "pack", out, (student, teacher, index, after), in_specs=[ON_CHIP] * 3 + [IN_HBM])


def join_kernel(n_in, n_after, firsts, bot, *refs):
    blocks = []
    for ref in refs[:n_in]:
        blocks += [ref] if len(ref.shape) == 3 else [ref.at[i] for i in range(ref.shape[0])]
    for first, ref in zip(firsts, refs[n_in + n_after:]):
        for i in range(ref.shape[0]):
            block = blocks[first + i][:, :bot, :]
            ref[i, :, :bot, :] = block
            if ref.shape[2] > bot:
                ref[i, :, bot:, :] = block[:, :ref.shape[2] - bot]


def join(parts, outs, after, bot):
    width = parts[0].shape[-1]
    shapes = [held(count, 2, rows, width, dtype=jnp.bfloat16) for _, count, rows in outs]
    kernel = functools.partial(join_kernel, len(parts), len(after), [first for first, _, _ in outs], bot)
    return call(kernel, "join", shapes, (*parts, *after), in_specs=[ON_CHIP] * len(parts) + [IN_HBM] * len(after))


def log_sum(parts):
    top = functools.reduce(jnp.maximum, parts)
    return top + jnp.log2(sum(jnp.exp2(part - top) for part in parts))


def combine(parts):
    half = parts[0].shape[0] // 2
    return sum(part[:half] for part in parts), log_sum([part[half:] for part in parts])


def slot(k, n):
    return lax.axis_index("fsdp") ^ k if n <= DIRECT else k


def score_kernel(part, n_feats, *refs):
    last = part == 3
    before, refs = (refs[:3], refs[3:]) if last else ((), refs)
    feats_refs, (ws_ref, wt_ref, peak_ref, *refs) = refs[:n_feats], refs[n_feats:]
    blocks = [ref.at[i] for ref in feats_refs for i in range(ref.shape[0])]
    exp_ref, unit_ref, total_ref, *mine = refs[1:] if part else refs
    own_ref = mine[0] if last else total_ref
    n, (_, bot, width) = len(blocks), blocks[0].shape
    cols = ws_ref.shape[0]
    step = min(STEP, cols)
    per = max(1, min(n, GROUP // width))
    row = lax.broadcasted_iota(jnp.int32, (DEPTH - bot, per * width), 0)
    for which, w_ref, gain in ((0, ws_ref, GAIN_S), (1, wt_ref, GAIN_T)):
        base = (2 * part + which) * n * width
        extra = jnp.where(row < 3 * which, 1.0, 0.0).astype(jnp.bfloat16)
        for group in range(n // per):
            unit = jnp.concatenate([blocks[group * per + k][which] for k in range(per)], axis=1)
            lanes = slice(group * per * width, (group + 1) * per * width)
            if which == 0:
                unit_ref[lanes, :] = unit.T
            stationary = jnp.concatenate([unit, extra], axis=0)
            total = jnp.zeros((8, per * width), jnp.float32)
            for at in range(0, cols, step):
                score = jnp.dot(w_ref[at:at + step, :], stationary, preferred_element_type=jnp.float32)
                exps = jnp.exp2(score * gain)
                total = total + jnp.sum(exps.reshape(step // 8, 8, per * width), axis=0)
                exp_ref[at:at + step, base + lanes.start:base + lanes.stop] = exps.astype(jnp.bfloat16)
            total = jnp.sum(total, axis=0, keepdims=True)
            if which == 1:
                total = jnp.log2(total) + GAIN_T * peak_ref[:, :1]
            own_ref[which:which + 1, lanes] = total
    if not last:
        return
    dp, _, core = here()
    own, pair, other = before
    parts = ((own, other), (pair, own_ref))
    rows = []
    for which in (0, 1):
        for half in (0, 1):
            pieces = []
            for view in (0, 1):
                first = (dp == view) if which == 0 else (dp != view)
                for place in range(n):
                    at = pl.ds(pl.multiple_of(slot(place, n) * width, width), width)
                    read = [[part[which:which + 1, at] for part in side] for side in parts]
                    mine, theirs = [jnp.where(first, *side) for side in read]
                    pieces.append(jnp.where(core == half, mine, theirs))
            rows.append(jnp.concatenate(pieces, axis=1))
    total_ref[...] = jnp.concatenate(rows, axis=0)


def scores(part, feats, weights, before=(), exps=None):
    _, _, bot, width = feats[0].shape
    cols, rows = weights[0].shape[0], sum(part.shape[0] for part in feats) * width
    args = (*before, *feats, *weights, *([exps] if part else []))
    return call(
        functools.partial(score_kernel, part, len(feats)),
        "scores",
        [
            held(cols, 8 * rows, dtype=jnp.bfloat16),
            held(rows, bot, dtype=jnp.bfloat16),
            held(4, 2 * rows) if part == 3 else held(2, rows),
        ],
        args,
        in_specs=[ON_CHIP] * (len(args) - bool(part)) + [IN_HBM] * bool(part),
        input_output_aliases={len(args) - 1: 0} if part else {},
        scratch_shapes=[held(2, rows)] if part == 3 else [],
    )


def relay_kernel(n_in, *refs):
    parts = [ref[...] for ref in refs[:n_in]]
    if len(parts[0].shape) == 3:
        parts = [parts[0][i] for i in range(parts[0].shape[0])]
    refs[-1][...] = jnp.concatenate(combine(parts), axis=0)


def add_up(parts):
    return call(functools.partial(relay_kernel, len(parts)), "relay", held(*parts[0].shape[-2:]), parts)


def across(total, up, over):
    n_proto, n_dp = lax.axis_size("proto"), lax.axis_size("dp")
    far = lambda p, d: (p ^ up, d ^ over) if p % 2 else (p, d)
    places = [(p, d) for p in range(n_proto) for d in range(n_dp)]
    pairs = [(p * n_dp + d, far(p, d)[0] * n_dp + far(p, d)[1]) for p, d in places]
    return lax.ppermute(total, ("proto", "dp"), pairs)


def along_fsdp(total):
    n, n_proto = lax.axis_size("fsdp"), lax.axis_size("proto")
    if n <= DIRECT:
        pairs = lambda k: [(i * n_proto + p, (i ^ k if p % 2 else i) * n_proto + p) for i in range(n) for p in range(n_proto)]
        return [total, *[lax.ppermute(total, ("fsdp", "proto"), pairs(k)) for k in range(1, n)]]
    return [lax.all_to_all(jnp.broadcast_to(total[None], (n, *total.shape)), "fsdp", 0, 0, tiled=True)]


def grad_kernel(led_ref, given_ref, peak_ref, weight_unit, weight_scale, *refs):
    units, exp_ref, out_hbm, scales, feats, *derivs, buf, sems = refs[:4], *refs[4:]
    dp, _, core = here()
    total = jnp.where(core == 1, led_ref[...], given_ref[...])
    scales[0:2, :] = 10.0 / total[0:2]
    scales[2:4, :] = 10.0 * jnp.exp2(GAIN_T * peak_ref[:, :1] - total[2:4])
    rows = units[0].shape[0]
    width = 128
    n = rows // width
    factors = []
    for part in range(4):
        view, half = divmod(part, 2)
        base = (dp ^ view) * rows
        at = [pl.ds(pl.multiple_of(base + slot(k, n) * width, width), width) for k in range(n)]
        for which in (0, 1):
            picked = [
                jnp.where(core == half, scales[2 * which:2 * which + 1, where], scales[2 * which + 1:2 * which + 2, where])
                for where in at
            ]
            factors.append(jnp.concatenate(picked, axis=1).astype(jnp.bfloat16))
    for part, unit in enumerate(units):
        feats[part * rows:(part + 1) * rows, :] = unit[...]
    chunks, _, step = buf.shape
    stores = []

    def derive(i):
        at = slice(i * step, (i + 1) * step)
        for part in range(4):
            lies_s, lies_t = 2 * part * rows, (2 * (part ^ 2) + 1) * rows
            probs_s = exp_ref[at, lies_s:lies_s + rows] * factors[2 * part]
            probs_t = exp_ref[at, lies_t:lies_t + rows] * factors[2 * part + 1]
            derivs[i % 2][:, part * rows:(part + 1) * rows] = probs_s - probs_t

    derive(0)
    for i in range(chunks):
        if i + 1 < chunks:
            derive(i + 1)
        at = slice(i * step, (i + 1) * step)
        grad = jnp.dot(derivs[i % 2][...], feats[...], preferred_element_type=jnp.float32).T
        unit = weight_unit[:, at]
        proj = unit * jnp.sum(unit * grad, axis=0, keepdims=True)
        buf[i] = (grad - proj) * weight_scale[:, at]
        stores.append(pltpu.make_async_copy(buf.at[i], out_hbm.at[:, at], sems.at[i]))
        stores[i].start()
    for store in stores:
        store.wait()


def gradient(led, given, peak, weight_unit, weight_scale, units, exps):
    cols = exps.shape[0]
    rows, bot = units[0].shape
    step = min(256, cols)
    args = (led, given, peak, weight_unit, weight_scale, *units, exps)
    return call(
        grad_kernel,
        "gradient",
        pltpu.HBM((bot, cols), jnp.float32),
        args,
        out_specs=IN_HBM,
        scratch_shapes=[
            held(4, 2 * rows),
            held(4 * rows, bot, dtype=jnp.bfloat16),
            *[held(step, 4 * rows, dtype=jnp.bfloat16)] * 2,
            held(cols // step, bot, step),
            pltpu.SemaphoreType.DMA((cols // step,)),
        ],
    )


def shards(teacher_weight, student_weight, teacher_feats, student_feats, pairing, center):
    n_dp, n_fsdp = lax.axis_size("dp"), lax.axis_size("fsdp")
    in_hbm = lambda array: pltpu.with_memory_space_constraint(array, pltpu.HBM)
    teacher_weight, student_weight, center = in_hbm(teacher_weight), in_hbm(student_weight), in_hbm(center[None, :])

    index = swap(pairing, "dp")
    own_cols = teacher_weight.shape[1] // n_dp
    middle = own_cols // 2
    new, done = update_rest(teacher_weight, student_weight, own_cols, 0, middle)
    mine = pack(*fetch(in_hbm(student_feats[0].T), in_hbm(teacher_feats[0].T)), index, done)
    teacher_new, wt, ws, unit, scale, peak = prepare(teacher_weight, student_weight, center, new, n_dp, own_cols - middle)
    weights = (ws, wt, peak)
    bot = mine.shape[1]
    if n_fsdp <= DIRECT:
        other = [swap(mine, "dp")]
        along = [swap(mine, "fsdp", k) for k in range(1, n_fsdp)]
        half = n_fsdp // 2
        outs = [(0, n_fsdp, bot), (2, n_fsdp - 2, bot + 16), (0, half, bot), (half, half, bot)]
        own, far, *halves = join([mine, *along], outs, (other[0], peak), bot)
        other += [swap(other[0], "fsdp"), swap(far, "dp")]
    else:
        own = lax.all_to_all(jnp.broadcast_to(mine[None], (n_fsdp, *mine.shape)), "fsdp", 0, 0, tiled=True)
        other, halves = [swap(own, "dp")], [own]
    exps, unit_a, total_a = scores(0, [own], weights)
    exps, unit_b, total_b = scores(1, [swap(half, "proto") for half in halves], weights, exps=exps)
    (other,) = join(other, [(0, n_fsdp, bot)], (total_b,), bot)
    exps, unit_c, total_c = scores(2, [other], weights, exps=exps)
    exps, unit_d, total = scores(3, [swap(other, "proto")], weights, (total_a, total_b, total_c), exps)
    total = add_up([total, swap(total, "proto")])
    steps = [(up, over) for up in range(0, lax.axis_size("proto"), 2) for over in range(n_dp)][1:]
    total = add_up([total, *[across(total, *step) for step in steps]])
    total = add_up(along_fsdp(total))
    units = (unit_a, unit_b, unit_c, unit_d)
    student_grad = gradient(total, swap(total, "proto"), peak, unit, scale, units, exps)
    return (teacher_new, student_grad)


def solution(mesh):
    placed = (
        P(None, ("proto", "fsdp")),
        P(None, ("proto", "fsdp")),
        P("dp", "fsdp", None),
        P("dp", "fsdp", None),
        P("dp", "fsdp"),
        P("proto"),
    )
    return jax.shard_map(
        shards,
        mesh=mesh,
        in_specs=placed,
        out_specs=(P(None, ("proto", "fsdp")), P(None, ("proto", "fsdp", "dp"))),
        check_vma=False,
    )
```

```python
import functools
import math

import jax
import jax.numpy as jnp
from jax import lax
from jax.experimental import pallas as pl
from jax.experimental.pallas import tpu as pltpu
from jax.sharding import PartitionSpec as P

EPS = 1e-06
DEPTH = 256
GROUP = 512
STEP = 256
DIRECT = 8
LOG2E = math.log2(math.e)
GAIN_T = LOG2E / 0.04
GAIN_S = LOG2E / 0.1
LIMIT = 24 * 1024 * 1024
ON_CHIP = pl.BlockSpec(memory_space=pltpu.VMEM)
IN_HBM = pl.BlockSpec(memory_space=pl.ANY)


def shape(*dims, dtype=jnp.float32):
    return jax.ShapeDtypeStruct(dims, dtype)


def held(*dims, dtype=jnp.float32):
    return pltpu.VMEM(dims, dtype)


def call(kernel, name, out_shape, args, **more):
    many = isinstance(out_shape, (list, tuple))
    specs = dict(in_specs=[ON_CHIP] * len(args), out_specs=[ON_CHIP] * len(out_shape) if many else ON_CHIP)
    return pl.pallas_call(
        kernel,
        out_shape=out_shape,
        compiler_params=pltpu.CompilerParams(vmem_limit_bytes=LIMIT),
        cost_estimate=pl.CostEstimate(flops=1, bytes_accessed=1, transcendentals=0),
        name=name,
        **{**specs, **more},
    )(*args)


def swap(block, axis, apart=1):
    return lax.ppermute(block, axis, [(i, i ^ apart) for i in range(lax.axis_size(axis))])


def here():
    return lax.axis_index("dp"), lax.axis_index("fsdp"), lax.rem(lax.axis_index("proto"), 2)


def cast_split(row):
    high = row.astype(jnp.bfloat16).astype(jnp.float32)
    mid = (row - high).astype(jnp.bfloat16).astype(jnp.float32)
    return high, mid, row - high - mid


def prep_kernel(n_dp, n_own, teacher_hbm, student_hbm, center_hbm, new_hbm, wt_ref, ws_ref, unit_ref, scale_ref, peak_ref, *scratch):
    teacher_buf, student_buf, new_buf, center_buf, in_t, in_s, out, in_c = scratch
    chunks, bot, width = new_buf.shape
    dp, fsdp, _ = here()
    own = n_own * width
    at = [slice(i * width, (i + 1) * width) for i in range(n_own)]
    firsts = [dp * own + i * width for i in range(n_own)]
    more = (chunks - n_own) // (n_dp - 1) if n_dp > 1 else 0
    firsts += [lax.rem(dp + 1 + i // more, n_dp) * own + (n_own - more + i % more) * width for i in range(chunks - n_own)]
    far = [pl.ds(pl.multiple_of(first, width), width) for first in firsts]
    start = pl.multiple_of((fsdp * n_dp + dp) * own, 128)
    center_load = pltpu.make_async_copy(center_hbm.at[:, pl.ds(start, own)], center_buf, in_c)
    loads = [
        (
            pltpu.make_async_copy(teacher_hbm.at[:, far[i]], teacher_buf.at[i], in_t.at[i]),
            pltpu.make_async_copy(student_hbm.at[:, far[i]], student_buf.at[i], in_s.at[i]),
        )
        for i in range(chunks)
    ]
    stores = [pltpu.make_async_copy(new_buf.at[i], new_hbm.at[:, far[i]], out.at[i]) for i in range(chunks)]
    center_load.start()
    for pair in loads:
        for load in pair:
            load.start()
    center_load.wait()
    center = center_buf[...]
    peak = jnp.max(-center, axis=1, keepdims=True)
    peak_ref[...] = jnp.broadcast_to(peak, peak_ref.shape)
    splits = cast_split(-center - peak)
    row = lax.broadcasted_iota(jnp.int32, (DEPTH - bot, width), 0)
    zero = jnp.zeros((DEPTH - bot, width), jnp.float32)
    for i in range(chunks):
        for load in loads[i]:
            load.wait()
        student = student_buf[i]
        new = 0.994 * teacher_buf[i] + 0.006 * student
        new_buf[i] = new
        stores[i].start()
        if i >= n_own:
            continue
        high, mid, low = [part[:, at[i]] for part in splits]
        extra = jnp.where(row == 0, high, jnp.where(row == 1, mid, jnp.where(row == 2, low, zero)))
        scale = lax.rsqrt(jnp.sum(student * student, axis=0, keepdims=True) + EPS)
        unit_s = student * scale
        unit_t = new * lax.rsqrt(jnp.sum(new * new, axis=0, keepdims=True) + EPS)
        wt_ref[at[i], :] = jnp.concatenate([unit_t, extra], axis=0).astype(jnp.bfloat16).T
        ws_ref[at[i], :] = jnp.concatenate([unit_s, zero], axis=0).astype(jnp.bfloat16).T
        unit_ref[:, at[i]] = unit_s
        scale_ref[:, at[i]] = scale
    for store in stores:
        store.wait()


def prepare(teacher_weight, student_weight, center, n_dp, more):
    bot, cols = teacher_weight.shape
    own = cols // n_dp
    width = math.gcd(min(512, own), more)
    n_own = own // width
    chunks = n_own + (n_dp - 1) * (more // width)
    return call(
        functools.partial(prep_kernel, n_dp, n_own),
        "prep",
        [
            pltpu.HBM((bot, cols), jnp.float32),
            held(own, DEPTH, dtype=jnp.bfloat16),
            held(own, DEPTH, dtype=jnp.bfloat16),
            held(bot, own),
            held(1, own),
            held(1, 128),
        ],
        (teacher_weight, student_weight, center),
        in_specs=[IN_HBM] * 3,
        out_specs=[IN_HBM] + [ON_CHIP] * 5,
        scratch_shapes=[held(chunks, bot, width)] * 3
        + [held(1, own)]
        + [pltpu.SemaphoreType.DMA((chunks,))] * 3
        + [pltpu.SemaphoreType.DMA],
    )


def rest_kernel(lo, hi, own, teacher_hbm, student_hbm, after, before_hbm, new_hbm, done_ref, *scratch):
    teacher_buf, student_buf, new_buf, in_t, in_s, out = scratch
    width = hi - lo
    parts = teacher_hbm.shape[1] // own - 1
    dp = here()[0]
    done_ref[...] = jnp.zeros_like(done_ref)
    far = [pl.ds(pl.multiple_of(lax.rem(dp + 1 + i, parts + 1) * own + lo, 128), width) for i in range(parts)]
    loads = [
        (
            pltpu.make_async_copy(teacher_hbm.at[:, far[i]], teacher_buf.at[i], in_t.at[i]),
            pltpu.make_async_copy(student_hbm.at[:, far[i]], student_buf.at[i], in_s.at[i]),
        )
        for i in range(parts)
    ]
    stores = [pltpu.make_async_copy(new_buf.at[i], new_hbm.at[:, far[i]], out.at[i]) for i in range(parts)]
    for pair in loads:
        for load in pair:
            load.start()
    for i in range(parts):
        for load in loads[i]:
            load.wait()
        new_buf[i] = 0.994 * teacher_buf[i] + 0.006 * student_buf[i]
        stores[i].start()
    for store in stores:
        store.wait()


def update_rest(teacher_weight, student_weight, after, new, own, lo, hi):
    bot, cols = teacher_weight.shape
    parts = cols // own - 1
    return call(
        functools.partial(rest_kernel, lo, hi, own),
        "rest",
        [pltpu.HBM((bot, cols), jnp.float32), held(8, 128)],
        (teacher_weight, student_weight, after, new),
        in_specs=[IN_HBM] * 4,
        out_specs=[IN_HBM, ON_CHIP],
        input_output_aliases={3: 0},
        scratch_shapes=[held(parts, bot, hi - lo)] * 3 + [pltpu.SemaphoreType.DMA((parts,))] * 3,
    )


def fetch_kernel(student_hbm, teacher_hbm, student_ref, teacher_ref, sems):
    half = student_ref.shape[1]
    side = pl.ds(pl.multiple_of(here()[2] * half, half), half)
    loads = [
        pltpu.make_async_copy(student_hbm.at[:, side], student_ref, sems.at[0]),
        pltpu.make_async_copy(teacher_hbm, teacher_ref, sems.at[1]),
    ]
    for load in loads:
        load.start()
    for load in loads:
        load.wait()


def fetch(student, teacher):
    bot, crops = student.shape
    return call(
        fetch_kernel,
        "fetch",
        [held(bot, crops // 2, dtype=jnp.bfloat16), held(bot, crops, dtype=jnp.bfloat16)],
        (student, teacher),
        in_specs=[IN_HBM] * 2,
        scratch_shapes=[pltpu.SemaphoreType.DMA((2,))],
    )


def normalize(values):
    return (values * lax.rsqrt(jnp.sum(values * values, axis=0, keepdims=True) + EPS)).astype(jnp.bfloat16)


def pack_kernel(student_ref, teacher_ref, index_ref, out_ref):
    half = out_ref.shape[2]
    lower = here()[2] == 0
    out_ref[0] = normalize(student_ref[...].astype(jnp.float32))
    index = jnp.where(lower, index_ref[:, :half], index_ref[:, half:])
    row = lax.broadcasted_iota(jnp.int32, (teacher_ref.shape[1], half), 0)
    pick = jnp.where(row == index, 1.0, 0.0).astype(jnp.bfloat16)
    out_ref[1] = normalize(jnp.dot(teacher_ref[...], pick, preferred_element_type=jnp.float32))


def pack(student, teacher, index):
    bot, half = student.shape
    return call(pack_kernel, "pack", held(2, bot, half, dtype=jnp.bfloat16), (student, teacher, index))


def join_kernel(n_in, n_after, firsts, bot, *refs):
    blocks = []
    for ref in refs[:n_in]:
        blocks += [ref] if len(ref.shape) == 3 else [ref.at[i] for i in range(ref.shape[0])]
    for first, ref in zip(firsts, refs[n_in + n_after:]):
        for i in range(ref.shape[0]):
            block = blocks[first + i][:, :bot, :]
            ref[i, :, :bot, :] = block
            if ref.shape[2] > bot:
                ref[i, :, bot:, :] = block[:, :ref.shape[2] - bot]


def join(parts, outs, after, bot):
    width = parts[0].shape[-1]
    shapes = [held(count, 2, rows, width, dtype=jnp.bfloat16) for _, count, rows in outs]
    kernel = functools.partial(join_kernel, len(parts), len(after), [first for first, _, _ in outs], bot)
    return call(kernel, "join", shapes, (*parts, *after), in_specs=[ON_CHIP] * len(parts) + [IN_HBM] * len(after))


def log_sum(parts):
    top = functools.reduce(jnp.maximum, parts)
    return top + jnp.log2(sum(jnp.exp2(part - top) for part in parts))


def combine(parts):
    half = parts[0].shape[0] // 2
    return sum(part[:half] for part in parts), log_sum([part[half:] for part in parts])


def slot(k, n):
    return lax.axis_index("fsdp") ^ k if n <= DIRECT else k


def score_kernel(part, n_feats, *refs):
    last = part == 3
    before, refs = (refs[:3], refs[3:]) if last else ((), refs)
    feats_refs, (ws_ref, wt_ref, peak_ref, *refs) = refs[:n_feats], refs[n_feats:]
    blocks = [ref.at[i] for ref in feats_refs for i in range(ref.shape[0])]
    exp_ref, unit_ref, total_ref, *mine = refs[1:] if part else refs
    own_ref = mine[0] if last else total_ref
    n, (_, bot, width) = len(blocks), blocks[0].shape
    cols = ws_ref.shape[0]
    step = min(STEP, cols)
    per = max(1, min(n, GROUP // width))
    row = lax.broadcasted_iota(jnp.int32, (DEPTH - bot, per * width), 0)
    for which, w_ref, gain in ((0, ws_ref, GAIN_S), (1, wt_ref, GAIN_T)):
        base = (2 * part + which) * n * width
        extra = jnp.where(row < 3 * which, 1.0, 0.0).astype(jnp.bfloat16)
        for group in range(n // per):
            unit = jnp.concatenate([blocks[group * per + k][which] for k in range(per)], axis=1)
            lanes = slice(group * per * width, (group + 1) * per * width)
            if which == 0:
                unit_ref[lanes, :] = unit.T
            stationary = jnp.concatenate([unit, extra], axis=0)
            total = jnp.zeros((8, per * width), jnp.float32)
            for at in range(0, cols, step):
                score = jnp.dot(w_ref[at:at + step, :], stationary, preferred_element_type=jnp.float32)
                exps = jnp.exp2(score * gain)
                total = total + jnp.sum(exps.reshape(step // 8, 8, per * width), axis=0)
                exp_ref[at:at + step, base + lanes.start:base + lanes.stop] = exps.astype(jnp.bfloat16)
            total = jnp.sum(total, axis=0, keepdims=True)
            if which == 1:
                total = jnp.log2(total) + GAIN_T * peak_ref[:, :1]
            own_ref[which:which + 1, lanes] = total
    if not last:
        return
    dp, _, core = here()
    own, pair, other = before
    parts = ((own, other), (pair, own_ref))
    rows = []
    for which in (0, 1):
        for half in (0, 1):
            pieces = []
            for view in (0, 1):
                first = (dp == view) if which == 0 else (dp != view)
                for place in range(n):
                    at = pl.ds(pl.multiple_of(slot(place, n) * width, width), width)
                    read = [[part[which:which + 1, at] for part in side] for side in parts]
                    mine, theirs = [jnp.where(first, *side) for side in read]
                    pieces.append(jnp.where(core == half, mine, theirs))
            rows.append(jnp.concatenate(pieces, axis=1))
    total_ref[...] = jnp.concatenate(rows, axis=0)


def scores(part, feats, weights, before=(), exps=None):
    _, _, bot, width = feats[0].shape
    cols, rows = weights[0].shape[0], sum(part.shape[0] for part in feats) * width
    args = (*before, *feats, *weights, *([exps] if part else []))
    return call(
        functools.partial(score_kernel, part, len(feats)),
        "scores",
        [
            held(cols, 8 * rows, dtype=jnp.bfloat16),
            held(rows, bot, dtype=jnp.bfloat16),
            held(4, 2 * rows) if part == 3 else held(2, rows),
        ],
        args,
        in_specs=[ON_CHIP] * (len(args) - bool(part)) + [IN_HBM] * bool(part),
        input_output_aliases={len(args) - 1: 0} if part else {},
        scratch_shapes=[held(2, rows)] if part == 3 else [],
    )


def relay_kernel(n_in, *refs):
    parts = [ref[...] for ref in refs[:n_in]]
    if len(parts[0].shape) == 3:
        parts = [parts[0][i] for i in range(parts[0].shape[0])]
    refs[-1][...] = jnp.concatenate(combine(parts), axis=0)


def add_up(parts):
    return call(functools.partial(relay_kernel, len(parts)), "relay", held(*parts[0].shape[-2:]), parts)


def aside(p, n_proto):
    return (p ^ 2) if n_proto % 4 == 0 else p ^ 1


def across(total, up, over):
    n_proto, n_dp = lax.axis_size("proto"), lax.axis_size("dp")
    far = lambda p, d: (p ^ up, d ^ over) if p % 2 else (aside(p, n_proto), d)
    places = [(p, d) for p in range(n_proto) for d in range(n_dp)]
    pairs = [(p * n_dp + d, far(p, d)[0] * n_dp + far(p, d)[1]) for p, d in places]
    return lax.ppermute(total, ("proto", "dp"), pairs)


def along_fsdp(total):
    n, n_proto = lax.axis_size("fsdp"), lax.axis_size("proto")
    if n > DIRECT:
        return [lax.all_to_all(jnp.broadcast_to(total[None], (n, *total.shape)), "fsdp", 0, 0, tiled=True)]
    far = lambda i, p, k: (i ^ k) * n_proto + p if p % 2 else i * n_proto + aside(p, n_proto)
    pairs = lambda k: [(i * n_proto + p, far(i, p, k)) for i in range(n) for p in range(n_proto)]
    return [total, *[lax.ppermute(total, ("fsdp", "proto"), pairs(k)) for k in range(1, n)]]


def grad_kernel(led_ref, given_ref, peak_ref, weight_unit, weight_scale, *refs):
    units, exp_ref, out_hbm, scales, feats, *derivs, buf, sems = refs[:4], *refs[4:]
    dp, _, core = here()
    total = jnp.where(core == 1, led_ref[...], given_ref[...])
    scales[0:2, :] = 10.0 / total[0:2]
    scales[2:4, :] = 10.0 * jnp.exp2(GAIN_T * peak_ref[:, :1] - total[2:4])
    rows = units[0].shape[0]
    width = 128
    n = rows // width
    factors = []
    for part in range(4):
        view, half = divmod(part, 2)
        base = (dp ^ view) * rows
        at = [pl.ds(pl.multiple_of(base + slot(k, n) * width, width), width) for k in range(n)]
        for which in (0, 1):
            picked = [
                jnp.where(core == half, scales[2 * which:2 * which + 1, where], scales[2 * which + 1:2 * which + 2, where])
                for where in at
            ]
            factors.append(jnp.concatenate(picked, axis=1).astype(jnp.bfloat16))
    for part, unit in enumerate(units):
        feats[part * rows:(part + 1) * rows, :] = unit[...]
    chunks, _, step = buf.shape
    stores = []

    def derive(i):
        at = slice(i * step, (i + 1) * step)
        for part in range(4):
            lies_s, lies_t = 2 * part * rows, (2 * (part ^ 2) + 1) * rows
            probs_s = exp_ref[at, lies_s:lies_s + rows] * factors[2 * part]
            probs_t = exp_ref[at, lies_t:lies_t + rows] * factors[2 * part + 1]
            derivs[i % 2][:, part * rows:(part + 1) * rows] = probs_s - probs_t

    derive(0)
    for i in range(chunks):
        if i + 1 < chunks:
            derive(i + 1)
        at = slice(i * step, (i + 1) * step)
        grad = jnp.dot(derivs[i % 2][...], feats[...], preferred_element_type=jnp.float32).T
        unit = weight_unit[:, at]
        proj = unit * jnp.sum(unit * grad, axis=0, keepdims=True)
        buf[i] = (grad - proj) * weight_scale[:, at]
        stores.append(pltpu.make_async_copy(buf.at[i], out_hbm.at[:, at], sems.at[i]))
        stores[i].start()
    for store in stores:
        store.wait()


def gradient(led, given, peak, weight_unit, weight_scale, units, exps):
    cols = exps.shape[0]
    rows, bot = units[0].shape
    step = min(256, cols)
    args = (led, given, peak, weight_unit, weight_scale, *units, exps)
    return call(
        grad_kernel,
        "gradient",
        pltpu.HBM((bot, cols), jnp.float32),
        args,
        out_specs=IN_HBM,
        scratch_shapes=[
            held(4, 2 * rows),
            held(4 * rows, bot, dtype=jnp.bfloat16),
            *[held(step, 4 * rows, dtype=jnp.bfloat16)] * 2,
            held(cols // step, bot, step),
            pltpu.SemaphoreType.DMA((cols // step,)),
        ],
    )


def shards(teacher_weight, student_weight, teacher_feats, student_feats, pairing, center):
    n_dp, n_fsdp = lax.axis_size("dp"), lax.axis_size("fsdp")
    in_hbm = lambda array: pltpu.with_memory_space_constraint(array, pltpu.HBM)
    teacher_weight, student_weight, center = in_hbm(teacher_weight), in_hbm(student_weight), in_hbm(center[None, :])

    index = swap(pairing, "dp")
    mine = pack(*fetch(in_hbm(student_feats[0].T), in_hbm(teacher_feats[0].T)), index)
    own_cols = teacher_weight.shape[1] // n_dp
    middle = own_cols // 2
    new, wt, ws, unit, scale, peak = prepare(teacher_weight, student_weight, center, n_dp, own_cols - middle)
    weights = (ws, wt, peak)
    bot = mine.shape[1]
    if n_fsdp <= DIRECT:
        other = [swap(mine, "dp")]
        along = [swap(mine, "fsdp", k) for k in range(1, n_fsdp)]
        half = n_fsdp // 2
        outs = [(0, n_fsdp, bot), (2, n_fsdp - 2, bot + 16), (0, half, bot), (half, half, bot)]
        own, far, *halves = join([mine, *along], outs, (other[0], peak), bot)
        other += [swap(other[0], "fsdp"), swap(far, "dp")]
    else:
        own = lax.all_to_all(jnp.broadcast_to(mine[None], (n_fsdp, *mine.shape)), "fsdp", 0, 0, tiled=True)
        other, halves = [swap(own, "dp")], [own]
    exps, unit_a, total_a = scores(0, [own], weights)
    exps, unit_b, total_b = scores(1, [swap(half, "proto") for half in halves], weights, exps=exps)
    teacher_new, done = update_rest(teacher_weight, student_weight, total_a, new, own_cols, 0, middle)
    (other,) = join(other, [(0, n_fsdp, bot)], (total_b, done), bot)
    exps, unit_c, total_c = scores(2, [other], weights, exps=exps)
    exps, unit_d, total = scores(3, [swap(other, "proto")], weights, (total_a, total_b, total_c), exps)
    total = add_up([total, swap(total, "proto")])
    steps = [(up, over) for up in range(0, lax.axis_size("proto"), 2) for over in range(n_dp)][1:]
    total = add_up([total, *[across(total, *step) for step in steps]])
    total = add_up(along_fsdp(total))
    units = (unit_a, unit_b, unit_c, unit_d)
    student_grad = gradient(total, swap(total, "proto"), peak, unit, scale, units, exps)
    return (teacher_new, student_grad)


def solution(mesh):
    placed = (
        P(None, ("proto", "fsdp")),
        P(None, ("proto", "fsdp")),
        P("dp", "fsdp", None),
        P("dp", "fsdp", None),
        P("dp", "fsdp"),
        P("proto"),
    )
    return jax.shard_map(
        shards,
        mesh=mesh,
        in_specs=placed,
        out_specs=(P(None, ("proto", "fsdp")), P(None, ("proto", "fsdp", "dp"))),
        check_vma=False,
    )
```

```python
import functools
import math

import jax
import jax.numpy as jnp
from jax import lax
from jax.experimental import pallas as pl
from jax.experimental.pallas import tpu as pltpu
from jax.sharding import PartitionSpec as P

EPS = 1e-06
DEPTH = 256
GROUP = 512
STEP = 256
DIRECT = 8
LOG2E = math.log2(math.e)
GAIN_T = LOG2E / 0.04
GAIN_S = LOG2E / 0.1
LIMIT = 24 * 1024 * 1024
ON_CHIP = pl.BlockSpec(memory_space=pltpu.VMEM)
IN_HBM = pl.BlockSpec(memory_space=pl.ANY)


def shape(*dims, dtype=jnp.float32):
    return jax.ShapeDtypeStruct(dims, dtype)


def held(*dims, dtype=jnp.float32):
    return pltpu.VMEM(dims, dtype)


def call(kernel, name, out_shape, args, **more):
    many = isinstance(out_shape, (list, tuple))
    specs = dict(in_specs=[ON_CHIP] * len(args), out_specs=[ON_CHIP] * len(out_shape) if many else ON_CHIP)
    return pl.pallas_call(
        kernel,
        out_shape=out_shape,
        compiler_params=pltpu.CompilerParams(vmem_limit_bytes=LIMIT),
        cost_estimate=pl.CostEstimate(flops=1, bytes_accessed=1, transcendentals=0),
        name=name,
        **{**specs, **more},
    )(*args)


def swap(block, axis, apart=1):
    return lax.ppermute(block, axis, [(i, i ^ apart) for i in range(lax.axis_size(axis))])


def here():
    return lax.axis_index("dp"), lax.axis_index("fsdp"), lax.rem(lax.axis_index("proto"), 2)


def cast_split(row):
    high = row.astype(jnp.bfloat16).astype(jnp.float32)
    mid = (row - high).astype(jnp.bfloat16).astype(jnp.float32)
    return high, mid, row - high - mid


def prep_kernel(n_dp, teacher_hbm, student_hbm, center_hbm, new_hbm, wt_ref, ws_ref, unit_ref, scale_ref, peak_ref, *scratch):
    teacher_buf, student_buf, new_buf, center_buf, in_t, in_s, out, in_c = scratch
    chunks, bot, width = new_buf.shape
    dp, fsdp, _ = here()
    first = dp * (chunks * width)
    at = [slice(i * width, (i + 1) * width) for i in range(chunks)]
    far = [pl.ds(pl.multiple_of(first + i * width, width), width) for i in range(chunks)]
    start = pl.multiple_of((fsdp * n_dp + dp) * (chunks * width), 128)
    center_load = pltpu.make_async_copy(center_hbm.at[:, pl.ds(start, chunks * width)], center_buf, in_c)
    loads = [
        (
            pltpu.make_async_copy(teacher_hbm.at[:, far[i]], teacher_buf.at[i], in_t.at[i]),
            pltpu.make_async_copy(student_hbm.at[:, far[i]], student_buf.at[i], in_s.at[i]),
        )
        for i in range(chunks)
    ]
    stores = [pltpu.make_async_copy(new_buf.at[i], new_hbm.at[:, far[i]], out.at[i]) for i in range(chunks)]
    center_load.start()
    for pair in loads:
        for load in pair:
            load.start()
    center_load.wait()
    center = center_buf[...]
    peak = jnp.max(-center, axis=1, keepdims=True)
    peak_ref[...] = jnp.broadcast_to(peak, peak_ref.shape)
    splits = cast_split(-center - peak)
    row = lax.broadcasted_iota(jnp.int32, (DEPTH - bot, width), 0)
    zero = jnp.zeros((DEPTH - bot, width), jnp.float32)
    for i in range(chunks):
        for load in loads[i]:
            load.wait()
        student = student_buf[i]
        new = 0.994 * teacher_buf[i] + 0.006 * student
        new_buf[i] = new
        stores[i].start()
        high, mid, low = [part[:, at[i]] for part in splits]
        extra = jnp.where(row == 0, high, jnp.where(row == 1, mid, jnp.where(row == 2, low, zero)))
        scale = lax.rsqrt(jnp.sum(student * student, axis=0, keepdims=True) + EPS)
        unit_s = student * scale
        unit_t = new * lax.rsqrt(jnp.sum(new * new, axis=0, keepdims=True) + EPS)
        wt_ref[at[i], :] = jnp.concatenate([unit_t, extra], axis=0).astype(jnp.bfloat16).T
        ws_ref[at[i], :] = jnp.concatenate([unit_s, zero], axis=0).astype(jnp.bfloat16).T
        unit_ref[:, at[i]] = unit_s
        scale_ref[:, at[i]] = scale
    for store in stores:
        store.wait()


def prepare(teacher_weight, student_weight, center, n_dp):
    bot, cols = teacher_weight.shape
    own = cols // n_dp
    width = min(512, own)
    chunks = own // width
    return call(
        functools.partial(prep_kernel, n_dp),
        "prep",
        [
            pltpu.HBM((bot, cols), jnp.float32),
            held(own, DEPTH, dtype=jnp.bfloat16),
            held(own, DEPTH, dtype=jnp.bfloat16),
            held(bot, own),
            held(1, own),
            held(1, 128),
        ],
        (teacher_weight, student_weight, center),
        in_specs=[IN_HBM] * 3,
        out_specs=[IN_HBM] + [ON_CHIP] * 5,
        scratch_shapes=[held(chunks, bot, width)] * 3
        + [held(1, own)]
        + [pltpu.SemaphoreType.DMA((chunks,))] * 3
        + [pltpu.SemaphoreType.DMA],
    )


def rest_kernel(lo, hi, own, teacher_hbm, student_hbm, after, before_hbm, new_hbm, done_ref, *scratch):
    teacher_buf, student_buf, new_buf, in_t, in_s, out = scratch
    width = hi - lo
    parts = teacher_hbm.shape[1] // own - 1
    dp = here()[0]
    done_ref[...] = jnp.zeros_like(done_ref)
    far = [pl.ds(pl.multiple_of(lax.rem(dp + 1 + i, parts + 1) * own + lo, 128), width) for i in range(parts)]
    loads = [
        (
            pltpu.make_async_copy(teacher_hbm.at[:, far[i]], teacher_buf.at[i], in_t.at[i]),
            pltpu.make_async_copy(student_hbm.at[:, far[i]], student_buf.at[i], in_s.at[i]),
        )
        for i in range(parts)
    ]
    stores = [pltpu.make_async_copy(new_buf.at[i], new_hbm.at[:, far[i]], out.at[i]) for i in range(parts)]
    for pair in loads:
        for load in pair:
            load.start()
    for i in range(parts):
        for load in loads[i]:
            load.wait()
        new_buf[i] = 0.994 * teacher_buf[i] + 0.006 * student_buf[i]
        stores[i].start()
    for store in stores:
        store.wait()


def update_rest(teacher_weight, student_weight, after, new, own, lo, hi):
    bot, cols = teacher_weight.shape
    parts = cols // own - 1
    return call(
        functools.partial(rest_kernel, lo, hi, own),
        "rest",
        [pltpu.HBM((bot, cols), jnp.float32), held(8, 128)],
        (teacher_weight, student_weight, after, new),
        in_specs=[IN_HBM] * 4,
        out_specs=[IN_HBM, ON_CHIP],
        input_output_aliases={3: 0},
        scratch_shapes=[held(parts, bot, hi - lo)] * 3 + [pltpu.SemaphoreType.DMA((parts,))] * 3,
    )


def fetch_kernel(student_hbm, teacher_hbm, student_ref, teacher_ref, sems):
    half = student_ref.shape[1]
    side = pl.ds(pl.multiple_of(here()[2] * half, half), half)
    loads = [
        pltpu.make_async_copy(student_hbm.at[:, side], student_ref, sems.at[0]),
        pltpu.make_async_copy(teacher_hbm, teacher_ref, sems.at[1]),
    ]
    for load in loads:
        load.start()
    for load in loads:
        load.wait()


def fetch(student, teacher):
    bot, crops = student.shape
    return call(
        fetch_kernel,
        "fetch",
        [held(bot, crops // 2, dtype=jnp.bfloat16), held(bot, crops, dtype=jnp.bfloat16)],
        (student, teacher),
        in_specs=[IN_HBM] * 2,
        scratch_shapes=[pltpu.SemaphoreType.DMA((2,))],
    )


def normalize(values):
    return (values * lax.rsqrt(jnp.sum(values * values, axis=0, keepdims=True) + EPS)).astype(jnp.bfloat16)


def pack_kernel(student_ref, teacher_ref, index_ref, out_ref):
    half = out_ref.shape[2]
    lower = here()[2] == 0
    out_ref[0] = normalize(student_ref[...].astype(jnp.float32))
    index = jnp.where(lower, index_ref[:, :half], index_ref[:, half:])
    row = lax.broadcasted_iota(jnp.int32, (teacher_ref.shape[1], half), 0)
    pick = jnp.where(row == index, 1.0, 0.0).astype(jnp.bfloat16)
    out_ref[1] = normalize(jnp.dot(teacher_ref[...], pick, preferred_element_type=jnp.float32))


def pack(student, teacher, index):
    bot, half = student.shape
    return call(pack_kernel, "pack", held(2, bot, half, dtype=jnp.bfloat16), (student, teacher, index))


def join_kernel(n_in, n_after, firsts, bot, *refs):
    blocks = []
    for ref in refs[:n_in]:
        blocks += [ref] if len(ref.shape) == 3 else [ref.at[i] for i in range(ref.shape[0])]
    for first, ref in zip(firsts, refs[n_in + n_after:]):
        for i in range(ref.shape[0]):
            block = blocks[first + i][:, :bot, :]
            ref[i, :, :bot, :] = block
            if ref.shape[2] > bot:
                ref[i, :, bot:, :] = block[:, :ref.shape[2] - bot]


def join(parts, outs, after, bot):
    width = parts[0].shape[-1]
    shapes = [held(count, 2, rows, width, dtype=jnp.bfloat16) for _, count, rows in outs]
    kernel = functools.partial(join_kernel, len(parts), len(after), [first for first, _, _ in outs], bot)
    return call(kernel, "join", shapes, (*parts, *after), in_specs=[ON_CHIP] * len(parts) + [IN_HBM] * len(after))


def log_sum(parts):
    top = functools.reduce(jnp.maximum, parts)
    return top + jnp.log2(sum(jnp.exp2(part - top) for part in parts))


def combine(parts):
    half = parts[0].shape[0] // 2
    return sum(part[:half] for part in parts), log_sum([part[half:] for part in parts])


def slot(k, n):
    return lax.axis_index("fsdp") ^ k if n <= DIRECT else k


def score_kernel(part, n_feats, *refs):
    last = part == 3
    before, refs = (refs[:3], refs[3:]) if last else ((), refs)
    feats_refs, (ws_ref, wt_ref, peak_ref, *refs) = refs[:n_feats], refs[n_feats:]
    blocks = [ref.at[i] for ref in feats_refs for i in range(ref.shape[0])]
    exp_ref, unit_ref, total_ref, *mine = refs[2:] if part else refs
    own_ref = mine[0] if last else total_ref
    n, (_, bot, width) = len(blocks), blocks[0].shape
    cols = ws_ref.shape[0]
    step = min(STEP, cols)
    per = max(1, min(n, GROUP // width))
    row = lax.broadcasted_iota(jnp.int32, (DEPTH - bot, per * width), 0)
    for which, w_ref, gain in ((0, ws_ref, GAIN_S), (1, wt_ref, GAIN_T)):
        base = (2 * part + which) * n * width
        extra = jnp.where(row < 3 * which, 1.0, 0.0).astype(jnp.bfloat16)
        for group in range(n // per):
            unit = jnp.concatenate([blocks[group * per + k][which] for k in range(per)], axis=1)
            lanes = slice(group * per * width, (group + 1) * per * width)
            if which == 0:
                unit_ref[part * n * width + lanes.start:part * n * width + lanes.stop, :] = unit.T
            stationary = jnp.concatenate([unit, extra], axis=0)
            total = jnp.zeros((8, per * width), jnp.float32)
            for at in range(0, cols, step):
                score = jnp.dot(w_ref[at:at + step, :], stationary, preferred_element_type=jnp.float32)
                exps = jnp.exp2(score * gain)
                total = total + jnp.sum(exps.reshape(step // 8, 8, per * width), axis=0)
                exp_ref[at:at + step, base + lanes.start:base + lanes.stop] = exps.astype(jnp.bfloat16)
            total = jnp.sum(total, axis=0, keepdims=True)
            if which == 1:
                total = jnp.log2(total) + GAIN_T * peak_ref[:, :1]
            own_ref[which:which + 1, lanes] = total
    if not last:
        return
    dp, _, core = here()
    own, pair, other = before
    parts = ((own, other), (pair, own_ref))
    rows = []
    for which in (0, 1):
        for half in (0, 1):
            pieces = []
            for view in (0, 1):
                first = (dp == view) if which == 0 else (dp != view)
                for place in range(n):
                    at = pl.ds(pl.multiple_of(slot(place, n) * width, width), width)
                    read = [[part[which:which + 1, at] for part in side] for side in parts]
                    mine, theirs = [jnp.where(first, *side) for side in read]
                    pieces.append(jnp.where(core == half, mine, theirs))
            rows.append(jnp.concatenate(pieces, axis=1))
    total_ref[...] = jnp.concatenate(rows, axis=0)


def scores(part, feats, weights, before=(), buffers=()):
    _, _, bot, width = feats[0].shape
    cols, rows = weights[0].shape[0], sum(part.shape[0] for part in feats) * width
    args = (*before, *feats, *weights, *buffers)
    plain = len(args) - len(buffers)
    exps, units, total = call(
        functools.partial(score_kernel, part, len(feats)),
        "scores",
        [
            held(cols, 8 * rows, dtype=jnp.bfloat16),
            held(4 * rows, bot, dtype=jnp.bfloat16),
            held(4, 2 * rows) if part == 3 else held(2, rows),
        ],
        args,
        in_specs=[ON_CHIP] * plain + [IN_HBM] * len(buffers),
        input_output_aliases={plain + i: i for i in range(len(buffers))},
        scratch_shapes=[held(2, rows)] if part == 3 else [],
    )
    return (exps, units), total


def relay_kernel(n_in, *refs):
    parts = [ref[...] for ref in refs[:n_in]]
    if len(parts[0].shape) == 3:
        parts = [parts[0][i] for i in range(parts[0].shape[0])]
    refs[-1][...] = jnp.concatenate(combine(parts), axis=0)


def add_up(parts, *after):
    specs = [ON_CHIP] * len(parts) + [IN_HBM] * len(after)
    out = held(*parts[0].shape[-2:])
    return call(functools.partial(relay_kernel, len(parts)), "relay", out, (*parts, *after), in_specs=specs)


def across(total, up, over):
    n_proto, n_dp = lax.axis_size("proto"), lax.axis_size("dp")
    places = [(p, d) for p in range(n_proto) for d in range(n_dp)]
    pairs = [(p * n_dp + d, (p ^ up) * n_dp + (d ^ over)) for p, d in places]
    return lax.ppermute(total, ("proto", "dp"), pairs)


def along_fsdp(total):
    n = lax.axis_size("fsdp")
    if n <= DIRECT:
        return [total, *[swap(total, "fsdp", k) for k in range(1, n)]]
    return [lax.all_to_all(jnp.broadcast_to(total[None], (n, *total.shape)), "fsdp", 0, 0, tiled=True)]


def grad_kernel(total_ref, peak_ref, weight_unit, weight_scale, unit_ref, exp_ref, out_hbm, scales, *refs):
    *derivs, buf, sems = refs
    dp, _, core = here()
    scales[0:2, :] = 10.0 / total_ref[0:2, :]
    scales[2:4, :] = 10.0 * jnp.exp2(GAIN_T * peak_ref[:, :1] - total_ref[2:4, :])
    rows = unit_ref.shape[0] // 4
    width = 128
    n = rows // width
    factors = []
    for part in range(4):
        view, half = divmod(part, 2)
        base = (dp ^ view) * rows
        at = [pl.ds(pl.multiple_of(base + slot(k, n) * width, width), width) for k in range(n)]
        for which in (0, 1):
            picked = [
                jnp.where(core == half, scales[2 * which:2 * which + 1, where], scales[2 * which + 1:2 * which + 2, where])
                for where in at
            ]
            factors.append(jnp.concatenate(picked, axis=1).astype(jnp.bfloat16))
    chunks, _, step = buf.shape
    stores = []

    def derive(i):
        at = slice(i * step, (i + 1) * step)
        for part in range(4):
            lies_s, lies_t = 2 * part * rows, (2 * (part ^ 2) + 1) * rows
            probs_s = exp_ref[at, lies_s:lies_s + rows] * factors[2 * part]
            probs_t = exp_ref[at, lies_t:lies_t + rows] * factors[2 * part + 1]
            derivs[i % 2][:, part * rows:(part + 1) * rows] = probs_s - probs_t

    derive(0)
    for i in range(chunks):
        if i + 1 < chunks:
            derive(i + 1)
        at = slice(i * step, (i + 1) * step)
        grad = jnp.dot(derivs[i % 2][...], unit_ref[...], preferred_element_type=jnp.float32).T
        unit = weight_unit[:, at]
        proj = unit * jnp.sum(unit * grad, axis=0, keepdims=True)
        buf[i] = (grad - proj) * weight_scale[:, at]
        stores.append(pltpu.make_async_copy(buf.at[i], out_hbm.at[:, at], sems.at[i]))
        stores[i].start()
    for store in stores:
        store.wait()


def gradient(total, peak, weight_unit, weight_scale, units, exps):
    cols = exps.shape[0]
    all_rows, bot = units.shape
    rows = all_rows // 4
    step = min(256, cols)
    args = (total, peak, weight_unit, weight_scale, units, exps)
    return call(
        grad_kernel,
        "gradient",
        pltpu.HBM((bot, cols), jnp.float32),
        args,
        out_specs=IN_HBM,
        scratch_shapes=[
            held(4, 2 * rows),
            *[held(step, 4 * rows, dtype=jnp.bfloat16)] * 2,
            held(cols // step, bot, step),
            pltpu.SemaphoreType.DMA((cols // step,)),
        ],
    )


def shards(teacher_weight, student_weight, teacher_feats, student_feats, pairing, center):
    n_dp, n_fsdp = lax.axis_size("dp"), lax.axis_size("fsdp")
    in_hbm = lambda array: pltpu.with_memory_space_constraint(array, pltpu.HBM)
    teacher_weight, student_weight, center = in_hbm(teacher_weight), in_hbm(student_weight), in_hbm(center[None, :])

    index = swap(pairing, "dp")
    mine = pack(*fetch(in_hbm(student_feats[0].T), in_hbm(teacher_feats[0].T)), index)
    new, wt, ws, unit, scale, peak = prepare(teacher_weight, student_weight, center, n_dp)
    weights = (ws, wt, peak)
    bot = mine.shape[1]
    if n_fsdp <= DIRECT:
        other = [swap(mine, "dp")]
        along = [swap(mine, "fsdp", k) for k in range(1, n_fsdp)]
        half = n_fsdp // 2
        outs = [(0, n_fsdp, bot), (1, n_fsdp - 1, bot), (0, half, bot), (half, n_fsdp - half, bot)]
        own, far, *halves = join([mine, *along], outs, (other[0], peak), bot)
        other.append(swap(far, "dp"))
    else:
        own = lax.all_to_all(jnp.broadcast_to(mine[None], (n_fsdp, *mine.shape)), "fsdp", 0, 0, tiled=True)
        other, halves = [swap(own, "dp")], [own]
    buffers, total_a = scores(0, [own], weights)
    buffers, total_b = scores(1, [swap(half, "proto") for half in halves], weights, (), buffers)
    (other,) = join(other, [(0, n_fsdp, bot)], (total_b,), bot)
    buffers, total_c = scores(2, [other], weights, (), buffers)
    (exps, units), total = scores(3, [swap(other, "proto")], weights, (total_a, total_b, total_c), buffers)
    n_proto, own_cols = lax.axis_size("proto"), ws.shape[0]
    middle = own_cols // 2
    total = add_up([total, swap(total, "proto")])
    new, done = update_rest(teacher_weight, student_weight, total, new, own_cols, 0, middle)
    steps = [(up, over) for up in range(0, n_proto, 2) for over in range(n_dp)][1:]
    total = add_up([total, *[across(total, *step) for step in steps]], done)
    teacher_new, done = update_rest(teacher_weight, student_weight, total, new, own_cols, middle, own_cols)
    total = add_up(along_fsdp(total), done)
    student_grad = gradient(total, peak, unit, scale, units, exps)
    return (teacher_new, student_grad)


def solution(mesh):
    placed = (
        P(None, ("proto", "fsdp")),
        P(None, ("proto", "fsdp")),
        P("dp", "fsdp", None),
        P("dp", "fsdp", None),
        P("dp", "fsdp"),
        P("proto"),
    )
    return jax.shard_map(
        shards,
        mesh=mesh,
        in_specs=placed,
        out_specs=(P(None, ("proto", "fsdp")), P(None, ("proto", "fsdp", "dp"))),
        check_vma=False,
    )
```

```python
import functools
import math

import jax
import jax.numpy as jnp
from jax import lax
from jax.experimental import pallas as pl
from jax.experimental.pallas import tpu as pltpu
from jax.sharding import PartitionSpec as P

EPS = 1e-06
DEPTH = 256
GROUP = 512
STEP = 256
DIRECT = 8
LOG2E = math.log2(math.e)
GAIN_T = LOG2E / 0.04
GAIN_S = LOG2E / 0.1
LIMIT = 24 * 1024 * 1024
ON_CHIP = pl.BlockSpec(memory_space=pltpu.VMEM)
IN_HBM = pl.BlockSpec(memory_space=pl.ANY)


def shape(*dims, dtype=jnp.float32):
    return jax.ShapeDtypeStruct(dims, dtype)


def held(*dims, dtype=jnp.float32):
    return pltpu.VMEM(dims, dtype)


def call(kernel, name, out_shape, args, **more):
    many = isinstance(out_shape, (list, tuple))
    specs = dict(in_specs=[ON_CHIP] * len(args), out_specs=[ON_CHIP] * len(out_shape) if many else ON_CHIP)
    return pl.pallas_call(
        kernel,
        out_shape=out_shape,
        compiler_params=pltpu.CompilerParams(vmem_limit_bytes=LIMIT),
        cost_estimate=pl.CostEstimate(flops=1, bytes_accessed=1, transcendentals=0),
        name=name,
        **{**specs, **more},
    )(*args)


def swap(block, axis, apart=1):
    return lax.ppermute(block, axis, [(i, i ^ apart) for i in range(lax.axis_size(axis))])


def here():
    return lax.axis_index("dp"), lax.axis_index("fsdp"), lax.rem(lax.axis_index("proto"), 2)


def cast_split(row):
    high = row.astype(jnp.bfloat16).astype(jnp.float32)
    mid = (row - high).astype(jnp.bfloat16).astype(jnp.float32)
    return high, mid, row - high - mid


def prep_kernel(n_dp, n_own, teacher_hbm, student_hbm, center_hbm, new_hbm, wt_ref, ws_ref, unit_ref, scale_ref, peak_ref, *scratch):
    teacher_buf, student_buf, new_buf, center_buf, in_t, in_s, out, in_c = scratch
    chunks, bot, width = new_buf.shape
    dp, fsdp, _ = here()
    own = n_own * width
    at = [slice(i * width, (i + 1) * width) for i in range(n_own)]
    firsts = [dp * own + i * width for i in range(n_own)]
    more = (chunks - n_own) // (n_dp - 1) if n_dp > 1 else 0
    firsts += [lax.rem(dp + 1 + i // more, n_dp) * own + (n_own - more + i % more) * width for i in range(chunks - n_own)]
    far = [pl.ds(pl.multiple_of(first, width), width) for first in firsts]
    start = pl.multiple_of((fsdp * n_dp + dp) * own, 128)
    center_load = pltpu.make_async_copy(center_hbm.at[:, pl.ds(start, own)], center_buf, in_c)
    loads = [
        (
            pltpu.make_async_copy(teacher_hbm.at[:, far[i]], teacher_buf.at[i], in_t.at[i]),
            pltpu.make_async_copy(student_hbm.at[:, far[i]], student_buf.at[i], in_s.at[i]),
        )
        for i in range(chunks)
    ]
    stores = [pltpu.make_async_copy(new_buf.at[i], new_hbm.at[:, far[i]], out.at[i]) for i in range(chunks)]
    center_load.start()
    for pair in loads:
        for load in pair:
            load.start()
    center_load.wait()
    center = center_buf[...]
    peak = jnp.max(-center, axis=1, keepdims=True)
    peak_ref[...] = jnp.broadcast_to(peak, peak_ref.shape)
    splits = cast_split(-center - peak)
    row = lax.broadcasted_iota(jnp.int32, (DEPTH - bot, width), 0)
    zero = jnp.zeros((DEPTH - bot, width), jnp.float32)
    for i in range(chunks):
        for load in loads[i]:
            load.wait()
        student = student_buf[i]
        new = 0.994 * teacher_buf[i] + 0.006 * student
        new_buf[i] = new
        stores[i].start()
        if i >= n_own:
            continue
        high, mid, low = [part[:, at[i]] for part in splits]
        extra = jnp.where(row == 0, high, jnp.where(row == 1, mid, jnp.where(row == 2, low, zero)))
        scale = lax.rsqrt(jnp.sum(student * student, axis=0, keepdims=True) + EPS)
        unit_s = student * scale
        unit_t = new * lax.rsqrt(jnp.sum(new * new, axis=0, keepdims=True) + EPS)
        wt_ref[at[i], :] = jnp.concatenate([unit_t, extra], axis=0).astype(jnp.bfloat16).T
        ws_ref[at[i], :] = jnp.concatenate([unit_s, zero], axis=0).astype(jnp.bfloat16).T
        unit_ref[:, at[i]] = unit_s
        scale_ref[:, at[i]] = scale
    for store in stores:
        store.wait()


def prepare(teacher_weight, student_weight, center, n_dp, more):
    bot, cols = teacher_weight.shape
    own = cols // n_dp
    width = math.gcd(min(512, own), more)
    n_own = own // width
    chunks = n_own + (n_dp - 1) * (more // width)
    return call(
        functools.partial(prep_kernel, n_dp, n_own),
        "prep",
        [
            pltpu.HBM((bot, cols), jnp.float32),
            held(own, DEPTH, dtype=jnp.bfloat16),
            held(own, DEPTH, dtype=jnp.bfloat16),
            held(bot, own),
            held(1, own),
            held(1, 128),
        ],
        (teacher_weight, student_weight, center),
        in_specs=[IN_HBM] * 3,
        out_specs=[IN_HBM] + [ON_CHIP] * 5,
        scratch_shapes=[held(chunks, bot, width)] * 3
        + [held(1, own)]
        + [pltpu.SemaphoreType.DMA((chunks,))] * 3
        + [pltpu.SemaphoreType.DMA],
    )


def rest_kernel(lo, hi, own, teacher_hbm, student_hbm, after, before_hbm, new_hbm, done_ref, *scratch):
    teacher_buf, student_buf, new_buf, in_t, in_s, out = scratch
    width = hi - lo
    parts = teacher_hbm.shape[1] // own - 1
    dp = here()[0]
    done_ref[...] = jnp.zeros_like(done_ref)
    far = [pl.ds(pl.multiple_of(lax.rem(dp + 1 + i, parts + 1) * own + lo, 128), width) for i in range(parts)]
    loads = [
        (
            pltpu.make_async_copy(teacher_hbm.at[:, far[i]], teacher_buf.at[i], in_t.at[i]),
            pltpu.make_async_copy(student_hbm.at[:, far[i]], student_buf.at[i], in_s.at[i]),
        )
        for i in range(parts)
    ]
    stores = [pltpu.make_async_copy(new_buf.at[i], new_hbm.at[:, far[i]], out.at[i]) for i in range(parts)]
    for pair in loads:
        for load in pair:
            load.start()
    for i in range(parts):
        for load in loads[i]:
            load.wait()
        new_buf[i] = 0.994 * teacher_buf[i] + 0.006 * student_buf[i]
        stores[i].start()
    for store in stores:
        store.wait()


def update_rest(teacher_weight, student_weight, after, new, own, lo, hi):
    bot, cols = teacher_weight.shape
    parts = cols // own - 1
    return call(
        functools.partial(rest_kernel, lo, hi, own),
        "rest",
        [pltpu.HBM((bot, cols), jnp.float32), held(8, 128)],
        (teacher_weight, student_weight, after, new),
        in_specs=[IN_HBM] * 4,
        out_specs=[IN_HBM, ON_CHIP],
        input_output_aliases={3: 0},
        scratch_shapes=[held(parts, bot, hi - lo)] * 3 + [pltpu.SemaphoreType.DMA((parts,))] * 3,
    )


def fetch_kernel(student_hbm, teacher_hbm, student_ref, teacher_ref, sems):
    half = student_ref.shape[1]
    side = pl.ds(pl.multiple_of(here()[2] * half, half), half)
    loads = [
        pltpu.make_async_copy(student_hbm.at[:, side], student_ref, sems.at[0]),
        pltpu.make_async_copy(teacher_hbm, teacher_ref, sems.at[1]),
    ]
    for load in loads:
        load.start()
    for load in loads:
        load.wait()


def fetch(student, teacher):
    bot, crops = student.shape
    return call(
        fetch_kernel,
        "fetch",
        [held(bot, crops // 2, dtype=jnp.bfloat16), held(bot, crops, dtype=jnp.bfloat16)],
        (student, teacher),
        in_specs=[IN_HBM] * 2,
        scratch_shapes=[pltpu.SemaphoreType.DMA((2,))],
    )


def normalize(values):
    return (values * lax.rsqrt(jnp.sum(values * values, axis=0, keepdims=True) + EPS)).astype(jnp.bfloat16)


def pack_kernel(student_ref, teacher_ref, index_ref, out_ref):
    half = out_ref.shape[2]
    lower = here()[2] == 0
    out_ref[0] = normalize(student_ref[...].astype(jnp.float32))
    index = jnp.where(lower, index_ref[:, :half], index_ref[:, half:])
    row = lax.broadcasted_iota(jnp.int32, (teacher_ref.shape[1], half), 0)
    pick = jnp.where(row == index, 1.0, 0.0).astype(jnp.bfloat16)
    out_ref[1] = normalize(jnp.dot(teacher_ref[...], pick, preferred_element_type=jnp.float32))


def pack(student, teacher, index):
    bot, half = student.shape
    return call(pack_kernel, "pack", held(2, bot, half, dtype=jnp.bfloat16), (student, teacher, index))


def join_kernel(n_in, n_after, firsts, bot, *refs):
    blocks = []
    for ref in refs[:n_in]:
        blocks += [ref] if len(ref.shape) == 3 else [ref.at[i] for i in range(ref.shape[0])]
    for first, ref in zip(firsts, refs[n_in + n_after:]):
        for i in range(ref.shape[0]):
            block = blocks[first + i][:, :bot, :]
            ref[i, :, :bot, :] = block
            if ref.shape[2] > bot:
                ref[i, :, bot:, :] = block[:, :ref.shape[2] - bot]


def join(parts, outs, after, bot):
    width = parts[0].shape[-1]
    shapes = [held(count, 2, rows, width, dtype=jnp.bfloat16) for _, count, rows in outs]
    kernel = functools.partial(join_kernel, len(parts), len(after), [first for first, _, _ in outs], bot)
    return call(kernel, "join", shapes, (*parts, *after), in_specs=[ON_CHIP] * len(parts) + [IN_HBM] * len(after))


def log_sum(parts):
    top = functools.reduce(jnp.maximum, parts)
    return top + jnp.log2(sum(jnp.exp2(part - top) for part in parts))


def combine(parts):
    half = parts[0].shape[0] // 2
    return sum(part[:half] for part in parts), log_sum([part[half:] for part in parts])


def slot(k, n):
    return lax.axis_index("fsdp") ^ k if n <= DIRECT else k


def score_kernel(part, n_feats, *refs):
    last = part == 3
    before, refs = (refs[:3], refs[3:]) if last else ((), refs)
    feats_refs, (ws_ref, wt_ref, peak_ref, *refs) = refs[:n_feats], refs[n_feats:]
    blocks = [ref.at[i] for ref in feats_refs for i in range(ref.shape[0])]
    exp_ref, unit_ref, total_ref, *mine = refs[1:] if part else refs
    own_ref = mine[0] if last else total_ref
    n, (_, bot, width) = len(blocks), blocks[0].shape
    cols = ws_ref.shape[0]
    step = min(STEP, cols)
    per = max(1, min(n, GROUP // width))
    row = lax.broadcasted_iota(jnp.int32, (DEPTH - bot, per * width), 0)
    for which, w_ref, gain in ((0, ws_ref, GAIN_S), (1, wt_ref, GAIN_T)):
        base = (2 * part + which) * n * width
        extra = jnp.where(row < 3 * which, 1.0, 0.0).astype(jnp.bfloat16)
        for group in range(n // per):
            unit = jnp.concatenate([blocks[group * per + k][which] for k in range(per)], axis=1)
            lanes = slice(group * per * width, (group + 1) * per * width)
            if which == 0:
                unit_ref[lanes, :] = unit.T
            stationary = jnp.concatenate([unit, extra], axis=0)
            total = jnp.zeros((8, per * width), jnp.float32)
            for at in range(0, cols, step):
                score = jnp.dot(w_ref[at:at + step, :], stationary, preferred_element_type=jnp.float32)
                exps = jnp.exp2(score * gain)
                total = total + jnp.sum(exps.reshape(step // 8, 8, per * width), axis=0)
                exp_ref[at:at + step, base + lanes.start:base + lanes.stop] = exps.astype(jnp.bfloat16)
            total = jnp.sum(total, axis=0, keepdims=True)
            if which == 1:
                total = jnp.log2(total) + GAIN_T * peak_ref[:, :1]
            own_ref[which:which + 1, lanes] = total
    if not last:
        return
    dp, _, core = here()
    own, pair, other = before
    parts = ((own, other), (pair, own_ref))
    rows = []
    for which in (0, 1):
        for half in (0, 1):
            pieces = []
            for view in (0, 1):
                first = (dp == view) if which == 0 else (dp != view)
                for place in range(n):
                    at = pl.ds(pl.multiple_of(slot(place, n) * width, width), width)
                    read = [[part[which:which + 1, at] for part in side] for side in parts]
                    mine, theirs = [jnp.where(first, *side) for side in read]
                    pieces.append(jnp.where(core == half, mine, theirs))
            rows.append(jnp.concatenate(pieces, axis=1))
    total_ref[...] = jnp.concatenate(rows, axis=0)


def scores(part, feats, weights, before=(), exps=None):
    _, _, bot, width = feats[0].shape
    cols, rows = weights[0].shape[0], sum(part.shape[0] for part in feats) * width
    args = (*before, *feats, *weights, *([exps] if part else []))
    return call(
        functools.partial(score_kernel, part, len(feats)),
        "scores",
        [
            held(cols, 8 * rows, dtype=jnp.bfloat16),
            held(rows, bot, dtype=jnp.bfloat16),
            held(4, 2 * rows) if part == 3 else held(2, rows),
        ],
        args,
        in_specs=[ON_CHIP] * (len(args) - bool(part)) + [IN_HBM] * bool(part),
        input_output_aliases={len(args) - 1: 0} if part else {},
        scratch_shapes=[held(2, rows)] if part == 3 else [],
    )


def relay_kernel(n_in, *refs):
    parts = [ref[...] for ref in refs[:n_in]]
    if len(parts[0].shape) == 3:
        parts = [parts[0][i] for i in range(parts[0].shape[0])]
    refs[-1][...] = jnp.concatenate(combine(parts), axis=0)


def add_up(parts):
    return call(functools.partial(relay_kernel, len(parts)), "relay", held(*parts[0].shape[-2:]), parts)


def exchange(total, axes, first, second):
    sizes = [lax.axis_size(axis) for axis in axes]
    proto = axes.index("proto")
    places = [(i, j) for i in range(sizes[0]) for j in range(sizes[1])]

    def permute(step):
        flat = lambda place: place[0] * sizes[1] + place[1]
        pairs = []
        for place in places:
            up = step(place[proto] % 2)
            pairs.append((flat(place), flat((place[0] ^ up[0], place[1] ^ up[1]))))
        return lax.ppermute(total, axes, pairs)

    mine = permute(first)
    return add_up([total, mine, swap(mine, "proto"), permute(second)])


def across(total, up, over):
    n_proto, n_dp = lax.axis_size("proto"), lax.axis_size("dp")
    places = [(p, d) for p in range(n_proto) for d in range(n_dp)]
    pairs = [(p * n_dp + d, (p ^ up) * n_dp + (d ^ over)) for p, d in places]
    return lax.ppermute(total, ("proto", "dp"), pairs)


def add_up_all(total):
    n_proto, n_dp, n_fsdp = [lax.axis_size(axis) for axis in ("proto", "dp", "fsdp")]
    total = add_up([total, swap(total, "proto")])
    if n_proto == 4 and n_dp == 2:
        total = exchange(total, ("proto", "dp"), lambda odd: (2 * odd, 1), lambda odd: (2, 0))
    else:
        steps = [(up, over) for up in range(0, n_proto, 2) for over in range(n_dp)][1:]
        total = add_up([total, *[across(total, *step) for step in steps]])
    if n_fsdp == 4:
        return exchange(total, ("fsdp", "proto"), lambda odd: (1 + 2 * odd, 0), lambda odd: (2, 0))
    if n_fsdp <= DIRECT:
        return add_up([total, *[swap(total, "fsdp", k) for k in range(1, n_fsdp)]])
    return add_up([lax.all_to_all(jnp.broadcast_to(total[None], (n_fsdp, *total.shape)), "fsdp", 0, 0, tiled=True)])


def grad_kernel(total_ref, peak_ref, weight_unit, weight_scale, *refs):
    units, exp_ref, out_hbm, scales, feats, *derivs, buf, sems = refs[:4], *refs[4:]
    dp, _, core = here()
    scales[0:2, :] = 10.0 / total_ref[0:2, :]
    scales[2:4, :] = 10.0 * jnp.exp2(GAIN_T * peak_ref[:, :1] - total_ref[2:4, :])
    rows = units[0].shape[0]
    width = 128
    n = rows // width
    factors = []
    for part in range(4):
        view, half = divmod(part, 2)
        base = (dp ^ view) * rows
        at = [pl.ds(pl.multiple_of(base + slot(k, n) * width, width), width) for k in range(n)]
        for which in (0, 1):
            picked = [
                jnp.where(core == half, scales[2 * which:2 * which + 1, where], scales[2 * which + 1:2 * which + 2, where])
                for where in at
            ]
            factors.append(jnp.concatenate(picked, axis=1).astype(jnp.bfloat16))
    for part, unit in enumerate(units):
        feats[part * rows:(part + 1) * rows, :] = unit[...]
    chunks, _, step = buf.shape
    stores = []

    def derive(i):
        at = slice(i * step, (i + 1) * step)
        for part in range(4):
            lies_s, lies_t = 2 * part * rows, (2 * (part ^ 2) + 1) * rows
            probs_s = exp_ref[at, lies_s:lies_s + rows] * factors[2 * part]
            probs_t = exp_ref[at, lies_t:lies_t + rows] * factors[2 * part + 1]
            derivs[i % 2][:, part * rows:(part + 1) * rows] = probs_s - probs_t

    derive(0)
    for i in range(chunks):
        if i + 1 < chunks:
            derive(i + 1)
        at = slice(i * step, (i + 1) * step)
        grad = jnp.dot(derivs[i % 2][...], feats[...], preferred_element_type=jnp.float32).T
        unit = weight_unit[:, at]
        proj = unit * jnp.sum(unit * grad, axis=0, keepdims=True)
        buf[i] = (grad - proj) * weight_scale[:, at]
        stores.append(pltpu.make_async_copy(buf.at[i], out_hbm.at[:, at], sems.at[i]))
        stores[i].start()
    for store in stores:
        store.wait()


def gradient(total, peak, weight_unit, weight_scale, units, exps):
    cols = exps.shape[0]
    rows, bot = units[0].shape
    step = min(256, cols)
    args = (total, peak, weight_unit, weight_scale, *units, exps)
    return call(
        grad_kernel,
        "gradient",
        pltpu.HBM((bot, cols), jnp.float32),
        args,
        out_specs=IN_HBM,
        scratch_shapes=[
            held(4, 2 * rows),
            held(4 * rows, bot, dtype=jnp.bfloat16),
            *[held(step, 4 * rows, dtype=jnp.bfloat16)] * 2,
            held(cols // step, bot, step),
            pltpu.SemaphoreType.DMA((cols // step,)),
        ],
    )


def shards(teacher_weight, student_weight, teacher_feats, student_feats, pairing, center):
    n_dp, n_fsdp = lax.axis_size("dp"), lax.axis_size("fsdp")
    in_hbm = lambda array: pltpu.with_memory_space_constraint(array, pltpu.HBM)
    teacher_weight, student_weight, center = in_hbm(teacher_weight), in_hbm(student_weight), in_hbm(center[None, :])

    index = swap(pairing, "dp")
    mine = pack(*fetch(in_hbm(student_feats[0].T), in_hbm(teacher_feats[0].T)), index)
    own_cols = teacher_weight.shape[1] // n_dp
    middle = own_cols // 2
    new, wt, ws, unit, scale, peak = prepare(teacher_weight, student_weight, center, n_dp, own_cols - middle)
    weights = (ws, wt, peak)
    bot = mine.shape[1]
    if n_fsdp <= DIRECT:
        other = [swap(mine, "dp")]
        along = [swap(mine, "fsdp", k) for k in range(1, n_fsdp)]
        half = n_fsdp // 2
        outs = [(0, n_fsdp, bot), (2, n_fsdp - 2, bot + 16), (0, half, bot), (half, half, bot)]
        own, far, *halves = join([mine, *along], outs, (other[0], peak), bot)
        other += [swap(other[0], "fsdp"), swap(far, "dp")]
    else:
        own = lax.all_to_all(jnp.broadcast_to(mine[None], (n_fsdp, *mine.shape)), "fsdp", 0, 0, tiled=True)
        other, halves = [swap(own, "dp")], [own]
    exps, unit_a, total_a = scores(0, [own], weights)
    exps, unit_b, total_b = scores(1, [swap(half, "proto") for half in halves], weights, exps=exps)
    teacher_new, done = update_rest(teacher_weight, student_weight, total_a, new, own_cols, 0, middle)
    (other,) = join(other, [(0, n_fsdp, bot)], (total_b, done), bot)
    exps, unit_c, total_c = scores(2, [other], weights, exps=exps)
    exps, unit_d, total = scores(3, [swap(other, "proto")], weights, (total_a, total_b, total_c), exps)
    total = add_up_all(total)
    units = (unit_a, unit_b, unit_c, unit_d)
    student_grad = gradient(total, peak, unit, scale, units, exps)
    return (teacher_new, student_grad)


def solution(mesh):
    placed = (
        P(None, ("proto", "fsdp")),
        P(None, ("proto", "fsdp")),
        P("dp", "fsdp", None),
        P("dp", "fsdp", None),
        P("dp", "fsdp"),
        P("proto"),
    )
    return jax.shard_map(
        shards,
        mesh=mesh,
        in_specs=placed,
        out_specs=(P(None, ("proto", "fsdp")), P(None, ("proto", "fsdp", "dp"))),
        check_vma=False,
    )
```

```python
import functools
import math

import jax
import jax.numpy as jnp
from jax import lax
from jax.experimental import pallas as pl
from jax.experimental.pallas import tpu as pltpu
from jax.sharding import PartitionSpec as P

EPS = 1e-06
DEPTH = 256
GROUP = 512
STEP = 256
DIRECT = 8
LOG2E = math.log2(math.e)
GAIN_T = LOG2E / 0.04
GAIN_S = LOG2E / 0.1
LIMIT = 24 * 1024 * 1024
ON_CHIP = pl.BlockSpec(memory_space=pltpu.VMEM)
IN_HBM = pl.BlockSpec(memory_space=pl.ANY)


def shape(*dims, dtype=jnp.float32):
    return jax.ShapeDtypeStruct(dims, dtype)


def held(*dims, dtype=jnp.float32):
    return pltpu.VMEM(dims, dtype)


def call(kernel, name, out_shape, args, **more):
    many = isinstance(out_shape, (list, tuple))
    specs = dict(in_specs=[ON_CHIP] * len(args), out_specs=[ON_CHIP] * len(out_shape) if many else ON_CHIP)
    return pl.pallas_call(
        kernel,
        out_shape=out_shape,
        compiler_params=pltpu.CompilerParams(vmem_limit_bytes=LIMIT),
        cost_estimate=pl.CostEstimate(flops=1, bytes_accessed=1, transcendentals=0),
        name=name,
        **{**specs, **more},
    )(*args)


def swap(block, axis, apart=1):
    return lax.ppermute(block, axis, [(i, i ^ apart) for i in range(lax.axis_size(axis))])


def here():
    return lax.axis_index("dp"), lax.axis_index("fsdp"), lax.rem(lax.axis_index("proto"), 2)


def cast_split(row):
    high = row.astype(jnp.bfloat16).astype(jnp.float32)
    mid = (row - high).astype(jnp.bfloat16).astype(jnp.float32)
    return high, mid, row - high - mid


def prep_kernel(n_dp, n_own, teacher_hbm, student_hbm, center_hbm, new_hbm, wt_ref, ws_ref, unit_ref, scale_ref, peak_ref, *scratch):
    teacher_buf, student_buf, new_buf, center_buf, in_t, in_s, out, in_c = scratch
    chunks, bot, width = new_buf.shape
    dp, fsdp, _ = here()
    own = n_own * width
    at = [slice(i * width, (i + 1) * width) for i in range(n_own)]
    firsts = [dp * own + i * width for i in range(n_own)]
    more = (chunks - n_own) // (n_dp - 1) if n_dp > 1 else 0
    firsts += [lax.rem(dp + 1 + i // more, n_dp) * own + (n_own - more + i % more) * width for i in range(chunks - n_own)]
    far = [pl.ds(pl.multiple_of(first, width), width) for first in firsts]
    start = pl.multiple_of((fsdp * n_dp + dp) * own, 128)
    center_load = pltpu.make_async_copy(center_hbm.at[:, pl.ds(start, own)], center_buf, in_c)
    loads = [
        (
            pltpu.make_async_copy(teacher_hbm.at[:, far[i]], teacher_buf.at[i], in_t.at[i]),
            pltpu.make_async_copy(student_hbm.at[:, far[i]], student_buf.at[i], in_s.at[i]),
        )
        for i in range(chunks)
    ]
    stores = [pltpu.make_async_copy(new_buf.at[i], new_hbm.at[:, far[i]], out.at[i]) for i in range(chunks)]
    center_load.start()
    for pair in loads:
        for load in pair:
            load.start()
    center_load.wait()
    center = center_buf[...]
    peak = jnp.max(-center, axis=1, keepdims=True)
    peak_ref[...] = jnp.broadcast_to(peak, peak_ref.shape)
    splits = cast_split(-center - peak)
    row = lax.broadcasted_iota(jnp.int32, (DEPTH - bot, width), 0)
    zero = jnp.zeros((DEPTH - bot, width), jnp.float32)
    for i in range(chunks):
        for load in loads[i]:
            load.wait()
        student = student_buf[i]
        new = 0.994 * teacher_buf[i] + 0.006 * student
        new_buf[i] = new
        stores[i].start()
        if i >= n_own:
            continue
        high, mid, low = [part[:, at[i]] for part in splits]
        extra = jnp.where(row == 0, high, jnp.where(row == 1, mid, jnp.where(row == 2, low, zero)))
        scale = lax.rsqrt(jnp.sum(student * student, axis=0, keepdims=True) + EPS)
        unit_s = student * scale
        unit_t = new * lax.rsqrt(jnp.sum(new * new, axis=0, keepdims=True) + EPS)
        wt_ref[at[i], :] = jnp.concatenate([unit_t, extra], axis=0).astype(jnp.bfloat16).T
        ws_ref[at[i], :] = jnp.concatenate([unit_s, zero], axis=0).astype(jnp.bfloat16).T
        unit_ref[:, at[i]] = unit_s
        scale_ref[:, at[i]] = scale
    for store in stores:
        store.wait()


def prepare(teacher_weight, student_weight, center, n_dp, more):
    bot, cols = teacher_weight.shape
    own = cols // n_dp
    width = math.gcd(min(512, own), more)
    n_own = own // width
    chunks = n_own + (n_dp - 1) * (more // width)
    return call(
        functools.partial(prep_kernel, n_dp, n_own),
        "prep",
        [
            pltpu.HBM((bot, cols), jnp.float32),
            held(own, DEPTH, dtype=jnp.bfloat16),
            held(own, DEPTH, dtype=jnp.bfloat16),
            held(bot, own),
            held(1, own),
            held(1, 128),
        ],
        (teacher_weight, student_weight, center),
        in_specs=[IN_HBM] * 3,
        out_specs=[IN_HBM] + [ON_CHIP] * 5,
        scratch_shapes=[held(chunks, bot, width)] * 3
        + [held(1, own)]
        + [pltpu.SemaphoreType.DMA((chunks,))] * 3
        + [pltpu.SemaphoreType.DMA],
    )


def rest_kernel(lo, hi, own, teacher_hbm, student_hbm, after, before_hbm, new_hbm, done_ref, *scratch):
    teacher_buf, student_buf, new_buf, in_t, in_s, out = scratch
    width = hi - lo
    parts = teacher_hbm.shape[1] // own - 1
    dp = here()[0]
    done_ref[...] = jnp.zeros_like(done_ref)
    far = [pl.ds(pl.multiple_of(lax.rem(dp + 1 + i, parts + 1) * own + lo, 128), width) for i in range(parts)]
    loads = [
        (
            pltpu.make_async_copy(teacher_hbm.at[:, far[i]], teacher_buf.at[i], in_t.at[i]),
            pltpu.make_async_copy(student_hbm.at[:, far[i]], student_buf.at[i], in_s.at[i]),
        )
        for i in range(parts)
    ]
    stores = [pltpu.make_async_copy(new_buf.at[i], new_hbm.at[:, far[i]], out.at[i]) for i in range(parts)]
    for pair in loads:
        for load in pair:
            load.start()
    for i in range(parts):
        for load in loads[i]:
            load.wait()
        new_buf[i] = 0.994 * teacher_buf[i] + 0.006 * student_buf[i]
        stores[i].start()
    for store in stores:
        store.wait()


def update_rest(teacher_weight, student_weight, after, new, own, lo, hi):
    bot, cols = teacher_weight.shape
    parts = cols // own - 1
    return call(
        functools.partial(rest_kernel, lo, hi, own),
        "rest",
        [pltpu.HBM((bot, cols), jnp.float32), held(8, 128)],
        (teacher_weight, student_weight, after, new),
        in_specs=[IN_HBM] * 4,
        out_specs=[IN_HBM, ON_CHIP],
        input_output_aliases={3: 0},
        scratch_shapes=[held(parts, bot, hi - lo)] * 3 + [pltpu.SemaphoreType.DMA((parts,))] * 3,
    )


def fetch_kernel(student_hbm, teacher_hbm, student_ref, teacher_ref, sems):
    half = student_ref.shape[1]
    side = pl.ds(pl.multiple_of(here()[2] * half, half), half)
    loads = [
        pltpu.make_async_copy(student_hbm.at[:, side], student_ref, sems.at[0]),
        pltpu.make_async_copy(teacher_hbm, teacher_ref, sems.at[1]),
    ]
    for load in loads:
        load.start()
    for load in loads:
        load.wait()


def fetch(student, teacher):
    bot, crops = student.shape
    return call(
        fetch_kernel,
        "fetch",
        [held(bot, crops // 2, dtype=jnp.bfloat16), held(bot, crops, dtype=jnp.bfloat16)],
        (student, teacher),
        in_specs=[IN_HBM] * 2,
        scratch_shapes=[pltpu.SemaphoreType.DMA((2,))],
    )


def normalize(values):
    return (values * lax.rsqrt(jnp.sum(values * values, axis=0, keepdims=True) + EPS)).astype(jnp.bfloat16)


def pack_kernel(student_ref, teacher_ref, index_ref, out_ref):
    half = out_ref.shape[2]
    lower = here()[2] == 0
    out_ref[0] = normalize(student_ref[...].astype(jnp.float32))
    index = jnp.where(lower, index_ref[:, :half], index_ref[:, half:])
    row = lax.broadcasted_iota(jnp.int32, (teacher_ref.shape[1], half), 0)
    pick = jnp.where(row == index, 1.0, 0.0).astype(jnp.bfloat16)
    out_ref[1] = normalize(jnp.dot(teacher_ref[...], pick, preferred_element_type=jnp.float32))


def pack(student, teacher, index):
    bot, half = student.shape
    return call(pack_kernel, "pack", held(2, bot, half, dtype=jnp.bfloat16), (student, teacher, index))


def join_kernel(n_in, n_after, firsts, bot, *refs):
    blocks = []
    for ref in refs[:n_in]:
        blocks += [ref] if len(ref.shape) == 3 else [ref.at[i] for i in range(ref.shape[0])]
    for first, ref in zip(firsts, refs[n_in + n_after:]):
        for i in range(ref.shape[0]):
            block = blocks[first + i][:, :bot, :]
            ref[i, :, :bot, :] = block
            if ref.shape[2] > bot:
                ref[i, :, bot:, :] = block[:, :ref.shape[2] - bot]


def join(parts, outs, after, bot):
    width = parts[0].shape[-1]
    shapes = [held(count, 2, rows, width, dtype=jnp.bfloat16) for _, count, rows in outs]
    kernel = functools.partial(join_kernel, len(parts), len(after), [first for first, _, _ in outs], bot)
    return call(kernel, "join", shapes, (*parts, *after), in_specs=[ON_CHIP] * len(parts) + [IN_HBM] * len(after))


def log_sum(parts):
    top = functools.reduce(jnp.maximum, parts)
    return top + jnp.log2(sum(jnp.exp2(part - top) for part in parts))


def combine(parts):
    half = parts[0].shape[0] // 2
    return sum(part[:half] for part in parts), log_sum([part[half:] for part in parts])


def slot(k, n):
    return lax.axis_index("fsdp") ^ k if n <= DIRECT else k


def score_kernel(part, n_feats, *refs):
    last = part == 3
    before, refs = (refs[:3], refs[3:]) if last else ((), refs)
    feats_refs, (ws_ref, wt_ref, peak_ref, *refs) = refs[:n_feats], refs[n_feats:]
    blocks = [ref.at[i] for ref in feats_refs for i in range(ref.shape[0])]
    exp_ref, unit_ref, total_ref, *mine = refs[1:] if part else refs
    own_ref = mine[0] if last else total_ref
    n, (_, bot, width) = len(blocks), blocks[0].shape
    cols = ws_ref.shape[0]
    step = min(STEP, cols)
    per = max(1, min(n, GROUP // width))
    row = lax.broadcasted_iota(jnp.int32, (DEPTH - bot, per * width), 0)
    for which, w_ref, gain in ((0, ws_ref, GAIN_S), (1, wt_ref, GAIN_T)):
        base = (2 * part + which) * n * width
        extra = jnp.where(row < 3 * which, 1.0, 0.0).astype(jnp.bfloat16)
        for group in range(n // per):
            unit = jnp.concatenate([blocks[group * per + k][which] for k in range(per)], axis=1)
            lanes = slice(group * per * width, (group + 1) * per * width)
            if which == 0:
                unit_ref[lanes, :] = unit.T
            stationary = jnp.concatenate([unit, extra], axis=0)
            total = jnp.zeros((8, per * width), jnp.float32)
            for at in range(0, cols, step):
                score = jnp.dot(w_ref[at:at + step, :], stationary, preferred_element_type=jnp.float32)
                exps = jnp.exp2(score * gain)
                total = total + jnp.sum(exps.reshape(step // 8, 8, per * width), axis=0)
                exp_ref[at:at + step, base + lanes.start:base + lanes.stop] = exps.astype(jnp.bfloat16)
            total = jnp.sum(total, axis=0, keepdims=True)
            if which == 1:
                total = jnp.log2(total) + GAIN_T * peak_ref[:, :1]
            own_ref[which:which + 1, lanes] = total
    if not last:
        return
    dp, _, core = here()
    own, pair, other = before
    parts = ((own, other), (pair, own_ref))
    rows = []
    for which in (0, 1):
        for half in (0, 1):
            pieces = []
            for view in (0, 1):
                first = (dp == view) if which == 0 else (dp != view)
                for place in range(n):
                    at = pl.ds(pl.multiple_of(slot(place, n) * width, width), width)
                    read = [[part[which:which + 1, at] for part in side] for side in parts]
                    mine, theirs = [jnp.where(first, *side) for side in read]
                    pieces.append(jnp.where(core == half, mine, theirs))
            rows.append(jnp.concatenate(pieces, axis=1))
    total_ref[...] = jnp.concatenate(rows, axis=0)


def scores(part, feats, weights, before=(), exps=None):
    _, _, bot, width = feats[0].shape
    cols, rows = weights[0].shape[0], sum(part.shape[0] for part in feats) * width
    args = (*before, *feats, *weights, *([exps] if part else []))
    return call(
        functools.partial(score_kernel, part, len(feats)),
        "scores",
        [
            held(cols, 8 * rows, dtype=jnp.bfloat16),
            held(rows, bot, dtype=jnp.bfloat16),
            held(4, 2 * rows) if part == 3 else held(2, rows),
        ],
        args,
        in_specs=[ON_CHIP] * (len(args) - bool(part)) + [IN_HBM] * bool(part),
        input_output_aliases={len(args) - 1: 0} if part else {},
        scratch_shapes=[held(2, rows)] if part == 3 else [],
    )


def relay_kernel(n_in, *refs):
    parts = [ref[...] for ref in refs[:n_in]]
    if len(parts[0].shape) == 3:
        parts = [parts[0][i] for i in range(parts[0].shape[0])]
    refs[-1][...] = jnp.concatenate(combine(parts), axis=0)


def add_up(parts, after=()):
    specs = [ON_CHIP] * len(parts) + [IN_HBM] * len(after)
    out = held(*parts[0].shape[-2:])
    return call(functools.partial(relay_kernel, len(parts)), "relay", out, (*parts, *after), in_specs=specs)


def hold_kernel(in_ref, after, out_ref):
    out_ref[...] = in_ref[...]


def hold(array, after):
    return call(hold_kernel, "hold", held(*array.shape), (array, after), in_specs=[ON_CHIP, IN_HBM])


def exchange(total, axes, first, second, after=()):
    sizes = [lax.axis_size(axis) for axis in axes]
    proto = axes.index("proto")
    places = [(i, j) for i in range(sizes[0]) for j in range(sizes[1])]

    def permute(step):
        flat = lambda place: place[0] * sizes[1] + place[1]
        pairs = []
        for place in places:
            up = step(place[proto] % 2)
            pairs.append((flat(place), flat((place[0] ^ up[0], place[1] ^ up[1]))))
        return lax.ppermute(total, axes, pairs)

    mine = permute(first)
    passed = hold(mine, *after) if after else mine
    return add_up([total, mine, swap(passed, "proto"), permute(second)])


def across(total, up, over):
    n_proto, n_dp = lax.axis_size("proto"), lax.axis_size("dp")
    places = [(p, d) for p in range(n_proto) for d in range(n_dp)]
    pairs = [(p * n_dp + d, (p ^ up) * n_dp + (d ^ over)) for p, d in places]
    return lax.ppermute(total, ("proto", "dp"), pairs)


def add_up_chip_and_across(total):
    n_proto, n_dp = lax.axis_size("proto"), lax.axis_size("dp")
    total = add_up([total, swap(total, "proto")])
    if n_proto == 4 and n_dp == 2:
        return exchange(total, ("proto", "dp"), lambda odd: (2 * odd, 1), lambda odd: (2, 0))
    steps = [(up, over) for up in range(0, n_proto, 2) for over in range(n_dp)][1:]
    return add_up([total, *[across(total, *step) for step in steps]])


def add_up_along(total, after):
    n = lax.axis_size("fsdp")
    if n == 4:
        return exchange(total, ("fsdp", "proto"), lambda odd: (2 + odd, 0), lambda odd: (1, 0), after)
    if n <= DIRECT:
        return add_up([total, *[swap(total, "fsdp", k) for k in range(1, n)]], after)
    return add_up([lax.all_to_all(jnp.broadcast_to(total[None], (n, *total.shape)), "fsdp", 0, 0, tiled=True)], after)


def grad_kernel(total_ref, peak_ref, weight_unit, weight_scale, *refs):
    units, exp_ref, out_hbm, scales, feats, *derivs, buf, sems = refs[:4], *refs[4:]
    dp, _, core = here()
    scales[0:2, :] = 10.0 / total_ref[0:2, :]
    scales[2:4, :] = 10.0 * jnp.exp2(GAIN_T * peak_ref[:, :1] - total_ref[2:4, :])
    rows = units[0].shape[0]
    width = 128
    n = rows // width
    factors = []
    for part in range(4):
        view, half = divmod(part, 2)
        base = (dp ^ view) * rows
        at = [pl.ds(pl.multiple_of(base + slot(k, n) * width, width), width) for k in range(n)]
        for which in (0, 1):
            picked = [
                jnp.where(core == half, scales[2 * which:2 * which + 1, where], scales[2 * which + 1:2 * which + 2, where])
                for where in at
            ]
            factors.append(jnp.concatenate(picked, axis=1).astype(jnp.bfloat16))
    for part, unit in enumerate(units):
        feats[part * rows:(part + 1) * rows, :] = unit[...]
    chunks, _, step = buf.shape
    stores = []

    def derive(i):
        at = slice(i * step, (i + 1) * step)
        for part in range(4):
            lies_s, lies_t = 2 * part * rows, (2 * (part ^ 2) + 1) * rows
            probs_s = exp_ref[at, lies_s:lies_s + rows] * factors[2 * part]
            probs_t = exp_ref[at, lies_t:lies_t + rows] * factors[2 * part + 1]
            derivs[i % 2][:, part * rows:(part + 1) * rows] = probs_s - probs_t

    derive(0)
    for i in range(chunks):
        if i + 1 < chunks:
            derive(i + 1)
        at = slice(i * step, (i + 1) * step)
        grad = jnp.dot(derivs[i % 2][...], feats[...], preferred_element_type=jnp.float32).T
        unit = weight_unit[:, at]
        proj = unit * jnp.sum(unit * grad, axis=0, keepdims=True)
        buf[i] = (grad - proj) * weight_scale[:, at]
        stores.append(pltpu.make_async_copy(buf.at[i], out_hbm.at[:, at], sems.at[i]))
        stores[i].start()
    for store in stores:
        store.wait()


def gradient(total, peak, weight_unit, weight_scale, units, exps):
    cols = exps.shape[0]
    rows, bot = units[0].shape
    step = min(256, cols)
    args = (total, peak, weight_unit, weight_scale, *units, exps)
    return call(
        grad_kernel,
        "gradient",
        pltpu.HBM((bot, cols), jnp.float32),
        args,
        out_specs=IN_HBM,
        scratch_shapes=[
            held(4, 2 * rows),
            held(4 * rows, bot, dtype=jnp.bfloat16),
            *[held(step, 4 * rows, dtype=jnp.bfloat16)] * 2,
            held(cols // step, bot, step),
            pltpu.SemaphoreType.DMA((cols // step,)),
        ],
    )


def shards(teacher_weight, student_weight, teacher_feats, student_feats, pairing, center):
    n_dp, n_fsdp = lax.axis_size("dp"), lax.axis_size("fsdp")
    in_hbm = lambda array: pltpu.with_memory_space_constraint(array, pltpu.HBM)
    teacher_weight, student_weight, center = in_hbm(teacher_weight), in_hbm(student_weight), in_hbm(center[None, :])

    index = swap(pairing, "dp")
    mine = pack(*fetch(in_hbm(student_feats[0].T), in_hbm(teacher_feats[0].T)), index)
    own_cols = teacher_weight.shape[1] // n_dp
    middle = own_cols // 2
    new, wt, ws, unit, scale, peak = prepare(teacher_weight, student_weight, center, n_dp, own_cols - middle)
    weights = (ws, wt, peak)
    bot = mine.shape[1]
    if n_fsdp <= DIRECT:
        other = [swap(mine, "dp")]
        along = [swap(mine, "fsdp", k) for k in range(1, n_fsdp)]
        half = n_fsdp // 2
        outs = [(0, n_fsdp, bot), (2, n_fsdp - 2, bot + 16), (0, half, bot), (half, half, bot)]
        own, far, *halves = join([mine, *along], outs, (other[0], peak), bot)
        other += [swap(other[0], "fsdp"), swap(far, "dp")]
    else:
        own = lax.all_to_all(jnp.broadcast_to(mine[None], (n_fsdp, *mine.shape)), "fsdp", 0, 0, tiled=True)
        other, halves = [swap(own, "dp")], [own]
    exps, unit_a, total_a = scores(0, [own], weights)
    exps, unit_b, total_b = scores(1, [swap(half, "proto") for half in halves], weights, exps=exps)
    (other,) = join(other, [(0, n_fsdp, bot)], (total_b,), bot)
    exps, unit_c, total_c = scores(2, [other], weights, exps=exps)
    exps, unit_d, total = scores(3, [swap(other, "proto")], weights, (total_a, total_b, total_c), exps)
    total = add_up_chip_and_across(total)
    teacher_new, done = update_rest(teacher_weight, student_weight, total, new, own_cols, 0, middle)
    total = add_up_along(total, (done,))
    units = (unit_a, unit_b, unit_c, unit_d)
    student_grad = gradient(total, peak, unit, scale, units, exps)
    return (teacher_new, student_grad)


def solution(mesh):
    placed = (
        P(None, ("proto", "fsdp")),
        P(None, ("proto", "fsdp")),
        P("dp", "fsdp", None),
        P("dp", "fsdp", None),
        P("dp", "fsdp"),
        P("proto"),
    )
    return jax.shard_map(
        shards,
        mesh=mesh,
        in_specs=placed,
        out_specs=(P(None, ("proto", "fsdp")), P(None, ("proto", "fsdp", "dp"))),
        check_vma=False,
    )
```

```python
import functools
import math

import jax
import jax.numpy as jnp
from jax import lax
from jax.experimental import pallas as pl
from jax.experimental.pallas import tpu as pltpu
from jax.sharding import PartitionSpec as P

EPS = 1e-06
DEPTH = 256
GROUP = 512
STEP = 256
DIRECT = 8
LOG2E = math.log2(math.e)
GAIN_T = LOG2E / 0.04
GAIN_S = LOG2E / 0.1
LIMIT = 24 * 1024 * 1024
ON_CHIP = pl.BlockSpec(memory_space=pltpu.VMEM)
IN_HBM = pl.BlockSpec(memory_space=pl.ANY)


def shape(*dims, dtype=jnp.float32):
    return jax.ShapeDtypeStruct(dims, dtype)


def held(*dims, dtype=jnp.float32):
    return pltpu.VMEM(dims, dtype)


def call(kernel, name, out_shape, args, **more):
    many = isinstance(out_shape, (list, tuple))
    specs = dict(in_specs=[ON_CHIP] * len(args), out_specs=[ON_CHIP] * len(out_shape) if many else ON_CHIP)
    return pl.pallas_call(
        kernel,
        out_shape=out_shape,
        compiler_params=pltpu.CompilerParams(vmem_limit_bytes=LIMIT),
        cost_estimate=pl.CostEstimate(flops=1, bytes_accessed=1, transcendentals=0),
        name=name,
        **{**specs, **more},
    )(*args)


def swap(block, axis, apart=1):
    return lax.ppermute(block, axis, [(i, i ^ apart) for i in range(lax.axis_size(axis))])


def here():
    return lax.axis_index("dp"), lax.axis_index("fsdp"), lax.rem(lax.axis_index("proto"), 2)


def cast_split(row):
    high = row.astype(jnp.bfloat16).astype(jnp.float32)
    mid = (row - high).astype(jnp.bfloat16).astype(jnp.float32)
    return high, mid, row - high - mid


def prep_kernel(n_dp, teacher_hbm, student_hbm, center_hbm, new_hbm, wt_ref, ws_ref, unit_ref, scale_ref, peak_ref, *scratch):
    teacher_buf, student_buf, new_buf, center_buf, in_t, in_s, out, in_c = scratch
    chunks, bot, width = new_buf.shape
    n_own = chunks // n_dp
    dp, fsdp, _ = here()
    order = [*range(n_own - 1), *range(n_own, chunks), n_own - 1]
    own = n_own * width
    at = [slice(i * width, (i + 1) * width) for i in range(n_own)]
    firsts = [lax.rem(dp + i // n_own, n_dp) * own + i % n_own * width for i in range(chunks)]
    far = [pl.ds(pl.multiple_of(first, width), width) for first in firsts]
    start = pl.multiple_of((fsdp * n_dp + dp) * own, 128)
    center_load = pltpu.make_async_copy(center_hbm.at[:, pl.ds(start, own)], center_buf, in_c)
    loads = [
        (
            pltpu.make_async_copy(teacher_hbm.at[:, far[i]], teacher_buf.at[i], in_t.at[i]),
            pltpu.make_async_copy(student_hbm.at[:, far[i]], student_buf.at[i], in_s.at[i]),
        )
        for i in range(chunks)
    ]
    stores = [pltpu.make_async_copy(new_buf.at[i], new_hbm.at[:, far[i]], out.at[i]) for i in range(chunks)]
    center_load.start()
    for i in order:
        for load in loads[i]:
            load.start()
    center_load.wait()
    center = center_buf[...]
    peak = jnp.max(-center, axis=1, keepdims=True)
    peak_ref[...] = jnp.broadcast_to(peak, peak_ref.shape)
    splits = cast_split(-center - peak)
    row = lax.broadcasted_iota(jnp.int32, (DEPTH - bot, width), 0)
    zero = jnp.zeros((DEPTH - bot, width), jnp.float32)
    for i in order:
        for load in loads[i]:
            load.wait()
        student = student_buf[i]
        new = 0.994 * teacher_buf[i] + 0.006 * student
        new_buf[i] = new
        stores[i].start()
        if i >= n_own:
            continue
        high, mid, low = [part[:, at[i]] for part in splits]
        extra = jnp.where(row == 0, high, jnp.where(row == 1, mid, jnp.where(row == 2, low, zero)))
        scale = lax.rsqrt(jnp.sum(student * student, axis=0, keepdims=True) + EPS)
        unit_s = student * scale
        unit_t = new * lax.rsqrt(jnp.sum(new * new, axis=0, keepdims=True) + EPS)
        wt_ref[at[i], :] = jnp.concatenate([unit_t, extra], axis=0).astype(jnp.bfloat16).T
        ws_ref[at[i], :] = jnp.concatenate([unit_s, zero], axis=0).astype(jnp.bfloat16).T
        unit_ref[:, at[i]] = unit_s
        scale_ref[:, at[i]] = scale
    for store in stores:
        store.wait()


def prepare(teacher_weight, student_weight, center, n_dp):
    bot, cols = teacher_weight.shape
    own = cols // n_dp
    width = min(512, own)
    chunks = cols // width
    return call(
        functools.partial(prep_kernel, n_dp),
        "prep",
        [
            pltpu.HBM((bot, cols), jnp.float32),
            held(own, DEPTH, dtype=jnp.bfloat16),
            held(own, DEPTH, dtype=jnp.bfloat16),
            held(bot, own),
            held(1, own),
            held(1, 128),
        ],
        (teacher_weight, student_weight, center),
        in_specs=[IN_HBM] * 3,
        out_specs=[IN_HBM] + [ON_CHIP] * 5,
        scratch_shapes=[held(chunks, bot, width)] * 3
        + [held(1, own)]
        + [pltpu.SemaphoreType.DMA((chunks,))] * 3
        + [pltpu.SemaphoreType.DMA],
    )


def fetch_kernel(student_hbm, teacher_hbm, student_ref, teacher_ref, sems):
    half = student_ref.shape[1]
    side = pl.ds(pl.multiple_of(here()[2] * half, half), half)
    loads = [
        pltpu.make_async_copy(student_hbm.at[:, side], student_ref, sems.at[0]),
        pltpu.make_async_copy(teacher_hbm, teacher_ref, sems.at[1]),
    ]
    for load in loads:
        load.start()
    for load in loads:
        load.wait()


def fetch(student, teacher):
    bot, crops = student.shape
    return call(
        fetch_kernel,
        "fetch",
        [held(bot, crops // 2, dtype=jnp.bfloat16), held(bot, crops, dtype=jnp.bfloat16)],
        (student, teacher),
        in_specs=[IN_HBM] * 2,
        scratch_shapes=[pltpu.SemaphoreType.DMA((2,))],
    )


def normalize(values):
    return (values * lax.rsqrt(jnp.sum(values * values, axis=0, keepdims=True) + EPS)).astype(jnp.bfloat16)


def pack_kernel(student_ref, teacher_ref, index_ref, out_ref):
    half = out_ref.shape[2]
    lower = here()[2] == 0
    out_ref[0] = normalize(student_ref[...].astype(jnp.float32))
    index = jnp.where(lower, index_ref[:, :half], index_ref[:, half:])
    row = lax.broadcasted_iota(jnp.int32, (teacher_ref.shape[1], half), 0)
    pick = jnp.where(row == index, 1.0, 0.0).astype(jnp.bfloat16)
    out_ref[1] = normalize(jnp.dot(teacher_ref[...], pick, preferred_element_type=jnp.float32))


def pack(student, teacher, index):
    bot, half = student.shape
    return call(pack_kernel, "pack", held(2, bot, half, dtype=jnp.bfloat16), (student, teacher, index))


def join_kernel(n_in, n_after, firsts, bot, *refs):
    blocks = []
    for ref in refs[:n_in]:
        blocks += [ref] if len(ref.shape) == 3 else [ref.at[i] for i in range(ref.shape[0])]
    for first, ref in zip(firsts, refs[n_in + n_after:]):
        for i in range(ref.shape[0]):
            block = blocks[first + i][:, :bot, :]
            ref[i, :, :bot, :] = block
            if ref.shape[2] > bot:
                ref[i, :, bot:, :] = block[:, :ref.shape[2] - bot]


def join(parts, outs, after, bot):
    width = parts[0].shape[-1]
    shapes = [held(count, 2, rows, width, dtype=jnp.bfloat16) for _, count, rows in outs]
    kernel = functools.partial(join_kernel, len(parts), len(after), [first for first, _, _ in outs], bot)
    return call(kernel, "join", shapes, (*parts, *after), in_specs=[ON_CHIP] * len(parts) + [IN_HBM] * len(after))


def log_sum(parts):
    top = functools.reduce(jnp.maximum, parts)
    return top + jnp.log2(sum(jnp.exp2(part - top) for part in parts))


def combine(parts):
    half = parts[0].shape[0] // 2
    return sum(part[:half] for part in parts), log_sum([part[half:] for part in parts])


def slot(k, n):
    return lax.axis_index("fsdp") ^ k if n <= DIRECT else k


def score_kernel(part, n_feats, *refs):
    last = part == 3
    before, refs = (refs[:3], refs[3:]) if last else ((), refs)
    feats_refs, (ws_ref, wt_ref, peak_ref, *refs) = refs[:n_feats], refs[n_feats:]
    blocks = [ref.at[i] for ref in feats_refs for i in range(ref.shape[0])]
    exp_ref, unit_ref, total_ref, *mine = refs[1:] if part else refs
    own_ref = mine[0] if last else total_ref
    n, (_, bot, width) = len(blocks), blocks[0].shape
    cols = ws_ref.shape[0]
    step = min(STEP, cols)
    per = max(1, min(n, GROUP // width))
    row = lax.broadcasted_iota(jnp.int32, (DEPTH - bot, per * width), 0)
    for which, w_ref, gain in ((0, ws_ref, GAIN_S), (1, wt_ref, GAIN_T)):
        base = (2 * part + which) * n * width
        extra = jnp.where(row < 3 * which, 1.0, 0.0).astype(jnp.bfloat16)
        for group in range(n // per):
            unit = jnp.concatenate([blocks[group * per + k][which] for k in range(per)], axis=1)
            lanes = slice(group * per * width, (group + 1) * per * width)
            if which == 0:
                unit_ref[lanes, :] = unit.T
            stationary = jnp.concatenate([unit, extra], axis=0)
            total = jnp.zeros((8, per * width), jnp.float32)
            for at in range(0, cols, step):
                score = jnp.dot(w_ref[at:at + step, :], stationary, preferred_element_type=jnp.float32)
                exps = jnp.exp2(score * gain)
                total = total + jnp.sum(exps.reshape(step // 8, 8, per * width), axis=0)
                exp_ref[at:at + step, base + lanes.start:base + lanes.stop] = exps.astype(jnp.bfloat16)
            total = jnp.sum(total, axis=0, keepdims=True)
            if which == 1:
                total = jnp.log2(total) + GAIN_T * peak_ref[:, :1]
            own_ref[which:which + 1, lanes] = total
    if not last:
        return
    dp, _, core = here()
    own, pair, other = before
    parts = ((own, other), (pair, own_ref))
    rows = []
    for which in (0, 1):
        for half in (0, 1):
            pieces = []
            for view in (0, 1):
                first = (dp == view) if which == 0 else (dp != view)
                for place in range(n):
                    at = pl.ds(pl.multiple_of(slot(place, n) * width, width), width)
                    read = [[part[which:which + 1, at] for part in side] for side in parts]
                    mine, theirs = [jnp.where(first, *side) for side in read]
                    pieces.append(jnp.where(core == half, mine, theirs))
            rows.append(jnp.concatenate(pieces, axis=1))
    total_ref[...] = jnp.concatenate(rows, axis=0)


def scores(part, feats, weights, before=(), exps=None):
    _, _, bot, width = feats[0].shape
    cols, rows = weights[0].shape[0], sum(part.shape[0] for part in feats) * width
    args = (*before, *feats, *weights, *([exps] if part else []))
    return call(
        functools.partial(score_kernel, part, len(feats)),
        "scores",
        [
            held(cols, 8 * rows, dtype=jnp.bfloat16),
            held(rows, bot, dtype=jnp.bfloat16),
            held(4, 2 * rows) if part == 3 else held(2, rows),
        ],
        args,
        in_specs=[ON_CHIP] * (len(args) - bool(part)) + [IN_HBM] * bool(part),
        input_output_aliases={len(args) - 1: 0} if part else {},
        scratch_shapes=[held(2, rows)] if part == 3 else [],
    )


def relay_kernel(n_in, *refs):
    parts = [ref[...] for ref in refs[:n_in]]
    if len(parts[0].shape) == 3:
        parts = [parts[0][i] for i in range(parts[0].shape[0])]
    refs[-1][...] = jnp.concatenate(combine(parts), axis=0)


def add_up(parts):
    return call(functools.partial(relay_kernel, len(parts)), "relay", held(*parts[0].shape[-2:]), parts)


def exchange(total, axes, first, second):
    sizes = [lax.axis_size(axis) for axis in axes]
    proto = axes.index("proto")
    places = [(i, j) for i in range(sizes[0]) for j in range(sizes[1])]

    def permute(step):
        flat = lambda place: place[0] * sizes[1] + place[1]
        pairs = []
        for place in places:
            up = step(place[proto] % 2)
            pairs.append((flat(place), flat((place[0] ^ up[0], place[1] ^ up[1]))))
        return lax.ppermute(total, axes, pairs)

    mine = permute(first)
    return add_up([total, mine, swap(mine, "proto"), permute(second)])


def across(total, up, over):
    n_proto, n_dp = lax.axis_size("proto"), lax.axis_size("dp")
    places = [(p, d) for p in range(n_proto) for d in range(n_dp)]
    pairs = [(p * n_dp + d, (p ^ up) * n_dp + (d ^ over)) for p, d in places]
    return lax.ppermute(total, ("proto", "dp"), pairs)


def add_up_chip_and_across(total):
    n_proto, n_dp = lax.axis_size("proto"), lax.axis_size("dp")
    total = add_up([total, swap(total, "proto")])
    if n_proto == 4 and n_dp == 2:
        return exchange(total, ("proto", "dp"), lambda odd: (2 * odd, 1), lambda odd: (2, 0))
    steps = [(up, over) for up in range(0, n_proto, 2) for over in range(n_dp)][1:]
    return add_up([total, *[across(total, *step) for step in steps]])


def add_up_along(total):
    n = lax.axis_size("fsdp")
    if n == 4:
        return exchange(total, ("fsdp", "proto"), lambda odd: (2 + odd, 0), lambda odd: (1, 0))
    if n <= DIRECT:
        return add_up([total, *[swap(total, "fsdp", k) for k in range(1, n)]])
    return add_up([lax.all_to_all(jnp.broadcast_to(total[None], (n, *total.shape)), "fsdp", 0, 0, tiled=True)])


def grad_kernel(total_ref, peak_ref, weight_unit, weight_scale, *refs):
    units, exp_ref, out_hbm, scales, feats, *derivs, buf, sems = refs[:4], *refs[4:]
    dp, _, core = here()
    scales[0:2, :] = 10.0 / total_ref[0:2, :]
    scales[2:4, :] = 10.0 * jnp.exp2(GAIN_T * peak_ref[:, :1] - total_ref[2:4, :])
    rows = units[0].shape[0]
    width = 128
    n = rows // width
    factors = []
    for part in range(4):
        view, half = divmod(part, 2)
        base = (dp ^ view) * rows
        at = [pl.ds(pl.multiple_of(base + slot(k, n) * width, width), width) for k in range(n)]
        for which in (0, 1):
            picked = [
                jnp.where(core == half, scales[2 * which:2 * which + 1, where], scales[2 * which + 1:2 * which + 2, where])
                for where in at
            ]
            factors.append(jnp.concatenate(picked, axis=1).astype(jnp.bfloat16))
    for part, unit in enumerate(units):
        feats[part * rows:(part + 1) * rows, :] = unit[...]
    chunks, _, step = buf.shape
    stores = []

    def derive(i):
        at = slice(i * step, (i + 1) * step)
        for part in range(4):
            lies_s, lies_t = 2 * part * rows, (2 * (part ^ 2) + 1) * rows
            probs_s = exp_ref[at, lies_s:lies_s + rows] * factors[2 * part]
            probs_t = exp_ref[at, lies_t:lies_t + rows] * factors[2 * part + 1]
            derivs[i % 2][:, part * rows:(part + 1) * rows] = probs_s - probs_t

    derive(0)
    for i in range(chunks):
        if i + 1 < chunks:
            derive(i + 1)
        at = slice(i * step, (i + 1) * step)
        grad = jnp.dot(derivs[i % 2][...], feats[...], preferred_element_type=jnp.float32).T
        unit = weight_unit[:, at]
        proj = unit * jnp.sum(unit * grad, axis=0, keepdims=True)
        buf[i] = (grad - proj) * weight_scale[:, at]
        stores.append(pltpu.make_async_copy(buf.at[i], out_hbm.at[:, at], sems.at[i]))
        stores[i].start()
    for store in stores:
        store.wait()


def gradient(total, peak, weight_unit, weight_scale, units, exps):
    cols = exps.shape[0]
    rows, bot = units[0].shape
    step = min(256, cols)
    args = (total, peak, weight_unit, weight_scale, *units, exps)
    return call(
        grad_kernel,
        "gradient",
        pltpu.HBM((bot, cols), jnp.float32),
        args,
        out_specs=IN_HBM,
        scratch_shapes=[
            held(4, 2 * rows),
            held(4 * rows, bot, dtype=jnp.bfloat16),
            *[held(step, 4 * rows, dtype=jnp.bfloat16)] * 2,
            held(cols // step, bot, step),
            pltpu.SemaphoreType.DMA((cols // step,)),
        ],
    )


def shards(teacher_weight, student_weight, teacher_feats, student_feats, pairing, center):
    n_dp, n_fsdp = lax.axis_size("dp"), lax.axis_size("fsdp")
    in_hbm = lambda array: pltpu.with_memory_space_constraint(array, pltpu.HBM)
    teacher_weight, student_weight, center = in_hbm(teacher_weight), in_hbm(student_weight), in_hbm(center[None, :])

    index = swap(pairing, "dp")
    mine = pack(*fetch(in_hbm(student_feats[0].T), in_hbm(teacher_feats[0].T)), index)
    teacher_new, wt, ws, unit, scale, peak = prepare(teacher_weight, student_weight, center, n_dp)
    weights = (ws, wt, peak)
    bot = mine.shape[1]
    if n_fsdp <= DIRECT:
        other = [swap(mine, "dp")]
        along = [swap(mine, "fsdp", k) for k in range(1, n_fsdp)]
        half = n_fsdp // 2
        outs = [(0, n_fsdp, bot), (2, n_fsdp - 2, bot + 16), (0, half, bot), (half, half, bot)]
        own, far, *halves = join([mine, *along], outs, (other[0], peak), bot)
        other += [swap(other[0], "fsdp"), swap(far, "dp")]
    else:
        own = lax.all_to_all(jnp.broadcast_to(mine[None], (n_fsdp, *mine.shape)), "fsdp", 0, 0, tiled=True)
        other, halves = [swap(own, "dp")], [own]
    exps, unit_a, total_a = scores(0, [own], weights)
    exps, unit_b, total_b = scores(1, [swap(half, "proto") for half in halves], weights, exps=exps)
    (other,) = join(other, [(0, n_fsdp, bot)], (total_b,), bot)
    exps, unit_c, total_c = scores(2, [other], weights, exps=exps)
    exps, unit_d, total = scores(3, [swap(other, "proto")], weights, (total_a, total_b, total_c), exps)
    total = add_up_chip_and_across(total)
    total = add_up_along(total)
    units = (unit_a, unit_b, unit_c, unit_d)
    student_grad = gradient(total, peak, unit, scale, units, exps)
    return (teacher_new, student_grad)


def solution(mesh):
    placed = (
        P(None, ("proto", "fsdp")),
        P(None, ("proto", "fsdp")),
        P("dp", "fsdp", None),
        P("dp", "fsdp", None),
        P("dp", "fsdp"),
        P("proto"),
    )
    return jax.shard_map(
        shards,
        mesh=mesh,
        in_specs=placed,
        out_specs=(P(None, ("proto", "fsdp")), P(None, ("proto", "fsdp", "dp"))),
        check_vma=False,
    )
```

```python
import functools
import math

import jax
import jax.numpy as jnp
from jax import lax
from jax.experimental import pallas as pl
from jax.experimental.pallas import tpu as pltpu
from jax.sharding import PartitionSpec as P

EPS = 1e-06
DEPTH = 256
GROUP = 512
STEP = 256
DIRECT = 8
LOG2E = math.log2(math.e)
GAIN_T = LOG2E / 0.04
GAIN_S = LOG2E / 0.1
LIMIT = 24 * 1024 * 1024
ON_CHIP = pl.BlockSpec(memory_space=pltpu.VMEM)
IN_HBM = pl.BlockSpec(memory_space=pl.ANY)


def shape(*dims, dtype=jnp.float32):
    return jax.ShapeDtypeStruct(dims, dtype)


def held(*dims, dtype=jnp.float32):
    return pltpu.VMEM(dims, dtype)


def call(kernel, name, out_shape, args, **more):
    many = isinstance(out_shape, (list, tuple))
    specs = dict(in_specs=[ON_CHIP] * len(args), out_specs=[ON_CHIP] * len(out_shape) if many else ON_CHIP)
    return pl.pallas_call(
        kernel,
        out_shape=out_shape,
        compiler_params=pltpu.CompilerParams(vmem_limit_bytes=LIMIT),
        cost_estimate=pl.CostEstimate(flops=1, bytes_accessed=1, transcendentals=0),
        name=name,
        **{**specs, **more},
    )(*args)


def swap(block, axis, apart=1):
    return lax.ppermute(block, axis, [(i, i ^ apart) for i in range(lax.axis_size(axis))])


def here():
    return lax.axis_index("dp"), lax.axis_index("fsdp"), lax.rem(lax.axis_index("proto"), 2)


def cast_split(row):
    high = row.astype(jnp.bfloat16).astype(jnp.float32)
    mid = (row - high).astype(jnp.bfloat16).astype(jnp.float32)
    return high, mid, row - high - mid


def prep_kernel(n_dp, teacher_hbm, student_hbm, center_hbm, new_hbm, wt_ref, ws_ref, unit_ref, scale_ref, peak_ref, *scratch):
    teacher_buf, student_buf, new_buf, center_buf, in_t, in_s, out, in_c = scratch
    chunks, bot, width = new_buf.shape
    n_own = chunks // n_dp
    dp, fsdp, _ = here()
    order = [*range(n_own - 1), *range(n_own, chunks), n_own - 1]
    own = n_own * width
    at = [slice(i * width, (i + 1) * width) for i in range(n_own)]
    firsts = [lax.rem(dp + i // n_own, n_dp) * own + i % n_own * width for i in range(chunks)]
    far = [pl.ds(pl.multiple_of(first, width), width) for first in firsts]
    start = pl.multiple_of((fsdp * n_dp + dp) * own, 128)
    center_load = pltpu.make_async_copy(center_hbm.at[:, pl.ds(start, own)], center_buf, in_c)
    loads = [
        (
            pltpu.make_async_copy(teacher_hbm.at[:, far[i]], teacher_buf.at[i], in_t.at[i]),
            pltpu.make_async_copy(student_hbm.at[:, far[i]], student_buf.at[i], in_s.at[i]),
        )
        for i in range(chunks)
    ]
    stores = [pltpu.make_async_copy(new_buf.at[i], new_hbm.at[:, far[i]], out.at[i]) for i in range(chunks)]
    center_load.start()
    for i in order:
        for load in loads[i]:
            load.start()
    center_load.wait()
    center = center_buf[...]
    peak = jnp.max(-center, axis=1, keepdims=True)
    peak_ref[...] = jnp.broadcast_to(peak, peak_ref.shape)
    splits = cast_split(-center - peak)
    row = lax.broadcasted_iota(jnp.int32, (DEPTH - bot, width), 0)
    zero = jnp.zeros((DEPTH - bot, width), jnp.float32)
    for i in order:
        for load in loads[i]:
            load.wait()
        student = student_buf[i]
        new = 0.994 * teacher_buf[i] + 0.006 * student
        new_buf[i] = new
        stores[i].start()
        if i >= n_own:
            continue
        high, mid, low = [part[:, at[i]] for part in splits]
        extra = jnp.where(row == 0, high, jnp.where(row == 1, mid, jnp.where(row == 2, low, zero)))
        scale = lax.rsqrt(jnp.sum(student * student, axis=0, keepdims=True) + EPS)
        unit_s = student * scale
        unit_t = new * lax.rsqrt(jnp.sum(new * new, axis=0, keepdims=True) + EPS)
        wt_ref[at[i], :] = jnp.concatenate([unit_t, extra], axis=0).astype(jnp.bfloat16).T
        ws_ref[at[i], :] = jnp.concatenate([unit_s, zero], axis=0).astype(jnp.bfloat16).T
        unit_ref[:, at[i]] = unit_s
        scale_ref[:, at[i]] = scale
    for store in stores:
        store.wait()


def prepare(teacher_weight, student_weight, center, n_dp):
    bot, cols = teacher_weight.shape
    own = cols // n_dp
    width = min(512, own)
    chunks = cols // width
    return call(
        functools.partial(prep_kernel, n_dp),
        "prep",
        [
            pltpu.HBM((bot, cols), jnp.float32),
            held(own, DEPTH, dtype=jnp.bfloat16),
            held(own, DEPTH, dtype=jnp.bfloat16),
            held(bot, own),
            held(1, own),
            held(1, 128),
        ],
        (teacher_weight, student_weight, center),
        in_specs=[IN_HBM] * 3,
        out_specs=[IN_HBM] + [ON_CHIP] * 5,
        scratch_shapes=[held(chunks, bot, width)] * 3
        + [held(1, own)]
        + [pltpu.SemaphoreType.DMA((chunks,))] * 3
        + [pltpu.SemaphoreType.DMA],
    )


def fetch_kernel(student_hbm, teacher_hbm, student_ref, teacher_ref, sems):
    half = student_ref.shape[1]
    side = pl.ds(pl.multiple_of(here()[2] * half, half), half)
    loads = [
        pltpu.make_async_copy(student_hbm.at[:, side], student_ref, sems.at[0]),
        pltpu.make_async_copy(teacher_hbm, teacher_ref, sems.at[1]),
    ]
    for load in loads:
        load.start()
    for load in loads:
        load.wait()


def fetch(student, teacher):
    bot, crops = student.shape
    return call(
        fetch_kernel,
        "fetch",
        [held(bot, crops // 2, dtype=jnp.bfloat16), held(bot, crops, dtype=jnp.bfloat16)],
        (student, teacher),
        in_specs=[IN_HBM] * 2,
        scratch_shapes=[pltpu.SemaphoreType.DMA((2,))],
    )


def normalize(values):
    return (values * lax.rsqrt(jnp.sum(values * values, axis=0, keepdims=True) + EPS)).astype(jnp.bfloat16)


def pack_kernel(student_ref, teacher_ref, index_ref, out_ref):
    half = out_ref.shape[2]
    lower = here()[2] == 0
    out_ref[0] = normalize(student_ref[...].astype(jnp.float32))
    index = jnp.where(lower, index_ref[:, :half], index_ref[:, half:])
    row = lax.broadcasted_iota(jnp.int32, (teacher_ref.shape[1], half), 0)
    pick = jnp.where(row == index, 1.0, 0.0).astype(jnp.bfloat16)
    out_ref[1] = normalize(jnp.dot(teacher_ref[...], pick, preferred_element_type=jnp.float32))


def pack(student, teacher, index):
    bot, half = student.shape
    return call(pack_kernel, "pack", held(2, bot, half, dtype=jnp.bfloat16), (student, teacher, index))


def join_kernel(n_in, n_after, firsts, bot, *refs):
    blocks = []
    for ref in refs[:n_in]:
        blocks += [ref] if len(ref.shape) == 3 else [ref.at[i] for i in range(ref.shape[0])]
    for first, ref in zip(firsts, refs[n_in + n_after:]):
        for i in range(ref.shape[0]):
            block = blocks[first + i][:, :bot, :]
            ref[i, :, :bot, :] = block
            if ref.shape[2] > bot:
                ref[i, :, bot:, :] = block[:, :ref.shape[2] - bot]


def join(parts, outs, after, bot):
    width = parts[0].shape[-1]
    shapes = [held(count, 2, rows, width, dtype=jnp.bfloat16) for _, count, rows in outs]
    kernel = functools.partial(join_kernel, len(parts), len(after), [first for first, _, _ in outs], bot)
    return call(kernel, "join", shapes, (*parts, *after), in_specs=[ON_CHIP] * len(parts) + [IN_HBM] * len(after))


def log_sum(parts):
    top = functools.reduce(jnp.maximum, parts)
    return top + jnp.log2(sum(jnp.exp2(part - top) for part in parts))


def combine(parts):
    half = parts[0].shape[0] // 2
    return sum(part[:half] for part in parts), log_sum([part[half:] for part in parts])


def slot(k, n):
    return lax.axis_index("fsdp") ^ k if n <= DIRECT else k


def score_kernel(part, n_feats, *refs):
    last = part == 3
    before, refs = (refs[:3], refs[3:]) if last else ((), refs)
    feats_refs, (ws_ref, wt_ref, peak_ref, *refs) = refs[:n_feats], refs[n_feats:]
    blocks = [ref.at[i] for ref in feats_refs for i in range(ref.shape[0])]
    exp_ref, unit_ref, total_ref, *mine = refs[1:] if part else refs
    own_ref = mine[0] if last else total_ref
    n, (_, bot, width) = len(blocks), blocks[0].shape
    cols = ws_ref.shape[0]
    step = min(STEP, cols)
    per = max(1, min(n, GROUP // width))
    row = lax.broadcasted_iota(jnp.int32, (DEPTH - bot, per * width), 0)
    for which, w_ref, gain in ((0, ws_ref, GAIN_S), (1, wt_ref, GAIN_T)):
        base = (2 * part + which) * n * width
        extra = jnp.where(row < 3 * which, 1.0, 0.0).astype(jnp.bfloat16)
        for group in range(n // per):
            unit = jnp.concatenate([blocks[group * per + k][which] for k in range(per)], axis=1)
            lanes = slice(group * per * width, (group + 1) * per * width)
            if which == 0:
                unit_ref[lanes, :] = unit.T
            stationary = jnp.concatenate([unit, extra], axis=0)
            total = jnp.zeros((8, per * width), jnp.float32)
            for at in range(0, cols, step):
                score = jnp.dot(w_ref[at:at + step, :], stationary, preferred_element_type=jnp.float32)
                exps = jnp.exp2(score * gain)
                total = total + jnp.sum(exps.reshape(step // 8, 8, per * width), axis=0)
                exp_ref[at:at + step, base + lanes.start:base + lanes.stop] = exps.astype(jnp.bfloat16)
            total = jnp.sum(total, axis=0, keepdims=True)
            if which == 1:
                total = jnp.log2(total) + GAIN_T * peak_ref[:, :1]
            own_ref[which:which + 1, lanes] = total
    if not last:
        return
    dp, _, core = here()
    own, pair, other = before
    parts = ((own, other), (pair, own_ref))
    rows = []
    for which in (0, 1):
        for half in (0, 1):
            pieces = []
            for view in (0, 1):
                first = (dp == view) if which == 0 else (dp != view)
                for place in range(n):
                    at = pl.ds(pl.multiple_of(slot(place, n) * width, width), width)
                    read = [[part[which:which + 1, at] for part in side] for side in parts]
                    mine, theirs = [jnp.where(first, *side) for side in read]
                    pieces.append(jnp.where(core == half, mine, theirs))
            rows.append(jnp.concatenate(pieces, axis=1))
    total_ref[...] = jnp.concatenate(rows, axis=0)


def scores(part, feats, weights, before=(), exps=None):
    _, _, bot, width = feats[0].shape
    cols, rows = weights[0].shape[0], sum(part.shape[0] for part in feats) * width
    args = (*before, *feats, *weights, *([exps] if part else []))
    return call(
        functools.partial(score_kernel, part, len(feats)),
        "scores",
        [
            held(cols, 8 * rows, dtype=jnp.bfloat16),
            held(rows, bot, dtype=jnp.bfloat16),
            held(4, 2 * rows) if part == 3 else held(2, rows),
        ],
        args,
        in_specs=[ON_CHIP] * (len(args) - bool(part)) + [IN_HBM] * bool(part),
        input_output_aliases={len(args) - 1: 0} if part else {},
        scratch_shapes=[held(2, rows)] if part == 3 else [],
    )


def relay_kernel(n_in, *refs):
    parts = [ref[...] for ref in refs[:n_in]]
    if len(parts[0].shape) == 3:
        parts = [parts[0][i] for i in range(parts[0].shape[0])]
    refs[-1][...] = jnp.concatenate(combine(parts), axis=0)


def add_up(parts):
    return call(functools.partial(relay_kernel, len(parts)), "relay", held(*parts[0].shape[-2:]), parts)


def exchange(total, axes, first, second):
    sizes = [lax.axis_size(axis) for axis in axes]
    proto = axes.index("proto")
    places = [(i, j) for i in range(sizes[0]) for j in range(sizes[1])]

    def permute(step):
        flat = lambda place: place[0] * sizes[1] + place[1]
        pairs = []
        for place in places:
            up = step(place[proto] % 2)
            pairs.append((flat(place), flat((place[0] ^ up[0], place[1] ^ up[1]))))
        return lax.ppermute(total, axes, pairs)

    mine = permute(first)
    return add_up([total, mine, swap(mine, "proto"), permute(second)])


def across(total, up, over):
    n_proto, n_dp = lax.axis_size("proto"), lax.axis_size("dp")
    places = [(p, d) for p in range(n_proto) for d in range(n_dp)]
    pairs = [(p * n_dp + d, (p ^ up) * n_dp + (d ^ over)) for p, d in places]
    return lax.ppermute(total, ("proto", "dp"), pairs)


def add_up_chip_and_across(total):
    n_proto, n_dp = lax.axis_size("proto"), lax.axis_size("dp")
    total = add_up([total, swap(total, "proto")])
    if n_proto == 4 and n_dp == 2:
        return exchange(total, ("proto", "dp"), lambda odd: (2 * odd, 1 - odd), lambda odd: (2, 1))
    steps = [(up, over) for up in range(0, n_proto, 2) for over in range(n_dp)][1:]
    return add_up([total, *[across(total, *step) for step in steps]])


def add_up_along(total):
    n = lax.axis_size("fsdp")
    if n == 4:
        return exchange(total, ("fsdp", "proto"), lambda odd: (1 + odd, 0), lambda odd: (3, 0))
    if n <= DIRECT:
        return add_up([total, *[swap(total, "fsdp", k) for k in range(1, n)]])
    return add_up([lax.all_to_all(jnp.broadcast_to(total[None], (n, *total.shape)), "fsdp", 0, 0, tiled=True)])


def grad_kernel(total_ref, peak_ref, weight_unit, weight_scale, *refs):
    units, exp_ref, out_hbm, scales, feats, *derivs, buf, sems = refs[:4], *refs[4:]
    dp, _, core = here()
    scales[0:2, :] = 10.0 / total_ref[0:2, :]
    scales[2:4, :] = 10.0 * jnp.exp2(GAIN_T * peak_ref[:, :1] - total_ref[2:4, :])
    rows = units[0].shape[0]
    width = 128
    n = rows // width
    factors = []
    for part in range(4):
        view, half = divmod(part, 2)
        base = (dp ^ view) * rows
        at = [pl.ds(pl.multiple_of(base + slot(k, n) * width, width), width) for k in range(n)]
        for which in (0, 1):
            picked = [
                jnp.where(core == half, scales[2 * which:2 * which + 1, where], scales[2 * which + 1:2 * which + 2, where])
                for where in at
            ]
            factors.append(jnp.concatenate(picked, axis=1).astype(jnp.bfloat16))
    for part, unit in enumerate(units):
        feats[part * rows:(part + 1) * rows, :] = unit[...]
    chunks, _, step = buf.shape
    stores = []

    def derive(i):
        at = slice(i * step, (i + 1) * step)
        for part in range(4):
            lies_s, lies_t = 2 * part * rows, (2 * (part ^ 2) + 1) * rows
            probs_s = exp_ref[at, lies_s:lies_s + rows] * factors[2 * part]
            probs_t = exp_ref[at, lies_t:lies_t + rows] * factors[2 * part + 1]
            derivs[i % 2][:, part * rows:(part + 1) * rows] = probs_s - probs_t

    derive(0)
    for i in range(chunks):
        if i + 1 < chunks:
            derive(i + 1)
        at = slice(i * step, (i + 1) * step)
        grad = jnp.dot(derivs[i % 2][...], feats[...], preferred_element_type=jnp.float32).T
        unit = weight_unit[:, at]
        proj = unit * jnp.sum(unit * grad, axis=0, keepdims=True)
        buf[i] = (grad - proj) * weight_scale[:, at]
        stores.append(pltpu.make_async_copy(buf.at[i], out_hbm.at[:, at], sems.at[i]))
        stores[i].start()
    for store in stores:
        store.wait()


def gradient(total, peak, weight_unit, weight_scale, units, exps):
    cols = exps.shape[0]
    rows, bot = units[0].shape
    step = min(256, cols)
    args = (total, peak, weight_unit, weight_scale, *units, exps)
    return call(
        grad_kernel,
        "gradient",
        pltpu.HBM((bot, cols), jnp.float32),
        args,
        out_specs=IN_HBM,
        scratch_shapes=[
            held(4, 2 * rows),
            held(4 * rows, bot, dtype=jnp.bfloat16),
            *[held(step, 4 * rows, dtype=jnp.bfloat16)] * 2,
            held(cols // step, bot, step),
            pltpu.SemaphoreType.DMA((cols // step,)),
        ],
    )


def shards(teacher_weight, student_weight, teacher_feats, student_feats, pairing, center):
    n_dp, n_fsdp = lax.axis_size("dp"), lax.axis_size("fsdp")
    in_hbm = lambda array: pltpu.with_memory_space_constraint(array, pltpu.HBM)
    teacher_weight, student_weight, center = in_hbm(teacher_weight), in_hbm(student_weight), in_hbm(center[None, :])

    index = swap(pairing, "dp")
    mine = pack(*fetch(in_hbm(student_feats[0].T), in_hbm(teacher_feats[0].T)), index)
    teacher_new, wt, ws, unit, scale, peak = prepare(teacher_weight, student_weight, center, n_dp)
    weights = (ws, wt, peak)
    bot = mine.shape[1]
    if n_fsdp <= DIRECT:
        other = [swap(mine, "dp")]
        along = [swap(mine, "fsdp", k) for k in range(1, n_fsdp)]
        half = n_fsdp // 2
        outs = [(0, n_fsdp, bot), (2, n_fsdp - 2, bot + 16), (0, half, bot), (half, half, bot)]
        own, far, *halves = join([mine, *along], outs, (other[0], peak), bot)
        other += [swap(other[0], "fsdp"), swap(far, "dp")]
    else:
        own = lax.all_to_all(jnp.broadcast_to(mine[None], (n_fsdp, *mine.shape)), "fsdp", 0, 0, tiled=True)
        other, halves = [swap(own, "dp")], [own]
    exps, unit_a, total_a = scores(0, [own], weights)
    exps, unit_b, total_b = scores(1, [swap(half, "proto") for half in halves], weights, exps=exps)
    (other,) = join(other, [(0, n_fsdp, bot)], (total_b,), bot)
    exps, unit_c, total_c = scores(2, [other], weights, exps=exps)
    exps, unit_d, total = scores(3, [swap(other, "proto")], weights, (total_a, total_b, total_c), exps)
    total = add_up_chip_and_across(total)
    total = add_up_along(total)
    units = (unit_a, unit_b, unit_c, unit_d)
    student_grad = gradient(total, peak, unit, scale, units, exps)
    return (teacher_new, student_grad)


def solution(mesh):
    placed = (
        P(None, ("proto", "fsdp")),
        P(None, ("proto", "fsdp")),
        P("dp", "fsdp", None),
        P("dp", "fsdp", None),
        P("dp", "fsdp"),
        P("proto"),
    )
    return jax.shard_map(
        shards,
        mesh=mesh,
        in_specs=placed,
        out_specs=(P(None, ("proto", "fsdp")), P(None, ("proto", "fsdp", "dp"))),
        check_vma=False,
    )
```

```python
import functools
import math

import jax
import jax.numpy as jnp
from jax import lax
from jax.experimental import pallas as pl
from jax.experimental.pallas import tpu as pltpu
from jax.sharding import PartitionSpec as P

EPS = 1e-06
DEPTH = 256
GROUP = 512
STEP = 512
DIRECT = 8
LOG2E = math.log2(math.e)
GAIN_T = LOG2E / 0.04
GAIN_S = LOG2E / 0.1
LIMIT = 24 * 1024 * 1024
ON_CHIP = pl.BlockSpec(memory_space=pltpu.VMEM)
IN_HBM = pl.BlockSpec(memory_space=pl.ANY)


def shape(*dims, dtype=jnp.float32):
    return jax.ShapeDtypeStruct(dims, dtype)


def held(*dims, dtype=jnp.float32):
    return pltpu.VMEM(dims, dtype)


def call(kernel, name, out_shape, args, **more):
    many = isinstance(out_shape, (list, tuple))
    specs = dict(in_specs=[ON_CHIP] * len(args), out_specs=[ON_CHIP] * len(out_shape) if many else ON_CHIP)
    return pl.pallas_call(
        kernel,
        out_shape=out_shape,
        compiler_params=pltpu.CompilerParams(vmem_limit_bytes=LIMIT),
        cost_estimate=pl.CostEstimate(flops=1, bytes_accessed=1, transcendentals=0),
        name=name,
        **{**specs, **more},
    )(*args)


def swap(block, axis, apart=1):
    return lax.ppermute(block, axis, [(i, i ^ apart) for i in range(lax.axis_size(axis))])


def here():
    return lax.axis_index("dp"), lax.axis_index("fsdp"), lax.rem(lax.axis_index("proto"), 2)


def cast_split(row):
    high = row.astype(jnp.bfloat16).astype(jnp.float32)
    mid = (row - high).astype(jnp.bfloat16).astype(jnp.float32)
    return high, mid, row - high - mid


def prep_kernel(n_dp, teacher_hbm, student_hbm, center_hbm, new_hbm, wt_ref, ws_ref, unit_ref, scale_ref, peak_ref, *scratch):
    teacher_buf, student_buf, new_buf, center_buf, in_t, in_s, out, in_c = scratch
    chunks, bot, width = new_buf.shape
    n_own = chunks // n_dp
    dp, fsdp, _ = here()
    order = [*range(n_own - 1), *range(n_own, chunks), n_own - 1]
    own = n_own * width
    at = [slice(i * width, (i + 1) * width) for i in range(n_own)]
    firsts = [lax.rem(dp + i // n_own, n_dp) * own + i % n_own * width for i in range(chunks)]
    far = [pl.ds(pl.multiple_of(first, width), width) for first in firsts]
    start = pl.multiple_of((fsdp * n_dp + dp) * own, 128)
    center_load = pltpu.make_async_copy(center_hbm.at[:, pl.ds(start, own)], center_buf, in_c)
    loads = [
        (
            pltpu.make_async_copy(teacher_hbm.at[:, far[i]], teacher_buf.at[i], in_t.at[i]),
            pltpu.make_async_copy(student_hbm.at[:, far[i]], student_buf.at[i], in_s.at[i]),
        )
        for i in range(chunks)
    ]
    stores = [pltpu.make_async_copy(new_buf.at[i], new_hbm.at[:, far[i]], out.at[i]) for i in range(chunks)]
    center_load.start()
    for i in order:
        for load in loads[i]:
            load.start()
    center_load.wait()
    center = center_buf[...]
    peak = jnp.max(-center, axis=1, keepdims=True)
    peak_ref[...] = jnp.broadcast_to(peak, peak_ref.shape)
    splits = cast_split(-center - peak)
    row = lax.broadcasted_iota(jnp.int32, (DEPTH - bot, width), 0)
    zero = jnp.zeros((DEPTH - bot, width), jnp.float32)
    for i in order:
        for load in loads[i]:
            load.wait()
        student = student_buf[i]
        new = 0.994 * teacher_buf[i] + 0.006 * student
        new_buf[i] = new
        stores[i].start()
        if i >= n_own:
            continue
        high, mid, low = [part[:, at[i]] for part in splits]
        extra = jnp.where(row == 0, high, jnp.where(row == 1, mid, jnp.where(row == 2, low, zero)))
        scale = lax.rsqrt(jnp.sum(student * student, axis=0, keepdims=True) + EPS)
        unit_s = student * scale
        unit_t = new * lax.rsqrt(jnp.sum(new * new, axis=0, keepdims=True) + EPS)
        wt_ref[at[i], :] = jnp.concatenate([unit_t, extra], axis=0).astype(jnp.bfloat16).T
        ws_ref[at[i], :] = jnp.concatenate([unit_s, zero], axis=0).astype(jnp.bfloat16).T
        unit_ref[:, at[i]] = unit_s
        scale_ref[:, at[i]] = scale
    for store in stores:
        store.wait()


def prepare(teacher_weight, student_weight, center, n_dp):
    bot, cols = teacher_weight.shape
    own = cols // n_dp
    width = min(512, own)
    chunks = cols // width
    return call(
        functools.partial(prep_kernel, n_dp),
        "prep",
        [
            pltpu.HBM((bot, cols), jnp.float32),
            held(own, DEPTH, dtype=jnp.bfloat16),
            held(own, DEPTH, dtype=jnp.bfloat16),
            held(bot, own),
            held(1, own),
            held(1, 128),
        ],
        (teacher_weight, student_weight, center),
        in_specs=[IN_HBM] * 3,
        out_specs=[IN_HBM] + [ON_CHIP] * 5,
        scratch_shapes=[held(chunks, bot, width)] * 3
        + [held(1, own)]
        + [pltpu.SemaphoreType.DMA((chunks,))] * 3
        + [pltpu.SemaphoreType.DMA],
    )


def fetch_kernel(student_hbm, teacher_hbm, student_ref, teacher_ref, sems):
    half = student_ref.shape[1]
    side = pl.ds(pl.multiple_of(here()[2] * half, half), half)
    loads = [
        pltpu.make_async_copy(student_hbm.at[:, side], student_ref, sems.at[0]),
        pltpu.make_async_copy(teacher_hbm, teacher_ref, sems.at[1]),
    ]
    for load in loads:
        load.start()
    for load in loads:
        load.wait()


def fetch(student, teacher):
    bot, crops = student.shape
    return call(
        fetch_kernel,
        "fetch",
        [held(bot, crops // 2, dtype=jnp.bfloat16), held(bot, crops, dtype=jnp.bfloat16)],
        (student, teacher),
        in_specs=[IN_HBM] * 2,
        scratch_shapes=[pltpu.SemaphoreType.DMA((2,))],
    )


def normalize(values):
    return (values * lax.rsqrt(jnp.sum(values * values, axis=0, keepdims=True) + EPS)).astype(jnp.bfloat16)


def pack_kernel(student_ref, teacher_ref, index_ref, out_ref):
    half = out_ref.shape[2]
    lower = here()[2] == 0
    out_ref[0] = normalize(student_ref[...].astype(jnp.float32))
    index = jnp.where(lower, index_ref[:, :half], index_ref[:, half:])
    row = lax.broadcasted_iota(jnp.int32, (teacher_ref.shape[1], half), 0)
    pick = jnp.where(row == index, 1.0, 0.0).astype(jnp.bfloat16)
    out_ref[1] = normalize(jnp.dot(teacher_ref[...], pick, preferred_element_type=jnp.float32))


def pack(student, teacher, index):
    bot, half = student.shape
    return call(pack_kernel, "pack", held(2, bot, half, dtype=jnp.bfloat16), (student, teacher, index))


def join_kernel(n_in, n_after, firsts, bot, *refs):
    blocks = []
    for ref in refs[:n_in]:
        blocks += [ref] if len(ref.shape) == 3 else [ref.at[i] for i in range(ref.shape[0])]
    for first, ref in zip(firsts, refs[n_in + n_after:]):
        for i in range(ref.shape[0]):
            block = blocks[first + i][:, :bot, :]
            ref[i, :, :bot, :] = block
            if ref.shape[2] > bot:
                ref[i, :, bot:, :] = block[:, :ref.shape[2] - bot]


def join(parts, outs, after, bot):
    width = parts[0].shape[-1]
    shapes = [held(count, 2, rows, width, dtype=jnp.bfloat16) for _, count, rows in outs]
    kernel = functools.partial(join_kernel, len(parts), len(after), [first for first, _, _ in outs], bot)
    return call(kernel, "join", shapes, (*parts, *after), in_specs=[ON_CHIP] * len(parts) + [IN_HBM] * len(after))


def log_sum(parts):
    top = functools.reduce(jnp.maximum, parts)
    return top + jnp.log2(sum(jnp.exp2(part - top) for part in parts))


def combine(parts):
    half = parts[0].shape[0] // 2
    return sum(part[:half] for part in parts), log_sum([part[half:] for part in parts])


def slot(k, n):
    return lax.axis_index("fsdp") ^ k if n <= DIRECT else k


def score_kernel(part, n_feats, *refs):
    last = part == 3
    before, refs = (refs[:3], refs[3:]) if last else ((), refs)
    feats_refs, (ws_ref, wt_ref, peak_ref, *refs) = refs[:n_feats], refs[n_feats:]
    blocks = [ref.at[i] for ref in feats_refs for i in range(ref.shape[0])]
    exp_ref, unit_ref, total_ref, *mine = refs[1:] if part else refs
    own_ref = mine[0] if last else total_ref
    n, (_, bot, width) = len(blocks), blocks[0].shape
    cols = ws_ref.shape[0]
    step = min(STEP, cols)
    per = max(1, min(n, GROUP // width))
    row = lax.broadcasted_iota(jnp.int32, (DEPTH - bot, per * width), 0)
    for which, w_ref, gain in ((0, ws_ref, GAIN_S), (1, wt_ref, GAIN_T)):
        base = (2 * part + which) * n * width
        extra = jnp.where(row < 3 * which, 1.0, 0.0).astype(jnp.bfloat16)
        for group in range(n // per):
            unit = jnp.concatenate([blocks[group * per + k][which] for k in range(per)], axis=1)
            lanes = slice(group * per * width, (group + 1) * per * width)
            if which == 0:
                unit_ref[lanes, :] = unit.T
            stationary = jnp.concatenate([unit, extra], axis=0)
            total = jnp.zeros((8, per * width), jnp.float32)
            for at in range(0, cols, step):
                score = jnp.dot(w_ref[at:at + step, :], stationary, preferred_element_type=jnp.float32)
                exps = jnp.exp2(score * gain)
                total = total + jnp.sum(exps.reshape(step // 8, 8, per * width), axis=0)
                exp_ref[at:at + step, base + lanes.start:base + lanes.stop] = exps.astype(jnp.bfloat16)
            total = jnp.sum(total, axis=0, keepdims=True)
            if which == 1:
                total = jnp.log2(total) + GAIN_T * peak_ref[:, :1]
            own_ref[which:which + 1, lanes] = total
    if not last:
        return
    dp, _, core = here()
    own, pair, other = before
    parts = ((own, other), (pair, own_ref))
    rows = []
    for which in (0, 1):
        for half in (0, 1):
            pieces = []
            for view in (0, 1):
                first = (dp == view) if which == 0 else (dp != view)
                for place in range(n):
                    at = pl.ds(pl.multiple_of(slot(place, n) * width, width), width)
                    read = [[part[which:which + 1, at] for part in side] for side in parts]
                    mine, theirs = [jnp.where(first, *side) for side in read]
                    pieces.append(jnp.where(core == half, mine, theirs))
            rows.append(jnp.concatenate(pieces, axis=1))
    total_ref[...] = jnp.concatenate(rows, axis=0)


def scores(part, feats, weights, before=(), exps=None):
    _, _, bot, width = feats[0].shape
    cols, rows = weights[0].shape[0], sum(part.shape[0] for part in feats) * width
    args = (*before, *feats, *weights, *([exps] if part else []))
    return call(
        functools.partial(score_kernel, part, len(feats)),
        "scores",
        [
            held(cols, 8 * rows, dtype=jnp.bfloat16),
            held(rows, bot, dtype=jnp.bfloat16),
            held(4, 2 * rows) if part == 3 else held(2, rows),
        ],
        args,
        in_specs=[ON_CHIP] * (len(args) - bool(part)) + [IN_HBM] * bool(part),
        input_output_aliases={len(args) - 1: 0} if part else {},
        scratch_shapes=[held(2, rows)] if part == 3 else [],
    )


def relay_kernel(n_in, *refs):
    parts = [ref[...] for ref in refs[:n_in]]
    if len(parts[0].shape) == 3:
        parts = [parts[0][i] for i in range(parts[0].shape[0])]
    refs[-1][...] = jnp.concatenate(combine(parts), axis=0)


def add_up(parts):
    return call(functools.partial(relay_kernel, len(parts)), "relay", held(*parts[0].shape[-2:]), parts)


def exchange(total, axes, first, second):
    sizes = [lax.axis_size(axis) for axis in axes]
    proto = axes.index("proto")
    places = [(i, j) for i in range(sizes[0]) for j in range(sizes[1])]

    def permute(step):
        flat = lambda place: place[0] * sizes[1] + place[1]
        pairs = []
        for place in places:
            up = step(place[proto] % 2)
            pairs.append((flat(place), flat((place[0] ^ up[0], place[1] ^ up[1]))))
        return lax.ppermute(total, axes, pairs)

    mine = permute(first)
    return add_up([total, mine, swap(mine, "proto"), permute(second)])


def across(total, up, over):
    n_proto, n_dp = lax.axis_size("proto"), lax.axis_size("dp")
    places = [(p, d) for p in range(n_proto) for d in range(n_dp)]
    pairs = [(p * n_dp + d, (p ^ up) * n_dp + (d ^ over)) for p, d in places]
    return lax.ppermute(total, ("proto", "dp"), pairs)


def add_up_chip_and_across(total):
    n_proto, n_dp = lax.axis_size("proto"), lax.axis_size("dp")
    total = add_up([total, swap(total, "proto")])
    if n_proto == 4 and n_dp == 2:
        return exchange(total, ("proto", "dp"), lambda odd: (2 * odd, 1), lambda odd: (2, 0))
    steps = [(up, over) for up in range(0, n_proto, 2) for over in range(n_dp)][1:]
    return add_up([total, *[across(total, *step) for step in steps]])


def add_up_along(total):
    n = lax.axis_size("fsdp")
    if n == 4:
        return exchange(total, ("fsdp", "proto"), lambda odd: (2 + odd, 0), lambda odd: (1, 0))
    if n <= DIRECT:
        return add_up([total, *[swap(total, "fsdp", k) for k in range(1, n)]])
    return add_up([lax.all_to_all(jnp.broadcast_to(total[None], (n, *total.shape)), "fsdp", 0, 0, tiled=True)])


def grad_kernel(total_ref, peak_ref, weight_unit, weight_scale, *refs):
    units, exp_ref, out_hbm, scales, feats, *derivs, buf, sems = refs[:4], *refs[4:]
    dp, _, core = here()
    scales[0:2, :] = 10.0 / total_ref[0:2, :]
    scales[2:4, :] = 10.0 * jnp.exp2(GAIN_T * peak_ref[:, :1] - total_ref[2:4, :])
    rows = units[0].shape[0]
    width = 128
    n = rows // width
    factors = []
    for part in range(4):
        view, half = divmod(part, 2)
        base = (dp ^ view) * rows
        at = [pl.ds(pl.multiple_of(base + slot(k, n) * width, width), width) for k in range(n)]
        for which in (0, 1):
            picked = [
                jnp.where(core == half, scales[2 * which:2 * which + 1, where], scales[2 * which + 1:2 * which + 2, where])
                for where in at
            ]
            factors.append(jnp.concatenate(picked, axis=1).astype(jnp.bfloat16))
    for part, unit in enumerate(units):
        feats[part * rows:(part + 1) * rows, :] = unit[...]
    chunks, _, step = buf.shape
    stores = []

    def derive(i):
        at = slice(i * step, (i + 1) * step)
        for part in range(4):
            lies_s, lies_t = 2 * part * rows, (2 * (part ^ 2) + 1) * rows
            probs_s = exp_ref[at, lies_s:lies_s + rows] * factors[2 * part]
            probs_t = exp_ref[at, lies_t:lies_t + rows] * factors[2 * part + 1]
            derivs[i % 2][:, part * rows:(part + 1) * rows] = probs_s - probs_t

    derive(0)
    for i in range(chunks):
        if i + 1 < chunks:
            derive(i + 1)
        at = slice(i * step, (i + 1) * step)
        grad = jnp.dot(derivs[i % 2][...], feats[...], preferred_element_type=jnp.float32).T
        unit = weight_unit[:, at]
        proj = unit * jnp.sum(unit * grad, axis=0, keepdims=True)
        buf[i] = (grad - proj) * weight_scale[:, at]
        stores.append(pltpu.make_async_copy(buf.at[i], out_hbm.at[:, at], sems.at[i]))
        stores[i].start()
    for store in stores:
        store.wait()


def gradient(total, peak, weight_unit, weight_scale, units, exps):
    cols = exps.shape[0]
    rows, bot = units[0].shape
    step = min(256, cols)
    args = (total, peak, weight_unit, weight_scale, *units, exps)
    return call(
        grad_kernel,
        "gradient",
        pltpu.HBM((bot, cols), jnp.float32),
        args,
        out_specs=IN_HBM,
        scratch_shapes=[
            held(4, 2 * rows),
            held(4 * rows, bot, dtype=jnp.bfloat16),
            *[held(step, 4 * rows, dtype=jnp.bfloat16)] * 2,
            held(cols // step, bot, step),
            pltpu.SemaphoreType.DMA((cols // step,)),
        ],
    )


def shards(teacher_weight, student_weight, teacher_feats, student_feats, pairing, center):
    n_dp, n_fsdp = lax.axis_size("dp"), lax.axis_size("fsdp")
    in_hbm = lambda array: pltpu.with_memory_space_constraint(array, pltpu.HBM)
    teacher_weight, student_weight, center = in_hbm(teacher_weight), in_hbm(student_weight), in_hbm(center[None, :])

    index = swap(pairing, "dp")
    mine = pack(*fetch(in_hbm(student_feats[0].T), in_hbm(teacher_feats[0].T)), index)
    teacher_new, wt, ws, unit, scale, peak = prepare(teacher_weight, student_weight, center, n_dp)
    weights = (ws, wt, peak)
    bot = mine.shape[1]
    if n_fsdp <= DIRECT:
        other = [swap(mine, "dp")]
        along = [swap(mine, "fsdp", k) for k in range(1, n_fsdp)]
        half = n_fsdp // 2
        outs = [(0, n_fsdp, bot), (2, n_fsdp - 2, bot + 16), (0, half, bot), (half, half, bot)]
        own, far, *halves = join([mine, *along], outs, (other[0], peak), bot)
        other += [swap(other[0], "fsdp"), swap(far, "dp")]
    else:
        own = lax.all_to_all(jnp.broadcast_to(mine[None], (n_fsdp, *mine.shape)), "fsdp", 0, 0, tiled=True)
        other, halves = [swap(own, "dp")], [own]
    exps, unit_a, total_a = scores(0, [own], weights)
    exps, unit_b, total_b = scores(1, [swap(half, "proto") for half in halves], weights, exps=exps)
    (other,) = join(other, [(0, n_fsdp, bot)], (total_b,), bot)
    exps, unit_c, total_c = scores(2, [other], weights, exps=exps)
    exps, unit_d, total = scores(3, [swap(other, "proto")], weights, (total_a, total_b, total_c), exps)
    total = add_up_chip_and_across(total)
    total = add_up_along(total)
    units = (unit_a, unit_b, unit_c, unit_d)
    student_grad = gradient(total, peak, unit, scale, units, exps)
    return (teacher_new, student_grad)


def solution(mesh):
    placed = (
        P(None, ("proto", "fsdp")),
        P(None, ("proto", "fsdp")),
        P("dp", "fsdp", None),
        P("dp", "fsdp", None),
        P("dp", "fsdp"),
        P("proto"),
    )
    return jax.shard_map(
        shards,
        mesh=mesh,
        in_specs=placed,
        out_specs=(P(None, ("proto", "fsdp")), P(None, ("proto", "fsdp", "dp"))),
        check_vma=False,
    )
```

```python
import functools
import math

import jax
import jax.numpy as jnp
from jax import lax
from jax.experimental import pallas as pl
from jax.experimental.pallas import tpu as pltpu
from jax.sharding import PartitionSpec as P

EPS = 1e-06
DEPTH = 256
GROUP = 512
STEP = 256
DIRECT = 8
LOG2E = math.log2(math.e)
GAIN_T = LOG2E / 0.04
GAIN_S = LOG2E / 0.1
LIMIT = 24 * 1024 * 1024
ON_CHIP = pl.BlockSpec(memory_space=pltpu.VMEM)
IN_HBM = pl.BlockSpec(memory_space=pl.ANY)


def shape(*dims, dtype=jnp.float32):
    return jax.ShapeDtypeStruct(dims, dtype)


def held(*dims, dtype=jnp.float32):
    return pltpu.VMEM(dims, dtype)


def call(kernel, name, out_shape, args, **more):
    many = isinstance(out_shape, (list, tuple))
    specs = dict(in_specs=[ON_CHIP] * len(args), out_specs=[ON_CHIP] * len(out_shape) if many else ON_CHIP)
    return pl.pallas_call(
        kernel,
        out_shape=out_shape,
        compiler_params=pltpu.CompilerParams(vmem_limit_bytes=LIMIT),
        cost_estimate=pl.CostEstimate(flops=1, bytes_accessed=1, transcendentals=0),
        name=name,
        **{**specs, **more},
    )(*args)


def swap(block, axis, apart=1):
    return lax.ppermute(block, axis, [(i, i ^ apart) for i in range(lax.axis_size(axis))])


def here():
    return lax.axis_index("dp"), lax.axis_index("fsdp"), lax.rem(lax.axis_index("proto"), 2)


def cast_split(row):
    high = row.astype(jnp.bfloat16).astype(jnp.float32)
    mid = (row - high).astype(jnp.bfloat16).astype(jnp.float32)
    return high, mid, row - high - mid


def prep_kernel(n_dp, teacher_hbm, student_hbm, center_hbm, new_hbm, wt_ref, ws_ref, unit_ref, scale_ref, peak_ref, *scratch):
    teacher_buf, student_buf, new_buf, center_buf, in_t, in_s, out, in_c = scratch
    chunks, bot, width = new_buf.shape
    n_own = chunks // n_dp
    dp, fsdp, _ = here()
    order = [*range(n_own - 1), *range(n_own, chunks), n_own - 1]
    own = n_own * width
    at = [slice(i * width, (i + 1) * width) for i in range(n_own)]
    firsts = [lax.rem(dp + i // n_own, n_dp) * own + i % n_own * width for i in range(chunks)]
    far = [pl.ds(pl.multiple_of(first, width), width) for first in firsts]
    start = pl.multiple_of((fsdp * n_dp + dp) * own, 128)
    center_load = pltpu.make_async_copy(center_hbm.at[:, pl.ds(start, own)], center_buf, in_c)
    loads = [
        (
            pltpu.make_async_copy(teacher_hbm.at[:, far[i]], teacher_buf.at[i], in_t.at[i]),
            pltpu.make_async_copy(student_hbm.at[:, far[i]], student_buf.at[i], in_s.at[i]),
        )
        for i in range(chunks)
    ]
    stores = [pltpu.make_async_copy(new_buf.at[i], new_hbm.at[:, far[i]], out.at[i]) for i in range(chunks)]
    center_load.start()
    for i in order:
        for load in loads[i]:
            load.start()
    center_load.wait()
    center = center_buf[...]
    peak = jnp.max(-center, axis=1, keepdims=True)
    peak_ref[...] = jnp.broadcast_to(peak, peak_ref.shape)
    splits = cast_split(-center - peak)
    row = lax.broadcasted_iota(jnp.int32, (DEPTH - bot, width), 0)
    zero = jnp.zeros((DEPTH - bot, width), jnp.float32)
    for i in order:
        for load in loads[i]:
            load.wait()
        student = student_buf[i]
        new = 0.994 * teacher_buf[i] + 0.006 * student
        new_buf[i] = new
        stores[i].start()
        if i >= n_own:
            continue
        high, mid, low = [part[:, at[i]] for part in splits]
        extra = jnp.where(row == 0, high, jnp.where(row == 1, mid, jnp.where(row == 2, low, zero)))
        scale = lax.rsqrt(jnp.sum(student * student, axis=0, keepdims=True) + EPS)
        unit_s = student * scale
        unit_t = new * lax.rsqrt(jnp.sum(new * new, axis=0, keepdims=True) + EPS)
        wt_ref[at[i], :] = jnp.concatenate([unit_t, extra], axis=0).astype(jnp.bfloat16).T
        ws_ref[at[i], :] = jnp.concatenate([unit_s, zero], axis=0).astype(jnp.bfloat16).T
        unit_ref[:, at[i]] = unit_s
        scale_ref[:, at[i]] = scale
    for store in stores:
        store.wait()


def prepare(teacher_weight, student_weight, center, n_dp):
    bot, cols = teacher_weight.shape
    own = cols // n_dp
    width = min(512, own)
    chunks = cols // width
    return call(
        functools.partial(prep_kernel, n_dp),
        "prep",
        [
            pltpu.HBM((bot, cols), jnp.float32),
            held(own, DEPTH, dtype=jnp.bfloat16),
            held(own, DEPTH, dtype=jnp.bfloat16),
            held(bot, own),
            held(1, own),
            held(1, 128),
        ],
        (teacher_weight, student_weight, center),
        in_specs=[IN_HBM] * 3,
        out_specs=[IN_HBM] + [ON_CHIP] * 5,
        scratch_shapes=[held(chunks, bot, width)] * 3
        + [held(1, own)]
        + [pltpu.SemaphoreType.DMA((chunks,))] * 3
        + [pltpu.SemaphoreType.DMA],
    )


def fetch_kernel(student_hbm, teacher_hbm, student_ref, teacher_ref, sems):
    half = student_ref.shape[1]
    side = pl.ds(pl.multiple_of(here()[2] * half, half), half)
    loads = [
        pltpu.make_async_copy(student_hbm.at[:, side], student_ref, sems.at[0]),
        pltpu.make_async_copy(teacher_hbm, teacher_ref, sems.at[1]),
    ]
    for load in loads:
        load.start()
    for load in loads:
        load.wait()


def fetch(student, teacher):
    bot, crops = student.shape
    return call(
        fetch_kernel,
        "fetch",
        [held(bot, crops // 2, dtype=jnp.bfloat16), held(bot, crops, dtype=jnp.bfloat16)],
        (student, teacher),
        in_specs=[IN_HBM] * 2,
        scratch_shapes=[pltpu.SemaphoreType.DMA((2,))],
    )


def normalize(values):
    return (values * lax.rsqrt(jnp.sum(values * values, axis=0, keepdims=True) + EPS)).astype(jnp.bfloat16)


def pack_kernel(student_ref, teacher_ref, index_ref, out_ref):
    half = out_ref.shape[2]
    lower = here()[2] == 0
    out_ref[0] = normalize(student_ref[...].astype(jnp.float32))
    index = jnp.where(lower, index_ref[:, :half], index_ref[:, half:])
    row = lax.broadcasted_iota(jnp.int32, (teacher_ref.shape[1], half), 0)
    pick = jnp.where(row == index, 1.0, 0.0).astype(jnp.bfloat16)
    out_ref[1] = normalize(jnp.dot(teacher_ref[...], pick, preferred_element_type=jnp.float32))


def pack(student, teacher, index):
    bot, half = student.shape
    return call(pack_kernel, "pack", held(2, bot, half, dtype=jnp.bfloat16), (student, teacher, index))


def join_kernel(n_in, n_after, firsts, bot, *refs):
    blocks = []
    for ref in refs[:n_in]:
        blocks += [ref] if len(ref.shape) == 3 else [ref.at[i] for i in range(ref.shape[0])]
    for first, ref in zip(firsts, refs[n_in + n_after:]):
        for i in range(ref.shape[0]):
            block = blocks[first + i][:, :bot, :]
            ref[i, :, :bot, :] = block
            if ref.shape[2] > bot:
                ref[i, :, bot:, :] = block[:, :ref.shape[2] - bot]


def join(parts, outs, after, bot):
    width = parts[0].shape[-1]
    shapes = [held(count, 2, rows, width, dtype=jnp.bfloat16) for _, count, rows in outs]
    kernel = functools.partial(join_kernel, len(parts), len(after), [first for first, _, _ in outs], bot)
    return call(kernel, "join", shapes, (*parts, *after), in_specs=[ON_CHIP] * len(parts) + [IN_HBM] * len(after))


def log_sum(parts):
    top = functools.reduce(jnp.maximum, parts)
    return top + jnp.log2(sum(jnp.exp2(part - top) for part in parts))


def combine(parts):
    half = parts[0].shape[0] // 2
    return sum(part[:half] for part in parts), log_sum([part[half:] for part in parts])


def slot(k, n):
    return lax.axis_index("fsdp") ^ k if n <= DIRECT else k


def score_kernel(part, n_feats, *refs):
    last = part == 3
    before, refs = (refs[:3], refs[3:]) if last else ((), refs)
    feats_refs, (ws_ref, wt_ref, peak_ref, *refs) = refs[:n_feats], refs[n_feats:]
    blocks = [ref.at[i] for ref in feats_refs for i in range(ref.shape[0])]
    exp_ref, unit_ref, total_ref, *mine = refs[1:] if part else refs
    own_ref = mine[0] if last else total_ref
    n, (_, bot, width) = len(blocks), blocks[0].shape
    cols = ws_ref.shape[0]
    step = min(STEP, cols)
    per = max(1, min(n, GROUP // width))
    row = lax.broadcasted_iota(jnp.int32, (DEPTH - bot, per * width), 0)
    for which, w_ref, gain in ((0, ws_ref, GAIN_S), (1, wt_ref, GAIN_T)):
        base = (2 * part + which) * n * width
        extra = jnp.where(row < 3 * which, 1.0, 0.0).astype(jnp.bfloat16)
        for group in range(n // per):
            unit = jnp.concatenate([blocks[group * per + k][which] for k in range(per)], axis=1)
            lanes = slice(group * per * width, (group + 1) * per * width)
            if which == 0:
                unit_ref[lanes, :] = unit.T
            stationary = jnp.concatenate([unit, extra], axis=0)
            total = jnp.zeros((8, per * width), jnp.float32)
            for at in range(0, cols, step):
                score = jnp.dot(w_ref[at:at + step, :], stationary, preferred_element_type=jnp.float32)
                exps = jnp.exp2(score * gain)
                total = total + jnp.sum(exps.reshape(step // 8, 8, per * width), axis=0)
                exp_ref[at:at + step, base + lanes.start:base + lanes.stop] = exps.astype(jnp.bfloat16)
            total = jnp.sum(total, axis=0, keepdims=True)
            if which == 1:
                total = jnp.log2(total) + GAIN_T * peak_ref[:, :1]
            own_ref[which:which + 1, lanes] = total
    if not last:
        return
    dp, _, core = here()
    own, pair, other = before
    parts = ((own, other), (pair, own_ref))
    rows = []
    for which in (0, 1):
        for half in (0, 1):
            pieces = []
            for view in (0, 1):
                first = (dp == view) if which == 0 else (dp != view)
                for place in range(n):
                    at = pl.ds(pl.multiple_of(slot(place, n) * width, width), width)
                    read = [[part[which:which + 1, at] for part in side] for side in parts]
                    mine, theirs = [jnp.where(first, *side) for side in read]
                    pieces.append(jnp.where(core == half, mine, theirs))
            rows.append(jnp.concatenate(pieces, axis=1))
    total_ref[...] = jnp.concatenate(rows, axis=0)


def scores(part, feats, weights, before=(), exps=None):
    _, _, bot, width = feats[0].shape
    cols, rows = weights[0].shape[0], sum(part.shape[0] for part in feats) * width
    args = (*before, *feats, *weights, *([exps] if part else []))
    return call(
        functools.partial(score_kernel, part, len(feats)),
        "scores",
        [
            held(cols, 8 * rows, dtype=jnp.bfloat16),
            held(rows, bot, dtype=jnp.bfloat16),
            held(4, 2 * rows) if part == 3 else held(2, rows),
        ],
        args,
        in_specs=[ON_CHIP] * (len(args) - bool(part)) + [IN_HBM] * bool(part),
        input_output_aliases={len(args) - 1: 0} if part else {},
        scratch_shapes=[held(2, rows)] if part == 3 else [],
    )


def relay_kernel(n_in, *refs):
    parts = [ref[...] for ref in refs[:n_in]]
    if len(parts[0].shape) == 3:
        parts = [parts[0][i] for i in range(parts[0].shape[0])]
    refs[-1][...] = jnp.concatenate(combine(parts), axis=0)


def add_up(parts):
    return call(functools.partial(relay_kernel, len(parts)), "relay", held(*parts[0].shape[-2:]), parts)


def exchange(total, axes, first, second):
    sizes = [lax.axis_size(axis) for axis in axes]
    proto = axes.index("proto")
    places = [(i, j) for i in range(sizes[0]) for j in range(sizes[1])]

    def permute(step):
        flat = lambda place: place[0] * sizes[1] + place[1]
        pairs = []
        for place in places:
            up = step(place[proto] % 2)
            pairs.append((flat(place), flat((place[0] ^ up[0], place[1] ^ up[1]))))
        return lax.ppermute(total, axes, pairs)

    mine = permute(first)
    return add_up([total, mine, swap(mine, "proto"), permute(second)])


def across(total, up, over):
    n_proto, n_dp = lax.axis_size("proto"), lax.axis_size("dp")
    places = [(p, d) for p in range(n_proto) for d in range(n_dp)]
    pairs = [(p * n_dp + d, (p ^ up) * n_dp + (d ^ over)) for p, d in places]
    return lax.ppermute(total, ("proto", "dp"), pairs)


def add_up_chip(total):
    return add_up([total, swap(total, "proto")])


def add_up_across(total):
    n_proto, n_dp = lax.axis_size("proto"), lax.axis_size("dp")
    if n_proto == 4 and n_dp == 2:
        return exchange(total, ("proto", "dp"), lambda odd: (2 * odd, 1), lambda odd: (2, 0))
    steps = [(up, over) for up in range(0, n_proto, 2) for over in range(n_dp)][1:]
    return add_up([total, *[across(total, *step) for step in steps]])


def add_up_along(total):
    n = lax.axis_size("fsdp")
    if n == 4:
        return exchange(total, ("fsdp", "proto"), lambda odd: (2 + odd, 0), lambda odd: (1, 0))
    if n <= DIRECT:
        return add_up([total, *[swap(total, "fsdp", k) for k in range(1, n)]])
    return add_up([lax.all_to_all(jnp.broadcast_to(total[None], (n, *total.shape)), "fsdp", 0, 0, tiled=True)])


def grad_kernel(total_ref, peak_ref, weight_unit, weight_scale, *refs):
    units, exp_ref, out_hbm, scales, feats, *derivs, buf, sems = refs[:4], *refs[4:]
    dp, _, core = here()
    scales[0:2, :] = 10.0 / total_ref[0:2, :]
    scales[2:4, :] = 10.0 * jnp.exp2(GAIN_T * peak_ref[:, :1] - total_ref[2:4, :])
    rows = units[0].shape[0]
    width = 128
    n = rows // width
    factors = []
    for part in range(4):
        view, half = divmod(part, 2)
        base = (dp ^ view) * rows
        at = [pl.ds(pl.multiple_of(base + slot(k, n) * width, width), width) for k in range(n)]
        for which in (0, 1):
            picked = [
                jnp.where(core == half, scales[2 * which:2 * which + 1, where], scales[2 * which + 1:2 * which + 2, where])
                for where in at
            ]
            factors.append(jnp.concatenate(picked, axis=1).astype(jnp.bfloat16))
    for part, unit in enumerate(units):
        feats[part * rows:(part + 1) * rows, :] = unit[...]
    chunks, _, step = buf.shape
    stores = []

    def derive(i):
        at = slice(i * step, (i + 1) * step)
        for part in range(4):
            lies_s, lies_t = 2 * part * rows, (2 * (part ^ 2) + 1) * rows
            probs_s = exp_ref[at, lies_s:lies_s + rows] * factors[2 * part]
            probs_t = exp_ref[at, lies_t:lies_t + rows] * factors[2 * part + 1]
            derivs[i % 2][:, part * rows:(part + 1) * rows] = probs_s - probs_t

    derive(0)
    for i in range(chunks):
        if i + 1 < chunks:
            derive(i + 1)
        at = slice(i * step, (i + 1) * step)
        grad = jnp.dot(derivs[i % 2][...], feats[...], preferred_element_type=jnp.float32).T
        unit = weight_unit[:, at]
        proj = unit * jnp.sum(unit * grad, axis=0, keepdims=True)
        buf[i] = (grad - proj) * weight_scale[:, at]
        stores.append(pltpu.make_async_copy(buf.at[i], out_hbm.at[:, at], sems.at[i]))
        stores[i].start()
    for store in stores:
        store.wait()


def gradient(total, peak, weight_unit, weight_scale, units, exps):
    cols = exps.shape[0]
    rows, bot = units[0].shape
    step = min(256, cols)
    args = (total, peak, weight_unit, weight_scale, *units, exps)
    return call(
        grad_kernel,
        "gradient",
        pltpu.HBM((bot, cols), jnp.float32),
        args,
        out_specs=IN_HBM,
        scratch_shapes=[
            held(4, 2 * rows),
            held(4 * rows, bot, dtype=jnp.bfloat16),
            *[held(step, 4 * rows, dtype=jnp.bfloat16)] * 2,
            held(cols // step, bot, step),
            pltpu.SemaphoreType.DMA((cols // step,)),
        ],
    )


def shards(teacher_weight, student_weight, teacher_feats, student_feats, pairing, center):
    n_dp, n_fsdp = lax.axis_size("dp"), lax.axis_size("fsdp")
    in_hbm = lambda array: pltpu.with_memory_space_constraint(array, pltpu.HBM)
    teacher_weight, student_weight, center = in_hbm(teacher_weight), in_hbm(student_weight), in_hbm(center[None, :])

    index = swap(pairing, "dp")
    mine = pack(*fetch(in_hbm(student_feats[0].T), in_hbm(teacher_feats[0].T)), index)
    teacher_new, wt, ws, unit, scale, peak = prepare(teacher_weight, student_weight, center, n_dp)
    weights = (ws, wt, peak)
    bot = mine.shape[1]
    if n_fsdp <= DIRECT:
        other = [swap(mine, "dp")]
        along = [swap(mine, "fsdp", k) for k in range(1, n_fsdp)]
        half = n_fsdp // 2
        outs = [(0, n_fsdp, bot), (2, n_fsdp - 2, bot + 16), (0, half, bot), (half, half, bot)]
        own, far, *halves = join([mine, *along], outs, (other[0], peak), bot)
        other += [swap(other[0], "fsdp"), swap(far, "dp")]
    else:
        own = lax.all_to_all(jnp.broadcast_to(mine[None], (n_fsdp, *mine.shape)), "fsdp", 0, 0, tiled=True)
        other, halves = [swap(own, "dp")], [own]
    exps, unit_a, total_a = scores(0, [own], weights)
    exps, unit_b, total_b = scores(1, [swap(half, "proto") for half in halves], weights, exps=exps)
    (other,) = join(other, [(0, n_fsdp, bot)], (total_b,), bot)
    exps, unit_c, total_c = scores(2, [other], weights, exps=exps)
    exps, unit_d, total = scores(3, [swap(other, "proto")], weights, (total_a, total_b, total_c), exps)
    total = add_up_across(add_up_along(add_up_chip(total)))
    units = (unit_a, unit_b, unit_c, unit_d)
    student_grad = gradient(total, peak, unit, scale, units, exps)
    return (teacher_new, student_grad)


def solution(mesh):
    placed = (
        P(None, ("proto", "fsdp")),
        P(None, ("proto", "fsdp")),
        P("dp", "fsdp", None),
        P("dp", "fsdp", None),
        P("dp", "fsdp"),
        P("proto"),
    )
    return jax.shard_map(
        shards,
        mesh=mesh,
        in_specs=placed,
        out_specs=(P(None, ("proto", "fsdp")), P(None, ("proto", "fsdp", "dp"))),
        check_vma=False,
    )
```

```python
import functools
import math

import jax
import jax.numpy as jnp
from jax import lax
from jax.experimental import pallas as pl
from jax.experimental.pallas import tpu as pltpu
from jax.sharding import PartitionSpec as P

EPS = 1e-06
DEPTH = 256
GROUP = 512
STEP = 256
DIRECT = 8
LOG2E = math.log2(math.e)
GAIN_T = LOG2E / 0.04
GAIN_S = LOG2E / 0.1
LIMIT = 24 * 1024 * 1024
ON_CHIP = pl.BlockSpec(memory_space=pltpu.VMEM)
IN_HBM = pl.BlockSpec(memory_space=pl.ANY)


def shape(*dims, dtype=jnp.float32):
    return jax.ShapeDtypeStruct(dims, dtype)


def held(*dims, dtype=jnp.float32):
    return pltpu.VMEM(dims, dtype)


def call(kernel, name, out_shape, args, **more):
    many = isinstance(out_shape, (list, tuple))
    specs = dict(in_specs=[ON_CHIP] * len(args), out_specs=[ON_CHIP] * len(out_shape) if many else ON_CHIP)
    return pl.pallas_call(
        kernel,
        out_shape=out_shape,
        compiler_params=pltpu.CompilerParams(vmem_limit_bytes=LIMIT),
        cost_estimate=pl.CostEstimate(flops=1, bytes_accessed=1, transcendentals=0),
        name=name,
        **{**specs, **more},
    )(*args)


def swap(block, axis, apart=1):
    return lax.ppermute(block, axis, [(i, i ^ apart) for i in range(lax.axis_size(axis))])


def here():
    return lax.axis_index("dp"), lax.axis_index("fsdp"), lax.rem(lax.axis_index("proto"), 2)


def cast_split(row):
    high = row.astype(jnp.bfloat16).astype(jnp.float32)
    mid = (row - high).astype(jnp.bfloat16).astype(jnp.float32)
    return high, mid, row - high - mid


def prep_kernel(n_dp, n_own, teacher_hbm, student_hbm, center_hbm, new_hbm, wt_ref, ws_ref, unit_ref, scale_ref, peak_ref, *scratch):
    teacher_buf, student_buf, new_buf, center_buf, in_t, in_s, out, in_c = scratch
    chunks, bot, width = new_buf.shape
    dp, fsdp, _ = here()
    own = n_own * width
    at = [slice(i * width, (i + 1) * width) for i in range(n_own)]
    firsts = [dp * own + i * width for i in range(n_own)]
    more = (chunks - n_own) // (n_dp - 1) if n_dp > 1 else 0
    firsts += [lax.rem(dp + 1 + i // more, n_dp) * own + (n_own - more + i % more) * width for i in range(chunks - n_own)]
    far = [pl.ds(pl.multiple_of(first, width), width) for first in firsts]
    start = pl.multiple_of((fsdp * n_dp + dp) * own, 128)
    center_load = pltpu.make_async_copy(center_hbm.at[:, pl.ds(start, own)], center_buf, in_c)
    loads = [
        (
            pltpu.make_async_copy(teacher_hbm.at[:, far[i]], teacher_buf.at[i], in_t.at[i]),
            pltpu.make_async_copy(student_hbm.at[:, far[i]], student_buf.at[i], in_s.at[i]),
        )
        for i in range(chunks)
    ]
    stores = [pltpu.make_async_copy(new_buf.at[i], new_hbm.at[:, far[i]], out.at[i]) for i in range(chunks)]
    center_load.start()
    for pair in loads:
        for load in pair:
            load.start()
    center_load.wait()
    center = center_buf[...]
    peak = jnp.max(-center, axis=1, keepdims=True)
    peak_ref[...] = jnp.broadcast_to(peak, peak_ref.shape)
    splits = cast_split(-center - peak)
    row = lax.broadcasted_iota(jnp.int32, (DEPTH - bot, width), 0)
    zero = jnp.zeros((DEPTH - bot, width), jnp.float32)
    for i in range(chunks):
        for load in loads[i]:
            load.wait()
        student = student_buf[i]
        new = 0.994 * teacher_buf[i] + 0.006 * student
        new_buf[i] = new
        stores[i].start()
        if i >= n_own:
            continue
        high, mid, low = [part[:, at[i]] for part in splits]
        extra = jnp.where(row == 0, high, jnp.where(row == 1, mid, jnp.where(row == 2, low, zero)))
        scale = lax.rsqrt(jnp.sum(student * student, axis=0, keepdims=True) + EPS)
        unit_s = student * scale
        unit_t = new * lax.rsqrt(jnp.sum(new * new, axis=0, keepdims=True) + EPS)
        wt_ref[at[i], :] = jnp.concatenate([unit_t, extra], axis=0).astype(jnp.bfloat16).T
        ws_ref[at[i], :] = jnp.concatenate([unit_s, zero], axis=0).astype(jnp.bfloat16).T
        unit_ref[:, at[i]] = unit_s
        scale_ref[:, at[i]] = scale
    for store in stores:
        store.wait()


def prepare(teacher_weight, student_weight, center, n_dp, more):
    bot, cols = teacher_weight.shape
    own = cols // n_dp
    width = math.gcd(min(512, own), more)
    n_own = own // width
    chunks = n_own + (n_dp - 1) * (more // width)
    return call(
        functools.partial(prep_kernel, n_dp, n_own),
        "prep",
        [
            pltpu.HBM((bot, cols), jnp.float32),
            held(own, DEPTH, dtype=jnp.bfloat16),
            held(own, DEPTH, dtype=jnp.bfloat16),
            held(bot, own),
            held(1, own),
            held(1, 128),
        ],
        (teacher_weight, student_weight, center),
        in_specs=[IN_HBM] * 3,
        out_specs=[IN_HBM] + [ON_CHIP] * 5,
        scratch_shapes=[held(chunks, bot, width)] * 3
        + [held(1, own)]
        + [pltpu.SemaphoreType.DMA((chunks,))] * 3
        + [pltpu.SemaphoreType.DMA],
    )


def rest_kernel(lo, hi, own, teacher_hbm, student_hbm, after, before_hbm, new_hbm, done_ref, *scratch):
    teacher_buf, student_buf, new_buf, in_t, in_s, out = scratch
    width = hi - lo
    parts = teacher_hbm.shape[1] // own - 1
    dp = here()[0]
    done_ref[...] = jnp.zeros_like(done_ref)
    far = [pl.ds(pl.multiple_of(lax.rem(dp + 1 + i, parts + 1) * own + lo, 128), width) for i in range(parts)]
    loads = [
        (
            pltpu.make_async_copy(teacher_hbm.at[:, far[i]], teacher_buf.at[i], in_t.at[i]),
            pltpu.make_async_copy(student_hbm.at[:, far[i]], student_buf.at[i], in_s.at[i]),
        )
        for i in range(parts)
    ]
    stores = [pltpu.make_async_copy(new_buf.at[i], new_hbm.at[:, far[i]], out.at[i]) for i in range(parts)]
    for pair in loads:
        for load in pair:
            load.start()
    for i in range(parts):
        for load in loads[i]:
            load.wait()
        new_buf[i] = 0.994 * teacher_buf[i] + 0.006 * student_buf[i]
        stores[i].start()
    for store in stores:
        store.wait()


def update_rest(teacher_weight, student_weight, after, new, own, lo, hi):
    bot, cols = teacher_weight.shape
    parts = cols // own - 1
    return call(
        functools.partial(rest_kernel, lo, hi, own),
        "rest",
        [pltpu.HBM((bot, cols), jnp.float32), held(8, 128)],
        (teacher_weight, student_weight, after, new),
        in_specs=[IN_HBM] * 4,
        out_specs=[IN_HBM, ON_CHIP],
        input_output_aliases={3: 0},
        scratch_shapes=[held(parts, bot, hi - lo)] * 3 + [pltpu.SemaphoreType.DMA((parts,))] * 3,
    )


def fetch_kernel(student_hbm, teacher_hbm, student_ref, teacher_ref, sems):
    half = student_ref.shape[1]
    side = pl.ds(pl.multiple_of(here()[2] * half, half), half)
    loads = [
        pltpu.make_async_copy(student_hbm.at[:, side], student_ref, sems.at[0]),
        pltpu.make_async_copy(teacher_hbm, teacher_ref, sems.at[1]),
    ]
    for load in loads:
        load.start()
    for load in loads:
        load.wait()


def fetch(student, teacher):
    bot, crops = student.shape
    return call(
        fetch_kernel,
        "fetch",
        [held(bot, crops // 2, dtype=jnp.bfloat16), held(bot, crops, dtype=jnp.bfloat16)],
        (student, teacher),
        in_specs=[IN_HBM] * 2,
        scratch_shapes=[pltpu.SemaphoreType.DMA((2,))],
    )


def normalize(values):
    return (values * lax.rsqrt(jnp.sum(values * values, axis=0, keepdims=True) + EPS)).astype(jnp.bfloat16)


def pack_kernel(student_ref, teacher_ref, index_ref, out_ref):
    half = out_ref.shape[2]
    lower = here()[2] == 0
    out_ref[0] = normalize(student_ref[...].astype(jnp.float32))
    index = jnp.where(lower, index_ref[:, :half], index_ref[:, half:])
    row = lax.broadcasted_iota(jnp.int32, (teacher_ref.shape[1], half), 0)
    pick = jnp.where(row == index, 1.0, 0.0).astype(jnp.bfloat16)
    out_ref[1] = normalize(jnp.dot(teacher_ref[...], pick, preferred_element_type=jnp.float32))


def pack(student, teacher, index):
    bot, half = student.shape
    return call(pack_kernel, "pack", held(2, bot, half, dtype=jnp.bfloat16), (student, teacher, index))


def join_kernel(n_in, n_after, firsts, bot, *refs):
    refs = refs[n_after:]
    blocks = []
    for ref in refs[:n_in]:
        blocks += [ref] if len(ref.shape) == 3 else [ref.at[i] for i in range(ref.shape[0])]
    for first, ref in zip(firsts, refs[n_in:]):
        for i in range(ref.shape[0]):
            block = blocks[first + i][:, :bot, :]
            ref[i, :, :bot, :] = block
            if ref.shape[2] > bot:
                ref[i, :, bot:, :] = block[:, :ref.shape[2] - bot]


def join(parts, outs, after, bot):
    width = parts[0].shape[-1]
    shapes = [held(count, 2, rows, width, dtype=jnp.bfloat16) for _, count, rows in outs]
    kernel = functools.partial(join_kernel, len(parts), len(after), [first for first, _, _ in outs], bot)
    return call(kernel, "join", shapes, (*after, *parts), in_specs=[IN_HBM] * len(after) + [ON_CHIP] * len(parts))


def log_sum(parts):
    top = functools.reduce(jnp.maximum, parts)
    return top + jnp.log2(sum(jnp.exp2(part - top) for part in parts))


def combine(parts):
    half = parts[0].shape[0] // 2
    return sum(part[:half] for part in parts), log_sum([part[half:] for part in parts])


def slot(k, n):
    return lax.axis_index("fsdp") ^ k if n <= DIRECT else k


def score_kernel(part, n_feats, *refs):
    last = part == 3
    before, refs = (refs[:3], refs[3:]) if last else ((), refs)
    feats_refs, (ws_ref, wt_ref, peak_ref, *refs) = refs[:n_feats], refs[n_feats:]
    blocks = [ref.at[i] for ref in feats_refs for i in range(ref.shape[0])]
    exp_ref, unit_ref, total_ref, *mine = refs[1:] if part else refs
    own_ref = mine[0] if last else total_ref
    n, (_, bot, width) = len(blocks), blocks[0].shape
    cols = ws_ref.shape[0]
    step = min(STEP, cols)
    per = max(1, min(n, GROUP // width))
    row = lax.broadcasted_iota(jnp.int32, (DEPTH - bot, per * width), 0)
    for which, w_ref, gain in ((0, ws_ref, GAIN_S), (1, wt_ref, GAIN_T)):
        base = (2 * part + which) * n * width
        extra = jnp.where(row < 3 * which, 1.0, 0.0).astype(jnp.bfloat16)
        for group in range(n // per):
            unit = jnp.concatenate([blocks[group * per + k][which] for k in range(per)], axis=1)
            lanes = slice(group * per * width, (group + 1) * per * width)
            if which == 0:
                unit_ref[lanes, :] = unit.T
            stationary = jnp.concatenate([unit, extra], axis=0)
            total = jnp.zeros((8, per * width), jnp.float32)
            for at in range(0, cols, step):
                score = jnp.dot(w_ref[at:at + step, :], stationary, preferred_element_type=jnp.float32)
                exps = jnp.exp2(score * gain)
                total = total + jnp.sum(exps.reshape(step // 8, 8, per * width), axis=0)
                exp_ref[at:at + step, base + lanes.start:base + lanes.stop] = exps.astype(jnp.bfloat16)
            total = jnp.sum(total, axis=0, keepdims=True)
            if which == 1:
                total = jnp.log2(total) + GAIN_T * peak_ref[:, :1]
            own_ref[which:which + 1, lanes] = total
    if not last:
        return
    dp, _, core = here()
    own, pair, other = before
    parts = ((own, other), (pair, own_ref))
    rows = []
    for which in (0, 1):
        for half in (0, 1):
            pieces = []
            for view in (0, 1):
                first = (dp == view) if which == 0 else (dp != view)
                for place in range(n):
                    at = pl.ds(pl.multiple_of(slot(place, n) * width, width), width)
                    read = [[part[which:which + 1, at] for part in side] for side in parts]
                    mine, theirs = [jnp.where(first, *side) for side in read]
                    pieces.append(jnp.where(core == half, mine, theirs))
            rows.append(jnp.concatenate(pieces, axis=1))
    total_ref[...] = jnp.concatenate(rows, axis=0)


def scores(part, feats, weights, before=(), exps=None):
    _, _, bot, width = feats[0].shape
    cols, rows = weights[0].shape[0], sum(part.shape[0] for part in feats) * width
    args = (*before, *feats, *weights, *([exps] if part else []))
    return call(
        functools.partial(score_kernel, part, len(feats)),
        "scores",
        [
            held(cols, 8 * rows, dtype=jnp.bfloat16),
            held(rows, bot, dtype=jnp.bfloat16),
            held(4, 2 * rows) if part == 3 else held(2, rows),
        ],
        args,
        in_specs=[ON_CHIP] * (len(args) - bool(part)) + [IN_HBM] * bool(part),
        input_output_aliases={len(args) - 1: 0} if part else {},
        scratch_shapes=[held(2, rows)] if part == 3 else [],
    )


def relay_kernel(n_in, *refs):
    parts = [ref[...] for ref in refs[:n_in]]
    if len(parts[0].shape) == 3:
        parts = [parts[0][i] for i in range(parts[0].shape[0])]
    refs[-1][...] = jnp.concatenate(combine(parts), axis=0)


def add_up(parts, after=()):
    specs = [ON_CHIP] * len(parts) + [IN_HBM] * len(after)
    out = held(*parts[0].shape[-2:])
    return call(functools.partial(relay_kernel, len(parts)), "relay", out, (*parts, *after), in_specs=specs)


def hold_kernel(in_ref, after, out_ref):
    out_ref[...] = in_ref[...]


def hold(array, after):
    return call(hold_kernel, "hold", held(*array.shape), (array, after), in_specs=[ON_CHIP, IN_HBM])


def exchange(total, axes, first, second, after=()):
    sizes = [lax.axis_size(axis) for axis in axes]
    proto = axes.index("proto")
    places = [(i, j) for i in range(sizes[0]) for j in range(sizes[1])]

    def permute(step):
        flat = lambda place: place[0] * sizes[1] + place[1]
        pairs = []
        for place in places:
            up = step(place[proto] % 2)
            pairs.append((flat(place), flat((place[0] ^ up[0], place[1] ^ up[1]))))
        return lax.ppermute(total, axes, pairs)

    mine = permute(first)
    passed = hold(mine, *after) if after else mine
    return add_up([total, mine, swap(passed, "proto"), permute(second)])


def across(total, up, over):
    n_proto, n_dp = lax.axis_size("proto"), lax.axis_size("dp")
    places = [(p, d) for p in range(n_proto) for d in range(n_dp)]
    pairs = [(p * n_dp + d, (p ^ up) * n_dp + (d ^ over)) for p, d in places]
    return lax.ppermute(total, ("proto", "dp"), pairs)


def add_up_chip_and_across(total):
    n_proto, n_dp = lax.axis_size("proto"), lax.axis_size("dp")
    total = add_up([total, swap(total, "proto")])
    if n_proto == 4 and n_dp == 2:
        return exchange(total, ("proto", "dp"), lambda odd: (2 * odd, 1), lambda odd: (2, 0))
    steps = [(up, over) for up in range(0, n_proto, 2) for over in range(n_dp)][1:]
    return add_up([total, *[across(total, *step) for step in steps]])


def add_up_along(total, after):
    n = lax.axis_size("fsdp")
    if n == 4:
        return exchange(total, ("fsdp", "proto"), lambda odd: (2 + odd, 0), lambda odd: (1, 0), after)
    if n <= DIRECT:
        return add_up([total, *[swap(total, "fsdp", k) for k in range(1, n)]], after)
    return add_up([lax.all_to_all(jnp.broadcast_to(total[None], (n, *total.shape)), "fsdp", 0, 0, tiled=True)], after)


def grad_kernel(total_ref, peak_ref, weight_unit, weight_scale, *refs):
    units, exp_ref, out_hbm, scales, feats, *derivs, buf, sems = refs[:4], *refs[4:]
    dp, _, core = here()
    scales[0:2, :] = 10.0 / total_ref[0:2, :]
    scales[2:4, :] = 10.0 * jnp.exp2(GAIN_T * peak_ref[:, :1] - total_ref[2:4, :])
    rows = units[0].shape[0]
    width = 128
    n = rows // width
    factors = []
    for part in range(4):
        view, half = divmod(part, 2)
        base = (dp ^ view) * rows
        at = [pl.ds(pl.multiple_of(base + slot(k, n) * width, width), width) for k in range(n)]
        for which in (0, 1):
            picked = [
                jnp.where(core == half, scales[2 * which:2 * which + 1, where], scales[2 * which + 1:2 * which + 2, where])
                for where in at
            ]
            factors.append(jnp.concatenate(picked, axis=1).astype(jnp.bfloat16))
    for part, unit in enumerate(units):
        feats[part * rows:(part + 1) * rows, :] = unit[...]
    chunks, _, step = buf.shape
    stores = []

    def derive(i):
        at = slice(i * step, (i + 1) * step)
        for part in range(4):
            lies_s, lies_t = 2 * part * rows, (2 * (part ^ 2) + 1) * rows
            probs_s = exp_ref[at, lies_s:lies_s + rows] * factors[2 * part]
            probs_t = exp_ref[at, lies_t:lies_t + rows] * factors[2 * part + 1]
            derivs[i % 2][:, part * rows:(part + 1) * rows] = probs_s - probs_t

    derive(0)
    for i in range(chunks):
        if i + 1 < chunks:
            derive(i + 1)
        at = slice(i * step, (i + 1) * step)
        grad = jnp.dot(derivs[i % 2][...], feats[...], preferred_element_type=jnp.float32).T
        unit = weight_unit[:, at]
        proj = unit * jnp.sum(unit * grad, axis=0, keepdims=True)
        buf[i] = (grad - proj) * weight_scale[:, at]
        stores.append(pltpu.make_async_copy(buf.at[i], out_hbm.at[:, at], sems.at[i]))
        stores[i].start()
    for store in stores:
        store.wait()


def gradient(total, peak, weight_unit, weight_scale, units, exps):
    cols = exps.shape[0]
    rows, bot = units[0].shape
    step = min(256, cols)
    args = (total, peak, weight_unit, weight_scale, *units, exps)
    return call(
        grad_kernel,
        "gradient",
        pltpu.HBM((bot, cols), jnp.float32),
        args,
        out_specs=IN_HBM,
        scratch_shapes=[
            held(4, 2 * rows),
            held(4 * rows, bot, dtype=jnp.bfloat16),
            *[held(step, 4 * rows, dtype=jnp.bfloat16)] * 2,
            held(cols // step, bot, step),
            pltpu.SemaphoreType.DMA((cols // step,)),
        ],
    )


def shards(teacher_weight, student_weight, teacher_feats, student_feats, pairing, center):
    n_dp, n_fsdp = lax.axis_size("dp"), lax.axis_size("fsdp")
    in_hbm = lambda array: pltpu.with_memory_space_constraint(array, pltpu.HBM)
    teacher_weight, student_weight, center = in_hbm(teacher_weight), in_hbm(student_weight), in_hbm(center[None, :])

    index = swap(pairing, "dp")
    mine = pack(*fetch(in_hbm(student_feats[0].T), in_hbm(teacher_feats[0].T)), index)
    own_cols = teacher_weight.shape[1] // n_dp
    middle = own_cols // 2
    new, wt, ws, unit, scale, peak = prepare(teacher_weight, student_weight, center, n_dp, own_cols - middle)
    weights = (ws, wt, peak)
    bot = mine.shape[1]
    if n_fsdp <= DIRECT:
        other = [swap(mine, "dp")]
        along = [swap(mine, "fsdp", k) for k in range(1, n_fsdp)]
        half = n_fsdp // 2
        outs = [(0, n_fsdp, bot), (2, n_fsdp - 2, bot + 16), (0, half, bot), (half, half, bot)]
        own, far, *halves = join([mine, *along], outs, (other[0], peak), bot)
        other += [swap(other[0], "fsdp"), swap(far, "dp")]
    else:
        own = lax.all_to_all(jnp.broadcast_to(mine[None], (n_fsdp, *mine.shape)), "fsdp", 0, 0, tiled=True)
        other, halves = [swap(own, "dp")], [own]
    exps, unit_a, total_a = scores(0, [own], weights)
    exps, unit_b, total_b = scores(1, [swap(half, "proto") for half in halves], weights, exps=exps)
    (other,) = join(other, [(0, n_fsdp, bot)], (total_b,), bot)
    exps, unit_c, total_c = scores(2, [other], weights, exps=exps)
    exps, unit_d, total = scores(3, [swap(other, "proto")], weights, (total_a, total_b, total_c), exps)
    total = add_up_chip_and_across(total)
    teacher_new, done = update_rest(teacher_weight, student_weight, total, new, own_cols, 0, middle)
    total = add_up_along(total, (done,))
    units = (unit_a, unit_b, unit_c, unit_d)
    student_grad = gradient(total, peak, unit, scale, units, exps)
    return (teacher_new, student_grad)


def solution(mesh):
    placed = (
        P(None, ("proto", "fsdp")),
        P(None, ("proto", "fsdp")),
        P("dp", "fsdp", None),
        P("dp", "fsdp", None),
        P("dp", "fsdp"),
        P("proto"),
    )
    return jax.shard_map(
        shards,
        mesh=mesh,
        in_specs=placed,
        out_specs=(P(None, ("proto", "fsdp")), P(None, ("proto", "fsdp", "dp"))),
        check_vma=False,
    )
```

```python
import functools
import math

import jax
import jax.numpy as jnp
from jax import lax
from jax.experimental import pallas as pl
from jax.experimental.pallas import tpu as pltpu
from jax.sharding import PartitionSpec as P

EPS = 1e-06
DEPTH = 256
GROUP = 512
STEP = 256
DIRECT = 8
LOG2E = math.log2(math.e)
GAIN_T = LOG2E / 0.04
GAIN_S = LOG2E / 0.1
LIMIT = 24 * 1024 * 1024
ON_CHIP = pl.BlockSpec(memory_space=pltpu.VMEM)
IN_HBM = pl.BlockSpec(memory_space=pl.ANY)


def shape(*dims, dtype=jnp.float32):
    return jax.ShapeDtypeStruct(dims, dtype)


def held(*dims, dtype=jnp.float32):
    return pltpu.VMEM(dims, dtype)


def call(kernel, name, out_shape, args, **more):
    many = isinstance(out_shape, (list, tuple))
    specs = dict(in_specs=[ON_CHIP] * len(args), out_specs=[ON_CHIP] * len(out_shape) if many else ON_CHIP)
    return pl.pallas_call(
        kernel,
        out_shape=out_shape,
        compiler_params=pltpu.CompilerParams(vmem_limit_bytes=LIMIT),
        cost_estimate=pl.CostEstimate(flops=1, bytes_accessed=1, transcendentals=0),
        name=name,
        **{**specs, **more},
    )(*args)


def swap(block, axis, apart=1):
    return lax.ppermute(block, axis, [(i, i ^ apart) for i in range(lax.axis_size(axis))])


def here():
    return lax.axis_index("dp"), lax.axis_index("fsdp"), lax.rem(lax.axis_index("proto"), 2)


def cast_split(row):
    high = row.astype(jnp.bfloat16).astype(jnp.float32)
    mid = (row - high).astype(jnp.bfloat16).astype(jnp.float32)
    return high, mid, row - high - mid


def prep_kernel(n_dp, teacher_hbm, student_hbm, center_hbm, new_hbm, wt_ref, ws_ref, unit_ref, scale_ref, peak_ref, *scratch):
    teacher_buf, student_buf, new_buf, center_buf, in_t, in_s, out, in_c = scratch
    chunks, bot, width = new_buf.shape
    n_own = chunks // n_dp
    dp, fsdp, _ = here()
    order = [*range(n_own - 1), *range(n_own, chunks), n_own - 1]
    own = n_own * width
    at = [slice(i * width, (i + 1) * width) for i in range(n_own)]
    firsts = [lax.rem(dp + i // n_own, n_dp) * own + i % n_own * width for i in range(chunks)]
    far = [pl.ds(pl.multiple_of(first, width), width) for first in firsts]
    start = pl.multiple_of((fsdp * n_dp + dp) * own, 128)
    center_load = pltpu.make_async_copy(center_hbm.at[:, pl.ds(start, own)], center_buf, in_c)
    loads = [
        (
            pltpu.make_async_copy(teacher_hbm.at[:, far[i]], teacher_buf.at[i], in_t.at[i]),
            pltpu.make_async_copy(student_hbm.at[:, far[i]], student_buf.at[i], in_s.at[i]),
        )
        for i in range(chunks)
    ]
    stores = [pltpu.make_async_copy(new_buf.at[i], new_hbm.at[:, far[i]], out.at[i]) for i in range(chunks)]
    center_load.start()
    for i in order:
        for load in loads[i]:
            load.start()
    center_load.wait()
    center = center_buf[...]
    peak = jnp.max(-center, axis=1, keepdims=True)
    peak_ref[...] = jnp.broadcast_to(peak, peak_ref.shape)
    splits = cast_split(-center - peak)
    row = lax.broadcasted_iota(jnp.int32, (DEPTH - bot, width), 0)
    zero = jnp.zeros((DEPTH - bot, width), jnp.float32)
    for i in order:
        for load in loads[i]:
            load.wait()
        student = student_buf[i]
        new = 0.994 * teacher_buf[i] + 0.006 * student
        new_buf[i] = new
        stores[i].start()
        if i >= n_own:
            continue
        high, mid, low = [part[:, at[i]] for part in splits]
        extra = jnp.where(row == 0, high, jnp.where(row == 1, mid, jnp.where(row == 2, low, zero)))
        scale = lax.rsqrt(jnp.sum(student * student, axis=0, keepdims=True) + EPS)
        unit_s = student * scale
        unit_t = new * lax.rsqrt(jnp.sum(new * new, axis=0, keepdims=True) + EPS)
        wt_ref[at[i], :] = jnp.concatenate([unit_t, extra], axis=0).astype(jnp.bfloat16).T
        ws_ref[at[i], :] = jnp.concatenate([unit_s, zero], axis=0).astype(jnp.bfloat16).T
        unit_ref[:, at[i]] = unit_s
        scale_ref[:, at[i]] = scale
    for store in stores:
        store.wait()


def prepare(teacher_weight, student_weight, center, n_dp):
    bot, cols = teacher_weight.shape
    own = cols // n_dp
    width = min(512, own)
    chunks = cols // width
    return call(
        functools.partial(prep_kernel, n_dp),
        "prep",
        [
            pltpu.HBM((bot, cols), jnp.float32),
            held(own, DEPTH, dtype=jnp.bfloat16),
            held(own, DEPTH, dtype=jnp.bfloat16),
            held(bot, own),
            held(1, own),
            held(1, 128),
        ],
        (teacher_weight, student_weight, center),
        in_specs=[IN_HBM] * 3,
        out_specs=[IN_HBM] + [ON_CHIP] * 5,
        scratch_shapes=[held(chunks, bot, width)] * 3
        + [held(1, own)]
        + [pltpu.SemaphoreType.DMA((chunks,))] * 3
        + [pltpu.SemaphoreType.DMA],
    )


def fetch_kernel(student_hbm, teacher_hbm, student_ref, teacher_ref, sems):
    half = student_ref.shape[1]
    side = pl.ds(pl.multiple_of(here()[2] * half, half), half)
    loads = [
        pltpu.make_async_copy(student_hbm.at[:, side], student_ref, sems.at[0]),
        pltpu.make_async_copy(teacher_hbm, teacher_ref, sems.at[1]),
    ]
    for load in loads:
        load.start()
    for load in loads:
        load.wait()


def fetch(student, teacher):
    bot, crops = student.shape
    return call(
        fetch_kernel,
        "fetch",
        [held(bot, crops // 2, dtype=jnp.bfloat16), held(bot, crops, dtype=jnp.bfloat16)],
        (student, teacher),
        in_specs=[IN_HBM] * 2,
        scratch_shapes=[pltpu.SemaphoreType.DMA((2,))],
    )


def normalize(values):
    return (values * lax.rsqrt(jnp.sum(values * values, axis=0, keepdims=True) + EPS)).astype(jnp.bfloat16)


def pack_kernel(student_ref, teacher_ref, index_ref, out_ref):
    half = out_ref.shape[2]
    lower = here()[2] == 0
    out_ref[0] = normalize(student_ref[...].astype(jnp.float32))
    index = jnp.where(lower, index_ref[:, :half], index_ref[:, half:])
    row = lax.broadcasted_iota(jnp.int32, (teacher_ref.shape[1], half), 0)
    pick = jnp.where(row == index, 1.0, 0.0).astype(jnp.bfloat16)
    out_ref[1] = normalize(jnp.dot(teacher_ref[...], pick, preferred_element_type=jnp.float32))


def pack(student, teacher, index):
    bot, half = student.shape
    return call(pack_kernel, "pack", held(2, bot, half, dtype=jnp.bfloat16), (student, teacher, index))


def join_kernel(n_in, n_after, firsts, bot, *refs):
    blocks = []
    for ref in refs[:n_in]:
        blocks += [ref] if len(ref.shape) == 3 else [ref.at[i] for i in range(ref.shape[0])]
    for first, ref in zip(firsts, refs[n_in + n_after:]):
        for i in range(ref.shape[0]):
            block = blocks[first + i][:, :bot, :]
            ref[i, :, :bot, :] = block
            if ref.shape[2] > bot:
                ref[i, :, bot:, :] = block[:, :ref.shape[2] - bot]


def join(parts, outs, after, bot):
    width = parts[0].shape[-1]
    shapes = [held(count, 2, rows, width, dtype=jnp.bfloat16) for _, count, rows in outs]
    kernel = functools.partial(join_kernel, len(parts), len(after), [first for first, _, _ in outs], bot)
    return call(kernel, "join", shapes, (*parts, *after), in_specs=[ON_CHIP] * len(parts) + [IN_HBM] * len(after))


def log_sum(parts):
    top = functools.reduce(jnp.maximum, parts)
    return top + jnp.log2(sum(jnp.exp2(part - top) for part in parts))


def combine(parts):
    half = parts[0].shape[0] // 2
    return sum(part[:half] for part in parts), log_sum([part[half:] for part in parts])


def slot(k, n):
    return lax.axis_index("fsdp") ^ k if n <= DIRECT else k


def score_kernel(part, n_feats, *refs):
    last = part == 3
    before, refs = (refs[:3], refs[3:]) if last else ((), refs)
    feats_refs, (ws_ref, wt_ref, peak_ref, *refs) = refs[:n_feats], refs[n_feats:]
    blocks = [ref.at[i] for ref in feats_refs for i in range(ref.shape[0])]
    exp_ref, unit_ref, total_ref, *mine = refs[1:] if part else refs
    own_ref = mine[0] if last else total_ref
    n, (_, bot, width) = len(blocks), blocks[0].shape
    cols = ws_ref.shape[0]
    step = min(STEP, cols)
    per = max(1, min(n, GROUP // width))
    row = lax.broadcasted_iota(jnp.int32, (DEPTH - bot, per * width), 0)
    for which, w_ref, gain in ((0, ws_ref, GAIN_S), (1, wt_ref, GAIN_T)):
        base = (2 * part + which) * n * width
        extra = jnp.where(row < 3 * which, 1.0, 0.0).astype(jnp.bfloat16)
        for group in range(n // per):
            unit = jnp.concatenate([blocks[group * per + k][which] for k in range(per)], axis=1)
            lanes = slice(group * per * width, (group + 1) * per * width)
            if which == 0:
                unit_ref[lanes, :] = unit.T
            stationary = jnp.concatenate([unit, extra], axis=0)
            total = jnp.zeros((8, per * width), jnp.float32)
            for at in range(0, cols, step):
                score = jnp.dot(w_ref[at:at + step, :], stationary, preferred_element_type=jnp.float32)
                exps = jnp.exp2(score * gain)
                total = total + jnp.sum(exps.reshape(step // 8, 8, per * width), axis=0)
                exp_ref[at:at + step, base + lanes.start:base + lanes.stop] = exps.astype(jnp.bfloat16)
            total = jnp.sum(total, axis=0, keepdims=True)
            if which == 1:
                total = jnp.log2(total) + GAIN_T * peak_ref[:, :1]
            own_ref[which:which + 1, lanes] = total
    if not last:
        return
    dp, _, core = here()
    own, pair, other = before
    parts = ((own, other), (pair, own_ref))
    rows = []
    for which in (0, 1):
        for half in (0, 1):
            pieces = []
            for view in (0, 1):
                first = (dp == view) if which == 0 else (dp != view)
                for place in range(n):
                    at = pl.ds(pl.multiple_of(slot(place, n) * width, width), width)
                    read = [[part[which:which + 1, at] for part in side] for side in parts]
                    mine, theirs = [jnp.where(first, *side) for side in read]
                    pieces.append(jnp.where(core == half, mine, theirs))
            rows.append(jnp.concatenate(pieces, axis=1))
    total_ref[...] = jnp.concatenate(rows, axis=0)


def scores(part, feats, weights, before=(), exps=None):
    _, _, bot, width = feats[0].shape
    cols, rows = weights[0].shape[0], sum(part.shape[0] for part in feats) * width
    args = (*before, *feats, *weights, *([exps] if part else []))
    return call(
        functools.partial(score_kernel, part, len(feats)),
        "scores",
        [
            held(cols, 8 * rows, dtype=jnp.bfloat16),
            held(rows, bot, dtype=jnp.bfloat16),
            held(4, 2 * rows) if part == 3 else held(2, rows),
        ],
        args,
        in_specs=[ON_CHIP] * (len(args) - bool(part)) + [IN_HBM] * bool(part),
        input_output_aliases={len(args) - 1: 0} if part else {},
        scratch_shapes=[held(2, rows)] if part == 3 else [],
    )


def relay_kernel(n_in, *refs):
    parts = [ref[...] for ref in refs[:n_in]]
    if len(parts[0].shape) == 3:
        parts = [parts[0][i] for i in range(parts[0].shape[0])]
    refs[-1][...] = jnp.concatenate(combine(parts), axis=0)


def add_up(parts):
    return call(functools.partial(relay_kernel, len(parts)), "relay", held(*parts[0].shape[-2:]), parts)


def exchange(total, axes, first, second):
    sizes = [lax.axis_size(axis) for axis in axes]
    proto = axes.index("proto")
    places = [(i, j) for i in range(sizes[0]) for j in range(sizes[1])]

    def permute(step):
        flat = lambda place: place[0] * sizes[1] + place[1]
        pairs = []
        for place in places:
            up = step(place[proto] % 2)
            pairs.append((flat(place), flat((place[0] ^ up[0], place[1] ^ up[1]))))
        return lax.ppermute(total, axes, pairs)

    mine = permute(first)
    return add_up([total, mine, swap(mine, "proto"), permute(second)])


def across(total, up, over):
    n_proto, n_dp = lax.axis_size("proto"), lax.axis_size("dp")
    places = [(p, d) for p in range(n_proto) for d in range(n_dp)]
    pairs = [(p * n_dp + d, (p ^ up) * n_dp + (d ^ over)) for p, d in places]
    return lax.ppermute(total, ("proto", "dp"), pairs)


def add_up_chip_and_across(total):
    n_proto, n_dp = lax.axis_size("proto"), lax.axis_size("dp")
    total = add_up([total, swap(total, "proto")])
    if n_proto == 4 and n_dp == 2:
        return exchange(total, ("proto", "dp"), lambda odd: (2 * odd, 1), lambda odd: (2, 0))
    steps = [(up, over) for up in range(0, n_proto, 2) for over in range(n_dp)][1:]
    return add_up([total, *[across(total, *step) for step in steps]])


def add_up_along(total):
    n = lax.axis_size("fsdp")
    if n == 4:
        return exchange(total, ("fsdp", "proto"), lambda odd: (1 + 2 * odd, 0), lambda odd: (2, 0))
    if n <= DIRECT:
        return add_up([total, *[swap(total, "fsdp", k) for k in range(1, n)]])
    return add_up([lax.all_to_all(jnp.broadcast_to(total[None], (n, *total.shape)), "fsdp", 0, 0, tiled=True)])


def grad_kernel(total_ref, peak_ref, weight_unit, weight_scale, *refs):
    units, exp_ref, out_hbm, scales, feats, *derivs, buf, sems = refs[:4], *refs[4:]
    dp, _, core = here()
    scales[0:2, :] = 10.0 / total_ref[0:2, :]
    scales[2:4, :] = 10.0 * jnp.exp2(GAIN_T * peak_ref[:, :1] - total_ref[2:4, :])
    rows = units[0].shape[0]
    width = 128
    n = rows // width
    factors = []
    for part in range(4):
        view, half = divmod(part, 2)
        base = (dp ^ view) * rows
        at = [pl.ds(pl.multiple_of(base + slot(k, n) * width, width), width) for k in range(n)]
        for which in (0, 1):
            picked = [
                jnp.where(core == half, scales[2 * which:2 * which + 1, where], scales[2 * which + 1:2 * which + 2, where])
                for where in at
            ]
            factors.append(jnp.concatenate(picked, axis=1).astype(jnp.bfloat16))
    for part, unit in enumerate(units):
        feats[part * rows:(part + 1) * rows, :] = unit[...]
    chunks, _, step = buf.shape
    stores = []

    def derive(i):
        at = slice(i * step, (i + 1) * step)
        for part in range(4):
            lies_s, lies_t = 2 * part * rows, (2 * (part ^ 2) + 1) * rows
            probs_s = exp_ref[at, lies_s:lies_s + rows] * factors[2 * part]
            probs_t = exp_ref[at, lies_t:lies_t + rows] * factors[2 * part + 1]
            derivs[i % 2][:, part * rows:(part + 1) * rows] = probs_s - probs_t

    derive(0)
    for i in range(chunks):
        if i + 1 < chunks:
            derive(i + 1)
        at = slice(i * step, (i + 1) * step)
        grad = jnp.dot(derivs[i % 2][...], feats[...], preferred_element_type=jnp.float32).T
        unit = weight_unit[:, at]
        proj = unit * jnp.sum(unit * grad, axis=0, keepdims=True)
        buf[i] = (grad - proj) * weight_scale[:, at]
        stores.append(pltpu.make_async_copy(buf.at[i], out_hbm.at[:, at], sems.at[i]))
        stores[i].start()
    for store in stores:
        store.wait()


def gradient(total, peak, weight_unit, weight_scale, units, exps):
    cols = exps.shape[0]
    rows, bot = units[0].shape
    step = min(256, cols)
    args = (total, peak, weight_unit, weight_scale, *units, exps)
    return call(
        grad_kernel,
        "gradient",
        pltpu.HBM((bot, cols), jnp.float32),
        args,
        out_specs=IN_HBM,
        scratch_shapes=[
            held(4, 2 * rows),
            held(4 * rows, bot, dtype=jnp.bfloat16),
            *[held(step, 4 * rows, dtype=jnp.bfloat16)] * 2,
            held(cols // step, bot, step),
            pltpu.SemaphoreType.DMA((cols // step,)),
        ],
    )


def shards(teacher_weight, student_weight, teacher_feats, student_feats, pairing, center):
    n_dp, n_fsdp = lax.axis_size("dp"), lax.axis_size("fsdp")
    in_hbm = lambda array: pltpu.with_memory_space_constraint(array, pltpu.HBM)
    teacher_weight, student_weight, center = in_hbm(teacher_weight), in_hbm(student_weight), in_hbm(center[None, :])

    index = swap(pairing, "dp")
    mine = pack(*fetch(in_hbm(student_feats[0].T), in_hbm(teacher_feats[0].T)), index)
    teacher_new, wt, ws, unit, scale, peak = prepare(teacher_weight, student_weight, center, n_dp)
    weights = (ws, wt, peak)
    bot = mine.shape[1]
    if n_fsdp <= DIRECT:
        other = [swap(mine, "dp")]
        along = [swap(mine, "fsdp", k) for k in range(1, n_fsdp)]
        half = n_fsdp // 2
        outs = [(0, n_fsdp, bot), (2, n_fsdp - 2, bot + 16), (0, half, bot), (half, half, bot)]
        own, far, *halves = join([mine, *along], outs, (other[0], peak), bot)
        other += [swap(other[0], "fsdp"), swap(far, "dp")]
    else:
        own = lax.all_to_all(jnp.broadcast_to(mine[None], (n_fsdp, *mine.shape)), "fsdp", 0, 0, tiled=True)
        other, halves = [swap(own, "dp")], [own]
    exps, unit_a, total_a = scores(0, [own], weights)
    exps, unit_b, total_b = scores(1, [swap(half, "proto") for half in halves], weights, exps=exps)
    (other,) = join(other, [(0, n_fsdp, bot)], (total_b,), bot)
    exps, unit_c, total_c = scores(2, [other], weights, exps=exps)
    exps, unit_d, total = scores(3, [swap(other, "proto")], weights, (total_a, total_b, total_c), exps)
    total = add_up_chip_and_across(total)
    total = add_up_along(total)
    units = (unit_a, unit_b, unit_c, unit_d)
    student_grad = gradient(total, peak, unit, scale, units, exps)
    return (teacher_new, student_grad)


def solution(mesh):
    placed = (
        P(None, ("proto", "fsdp")),
        P(None, ("proto", "fsdp")),
        P("dp", "fsdp", None),
        P("dp", "fsdp", None),
        P("dp", "fsdp"),
        P("proto"),
    )
    return jax.shard_map(
        shards,
        mesh=mesh,
        in_specs=placed,
        out_specs=(P(None, ("proto", "fsdp")), P(None, ("proto", "fsdp", "dp"))),
        check_vma=False,
    )
```

```python
import functools
import math

import jax
import jax.numpy as jnp
from jax import lax
from jax.experimental import pallas as pl
from jax.experimental.pallas import tpu as pltpu
from jax.sharding import PartitionSpec as P

EPS = 1e-06
DEPTH = 256
GROUP = 512
STEP = 256
DIRECT = 8
LOG2E = math.log2(math.e)
GAIN_T = LOG2E / 0.04
GAIN_S = LOG2E / 0.1
LIMIT = 24 * 1024 * 1024
ON_CHIP = pl.BlockSpec(memory_space=pltpu.VMEM)
IN_HBM = pl.BlockSpec(memory_space=pl.ANY)


def shape(*dims, dtype=jnp.float32):
    return jax.ShapeDtypeStruct(dims, dtype)


def held(*dims, dtype=jnp.float32):
    return pltpu.VMEM(dims, dtype)


def call(kernel, name, out_shape, args, **more):
    many = isinstance(out_shape, (list, tuple))
    specs = dict(in_specs=[ON_CHIP] * len(args), out_specs=[ON_CHIP] * len(out_shape) if many else ON_CHIP)
    return pl.pallas_call(
        kernel,
        out_shape=out_shape,
        compiler_params=pltpu.CompilerParams(vmem_limit_bytes=LIMIT),
        cost_estimate=pl.CostEstimate(flops=1, bytes_accessed=1, transcendentals=0),
        name=name,
        **{**specs, **more},
    )(*args)


def swap(block, axis, apart=1):
    return lax.ppermute(block, axis, [(i, i ^ apart) for i in range(lax.axis_size(axis))])


def here():
    return lax.axis_index("dp"), lax.axis_index("fsdp"), lax.rem(lax.axis_index("proto"), 2)


def cast_split(row):
    high = row.astype(jnp.bfloat16).astype(jnp.float32)
    mid = (row - high).astype(jnp.bfloat16).astype(jnp.float32)
    return high, mid, row - high - mid


def prep_kernel(n_dp, teacher_hbm, student_hbm, center_hbm, new_hbm, wt_ref, ws_ref, unit_ref, scale_ref, peak_ref, *scratch):
    teacher_buf, student_buf, new_buf, center_buf, in_t, in_s, out, in_c = scratch
    chunks, bot, width = new_buf.shape
    n_own = chunks // n_dp
    dp, fsdp, _ = here()
    order = [*range(n_own - 1), *range(n_own, chunks), n_own - 1]
    own = n_own * width
    at = [slice(i * width, (i + 1) * width) for i in range(n_own)]
    firsts = [lax.rem(dp + i // n_own, n_dp) * own + i % n_own * width for i in range(chunks)]
    far = [pl.ds(pl.multiple_of(first, width), width) for first in firsts]
    start = pl.multiple_of((fsdp * n_dp + dp) * own, 128)
    center_load = pltpu.make_async_copy(center_hbm.at[:, pl.ds(start, own)], center_buf, in_c)
    loads = [
        (
            pltpu.make_async_copy(teacher_hbm.at[:, far[i]], teacher_buf.at[i], in_t.at[i]),
            pltpu.make_async_copy(student_hbm.at[:, far[i]], student_buf.at[i], in_s.at[i]),
        )
        for i in range(chunks)
    ]
    stores = [pltpu.make_async_copy(new_buf.at[i], new_hbm.at[:, far[i]], out.at[i]) for i in range(chunks)]
    center_load.start()
    for i in order:
        for load in loads[i]:
            load.start()
    center_load.wait()
    center = center_buf[...]
    peak = jnp.max(-center, axis=1, keepdims=True)
    peak_ref[...] = jnp.broadcast_to(peak, peak_ref.shape)
    splits = cast_split(-center - peak)
    row = lax.broadcasted_iota(jnp.int32, (DEPTH - bot, width), 0)
    zero = jnp.zeros((DEPTH - bot, width), jnp.float32)
    for i in order:
        for load in loads[i]:
            load.wait()
        student = student_buf[i]
        new = 0.994 * teacher_buf[i] + 0.006 * student
        new_buf[i] = new
        stores[i].start()
        if i >= n_own:
            continue
        high, mid, low = [part[:, at[i]] for part in splits]
        extra = jnp.where(row == 0, high, jnp.where(row == 1, mid, jnp.where(row == 2, low, zero)))
        scale = lax.rsqrt(jnp.sum(student * student, axis=0, keepdims=True) + EPS)
        unit_s = student * scale
        unit_t = new * lax.rsqrt(jnp.sum(new * new, axis=0, keepdims=True) + EPS)
        wt_ref[at[i], :] = jnp.concatenate([unit_t, extra], axis=0).astype(jnp.bfloat16).T
        ws_ref[at[i], :] = jnp.concatenate([unit_s, zero], axis=0).astype(jnp.bfloat16).T
        unit_ref[:, at[i]] = unit_s
        scale_ref[:, at[i]] = scale
    for store in stores:
        store.wait()


def prepare(teacher_weight, student_weight, center, n_dp):
    bot, cols = teacher_weight.shape
    own = cols // n_dp
    width = min(512, own)
    chunks = cols // width
    return call(
        functools.partial(prep_kernel, n_dp),
        "prep",
        [
            pltpu.HBM((bot, cols), jnp.float32),
            held(own, DEPTH, dtype=jnp.bfloat16),
            held(own, DEPTH, dtype=jnp.bfloat16),
            held(bot, own),
            held(1, own),
            held(1, 128),
        ],
        (teacher_weight, student_weight, center),
        in_specs=[IN_HBM] * 3,
        out_specs=[IN_HBM] + [ON_CHIP] * 5,
        scratch_shapes=[held(chunks, bot, width)] * 3
        + [held(1, own)]
        + [pltpu.SemaphoreType.DMA((chunks,))] * 3
        + [pltpu.SemaphoreType.DMA],
    )


def fetch_kernel(student_hbm, teacher_hbm, student_ref, teacher_ref, sems):
    half = student_ref.shape[1]
    side = pl.ds(pl.multiple_of(here()[2] * half, half), half)
    loads = [
        pltpu.make_async_copy(student_hbm.at[:, side], student_ref, sems.at[0]),
        pltpu.make_async_copy(teacher_hbm, teacher_ref, sems.at[1]),
    ]
    for load in loads:
        load.start()
    for load in loads:
        load.wait()


def fetch(student, teacher):
    bot, crops = student.shape
    return call(
        fetch_kernel,
        "fetch",
        [held(bot, crops // 2, dtype=jnp.bfloat16), held(bot, crops, dtype=jnp.bfloat16)],
        (student, teacher),
        in_specs=[IN_HBM] * 2,
        scratch_shapes=[pltpu.SemaphoreType.DMA((2,))],
    )


def normalize(values):
    return (values * lax.rsqrt(jnp.sum(values * values, axis=0, keepdims=True) + EPS)).astype(jnp.bfloat16)


def pack_kernel(student_ref, teacher_ref, index_ref, out_ref):
    half = out_ref.shape[2]
    lower = here()[2] == 0
    out_ref[0] = normalize(student_ref[...].astype(jnp.float32))
    index = jnp.where(lower, index_ref[:, :half], index_ref[:, half:])
    row = lax.broadcasted_iota(jnp.int32, (teacher_ref.shape[1], half), 0)
    pick = jnp.where(row == index, 1.0, 0.0).astype(jnp.bfloat16)
    out_ref[1] = normalize(jnp.dot(teacher_ref[...], pick, preferred_element_type=jnp.float32))


def pack(student, teacher, index):
    bot, half = student.shape
    return call(pack_kernel, "pack", held(2, bot, half, dtype=jnp.bfloat16), (student, teacher, index))


def join_kernel(n_in, n_after, firsts, bot, *refs):
    blocks = []
    for ref in refs[:n_in]:
        blocks += [ref] if len(ref.shape) == 3 else [ref.at[i] for i in range(ref.shape[0])]
    for first, ref in zip(firsts, refs[n_in + n_after:]):
        for i in range(ref.shape[0]):
            block = blocks[first + i][:, :bot, :]
            ref[i, :, :bot, :] = block
            if ref.shape[2] > bot:
                ref[i, :, bot:, :] = block[:, :ref.shape[2] - bot]


def join(parts, outs, after, bot):
    width = parts[0].shape[-1]
    shapes = [held(count, 2, rows, width, dtype=jnp.bfloat16) for _, count, rows in outs]
    kernel = functools.partial(join_kernel, len(parts), len(after), [first for first, _, _ in outs], bot)
    return call(kernel, "join", shapes, (*parts, *after), in_specs=[ON_CHIP] * len(parts) + [IN_HBM] * len(after))


def log_sum(parts):
    top = functools.reduce(jnp.maximum, parts)
    return top + jnp.log2(sum(jnp.exp2(part - top) for part in parts))


def combine(parts):
    half = parts[0].shape[0] // 2
    return sum(part[:half] for part in parts), log_sum([part[half:] for part in parts])


def slot(k, n):
    return lax.axis_index("fsdp") ^ k if n <= DIRECT else k


def score_kernel(part, n_feats, *refs):
    last = part == 3
    before, refs = (refs[:3], refs[3:]) if last else ((), refs)
    feats_refs, (ws_ref, wt_ref, peak_ref, *refs) = refs[:n_feats], refs[n_feats:]
    blocks = [ref.at[i] for ref in feats_refs for i in range(ref.shape[0])]
    exp_ref, unit_ref, total_ref, *mine = refs[1:] if part else refs
    own_ref = mine[0] if last else total_ref
    n, (_, bot, width) = len(blocks), blocks[0].shape
    cols = ws_ref.shape[0]
    step = min(STEP, cols)
    per = max(1, min(n, GROUP // width))
    row = lax.broadcasted_iota(jnp.int32, (DEPTH - bot, per * width), 0)
    for which, w_ref, gain in ((0, ws_ref, GAIN_S), (1, wt_ref, GAIN_T)):
        base = (2 * part + which) * n * width
        extra = jnp.where(row < 3 * which, 1.0, 0.0).astype(jnp.bfloat16)
        for group in range(n // per):
            unit = jnp.concatenate([blocks[group * per + k][which] for k in range(per)], axis=1)
            lanes = slice(group * per * width, (group + 1) * per * width)
            if which == 0:
                unit_ref[lanes, :] = unit.T
            stationary = jnp.concatenate([unit, extra], axis=0)
            total = jnp.zeros((8, per * width), jnp.float32)
            for at in range(0, cols, step):
                score = jnp.dot(w_ref[at:at + step, :], stationary, preferred_element_type=jnp.float32)
                exps = jnp.exp2(score * gain)
                total = total + jnp.sum(exps.reshape(step // 8, 8, per * width), axis=0)
                exp_ref[at:at + step, base + lanes.start:base + lanes.stop] = exps.astype(jnp.bfloat16)
            total = jnp.sum(total, axis=0, keepdims=True)
            if which == 1:
                total = jnp.log2(total) + GAIN_T * peak_ref[:, :1]
            own_ref[which:which + 1, lanes] = total
    if not last:
        return
    dp, _, core = here()
    own, pair, other = before
    parts = ((own, other), (pair, own_ref))
    rows = []
    for which in (0, 1):
        for half in (0, 1):
            pieces = []
            for view in (0, 1):
                first = (dp == view) if which == 0 else (dp != view)
                for place in range(n):
                    at = pl.ds(pl.multiple_of(slot(place, n) * width, width), width)
                    read = [[part[which:which + 1, at] for part in side] for side in parts]
                    mine, theirs = [jnp.where(first, *side) for side in read]
                    pieces.append(jnp.where(core == half, mine, theirs))
            rows.append(jnp.concatenate(pieces, axis=1))
    total_ref[...] = jnp.concatenate(rows, axis=0)


def scores(part, feats, weights, before=(), exps=None):
    _, _, bot, width = feats[0].shape
    cols, rows = weights[0].shape[0], sum(part.shape[0] for part in feats) * width
    args = (*before, *feats, *weights, *([exps] if part else []))
    return call(
        functools.partial(score_kernel, part, len(feats)),
        "scores",
        [
            held(cols, 8 * rows, dtype=jnp.bfloat16),
            held(rows, bot, dtype=jnp.bfloat16),
            held(4, 2 * rows) if part == 3 else held(2, rows),
        ],
        args,
        in_specs=[ON_CHIP] * (len(args) - bool(part)) + [IN_HBM] * bool(part),
        input_output_aliases={len(args) - 1: 0} if part else {},
        scratch_shapes=[held(2, rows)] if part == 3 else [],
    )


def relay_kernel(n_in, *refs):
    parts = [ref[...] for ref in refs[:n_in]]
    if len(parts[0].shape) == 3:
        parts = [parts[0][i] for i in range(parts[0].shape[0])]
    refs[-1][...] = jnp.concatenate(combine(parts), axis=0)


def add_up(parts):
    return call(functools.partial(relay_kernel, len(parts)), "relay", held(*parts[0].shape[-2:]), parts)


def exchange(total, axes, first, second):
    sizes = [lax.axis_size(axis) for axis in axes]
    proto = axes.index("proto")
    places = [(i, j) for i in range(sizes[0]) for j in range(sizes[1])]

    def permute(step):
        flat = lambda place: place[0] * sizes[1] + place[1]
        pairs = []
        for place in places:
            up = step(place[proto] % 2)
            pairs.append((flat(place), flat((place[0] ^ up[0], place[1] ^ up[1]))))
        return lax.ppermute(total, axes, pairs)

    mine = permute(first)
    return add_up([total, mine, swap(mine, "proto"), permute(second)])


def across(total, up, over):
    n_proto, n_dp = lax.axis_size("proto"), lax.axis_size("dp")
    places = [(p, d) for p in range(n_proto) for d in range(n_dp)]
    pairs = [(p * n_dp + d, (p ^ up) * n_dp + (d ^ over)) for p, d in places]
    return lax.ppermute(total, ("proto", "dp"), pairs)


def add_up_chip_and_across(total):
    n_proto, n_dp = lax.axis_size("proto"), lax.axis_size("dp")
    total = add_up([total, swap(total, "proto")])
    if n_proto == 4 and n_dp == 2:
        return exchange(total, ("proto", "dp"), lambda odd: (2, odd), lambda odd: (0, 1))
    steps = [(up, over) for up in range(0, n_proto, 2) for over in range(n_dp)][1:]
    return add_up([total, *[across(total, *step) for step in steps]])


def add_up_along(total):
    n = lax.axis_size("fsdp")
    if n == 4:
        return exchange(total, ("fsdp", "proto"), lambda odd: (1 + 2 * odd, 0), lambda odd: (2, 0))
    if n <= DIRECT:
        return add_up([total, *[swap(total, "fsdp", k) for k in range(1, n)]])
    return add_up([lax.all_to_all(jnp.broadcast_to(total[None], (n, *total.shape)), "fsdp", 0, 0, tiled=True)])


def grad_kernel(total_ref, peak_ref, weight_unit, weight_scale, *refs):
    units, exp_ref, out_hbm, scales, feats, *derivs, buf, sems = refs[:4], *refs[4:]
    dp, _, core = here()
    scales[0:2, :] = 10.0 / total_ref[0:2, :]
    scales[2:4, :] = 10.0 * jnp.exp2(GAIN_T * peak_ref[:, :1] - total_ref[2:4, :])
    rows = units[0].shape[0]
    width = 128
    n = rows // width
    factors = []
    for part in range(4):
        view, half = divmod(part, 2)
        base = (dp ^ view) * rows
        at = [pl.ds(pl.multiple_of(base + slot(k, n) * width, width), width) for k in range(n)]
        for which in (0, 1):
            picked = [
                jnp.where(core == half, scales[2 * which:2 * which + 1, where], scales[2 * which + 1:2 * which + 2, where])
                for where in at
            ]
            factors.append(jnp.concatenate(picked, axis=1).astype(jnp.bfloat16))
    for part, unit in enumerate(units):
        feats[part * rows:(part + 1) * rows, :] = unit[...]
    chunks, _, step = buf.shape
    stores = []

    def derive(i):
        at = slice(i * step, (i + 1) * step)
        for part in range(4):
            lies_s, lies_t = 2 * part * rows, (2 * (part ^ 2) + 1) * rows
            probs_s = exp_ref[at, lies_s:lies_s + rows] * factors[2 * part]
            probs_t = exp_ref[at, lies_t:lies_t + rows] * factors[2 * part + 1]
            derivs[i % 2][:, part * rows:(part + 1) * rows] = probs_s - probs_t

    derive(0)
    for i in range(chunks):
        if i + 1 < chunks:
            derive(i + 1)
        at = slice(i * step, (i + 1) * step)
        grad = jnp.dot(derivs[i % 2][...], feats[...], preferred_element_type=jnp.float32).T
        unit = weight_unit[:, at]
        proj = unit * jnp.sum(unit * grad, axis=0, keepdims=True)
        buf[i] = (grad - proj) * weight_scale[:, at]
        stores.append(pltpu.make_async_copy(buf.at[i], out_hbm.at[:, at], sems.at[i]))
        stores[i].start()
    for store in stores:
        store.wait()


def gradient(total, peak, weight_unit, weight_scale, units, exps):
    cols = exps.shape[0]
    rows, bot = units[0].shape
    step = min(256, cols)
    args = (total, peak, weight_unit, weight_scale, *units, exps)
    return call(
        grad_kernel,
        "gradient",
        pltpu.HBM((bot, cols), jnp.float32),
        args,
        out_specs=IN_HBM,
        scratch_shapes=[
            held(4, 2 * rows),
            held(4 * rows, bot, dtype=jnp.bfloat16),
            *[held(step, 4 * rows, dtype=jnp.bfloat16)] * 2,
            held(cols // step, bot, step),
            pltpu.SemaphoreType.DMA((cols // step,)),
        ],
    )


def shards(teacher_weight, student_weight, teacher_feats, student_feats, pairing, center):
    n_dp, n_fsdp = lax.axis_size("dp"), lax.axis_size("fsdp")
    in_hbm = lambda array: pltpu.with_memory_space_constraint(array, pltpu.HBM)
    teacher_weight, student_weight, center = in_hbm(teacher_weight), in_hbm(student_weight), in_hbm(center[None, :])

    index = swap(pairing, "dp")
    mine = pack(*fetch(in_hbm(student_feats[0].T), in_hbm(teacher_feats[0].T)), index)
    teacher_new, wt, ws, unit, scale, peak = prepare(teacher_weight, student_weight, center, n_dp)
    weights = (ws, wt, peak)
    bot = mine.shape[1]
    if n_fsdp <= DIRECT:
        other = [swap(mine, "dp")]
        along = [swap(mine, "fsdp", k) for k in range(1, n_fsdp)]
        half = n_fsdp // 2
        outs = [(0, n_fsdp, bot), (2, n_fsdp - 2, bot + 16), (0, half, bot), (half, half, bot)]
        own, far, *halves = join([mine, *along], outs, (other[0], peak), bot)
        other += [swap(other[0], "fsdp"), swap(far, "dp")]
    else:
        own = lax.all_to_all(jnp.broadcast_to(mine[None], (n_fsdp, *mine.shape)), "fsdp", 0, 0, tiled=True)
        other, halves = [swap(own, "dp")], [own]
    exps, unit_a, total_a = scores(0, [own], weights)
    exps, unit_b, total_b = scores(1, [swap(half, "proto") for half in halves], weights, exps=exps)
    (other,) = join(other, [(0, n_fsdp, bot)], (total_b,), bot)
    exps, unit_c, total_c = scores(2, [other], weights, exps=exps)
    exps, unit_d, total = scores(3, [swap(other, "proto")], weights, (total_a, total_b, total_c), exps)
    total = add_up_chip_and_across(total)
    total = add_up_along(total)
    units = (unit_a, unit_b, unit_c, unit_d)
    student_grad = gradient(total, peak, unit, scale, units, exps)
    return (teacher_new, student_grad)


def solution(mesh):
    placed = (
        P(None, ("proto", "fsdp")),
        P(None, ("proto", "fsdp")),
        P("dp", "fsdp", None),
        P("dp", "fsdp", None),
        P("dp", "fsdp"),
        P("proto"),
    )
    return jax.shard_map(
        shards,
        mesh=mesh,
        in_specs=placed,
        out_specs=(P(None, ("proto", "fsdp")), P(None, ("proto", "fsdp", "dp"))),
        check_vma=False,
    )
```

```python
import functools
import math

import jax
import jax.numpy as jnp
from jax import lax
from jax.experimental import pallas as pl
from jax.experimental.pallas import tpu as pltpu
from jax.sharding import PartitionSpec as P

EPS = 1e-06
DEPTH = 256
GROUP = 512
STEP = 256
DIRECT = 8
LOG2E = math.log2(math.e)
GAIN_T = LOG2E / 0.04
GAIN_S = LOG2E / 0.1
LIMIT = 24 * 1024 * 1024
ON_CHIP = pl.BlockSpec(memory_space=pltpu.VMEM)
IN_HBM = pl.BlockSpec(memory_space=pl.ANY)


def shape(*dims, dtype=jnp.float32):
    return jax.ShapeDtypeStruct(dims, dtype)


def held(*dims, dtype=jnp.float32):
    return pltpu.VMEM(dims, dtype)


def call(kernel, name, out_shape, args, **more):
    many = isinstance(out_shape, (list, tuple))
    specs = dict(in_specs=[ON_CHIP] * len(args), out_specs=[ON_CHIP] * len(out_shape) if many else ON_CHIP)
    return pl.pallas_call(
        kernel,
        out_shape=out_shape,
        compiler_params=pltpu.CompilerParams(vmem_limit_bytes=LIMIT),
        cost_estimate=pl.CostEstimate(flops=1, bytes_accessed=1, transcendentals=0),
        name=name,
        **{**specs, **more},
    )(*args)


def swap(block, axis, apart=1):
    return lax.ppermute(block, axis, [(i, i ^ apart) for i in range(lax.axis_size(axis))])


def here():
    return lax.axis_index("dp"), lax.axis_index("fsdp"), lax.rem(lax.axis_index("proto"), 2)


def cast_split(row):
    high = row.astype(jnp.bfloat16).astype(jnp.float32)
    mid = (row - high).astype(jnp.bfloat16).astype(jnp.float32)
    return high, mid, row - high - mid


def prep_kernel(n_dp, teacher_hbm, student_hbm, center_hbm, new_hbm, wt_ref, ws_ref, unit_ref, scale_ref, peak_ref, *scratch):
    teacher_buf, student_buf, new_buf, center_buf, in_t, in_s, out, in_c = scratch
    chunks, bot, width = new_buf.shape
    n_own = chunks // n_dp
    dp, fsdp, _ = here()
    order = [*range(n_own - 1), *range(n_own, chunks), n_own - 1]
    own = n_own * width
    at = [slice(i * width, (i + 1) * width) for i in range(n_own)]
    firsts = [lax.rem(dp + i // n_own, n_dp) * own + i % n_own * width for i in range(chunks)]
    far = [pl.ds(pl.multiple_of(first, width), width) for first in firsts]
    start = pl.multiple_of((fsdp * n_dp + dp) * own, 128)
    center_load = pltpu.make_async_copy(center_hbm.at[:, pl.ds(start, own)], center_buf, in_c)
    loads = [
        (
            pltpu.make_async_copy(teacher_hbm.at[:, far[i]], teacher_buf.at[i], in_t.at[i]),
            pltpu.make_async_copy(student_hbm.at[:, far[i]], student_buf.at[i], in_s.at[i]),
        )
        for i in range(chunks)
    ]
    stores = [pltpu.make_async_copy(new_buf.at[i], new_hbm.at[:, far[i]], out.at[i]) for i in range(chunks)]
    center_load.start()
    for i in order:
        for load in loads[i]:
            load.start()
    center_load.wait()
    center = center_buf[...]
    peak = jnp.max(-center, axis=1, keepdims=True)
    peak_ref[...] = jnp.broadcast_to(peak, peak_ref.shape)
    splits = cast_split(-center - peak)
    row = lax.broadcasted_iota(jnp.int32, (DEPTH - bot, width), 0)
    zero = jnp.zeros((DEPTH - bot, width), jnp.float32)
    for i in order:
        for load in loads[i]:
            load.wait()
        student = student_buf[i]
        new = 0.994 * teacher_buf[i] + 0.006 * student
        new_buf[i] = new
        stores[i].start()
        if i >= n_own:
            continue
        high, mid, low = [part[:, at[i]] for part in splits]
        extra = jnp.where(row == 0, high, jnp.where(row == 1, mid, jnp.where(row == 2, low, zero)))
        scale = lax.rsqrt(jnp.sum(student * student, axis=0, keepdims=True) + EPS)
        unit_s = student * scale
        unit_t = new * lax.rsqrt(jnp.sum(new * new, axis=0, keepdims=True) + EPS)
        wt_ref[at[i], :] = jnp.concatenate([unit_t, extra], axis=0).astype(jnp.bfloat16).T
        ws_ref[at[i], :] = jnp.concatenate([unit_s, zero], axis=0).astype(jnp.bfloat16).T
        unit_ref[:, at[i]] = unit_s
        scale_ref[:, at[i]] = scale
    for store in stores:
        store.wait()


def prepare(teacher_weight, student_weight, center, n_dp):
    bot, cols = teacher_weight.shape
    own = cols // n_dp
    width = min(512, own)
    chunks = cols // width
    return call(
        functools.partial(prep_kernel, n_dp),
        "prep",
        [
            pltpu.HBM((bot, cols), jnp.float32),
            held(own, DEPTH, dtype=jnp.bfloat16),
            held(own, DEPTH, dtype=jnp.bfloat16),
            held(bot, own),
            held(1, own),
            held(1, 128),
        ],
        (teacher_weight, student_weight, center),
        in_specs=[IN_HBM] * 3,
        out_specs=[IN_HBM] + [ON_CHIP] * 5,
        scratch_shapes=[held(chunks, bot, width)] * 3
        + [held(1, own)]
        + [pltpu.SemaphoreType.DMA((chunks,))] * 3
        + [pltpu.SemaphoreType.DMA],
    )


def fetch_kernel(student_hbm, teacher_hbm, student_ref, teacher_ref, sems):
    half = student_ref.shape[1]
    side = pl.ds(pl.multiple_of(here()[2] * half, half), half)
    loads = [
        pltpu.make_async_copy(student_hbm.at[:, side], student_ref, sems.at[0]),
        pltpu.make_async_copy(teacher_hbm, teacher_ref, sems.at[1]),
    ]
    for load in loads:
        load.start()
    for load in loads:
        load.wait()


def fetch(student, teacher):
    bot, crops = student.shape
    return call(
        fetch_kernel,
        "fetch",
        [held(bot, crops // 2, dtype=jnp.bfloat16), held(bot, crops, dtype=jnp.bfloat16)],
        (student, teacher),
        in_specs=[IN_HBM] * 2,
        scratch_shapes=[pltpu.SemaphoreType.DMA((2,))],
    )


def normalize(values):
    return (values * lax.rsqrt(jnp.sum(values * values, axis=0, keepdims=True) + EPS)).astype(jnp.bfloat16)


def pack_kernel(student_ref, teacher_ref, index_ref, out_ref):
    half = out_ref.shape[2]
    lower = here()[2] == 0
    out_ref[0] = normalize(student_ref[...].astype(jnp.float32))
    index = jnp.where(lower, index_ref[:, :half], index_ref[:, half:])
    row = lax.broadcasted_iota(jnp.int32, (teacher_ref.shape[1], half), 0)
    pick = jnp.where(row == index, 1.0, 0.0).astype(jnp.bfloat16)
    out_ref[1] = normalize(jnp.dot(teacher_ref[...], pick, preferred_element_type=jnp.float32))


def pack(student, teacher, index):
    bot, half = student.shape
    return call(pack_kernel, "pack", held(2, bot, half, dtype=jnp.bfloat16), (student, teacher, index))


def join_kernel(n_in, n_after, firsts, bot, *refs):
    blocks = []
    for ref in refs[:n_in]:
        blocks += [ref] if len(ref.shape) == 3 else [ref.at[i] for i in range(ref.shape[0])]
    for first, ref in zip(firsts, refs[n_in + n_after:]):
        for i in range(ref.shape[0]):
            block = blocks[first + i][:, :bot, :]
            ref[i, :, :bot, :] = block
            if ref.shape[2] > bot:
                ref[i, :, bot:, :] = block[:, :ref.shape[2] - bot]


def join(parts, outs, after, bot):
    width = parts[0].shape[-1]
    shapes = [held(count, 2, rows, width, dtype=jnp.bfloat16) for _, count, rows in outs]
    kernel = functools.partial(join_kernel, len(parts), len(after), [first for first, _, _ in outs], bot)
    return call(kernel, "join", shapes, (*parts, *after), in_specs=[ON_CHIP] * len(parts) + [IN_HBM] * len(after))


def log_sum(parts):
    top = functools.reduce(jnp.maximum, parts)
    return top + jnp.log2(sum(jnp.exp2(part - top) for part in parts))


def combine(parts):
    half = parts[0].shape[0] // 2
    return sum(part[:half] for part in parts), log_sum([part[half:] for part in parts])


def slot(k, n):
    return lax.axis_index("fsdp") ^ k if n <= DIRECT else k


def score_kernel(part, n_feats, *refs):
    last = part == 3
    before, refs = (refs[:3], refs[3:]) if last else ((), refs)
    feats_refs, (ws_ref, wt_ref, peak_ref, *refs) = refs[:n_feats], refs[n_feats:]
    blocks = [ref.at[i] for ref in feats_refs for i in range(ref.shape[0])]
    exp_ref, unit_ref, total_ref, *mine = refs[1:] if part else refs
    own_ref = mine[0] if last else total_ref
    n, (_, bot, width) = len(blocks), blocks[0].shape
    cols = ws_ref.shape[0]
    step = min(STEP, cols)
    per = max(1, min(n, GROUP // width))
    row = lax.broadcasted_iota(jnp.int32, (DEPTH - bot, per * width), 0)
    for which, w_ref, gain in ((0, ws_ref, GAIN_S), (1, wt_ref, GAIN_T)):
        base = (2 * part + which) * n * width
        extra = jnp.where(row < 3 * which, 1.0, 0.0).astype(jnp.bfloat16)
        for group in range(n // per):
            unit = jnp.concatenate([blocks[group * per + k][which] for k in range(per)], axis=1)
            lanes = slice(group * per * width, (group + 1) * per * width)
            if which == 0:
                unit_ref[lanes, :] = unit.T
            stationary = jnp.concatenate([unit, extra], axis=0)
            total = jnp.zeros((8, per * width), jnp.float32)
            for at in range(0, cols, step):
                score = jnp.dot(w_ref[at:at + step, :], stationary, preferred_element_type=jnp.float32)
                exps = jnp.exp2(score * gain)
                total = total + jnp.sum(exps.reshape(step // 8, 8, per * width), axis=0)
                exp_ref[at:at + step, base + lanes.start:base + lanes.stop] = exps.astype(jnp.bfloat16)
            total = jnp.sum(total, axis=0, keepdims=True)
            if which == 1:
                total = jnp.log2(total) + GAIN_T * peak_ref[:, :1]
            own_ref[which:which + 1, lanes] = total
    if not last:
        return
    dp, _, core = here()
    own, pair, other = before
    parts = ((own, other), (pair, own_ref))
    rows = []
    for which in (0, 1):
        for half in (0, 1):
            pieces = []
            for view in (0, 1):
                first = (dp == view) if which == 0 else (dp != view)
                for place in range(n):
                    at = pl.ds(pl.multiple_of(slot(place, n) * width, width), width)
                    read = [[part[which:which + 1, at] for part in side] for side in parts]
                    mine, theirs = [jnp.where(first, *side) for side in read]
                    pieces.append(jnp.where(core == half, mine, theirs))
            rows.append(jnp.concatenate(pieces, axis=1))
    total_ref[...] = jnp.concatenate(rows, axis=0)


def scores(part, feats, weights, before=(), exps=None):
    _, _, bot, width = feats[0].shape
    cols, rows = weights[0].shape[0], sum(part.shape[0] for part in feats) * width
    args = (*before, *feats, *weights, *([exps] if part else []))
    return call(
        functools.partial(score_kernel, part, len(feats)),
        "scores",
        [
            held(cols, 8 * rows, dtype=jnp.bfloat16),
            held(rows, bot, dtype=jnp.bfloat16),
            held(4, 2 * rows) if part == 3 else held(2, rows),
        ],
        args,
        in_specs=[ON_CHIP] * (len(args) - bool(part)) + [IN_HBM] * bool(part),
        input_output_aliases={len(args) - 1: 0} if part else {},
        scratch_shapes=[held(2, rows)] if part == 3 else [],
    )


def relay_kernel(n_in, *refs):
    parts = [ref[...] for ref in refs[:n_in]]
    if len(parts[0].shape) == 3:
        parts = [parts[0][i] for i in range(parts[0].shape[0])]
    refs[-1][...] = jnp.concatenate(combine(parts), axis=0)


def add_up(parts):
    return call(functools.partial(relay_kernel, len(parts)), "relay", held(*parts[0].shape[-2:]), parts)


def exchange(total, axes, first, second):
    sizes = [lax.axis_size(axis) for axis in axes]
    proto = axes.index("proto")
    places = [(i, j) for i in range(sizes[0]) for j in range(sizes[1])]

    def permute(step):
        flat = lambda place: place[0] * sizes[1] + place[1]
        pairs = []
        for place in places:
            up = step(place[proto] % 2)
            pairs.append((flat(place), flat((place[0] ^ up[0], place[1] ^ up[1]))))
        return lax.ppermute(total, axes, pairs)

    mine = permute(first)
    return add_up([total, mine, swap(mine, "proto"), permute(second)])


def across(total, up, over):
    n_proto, n_dp = lax.axis_size("proto"), lax.axis_size("dp")
    places = [(p, d) for p in range(n_proto) for d in range(n_dp)]
    pairs = [(p * n_dp + d, (p ^ up) * n_dp + (d ^ over)) for p, d in places]
    return lax.ppermute(total, ("proto", "dp"), pairs)


def add_up_chip(total):
    return add_up([total, swap(total, "proto")])


def add_up_across(total):
    n_proto, n_dp = lax.axis_size("proto"), lax.axis_size("dp")
    if n_proto == 4 and n_dp == 2:
        return exchange(total, ("proto", "dp"), lambda odd: (2 * odd, 1), lambda odd: (2, 0))
    steps = [(up, over) for up in range(0, n_proto, 2) for over in range(n_dp)][1:]
    return add_up([total, *[across(total, *step) for step in steps]])


def add_up_along(total):
    n = lax.axis_size("fsdp")
    if n == 4:
        return exchange(total, ("fsdp", "proto"), lambda odd: (1 + 2 * odd, 0), lambda odd: (2, 0))
    if n <= DIRECT:
        return add_up([total, *[swap(total, "fsdp", k) for k in range(1, n)]])
    return add_up([lax.all_to_all(jnp.broadcast_to(total[None], (n, *total.shape)), "fsdp", 0, 0, tiled=True)])


def grad_kernel(total_ref, peak_ref, weight_unit, weight_scale, *refs):
    units, exp_ref, out_hbm, scales, feats, *derivs, buf, sems = refs[:4], *refs[4:]
    dp, _, core = here()
    scales[0:2, :] = 10.0 / total_ref[0:2, :]
    scales[2:4, :] = 10.0 * jnp.exp2(GAIN_T * peak_ref[:, :1] - total_ref[2:4, :])
    rows = units[0].shape[0]
    width = 128
    n = rows // width
    factors = []
    for part in range(4):
        view, half = divmod(part, 2)
        base = (dp ^ view) * rows
        at = [pl.ds(pl.multiple_of(base + slot(k, n) * width, width), width) for k in range(n)]
        for which in (0, 1):
            picked = [
                jnp.where(core == half, scales[2 * which:2 * which + 1, where], scales[2 * which + 1:2 * which + 2, where])
                for where in at
            ]
            factors.append(jnp.concatenate(picked, axis=1).astype(jnp.bfloat16))
    for part, unit in enumerate(units):
        feats[part * rows:(part + 1) * rows, :] = unit[...]
    chunks, _, step = buf.shape
    stores = []

    def derive(i):
        at = slice(i * step, (i + 1) * step)
        for part in range(4):
            lies_s, lies_t = 2 * part * rows, (2 * (part ^ 2) + 1) * rows
            probs_s = exp_ref[at, lies_s:lies_s + rows] * factors[2 * part]
            probs_t = exp_ref[at, lies_t:lies_t + rows] * factors[2 * part + 1]
            derivs[i % 2][:, part * rows:(part + 1) * rows] = probs_s - probs_t

    derive(0)
    for i in range(chunks):
        if i + 1 < chunks:
            derive(i + 1)
        at = slice(i * step, (i + 1) * step)
        grad = jnp.dot(derivs[i % 2][...], feats[...], preferred_element_type=jnp.float32).T
        unit = weight_unit[:, at]
        proj = unit * jnp.sum(unit * grad, axis=0, keepdims=True)
        buf[i] = (grad - proj) * weight_scale[:, at]
        stores.append(pltpu.make_async_copy(buf.at[i], out_hbm.at[:, at], sems.at[i]))
        stores[i].start()
    for store in stores:
        store.wait()


def gradient(total, peak, weight_unit, weight_scale, units, exps):
    cols = exps.shape[0]
    rows, bot = units[0].shape
    step = min(256, cols)
    args = (total, peak, weight_unit, weight_scale, *units, exps)
    return call(
        grad_kernel,
        "gradient",
        pltpu.HBM((bot, cols), jnp.float32),
        args,
        out_specs=IN_HBM,
        scratch_shapes=[
            held(4, 2 * rows),
            held(4 * rows, bot, dtype=jnp.bfloat16),
            *[held(step, 4 * rows, dtype=jnp.bfloat16)] * 2,
            held(cols // step, bot, step),
            pltpu.SemaphoreType.DMA((cols // step,)),
        ],
    )


def shards(teacher_weight, student_weight, teacher_feats, student_feats, pairing, center):
    n_dp, n_fsdp = lax.axis_size("dp"), lax.axis_size("fsdp")
    in_hbm = lambda array: pltpu.with_memory_space_constraint(array, pltpu.HBM)
    teacher_weight, student_weight, center = in_hbm(teacher_weight), in_hbm(student_weight), in_hbm(center[None, :])

    index = swap(pairing, "dp")
    mine = pack(*fetch(in_hbm(student_feats[0].T), in_hbm(teacher_feats[0].T)), index)
    teacher_new, wt, ws, unit, scale, peak = prepare(teacher_weight, student_weight, center, n_dp)
    weights = (ws, wt, peak)
    bot = mine.shape[1]
    if n_fsdp <= DIRECT:
        other = [swap(mine, "dp")]
        along = [swap(mine, "fsdp", k) for k in range(1, n_fsdp)]
        half = n_fsdp // 2
        outs = [(0, n_fsdp, bot), (2, n_fsdp - 2, bot + 16), (0, half, bot), (half, half, bot)]
        own, far, *halves = join([mine, *along], outs, (other[0], peak), bot)
        other += [swap(other[0], "fsdp"), swap(far, "dp")]
    else:
        own = lax.all_to_all(jnp.broadcast_to(mine[None], (n_fsdp, *mine.shape)), "fsdp", 0, 0, tiled=True)
        other, halves = [swap(own, "dp")], [own]
    exps, unit_a, total_a = scores(0, [own], weights)
    exps, unit_b, total_b = scores(1, [swap(half, "proto") for half in halves], weights, exps=exps)
    (other,) = join(other, [(0, n_fsdp, bot)], (total_b,), bot)
    exps, unit_c, total_c = scores(2, [other], weights, exps=exps)
    exps, unit_d, total = scores(3, [swap(other, "proto")], weights, (total_a, total_b, total_c), exps)
    total = add_up_across(add_up_along(add_up_chip(total)))
    units = (unit_a, unit_b, unit_c, unit_d)
    student_grad = gradient(total, peak, unit, scale, units, exps)
    return (teacher_new, student_grad)


def solution(mesh):
    placed = (
        P(None, ("proto", "fsdp")),
        P(None, ("proto", "fsdp")),
        P("dp", "fsdp", None),
        P("dp", "fsdp", None),
        P("dp", "fsdp"),
        P("proto"),
    )
    return jax.shard_map(
        shards,
        mesh=mesh,
        in_specs=placed,
        out_specs=(P(None, ("proto", "fsdp")), P(None, ("proto", "fsdp", "dp"))),
        check_vma=False,
    )
```
